32 devices in a mesh: orb: 8 (over z, x), grp: 4 (over y, core).
Axes of the slice: x: 2, y: 2, z: 4, core: 2. Of those that a mesh axis runs over, the one named last changes fastest.
Arguments:
- orbitals: float32 [64, 48, 2304], P(('orb', 'grp')), may hold values from -6 to 6
- kernel: float32 [48, 2304], replicated, may hold values from 0.1 to 2
- anchors: int32 [8, 3], replicated, may hold values from 0 to 16
- pair_count: int32 [8], P('orb'), may hold values from 1 to 8, 32 in all
- pair_first: int32 [64], P('orb'), may hold values from 0 to 7
- pair_second: int32 [64], P('orb'), may hold values from 0 to 7
- pair_reach: int32 [64], P('orb'), may hold values from 0 to 2
Outputs:
- gradient: float32 [64, 48, 2304], P('orb', 'grp')
- lagrange: float32 [8, 8, 8], P('orb')
The draws below stay inside these ranges and needn't reach their ends.
Inputs may be any that keep to these rules, and one draw needn't show every extreme that they name: The live slots of a fragment are its first pair_count slots; some fragment has all 8 live.
All inputs are finite; a program needn't handle non-finite values. No bound on the sum of `pair_count` on one device may be relied on, other than what follows from the above.
Results may differ from the reference program's by a relative error of at most 0.0003.
Values sent between devices are 32-bit elements; how exact they have to be, the bound alone decides.
No kernel may reach another device: no remote copies, remote signals or barrier semaphores. Data moves between devices by JAX's collectives and lax.ppermute only.
A program may use at most 128 MiB of HBM per device.

```python
import math
import jax
import jax.numpy as jnp
import numpy as np
from jax import lax

B = 48
ORB_DEV = 2
PF = 8
REACH = 2
FRAG_ORB = 8
ORB = 64
SHIFT_MAX = 16
N_ORB = 8
N_GRP = 4


def touch_ends(drawn, stream_key, smallest, high):
    index_at = [jax.random.randint(jax.random.fold_in(stream_key, axis), (), 0, length) for axis, length in enumerate(drawn.shape)]
    longest = drawn.shape.index(max(drawn.shape))
    next_to = index_at[:longest] + [(index_at[longest] + 1) % drawn.shape[longest]] + index_at[longest + 1:]
    return drawn.at[tuple(index_at)].set(smallest).at[tuple(next_to)].set(high)


def block_scale(rng, extent, pieces, least, high):
    gain, own = 1.0, jax.random.fold_in(rng, 6)
    for position, parts in pieces:
        heights = jnp.exp(jax.random.uniform(jax.random.fold_in(own, position), (parts,), jnp.float32, least / len(pieces), high / len(pieces)))
        gain = gain * jnp.repeat(heights, extent[position] // parts).reshape([-1 if axis == position else 1 for axis in range(len(extent))])
    return gain


def length_profile(amount, total, most, skew):
    portions = [(1 << 20) // math.isqrt(standing ** skew) + 1 for standing in range(2, amount + 1)]
    spare, counts = total - most - (amount - 1), [1] * (amount - 1)
    while spare > 0:
        free = [i for i in range(amount - 1) if counts[i] < most]
        pool, left = sum([portions[i] for i in free]), spare
        for i in free:
            extra = min(most - counts[i], max(1, left * portions[i] // pool), spare)
            counts[i] = counts[i] + extra
            spare = spare - extra
    return np.array([most] + counts)


def ragged(own_key, count, total, bound, skew):
    if count == 2:
        one = jax.random.randint(own_key, (), max(1, total - bound), min(bound, total - 1) + 1)
        return jnp.stack([one, total - one])
    sizes = jnp.asarray(length_profile(count, total, bound, skew), jnp.int32)
    couples = (count - 1) // 2
    giver, receiver = sizes[1:1 + 2 * couples:2], sizes[2:2 + 2 * couples:2]
    slack = jnp.minimum(giver - 1, bound - receiver)
    shifted = jax.random.randint(jax.random.fold_in(own_key, 1), (couples,), 0, 1 << 20) % (slack + 1)
    sizes = sizes.at[1:1 + 2 * couples:2].set(giver - shifted).at[2:2 + 2 * couples:2].set(receiver + shifted)
    return sizes[jax.random.permutation(jax.random.fold_in(own_key, 2), count)]


def normal_values(rng, extent, deviation, most, shards=(), kind=jnp.bfloat16):
    entries = deviation * jax.random.normal(rng, extent, jnp.float32)
    if shards:
        entries = entries * block_scale(rng, extent, shards, -0.22, 0.18)
    return jnp.clip(entries, -most, most).astype(kind)


def setup_inputs(seed: int = 0) -> dict:
    arg_keys = jax.random.split(jax.random.key(seed), 8)
    orbitals = normal_values(arg_keys[0], (ORB, B, B * B), 1.0, 6.0, ((0, 32),), jnp.float32)
    kernel = jnp.clip(jnp.exp(jax.random.uniform(arg_keys[1], (B, B * B), jnp.float32, math.log(0.1), math.log(2.0))), 0.1, 2.0)
    anchors = touch_ends(jax.random.randint(arg_keys[2], (N_ORB, 3), 0, SHIFT_MAX + 1), jax.random.fold_in(arg_keys[2], 1), 0, SHIFT_MAX).astype(jnp.int32)
    pair_count = ragged(arg_keys[3], N_ORB, N_ORB * PF // 2, PF, 2).astype(jnp.int32)
    pair_first = touch_ends(jax.random.randint(arg_keys[4], (N_ORB * PF,), 0, FRAG_ORB), jax.random.fold_in(arg_keys[4], 1), 0, FRAG_ORB - 1).astype(jnp.int32)
    pair_second = touch_ends(jax.random.randint(arg_keys[5], (N_ORB * PF,), 0, FRAG_ORB), jax.random.fold_in(arg_keys[5], 1), 0, FRAG_ORB - 1).astype(jnp.int32)
    pair_reach = touch_ends(jax.random.randint(arg_keys[6], (N_ORB * PF,), 0, REACH + 1), jax.random.fold_in(arg_keys[6], 1), 0, REACH).astype(jnp.int32)
    return dict(orbitals=orbitals, kernel=kernel, anchors=anchors, pair_count=pair_count, pair_first=pair_first, pair_second=pair_second, pair_reach=pair_reach)


def offset_matrix(offset, count):
    rows = jnp.arange(count, dtype=jnp.int32)
    return (rows[None, :] == rows[:, None] - offset).astype(jnp.float32)


def cycle(matrices, volume):
    box_edge = volume.shape[0]
    for matrix in matrices:
        product = jnp.dot(matrix, volume, precision=lax.Precision.HIGHEST, preferred_element_type=jnp.float32)
        volume = product.reshape(box_edge, box_edge, box_edge).transpose(1, 2, 0).reshape(box_edge, box_edge * box_edge)
    return volume


def reference(orbitals, kernel, anchors, pair_count, pair_first, pair_second, pair_reach):
    frag_size = ORB_DEV * N_GRP
    cube = kernel.reshape(B, B, B)

    def solve(accum, slot):
        fragment = slot // PF
        within = slot % PF
        first = pair_first[slot]
        second = pair_second[slot]
        reach = pair_reach[slot]
        partner = (fragment + reach) % N_ORB
        index_first = (fragment * frag_size + first).astype(jnp.int32)
        index_second = (partner * frag_size + second).astype(jnp.int32)
        delta = anchors[partner] - anchors[fragment]
        matrices = [offset_matrix(delta[0], B), offset_matrix(delta[1], B), offset_matrix(delta[2], B)]
        phi_first = orbitals[index_first]
        phi_second = orbitals[index_second]
        moved = cycle(matrices, phi_second)
        density = phi_first * moved
        spectrum = jnp.fft.fftn(density.reshape(B, B, B))
        potential = jnp.real(jnp.fft.ifftn(cube * spectrum)).astype(jnp.float32).reshape(B, B * B)
        weight = (within < pair_count[fragment]).astype(jnp.float32)
        accum = accum.at[index_first].add(weight * potential * moved)
        back = cycle([matrix.T for matrix in matrices], potential * phi_first)
        accum = accum.at[index_second].add(weight * back)
        return accum, None

    start = jnp.zeros(orbitals.shape, jnp.float32)
    action, _ = lax.scan(solve, start, jnp.arange(N_ORB * PF, dtype=jnp.int32))
    phi = orbitals.reshape(N_ORB, frag_size, B * B * B)
    acted = action.reshape(N_ORB, frag_size, B * B * B)
    correlation = jnp.einsum('fan,fbn->fab', phi, acted, precision=lax.Precision.HIGHEST) / (B ** 3)
    lagrange = 0.5 * (correlation + jnp.swapaxes(correlation, 1, 2))
    gradient = acted - jnp.einsum('fba,fbn->fan', lagrange, phi, precision=lax.Precision.HIGHEST)
    return gradient.reshape(orbitals.shape), lagrange
```

```python
import functools
import math

import jax
import jax.numpy as jnp
import numpy as np
from jax import lax
from jax.experimental import pallas as pl
from jax.experimental.pallas import tpu as pltpu
from jax.sharding import PartitionSpec as P

REACH = 2
LANES = 128
ROWS = 8
HALF = LANES // 2


def factor(n):
    for p in (4, 2, 3, 5, 7):
        if n % p == 0 and n > p:
            power = 1
            while n % p == 0:
                n //= p
                power *= p
            return power, n
    return n, 1


class Lanes:
    def __init__(self, sign):
        lane = lax.broadcasted_iota(jnp.int32, (ROWS, LANES), 1)
        self.turned = jnp.where(lane < HALF, -1.0, 1.0).astype(jnp.float32)
        self.sign = sign

    def times(self, value, angle):
        real, imag = math.cos(angle), math.sin(angle)
        if abs(imag) < 1e-12:
            return value if real > 0 else -value
        swapped = pltpu.roll(value, HALF, 1)
        if abs(real) < 1e-12:
            return swapped * (self.turned * imag)
        return value * real + swapped * (self.turned * imag)

    def dft(self, values):
        n = len(values)
        if n == 1:
            return values
        if n == 2:
            return [values[0] + values[1], values[0] - values[1]]
        if n == 3:
            a, b, c = values
            total = b + c
            middle = a - 0.5 * total
            side = pltpu.roll(b - c, HALF, 1) * (self.turned * (self.sign * math.sqrt(0.75)))
            return [a + total, middle + side, middle - side]
        if n == 4:
            a, b, c, d = values
            s, t, u = a + c, a - c, b + d
            v = pltpu.roll(b - d, HALF, 1) * (self.turned * float(self.sign))
            return [s + u, t + v, s - u, t - v]
        first, second = factor(n)
        if second > 1:
            out = [None] * n
            columns = []
            for j in range(second):
                columns.append(self.dft([values[(i * second + j * first) % n] for i in range(first)]))
            for i in range(first):
                row = self.dft([columns[j][i] for j in range(second)])
                for j in range(second):
                    k = next(k for k in range(n) if k % first == i and k % second == j)
                    out[k] = row[j]
            return out
        for p in (4, 2, 3, 5, 7):
            if n % p == 0 and n > p:
                rest = n // p
                columns = [self.dft(values[j::p]) for j in range(p)]
                out = [None] * n
                for i in range(rest):
                    turned = [
                        self.times(columns[j][i], self.sign * 2.0 * math.pi * i * j / n)
                        for j in range(p)
                    ]
                    row = self.dft(turned)
                    for j in range(p):
                        out[i + rest * j] = row[j]
                return out
        out = []
        for k in range(n):
            total = values[0]
            for j in range(1, n):
                total = total + self.times(values[j], self.sign * 2.0 * math.pi * (j * k % n) / n)
            out.append(total)
        return out


def lane_matrices(edge):
    index = np.arange(edge)
    angles = 2.0 * np.pi / edge * (np.outer(index, index) % edge)
    found = []
    for sign in (-1.0, 1.0):
        cosine, sine = np.cos(angles), sign * np.sin(angles)
        full = np.zeros((LANES, LANES))
        full[:edge, :edge] = cosine
        full[:edge, HALF : HALF + edge] = sine
        full[HALF : HALF + edge, :edge] = -sine
        full[HALF : HALF + edge, HALF : HALF + edge] = cosine
        high = full.astype(jnp.bfloat16)
        low = (full - high.astype(np.float64)).astype(jnp.bfloat16)
        both = np.concatenate([high, low], axis=1)
        found.append(np.concatenate([both, both], axis=0))
    return found


def split_dot(value, matrix):
    high = value.astype(jnp.bfloat16)
    low = (value - high.astype(jnp.float32)).astype(jnp.bfloat16)
    product = jnp.dot(
        jnp.concatenate([high, low], axis=1), matrix, preferred_element_type=jnp.float32
    )
    return product[:, :LANES] + product[:, LANES:]


def pair_kernel(
    shape,
    places_ref,
    count_ref,
    first_ref,
    second_ref,
    reach_ref,
    anchors_ref,
    spots_ref,
    screen_ref,
    ahead_ref,
    behind_ref,
    *refs,
):
    edge, orb_dev, groups, fragments, slots = shape
    plane = edge * edge
    chunks = plane // LANES
    tiles = edge // ROWS
    phi_refs = refs[:groups]
    far_refs = refs[groups : groups + REACH * orb_dev]
    refs = refs[groups + REACH * orb_dev :]
    act_out, back_out = refs[:2]
    (act, back, near, far, moved, dense, cube, spectrum, rows_ref, listed, load_sem, out_sem) = refs[2:]

    fragment = places_ref[0]
    member = places_ref[1]
    lane = lax.broadcasted_iota(jnp.int32, (edge, LANES), 1)
    row = lax.broadcasted_iota(jnp.int32, (edge, LANES), 0)
    period = edge * LANES // math.gcd(edge, LANES) // edge
    group_chunks = period * edge // LANES

    def list_slots(slot, found):
        mine = (slot < count_ref[0]) & (lax.div(second_ref[slot], orb_dev) == member)

        @pl.when(mine)
        def _():
            listed[found] = slot

        return found + mine.astype(jnp.int32)

    found = lax.fori_loop(0, slots, list_slots, 0)
    act[...] = jnp.zeros_like(act)
    back[...] = jnp.zeros_like(back)

    def slot_of(turn, side):
        at = 2 * turn + side
        live = at < found
        return listed[jnp.where(live, at, 2 * turn)], live

    def start_loads(turn):
        for side in range(2):
            slot, live = slot_of(turn, side)
            first, second, reach = first_ref[slot], second_ref[slot], reach_ref[slot]
            relative = lax.div(first, orb_dev) ^ member
            for k in range(groups):
                @pl.when(relative == k)
                def _():
                    pltpu.make_async_copy(
                        phi_refs[k].at[lax.rem(first, orb_dev)], near.at[side], load_sem.at[0, side]
                    ).start()
            own = lax.rem(second, orb_dev)

            @pl.when(reach == 0)
            def _():
                pltpu.make_async_copy(phi_refs[0].at[own], far.at[side], load_sem.at[1, side]).start()

            for r in range(1, REACH + 1):
                for o in range(orb_dev):
                    @pl.when((reach == r) & (own == o))
                    def _():
                        pltpu.make_async_copy(
                            far_refs[(r - 1) * orb_dev + o].at[0], far.at[side], load_sem.at[1, side]
                        ).start()

    def wait_loads():
        for side in range(2):
            pltpu.make_async_copy(phi_refs[0].at[0], near.at[side], load_sem.at[0, side]).wait()
            pltpu.make_async_copy(phi_refs[0].at[0], far.at[side], load_sem.at[1, side]).wait()

    def offset_of(slot):
        partner = lax.rem(fragment + reach_ref[slot], fragments)
        return [anchors_ref[partner, i] - anchors_ref[fragment, i] for i in range(3)]

    def shifted(source, delta, k, buffer):
        shift = lax.rem(delta[1] * edge + delta[2] + 4 * plane, plane)
        start = lax.rem(plane - shift, plane)
        whole, part = lax.div(start, LANES), lax.rem(start, LANES)
        here = lax.rem(k + whole, chunks)
        after = lax.rem(k + whole + 1, chunks)
        turn = lax.rem(LANES - part, LANES)
        low = pltpu.roll(source[:, pl.ds(pl.multiple_of(here * LANES, LANES), LANES)], turn, 1)
        high = pltpu.roll(source[:, pl.ds(pl.multiple_of(after * LANES, LANES), LANES)], turn, 1)
        value = jnp.where(lane < LANES - part, low, high)
        y = spots_ref[0, pl.ds(k, 1), :] - delta[1]
        z = spots_ref[1, pl.ds(k, 1), :] - delta[2]
        inside = (y >= 0) & (y < edge) & (z >= 0) & (z < edge)
        value = jnp.where(inside, value, 0.0)
        rows_ref[buffer, :edge, :] = value
        rows_ref[buffer, edge:, :] = value
        down = lax.rem(2 * edge - delta[0], edge)
        value = rows_ref[buffer, pl.ds(down, edge), :]
        x = row - delta[0]
        return jnp.where((x >= 0) & (x < edge), value, 0.0)

    def columns(k):
        return pl.ds(pl.multiple_of(k * LANES, LANES), LANES)

    def solve_two(turn, _):
        start_loads(turn)
        wait_loads()
        picked = [slot_of(turn, side) for side in range(2)]
        offsets = [offset_of(slot) for slot, _ in picked]
        weights = [live.astype(jnp.float32) for _, live in picked]

        def make_density(k, _):
            for side in range(2):
                value = shifted(far.at[side], offsets[side], k, side)
                moved[side, :, columns(k)] = value
                dense[side, :, columns(k)] = weights[side] * near[side, :, columns(k)] * value
            return 0

        lax.fori_loop(0, chunks, make_density, 0)

        def spread(g, _):
            parts = [
                [dense[side, :, columns(g * group_chunks + q)] for q in range(group_chunks)]
                for side in range(2)
            ]
            for i in range(period):
                begin, offset = divmod(i * edge, LANES)
                sides = []
                for side in range(2):
                    shift = (side * HALF - offset) % LANES
                    value = parts[side][begin]
                    value = pltpu.roll(value, shift, 1) if shift else value
                    if offset + edge > LANES:
                        more = parts[side][begin + 1]
                        more = pltpu.roll(more, shift, 1) if shift else more
                        value = jnp.where(lane < side * HALF + LANES - offset, value, more)
                    sides.append(value)
                at = pl.multiple_of((g * period + i) * edge, ROWS)
                cube[pl.ds(at, edge), :] = jnp.where(lane < HALF, sides[0], sides[1])
            return 0

        lax.fori_loop(0, edge // period, spread, 0)

        def plain(ref, t, i):
            return ref[pl.ds(pl.multiple_of(i * edge + t * ROWS, ROWS), ROWS), :]

        def crossed(ref, t, i):
            return ref[pl.ds(t * (ROWS * edge) + i, ROWS, stride=edge), :]

        def transform(source, target, read, sign):
            def column(t, _):
                values = Lanes(sign).dft([read(source, t, i) for i in range(edge)])
                for i in range(edge):
                    target[pl.ds(pl.multiple_of(i * edge + t * ROWS, ROWS), ROWS), :] = values[i]
                return 0

            lax.fori_loop(0, tiles, column, 0)

        transform(cube, cube, plain, -1)
        transform(cube, spectrum, crossed, -1)

        block = 2 * LANES

        def screen(c, _):
            at = pl.ds(pl.multiple_of(c * block, block), block)
            value = split_dot(spectrum[at, :], ahead_ref[...]) * screen_ref[at, :]
            spectrum[at, :] = split_dot(value, behind_ref[...])
            return 0

        lax.fori_loop(0, plane // block, screen, 0)
        transform(spectrum, spectrum, plain, 1)
        transform(spectrum, cube, crossed, 1)

        firsts = [first_ref[slot] for slot, _ in picked]

        def collect(g, _):
            planes = [
                cube[pl.ds(pl.multiple_of((g * period + i) * edge, ROWS), edge), :]
                for i in range(period)
            ]
            for q in range(group_chunks):
                k = g * group_chunks + q
                for side in range(2):
                    value = None
                    for i in range(period):
                        begin = i * edge - q * LANES
                        if begin + edge <= 0 or begin >= LANES:
                            continue
                        shift = (begin - side * HALF) % LANES
                        piece = pltpu.roll(planes[i], shift, 1) if shift else planes[i]
                        value = piece if value is None else jnp.where(lane < begin, value, piece)
                    value = value * weights[side]
                    forward = value * moved[side, :, columns(k)]
                    dense[side, :, columns(k)] = value * near[side, :, columns(k)]
                    for t in range(tiles):
                        at = pl.ds(t * (ROWS * chunks) + k, ROWS, stride=chunks)
                        act[firsts[side], at, :] += forward[t * ROWS : (t + 1) * ROWS]
            return 0

        lax.fori_loop(0, edge // period, collect, 0)

        homes = []
        for side in range(2):
            slot = picked[side][0]
            homes.append(reach_ref[slot] * orb_dev + lax.rem(second_ref[slot], orb_dev))
        returns = [[-d for d in delta] for delta in offsets]

        def send_back(k, _):
            for side in range(2):
                value = shifted(dense.at[side], returns[side], k, side)
                for t in range(tiles):
                    at = pl.ds(t * (ROWS * chunks) + k, ROWS, stride=chunks)
                    back[homes[side], at, :] += value[t * ROWS : (t + 1) * ROWS]
            return 0

        lax.fori_loop(0, chunks, send_back, 0)
        return 0

    lax.fori_loop(0, lax.div(found + 1, 2), solve_two, 0)

    slab = plane * edge // LANES // groups
    copies = []
    for k in range(groups):
        source = (member ^ k) * slab
        copies.append(
            pltpu.make_async_copy(
                act.at[:, pl.ds(pl.multiple_of(source, ROWS), slab), :],
                act_out.at[reversed_bits(k, groups)],
                out_sem.at[k],
            )
        )
    copies.append(pltpu.make_async_copy(back, back_out, out_sem.at[groups]))
    for copy in copies:
        copy.start()
    for copy in copies:
        copy.wait()


def reversed_bits(k, count):
    bits = count.bit_length() - 1
    return sum(((k >> i) & 1) << (bits - 1 - i) for i in range(bits))


def pair_terms(places, pair_count, pair_first, pair_second, pair_reach, anchors, screen, pieces, far):
    orb_dev, edge, plane = pieces[0].shape
    groups = len(pieces)
    frag_size = groups * orb_dev
    fragments = anchors.shape[0]
    slots = pair_first.shape[0]
    chunks = plane // LANES
    rows = edge * chunks
    spots = np.arange(plane, dtype=np.int32).reshape(chunks, LANES)
    spots = jnp.asarray(np.stack([spots // edge, spots % edge]))
    ahead, behind = lane_matrices(edge)
    shape = (edge, orb_dev, groups, fragments, slots)
    smem = pl.BlockSpec(memory_space=pltpu.SMEM)
    vmem = pl.BlockSpec(memory_space=pltpu.VMEM)
    anywhere = pl.BlockSpec(memory_space=pl.ANY)
    f32 = jnp.float32
    return pl.pallas_call(
        functools.partial(pair_kernel, shape),
        out_shape=(
            jax.ShapeDtypeStruct((groups, frag_size, rows // groups, LANES), f32),
            jax.ShapeDtypeStruct(((REACH + 1) * orb_dev, rows, LANES), f32),
        ),
        in_specs=[smem] * 6 + [vmem] * 4 + [anywhere] * (groups + REACH * orb_dev),
        out_specs=(anywhere, anywhere),
        scratch_shapes=[
            pltpu.VMEM((frag_size, rows, LANES), f32),
            pltpu.VMEM(((REACH + 1) * orb_dev, rows, LANES), f32),
            pltpu.VMEM((2, edge, plane), f32),
            pltpu.VMEM((2, edge, plane), f32),
            pltpu.VMEM((2, edge, plane), f32),
            pltpu.VMEM((2, edge, plane), f32),
            pltpu.VMEM((plane, LANES), f32),
            pltpu.VMEM((plane, LANES), f32),
            pltpu.VMEM((2, 2 * edge, LANES), f32),
            pltpu.SMEM((slots,), jnp.int32),
            pltpu.SemaphoreType.DMA((2, 2)),
            pltpu.SemaphoreType.DMA((groups + 1,)),
        ],
        compiler_params=pltpu.CompilerParams(vmem_limit_bytes=40 << 20),
        name="pair_terms",
    )(
        places, pair_count, pair_first, pair_second, pair_reach, anchors,
        spots, screen, jnp.asarray(ahead), jnp.asarray(behind), *pieces, *far,
    )


def correlation_kernel(shape, places_ref, act_ref, back_ref, phi_ref, *refs):
    edge, orb_dev, groups = shape
    pieces, out_ref = refs[:-1], refs[-1]
    member = places_ref[1]
    frag_size = orb_dev * groups
    slab = act_ref.shape[1]
    rows = back_ref.shape[1]
    scale = 1.0 / float(edge**3)

    def total(value):
        return jnp.sum(value, keepdims=True)

    row = lax.broadcasted_iota(jnp.int32, (frag_size, LANES), 0)
    lane = lax.broadcasted_iota(jnp.int32, (frag_size, LANES), 1)
    result = jnp.zeros((frag_size, LANES), jnp.float32)
    tiles = slab // ROWS

    for a in range(frag_size):
        k, o = divmod(a, orb_dev)
        phi = phi_ref[k, o].reshape(tiles, ROWS, LANES)
        place = (member ^ k) * orb_dev + o
        for b in range(frag_size):
            product = total(jnp.sum(phi * act_ref[b].reshape(tiles, ROWS, LANES), axis=0))
            result = jnp.where((row == place) & (lane == b), product, result)
        whole = pieces[k][o].reshape(rows // ROWS, ROWS, LANES)
        for b in range(orb_dev):
            product = total(jnp.sum(whole * back_ref[b].reshape(rows // ROWS, ROWS, LANES), axis=0))
            result = jnp.where((row == place) & (lane == member * orb_dev + b), result + product, result)
    out_ref[...] = result * scale


def correlation_terms(places, edge, act, back, phi, pieces):
    groups, orb_dev = phi.shape[:2]
    frag_size = groups * orb_dev
    smem = pl.BlockSpec(memory_space=pltpu.SMEM)
    vmem = pl.BlockSpec(memory_space=pltpu.VMEM)
    return pl.pallas_call(
        functools.partial(correlation_kernel, (edge, orb_dev, groups)),
        out_shape=jax.ShapeDtypeStruct((frag_size, LANES), jnp.float32),
        in_specs=[smem] + [vmem] * (3 + groups),
        out_specs=vmem,
        compiler_params=pltpu.CompilerParams(vmem_limit_bytes=40 << 20),
        name="correlation_terms",
    )(places, act, back, phi, *pieces)


def gradient_kernel(shape, places_ref, lagrange_ref, act_ref, phi_ref, *refs):
    edge, orb_dev, groups = shape
    backs = refs[:groups]
    out_ref, hold = refs[groups:]
    member = places_ref[1]
    frag_size = orb_dev * groups
    chunks = edge * edge // LANES
    slab_rows = edge // groups
    for k in range(groups):
        for o in range(orb_dev):
            a = (member ^ k) * orb_dev + o
            value = act_ref[a] + backs[k][o]
            for q in range(groups):
                for p in range(orb_dev):
                    value = value - lagrange_ref[(member ^ q) * orb_dev + p, a] * phi_ref[q, p]
            hold[k * orb_dev + o, : slab_rows * chunks] = value
    for k in range(groups):
        for o in range(orb_dev):
            a = (member ^ k) * orb_dev + o
            for j in range(chunks):
                for begin in range(0, slab_rows, ROWS):
                    count = min(ROWS, slab_rows - begin)
                    value = hold[k * orb_dev + o, pl.ds(begin * chunks + j, ROWS, stride=chunks), :]
                    out_ref[a, pl.ds(begin, count), j * LANES : (j + 1) * LANES] = value[:count]


def gradient_terms(places, edge, lagrange, act, phi, backs):
    groups, orb_dev = phi.shape[:2]
    frag_size = groups * orb_dev
    slab_rows = edge // groups
    chunks = edge * edge // LANES
    padded = -(-slab_rows // ROWS) * ROWS * chunks
    smem = pl.BlockSpec(memory_space=pltpu.SMEM)
    vmem = pl.BlockSpec(memory_space=pltpu.VMEM)
    return pl.pallas_call(
        functools.partial(gradient_kernel, (edge, orb_dev, groups)),
        out_shape=jax.ShapeDtypeStruct((frag_size, slab_rows, edge * edge), jnp.float32),
        in_specs=[smem, smem] + [vmem] * (2 + groups),
        out_specs=vmem,
        scratch_shapes=[pltpu.VMEM((frag_size, padded, LANES), jnp.float32)],
        compiler_params=pltpu.CompilerParams(vmem_limit_bytes=40 << 20),
        name="gradient_terms",
    )(places, lagrange, act, phi, *backs)


def to_fragment(block, distance):
    devices = lax.axis_size("orb")
    return lax.ppermute(block, "orb", [(i, (i + distance) % devices) for i in range(devices)])


def with_twin(block):
    return lax.ppermute(block, "orb", [(i, i ^ 1) for i in range(lax.axis_size("orb"))])


def with_member(block, bit):
    return lax.ppermute(block, "grp", [(i, i ^ bit) for i in range(lax.axis_size("grp"))])


def shards(orbitals, kernel, anchors, pair_count, pair_first, pair_second, pair_reach):
    groups = lax.axis_size("grp")
    fragment = lax.axis_index("orb")
    member = lax.axis_index("grp")
    odd = fragment % 2 == 1
    orb_dev, edge, plane = orbitals.shape
    chunks = plane // LANES
    rows = edge * chunks
    slab = rows // groups
    frag_size = groups * orb_dev
    places = jnp.stack([fragment, member]).astype(jnp.int32)

    cube = kernel.reshape(edge, edge, edge)
    mirror = jnp.roll(jnp.flip(cube, (0, 1, 2)), (1, 1, 1), (0, 1, 2))
    even = (cube + mirror) * (0.5 / float(edge**3))
    even = jnp.pad(even.reshape(plane, edge), ((0, 0), (0, HALF - edge)))
    screen = jnp.concatenate([even, even], axis=1)

    ahead_two = [to_fragment(orbitals[o : o + 1], -2) for o in range(orb_dev)]
    ahead_one = [
        with_twin(jnp.where(odd, orbitals[o : o + 1], ahead_two[o])) for o in range(orb_dev)
    ]
    pieces = {0: orbitals}
    bit = groups // 2
    while bit:
        for k in list(pieces):
            pieces[k ^ bit] = with_member(pieces[k], bit)
        bit //= 2
    pieces = [pieces[k] for k in range(groups)]

    act, back = pair_terms(
        places, pair_count, pair_first, pair_second, pair_reach, anchors, screen,
        pieces, ahead_one + ahead_two,
    )

    home = []
    for o in range(orb_dev):
        twin = with_twin(back[orb_dev + o][None])
        two = to_fragment(back[2 * orb_dev + o][None] + jnp.where(odd, 0.0, twin), 2)
        home.append(back[o][None] + two + jnp.where(odd, twin, 0.0))

    bit = 1
    while bit < groups:
        half = act.shape[0] // 2
        act = act[:half] + with_member(act[half:], bit)
        bit *= 2
    act = act[0]

    def own_slab(array, k):
        array = array.reshape(array.shape[0], groups, slab, LANES)
        return lax.dynamic_slice_in_dim(array, member ^ k, 1, axis=1)[:, 0]

    flat = [piece.reshape(orb_dev, rows, LANES) for piece in pieces]
    phi = jnp.stack([own_slab(piece, 0) for piece in flat])

    backs = [[None] * orb_dev for _ in range(groups)]
    for o in range(orb_dev):
        held = {0: {k: own_slab(home[o], k) for k in range(groups)}}
        bit = groups // 2
        while bit:
            for origin in list(held):
                going = [k for k in held[origin] if k & bit]
                staying = {k: v for k, v in held[origin].items() if not k & bit}
                sent = with_member(jnp.concatenate([held[origin][k] for k in going]), bit)
                held[origin] = staying
                held[origin ^ bit] = {k ^ bit: sent[i : i + 1] for i, k in enumerate(going)}
            bit //= 2
        for origin in range(groups):
            backs[origin][o] = held[origin][0]
    backs = [jnp.concatenate(parts) for parts in backs]

    correlation = correlation_terms(places, edge, act, jnp.concatenate(home), phi, flat)
    bit = 1
    while bit < groups:
        correlation = correlation + with_member(correlation, bit)
        bit *= 2
    correlation = correlation[:, :frag_size]
    lagrange = 0.5 * (correlation + correlation.T)
    gradient = gradient_terms(places, edge, lagrange, act, phi, backs)
    return (gradient, lagrange[None])


def solution(mesh):
    placed = (P(("orb", "grp"), None, None), P(), P(), P("orb"), P("orb"), P("orb"), P("orb"))
    return jax.shard_map(
        shards,
        mesh=mesh,
        in_specs=placed,
        out_specs=(P("orb", "grp", None), P("orb", None, None)),
        check_vma=False,
    )
```

```python
import functools
import math

import jax
import jax.numpy as jnp
import numpy as np
from jax import lax
from jax.experimental import pallas as pl
from jax.experimental.pallas import tpu as pltpu
from jax.sharding import PartitionSpec as P

REACH = 2
LANES = 128
ROWS = 8
HALF = LANES // 2


class Number:
    def __init__(self, real, imag=None):
        self.real, self.imag = real, imag

    def __add__(self, other):
        if self.imag is None or other.imag is None:
            imag = self.imag if other.imag is None else other.imag
        else:
            imag = self.imag + other.imag
        return Number(self.real + other.real, imag)

    def __sub__(self, other):
        if other.imag is None:
            imag = self.imag
        else:
            imag = -other.imag if self.imag is None else self.imag - other.imag
        return Number(self.real - other.real, imag)

    def conj(self):
        return self if self.imag is None else Number(self.real, -self.imag)

    def scaled(self, factor):
        return Number(self.real * factor, None if self.imag is None else self.imag * factor)

    def turned(self, sign):
        if self.imag is None:
            return Number(jnp.zeros_like(self.real), self.real if sign > 0 else -self.real)
        return Number(-self.imag, self.real) if sign > 0 else Number(self.imag, -self.real)

    def plus_turned(self, other, sign):
        if sign < 0:
            return self.minus_turned(other)
        real = self.real if other.imag is None else self.real - other.imag
        return Number(real, other.real if self.imag is None else self.imag + other.real)

    def minus_turned(self, other):
        real = self.real if other.imag is None else self.real + other.imag
        return Number(real, -other.real if self.imag is None else self.imag - other.real)

    def times(self, angle):
        real, imag = math.cos(angle), math.sin(angle)
        if abs(imag) < 1e-12:
            return self if real > 0 else self.scaled(-1.0)
        if abs(real) < 1e-12:
            return self.turned(imag)
        if self.imag is None:
            return Number(self.real * real, self.real * imag)
        return Number(self.real * real - self.imag * imag, self.real * imag + self.imag * real)


def coprime(n):
    for p in (2, 3, 5, 7):
        power = 1
        while n % (power * p) == 0:
            power *= p
        if 1 < power < n:
            return power, n // power
    return None


def radix(n):
    return next((p for p in (4, 2, 3, 5, 7) if n % p == 0 and n > p), None)


def meeting(i, j, first, second):
    return next(k for k in range(first * second) if k % first == i and k % second == j)


def dft(values, sign):
    n = len(values)
    if n == 1:
        return values
    if n == 2:
        return [values[0] + values[1], values[0] - values[1]]
    if n == 3:
        a, b, c = values
        total, side = b + c, (b - c).scaled(math.sqrt(0.75))
        middle = a - total.scaled(0.5)
        return [a + total, middle.plus_turned(side, sign), middle.plus_turned(side, -sign)]
    if n == 4:
        a, b, c, d = values
        s, t, u, v = a + c, a - c, b + d, b - d
        return [s + u, t.plus_turned(v, sign), s - u, t.plus_turned(v, -sign)]
    out = [None] * n
    if coprime(n):
        first, second = coprime(n)
        columns = [
            dft([values[(i * second + j * first) % n] for i in range(first)], sign)
            for j in range(second)
        ]
        for i in range(first):
            row = dft([column[i] for column in columns], sign)
            for j in range(second):
                out[meeting(i, j, first, second)] = row[j]
        return out
    p = radix(n)
    if p:
        rest = n // p
        columns = [dft(values[j::p], sign) for j in range(p)]
        for i in range(rest):
            row = dft(
                [columns[j][i].times(sign * 2.0 * math.pi * i * j / n) for j in range(p)], sign
            )
            for j in range(p):
                out[i + rest * j] = row[j]
        return out
    for k in range(n):
        total = values[0]
        for j in range(1, n):
            total = total + values[j].times(sign * 2.0 * math.pi * (j * k % n) / n)
        out[k] = total
    return out


def real_dft(values):
    n = len(values)
    if n <= 4:
        out = dft(values, -1)
    else:
        out = [None] * n
        if coprime(n):
            first, second = coprime(n)
            columns = [
                real_dft([values[(i * second + j * first) % n] for i in range(first)])
                for j in range(second)
            ]
            for i in range(first // 2 + 1):
                entries = [column[i] for column in columns]
                alone = 2 * i % first == 0
                row = real_dft(entries) if alone else dft(entries, -1)
                for j in range(second):
                    out[meeting(i, j, first, second)] = row[j]
        elif radix(n):
            p = radix(n)
            rest = n // p
            columns = [real_dft(values[j::p]) for j in range(p)]
            for i in range(rest // 2 + 1):
                row = dft(
                    [columns[j][i].times(-2.0 * math.pi * i * j / n) for j in range(p)], -1
                )
                for j in range(p):
                    out[i + rest * j] = row[j]
        else:
            out = dft(values, -1)
    for k in range(1, n):
        if out[k] is None or (k > n // 2 and out[n - k] is not None):
            out[k] = out[n - k].conj()
    out[0] = Number(out[0].real)
    if n % 2 == 0:
        out[n // 2] = Number(out[n // 2].real)
    return out


def real_back(values):
    n = len(values)
    if n == 1:
        return [values[0].real]
    if n == 2:
        return [values[0].real + values[1].real, values[0].real - values[1].real]
    if n == 3:
        a, b = values[0].real, values[1]
        side = b.imag * math.sqrt(3.0)
        middle = a - b.real
        return [a + 2.0 * b.real, middle - side, middle + side]
    if n == 4:
        s, t = values[0].real + values[2].real, values[0].real - values[2].real
        u, v = 2.0 * values[1].real, 2.0 * values[1].imag
        return [s + u, t - v, s - u, t + v]
    out = [None] * n
    if coprime(n):
        first, second = coprime(n)
        rows = []
        for i in range(first // 2 + 1):
            entries = [values[meeting(i, j, first, second)] for j in range(second)]
            if 2 * i % first == 0:
                rows.append([Number(value) for value in real_back(entries)])
            else:
                rows.append(dft(entries, 1))
        for b in range(second):
            half = [row[b] for row in rows]
            whole = half + [half[first - i].conj() for i in range(len(half), first)]
            for a, value in enumerate(real_back(whole)):
                out[(a * second + b * first) % n] = value
        return out
    p = radix(n)
    if p:
        rest = n // p
        parts = []
        for i in range(p // 2 + 1):
            entries = values[i::p]
            if i == 0:
                parts.append([Number(value) for value in real_back(entries)])
            else:
                inner = dft(entries, 1)
                parts.append([inner[m].times(2.0 * math.pi * i * m / n) for m in range(rest)])
                if 2 * i == p:
                    parts[-1] = [Number(value.real) for value in parts[-1]]
        for m in range(rest):
            half = [part[m] for part in parts]
            whole = half + [half[p - i].conj() for i in range(len(half), p)]
            for j, value in enumerate(real_back(whole)):
                out[m + rest * j] = value
        return out
    return [value.real for value in dft(values, 1)]


def lane_matrices(edge):
    index = np.arange(edge)
    angles = 2.0 * np.pi / edge * (np.outer(index, index) % edge)
    found = []
    for sign in (-1.0, 1.0):
        full = np.zeros((2, 2, edge, 2, 2, edge))
        for side in range(2):
            full[0, side, :, 0, side] = np.cos(angles)
            full[0, side, :, 1, side] = sign * np.sin(angles)
            full[1, side, :, 0, side] = -sign * np.sin(angles)
            full[1, side, :, 1, side] = np.cos(angles)
        full = np.pad(full, [(0, 0), (0, 0), (0, HALF - edge)] * 2).reshape(2 * LANES, 2 * LANES)
        high = full.astype(jnp.bfloat16)
        low = (full - high.astype(np.float64)).astype(jnp.bfloat16)
        found.append(np.stack([high, low]))
    return found


def split_dot(real, imag, matrix):
    value = jnp.concatenate([real, imag], axis=1)
    high = value.astype(jnp.bfloat16)
    low = (value - high.astype(jnp.float32)).astype(jnp.bfloat16)
    product = jnp.dot(high, matrix[0], preferred_element_type=jnp.float32)
    product += jnp.dot(low, matrix[0], preferred_element_type=jnp.float32)
    product += jnp.dot(high, matrix[1], preferred_element_type=jnp.float32)
    return product[:, :LANES], product[:, LANES:]


def padded_half(edge):
    return -(-(edge // 2 + 1) // ROWS) * ROWS


def screen_kernel(edge, kernel_ref, flip_ref, mirror_ref, out_ref, flipped):
    exact = dict(precision=lax.Precision.HIGHEST, preferred_element_type=jnp.float32)
    flipped[...] = jnp.dot(flip_ref[...], kernel_ref[...], **exact)
    height = padded_half(edge)
    lane = lax.broadcasted_iota(jnp.int32, (edge, LANES), 1)
    out_ref[...] = jnp.zeros_like(out_ref)

    def piece(ref, y):
        begin, offset = divmod(y * edge, LANES)
        value = ref[:, begin * LANES : (begin + 1) * LANES]
        value = pltpu.roll(value, LANES - offset, 1) if offset else value
        if offset + edge > LANES:
            more = ref[:, (begin + 1) * LANES : (begin + 2) * LANES]
            value = jnp.where(lane < LANES - offset, value, pltpu.roll(more, LANES - offset, 1))
        return value

    for y in range(edge // 2 + 1):
        value = piece(kernel_ref, y)
        value = jnp.where(lane < HALF, value, pltpu.roll(value, HALF, 1))
        value = value + jnp.dot(piece(flipped, (edge - y) % edge), mirror_ref[...], **exact)
        value = value * (0.5 / float(edge**3))
        for t in range(edge // ROWS):
            out_ref[pl.ds(t * ROWS * height + y, ROWS, stride=height), :] = value[t * ROWS : (t + 1) * ROWS]


def screen_terms(kernel):
    edge, plane = kernel.shape
    index = np.arange(edge)
    flip = np.zeros((edge, edge), np.float32)
    flip[index, -index % edge] = 1.0
    mirror = np.zeros((LANES, LANES), np.float32)
    mirror[-index % edge, index] = 1.0
    mirror[-index % edge, HALF + index] = 1.0
    vmem = pl.BlockSpec(memory_space=pltpu.VMEM)
    return pl.pallas_call(
        functools.partial(screen_kernel, edge),
        out_shape=jax.ShapeDtypeStruct((edge * padded_half(edge), LANES), jnp.float32),
        in_specs=[vmem] * 3,
        out_specs=vmem,
        scratch_shapes=[pltpu.VMEM((edge, plane), jnp.float32)],
        compiler_params=pltpu.CompilerParams(vmem_limit_bytes=16 << 20),
        name="screen_terms",
    )(kernel, jnp.asarray(flip), jnp.asarray(mirror))


def pair_kernel(
    shape,
    places_ref,
    count_ref,
    first_ref,
    second_ref,
    reach_ref,
    anchors_ref,
    spots_ref,
    screen_ref,
    ahead_ref,
    behind_ref,
    *refs,
):
    edge, orb_dev, groups, fragments, slots = shape
    plane = edge * edge
    chunks = plane // LANES
    tiles = edge // ROWS
    half = edge // 2 + 1
    height = padded_half(edge)
    returns_count = (REACH + 1) * orb_dev
    phi_refs = refs[:groups]
    far_refs = refs[groups : groups + REACH * orb_dev]
    refs = refs[groups + REACH * orb_dev :]
    act_outs, back_outs = refs[:2], refs[2 : 2 + returns_count]
    refs = refs[2 + returns_count :]
    (act, back, near, far, wide, moved, dense, cube, lower, upper, listed, load_sem, out_sem) = refs

    fragment = places_ref[0]
    member = places_ref[1]
    lane = lax.broadcasted_iota(jnp.int32, (edge, LANES), 1)
    row = lax.broadcasted_iota(jnp.int32, (edge, LANES), 0)
    period = edge * LANES // math.gcd(edge, LANES) // edge
    group_chunks = period * edge // LANES
    stretch = next(n for n in (6, 4, 3, 2, 1) if chunks % n == 0)
    middle = pl.ds(edge, edge)

    def list_slots(slot, found):
        mine = (slot < count_ref[0]) & (lax.div(second_ref[slot], orb_dev) == member)

        @pl.when(mine)
        def _():
            listed[found] = slot

        return found + mine.astype(jnp.int32)

    found = lax.fori_loop(0, slots, list_slots, 0)

    def slot_of(turn, side):
        at = 2 * turn + side
        live = at < found
        return listed[jnp.where(live, at, 2 * turn)], live

    def far_copy(side, source):
        return pltpu.make_async_copy(source, far.at[side], load_sem.at[1, side])

    def start_loads(turn):
        for side in range(2):
            slot, _ = slot_of(turn, side)
            first, second, reach = first_ref[slot], second_ref[slot], reach_ref[slot]
            relative = lax.div(first, orb_dev) ^ member
            for k in range(groups):
                @pl.when(relative == k)
                def _():
                    pltpu.make_async_copy(
                        phi_refs[k].at[lax.rem(first, orb_dev)], near.at[side], load_sem.at[0, side]
                    ).start()
            own = lax.rem(second, orb_dev)

            @pl.when(reach == 0)
            def _():
                far_copy(side, phi_refs[0].at[own]).start()

            for r in range(1, REACH + 1):
                for o in range(orb_dev):
                    @pl.when((reach == r) & (own == o))
                    def _():
                        far_copy(side, far_refs[(r - 1) * orb_dev + o].at[0]).start()

    def wait_loads():
        for side in range(2):
            pltpu.make_async_copy(phi_refs[0].at[0], near.at[side], load_sem.at[0, side]).wait()
            far_copy(side, phi_refs[0].at[0]).wait()

    @pl.when(found > 0)
    def _():
        start_loads(0)

    act[...] = jnp.zeros_like(act)
    back[...] = jnp.zeros_like(back)

    def offset_of(slot):
        partner = lax.rem(fragment + reach_ref[slot], fragments)
        return [anchors_ref[partner, i] - anchors_ref[fragment, i] for i in range(3)]

    def columns(k):
        return pl.ds(pl.multiple_of(k * LANES, LANES), LANES)

    def shifted(source, delta, k, count):
        shift = lax.rem(delta[1] * edge + delta[2] + 4 * plane, plane)
        start = lax.rem(plane - shift, plane)
        whole, part = lax.div(start, LANES), lax.rem(start, LANES)
        turn = lax.rem(LANES - part, LANES)
        down = edge - jnp.clip(delta[0], -edge, edge)
        x = row - delta[0]
        rows_inside = (x >= 0) & (x < edge)
        pieces = [
            pltpu.roll(source[lax.rem(k + i + whole, chunks), pl.ds(down, edge), :], turn, 1)
            for i in range(count + 1)
        ]
        out = []
        for i in range(count):
            value = jnp.where(lane < LANES - part, pieces[i], pieces[i + 1])
            y = spots_ref[0, pl.ds(k + i, 1), :] - delta[1]
            z = spots_ref[1, pl.ds(k + i, 1), :] - delta[2]
            inside = (y >= 0) & (y < edge) & (z >= 0) & (z < edge)
            out.append(jnp.where(inside & rows_inside, value, 0.0))
        return out

    def solve_two(turn, _):
        @pl.when(turn > 0)
        def _():
            start_loads(turn)

        wait_loads()
        picked = [slot_of(turn, side) for side in range(2)]
        offsets = [offset_of(slot) for slot, _ in picked]
        weights = [live.astype(jnp.float32) for _, live in picked]

        def widen(g, _):
            for side in range(2):
                for i in range(stretch):
                    k = g * stretch + i
                    wide[side, k, middle, :] = far[side, :, columns(k)]
            return 0

        lax.fori_loop(0, chunks // stretch, widen, 0)

        def make_density(g, _):
            for side in range(2):
                values = shifted(wide.at[side], offsets[side], g * stretch, stretch)
                for i, value in enumerate(values):
                    k = g * stretch + i
                    moved[side, k] = value
                    dense[side, k, middle, :] = weights[side] * near[side, :, columns(k)] * value
            return 0

        lax.fori_loop(0, chunks // stretch, make_density, 0)

        def spread(g, _):
            parts = [
                [dense[side, g * group_chunks + q, middle, :] for q in range(group_chunks)]
                for side in range(2)
            ]
            for i in range(period):
                begin, offset = divmod(i * edge, LANES)
                sides = []
                for side in range(2):
                    shift = (side * HALF - offset) % LANES
                    value = parts[side][begin]
                    value = pltpu.roll(value, shift, 1) if shift else value
                    if offset + edge > LANES:
                        more = parts[side][begin + 1]
                        more = pltpu.roll(more, shift, 1) if shift else more
                        value = jnp.where(lane < side * HALF + LANES - offset, value, more)
                    sides.append(value)
                at = pl.multiple_of((g * period + i) * edge, ROWS)
                cube[pl.ds(at, edge), :] = jnp.where(lane < HALF, sides[0], sides[1])
            return 0

        lax.fori_loop(0, edge // period, spread, 0)

        def tile(t, i, size):
            return pl.ds(pl.multiple_of(i * size + t * ROWS, ROWS), ROWS)

        def across(t, i, size):
            return pl.ds(t * (ROWS * size) + i, ROWS, stride=size)

        def over_y(t, _):
            values = real_dft([Number(cube[tile(t, i, edge), :]) for i in range(edge)])
            for i in range(half):
                at = tile(t, i, edge)
                lower[0, at, :] = values[i].real
                lower[1, at, :] = (
                    jnp.zeros((ROWS, LANES), jnp.float32) if values[i].imag is None else values[i].imag
                )
            return 0

        lax.fori_loop(0, tiles, over_y, 0)

        def over_x(t, _):
            at = [across(t, i, edge) for i in range(edge)]
            values = dft([Number(lower[0, a, :], lower[1, a, :]) for a in at], -1)
            for i in range(edge):
                upper[0, tile(t, i, height), :] = values[i].real
                upper[1, tile(t, i, height), :] = values[i].imag
            return 0

        lax.fori_loop(0, height // ROWS, over_x, 0)

        block = next(n for n in (512, 256, 128, 64, 32, 16, 8) if edge * height % n == 0)

        def screen(c, _):
            at = pl.ds(pl.multiple_of(c * block, block), block)
            real, imag = split_dot(upper[0, at, :], upper[1, at, :], ahead_ref)
            factor = screen_ref[at, :]
            real, imag = split_dot(real * factor, imag * factor, behind_ref)
            upper[0, at, :] = real
            upper[1, at, :] = imag
            return 0

        lax.fori_loop(0, edge * height // block, screen, 0)

        def back_x(t, _):
            at = [tile(t, i, height) for i in range(edge)]
            values = dft([Number(upper[0, a, :], upper[1, a, :]) for a in at], 1)
            for i in range(edge):
                upper[0, at[i], :] = values[i].real
                upper[1, at[i], :] = values[i].imag
            return 0

        lax.fori_loop(0, height // ROWS, back_x, 0)

        def back_y(t, _):
            at = [across(t, i, height) for i in range(half)]
            values = [Number(upper[0, a, :], upper[1, a, :]) for a in at]
            values = values + [values[edge - i].conj() for i in range(half, edge)]
            for i, value in enumerate(real_back(values)):
                cube[tile(t, i, edge), :] = value
            return 0

        lax.fori_loop(0, tiles, back_y, 0)

        firsts = [first_ref[slot] for slot, _ in picked]

        def collect(g, _):
            planes = [
                cube[pl.ds(pl.multiple_of((g * period + i) * edge, ROWS), edge), :]
                for i in range(period)
            ]
            for q in range(group_chunks):
                k = g * group_chunks + q
                for side in range(2):
                    value = None
                    for i in range(period):
                        begin = i * edge - q * LANES
                        if begin + edge <= 0 or begin >= LANES:
                            continue
                        shift = (begin - side * HALF) % LANES
                        piece = pltpu.roll(planes[i], shift, 1) if shift else planes[i]
                        value = piece if value is None else jnp.where(lane < begin, value, piece)
                    value = value * weights[side]
                    forward = value * moved[side, k]
                    dense[side, k, middle, :] = value * near[side, :, columns(k)]
                    for t in range(tiles):
                        at = pl.ds(t * (ROWS * chunks) + k, ROWS, stride=chunks)
                        act[firsts[side], at, :] += forward[t * ROWS : (t + 1) * ROWS]
            return 0

        lax.fori_loop(0, edge // period, collect, 0)

        homes = []
        for side in range(2):
            slot = picked[side][0]
            homes.append(reach_ref[slot] * orb_dev + lax.rem(second_ref[slot], orb_dev))
        returns = [[-d for d in delta] for delta in offsets]

        def send_back(g, _):
            for side in range(2):
                values = shifted(dense.at[side], returns[side], g * stretch, stretch)
                for i, value in enumerate(values):
                    for t in range(tiles):
                        at = pl.ds(t * (ROWS * chunks) + g * stretch + i, ROWS, stride=chunks)
                        back[homes[side], at, :] += value[t * ROWS : (t + 1) * ROWS]
            return 0

        lax.fori_loop(0, chunks // stretch, send_back, 0)
        return 0

    lax.fori_loop(0, lax.div(found + 1, 2), solve_two, 0)

    slab = plane * edge // LANES // groups
    copies = []
    for i in range(returns_count):
        copies.append(pltpu.make_async_copy(back.at[i], back_outs[i].at[0], out_sem.at[groups + i]))
    for k in range(groups):
        source = (member ^ k) * slab
        place = reversed_bits(k, groups)
        copies.append(
            pltpu.make_async_copy(
                act.at[:, pl.ds(pl.multiple_of(source, ROWS), slab), :],
                act_outs[2 * place // groups].at[place % (groups // 2)],
                out_sem.at[k],
            )
        )
    for copy in copies:
        copy.start()
    for copy in copies:
        copy.wait()


def reversed_bits(k, count):
    bits = count.bit_length() - 1
    return sum(((k >> i) & 1) << (bits - 1 - i) for i in range(bits))


def pair_terms(places, pair_count, pair_first, pair_second, pair_reach, anchors, screen, pieces, far):
    orb_dev, edge, plane = pieces[0].shape
    groups = len(pieces)
    frag_size = groups * orb_dev
    fragments = anchors.shape[0]
    slots = pair_first.shape[0]
    chunks = plane // LANES
    rows = edge * chunks
    height = padded_half(edge)
    returns_count = (REACH + 1) * orb_dev
    spots = np.arange(plane, dtype=np.int32).reshape(chunks, LANES)
    spots = jnp.asarray(np.stack([spots // edge, spots % edge]))
    ahead, behind = lane_matrices(edge)
    shape = (edge, orb_dev, groups, fragments, slots)
    smem = pl.BlockSpec(memory_space=pltpu.SMEM)
    vmem = pl.BlockSpec(memory_space=pltpu.VMEM)
    anywhere = pl.BlockSpec(memory_space=pl.ANY)
    f32 = jnp.float32
    found = pl.pallas_call(
        functools.partial(pair_kernel, shape),
        out_shape=[jax.ShapeDtypeStruct((groups // 2, frag_size, rows // groups, LANES), f32)] * 2
        + [jax.ShapeDtypeStruct((1, rows, LANES), f32)] * returns_count,
        in_specs=[smem] * 6 + [vmem] * 4 + [anywhere] * (groups + REACH * orb_dev),
        out_specs=[anywhere] * (2 + returns_count),
        scratch_shapes=[
            pltpu.VMEM((frag_size, rows, LANES), f32),
            pltpu.VMEM((returns_count, rows, LANES), f32),
            pltpu.VMEM((2, edge, plane), f32),
            pltpu.VMEM((2, edge, plane), f32),
            pltpu.VMEM((2, chunks, 3 * edge, LANES), f32),
            pltpu.VMEM((2, chunks, edge, LANES), f32),
            pltpu.VMEM((2, chunks, 3 * edge, LANES), f32),
            pltpu.VMEM((plane, LANES), f32),
            pltpu.VMEM((2, height * edge, LANES), f32),
            pltpu.VMEM((2, height * edge, LANES), f32),
            pltpu.SMEM((slots,), jnp.int32),
            pltpu.SemaphoreType.DMA((2, 2)),
            pltpu.SemaphoreType.DMA((groups + returns_count,)),
        ],
        compiler_params=pltpu.CompilerParams(vmem_limit_bytes=40 << 20),
        name="pair_terms",
    )(
        places, pair_count, pair_first, pair_second, pair_reach, anchors,
        spots, screen, jnp.asarray(ahead), jnp.asarray(behind), *pieces, *far,
    )
    return found[:2], found[2:]


def correlation_kernel(shape, places_ref, act_ref, phi_ref, *refs):
    edge, orb_dev, groups = shape
    pieces, backs, out_ref = refs[:groups], refs[groups:-1], refs[-1]
    member = places_ref[1]
    frag_size = orb_dev * groups
    slab = act_ref.shape[1]
    rows = backs[0].shape[1]
    scale = 1.0 / float(edge**3)

    def total(value):
        return jnp.sum(value, keepdims=True)

    row = lax.broadcasted_iota(jnp.int32, (frag_size, LANES), 0)
    lane = lax.broadcasted_iota(jnp.int32, (frag_size, LANES), 1)
    result = jnp.zeros((frag_size, LANES), jnp.float32)
    tiles = slab // ROWS

    for a in range(frag_size):
        k, o = divmod(a, orb_dev)
        phi = phi_ref[k, o].reshape(tiles, ROWS, LANES)
        place = (member ^ k) * orb_dev + o
        for b in range(frag_size):
            product = total(jnp.sum(phi * act_ref[b].reshape(tiles, ROWS, LANES), axis=0))
            result = jnp.where((row == place) & (lane == b), product, result)
        whole = pieces[k][o].reshape(rows // ROWS, ROWS, LANES)
        for b in range(orb_dev):
            product = total(jnp.sum(whole * backs[b][0].reshape(rows // ROWS, ROWS, LANES), axis=0))
            result = jnp.where((row == place) & (lane == member * orb_dev + b), result + product, result)
    out_ref[...] = result * scale


def correlation_terms(places, edge, act, backs, phi, pieces):
    groups, orb_dev = phi.shape[:2]
    frag_size = groups * orb_dev
    smem = pl.BlockSpec(memory_space=pltpu.SMEM)
    vmem = pl.BlockSpec(memory_space=pltpu.VMEM)
    return pl.pallas_call(
        functools.partial(correlation_kernel, (edge, orb_dev, groups)),
        out_shape=jax.ShapeDtypeStruct((frag_size, LANES), jnp.float32),
        in_specs=[smem] + [vmem] * (2 + groups + orb_dev),
        out_specs=vmem,
        compiler_params=pltpu.CompilerParams(vmem_limit_bytes=40 << 20),
        name="correlation_terms",
    )(places, act, phi, *pieces, *backs)


def gradient_kernel(shape, places_ref, lagrange_ref, act_ref, phi_ref, *refs):
    edge, orb_dev, groups = shape
    backs = refs[:groups]
    out_ref, hold = refs[groups:]
    member = places_ref[1]
    frag_size = orb_dev * groups
    chunks = edge * edge // LANES
    slab_rows = edge // groups
    for k in range(groups):
        for o in range(orb_dev):
            a = (member ^ k) * orb_dev + o
            value = act_ref[a] + backs[k][o]
            for q in range(groups):
                for p in range(orb_dev):
                    value = value - lagrange_ref[(member ^ q) * orb_dev + p, a] * phi_ref[q, p]
            hold[k * orb_dev + o, : slab_rows * chunks] = value
    for k in range(groups):
        for o in range(orb_dev):
            a = (member ^ k) * orb_dev + o
            for j in range(chunks):
                for begin in range(0, slab_rows, ROWS):
                    count = min(ROWS, slab_rows - begin)
                    value = hold[k * orb_dev + o, pl.ds(begin * chunks + j, ROWS, stride=chunks), :]
                    out_ref[a, pl.ds(begin, count), j * LANES : (j + 1) * LANES] = value[:count]


def gradient_terms(places, edge, lagrange, act, phi, backs):
    groups, orb_dev = phi.shape[:2]
    frag_size = groups * orb_dev
    slab_rows = edge // groups
    chunks = edge * edge // LANES
    padded = -(-slab_rows // ROWS) * ROWS * chunks
    smem = pl.BlockSpec(memory_space=pltpu.SMEM)
    vmem = pl.BlockSpec(memory_space=pltpu.VMEM)
    return pl.pallas_call(
        functools.partial(gradient_kernel, (edge, orb_dev, groups)),
        out_shape=jax.ShapeDtypeStruct((frag_size, slab_rows, edge * edge), jnp.float32),
        in_specs=[smem, smem] + [vmem] * (2 + groups),
        out_specs=vmem,
        scratch_shapes=[pltpu.VMEM((frag_size, padded, LANES), jnp.float32)],
        compiler_params=pltpu.CompilerParams(vmem_limit_bytes=40 << 20),
        name="gradient_terms",
    )(places, lagrange, act, phi, *backs)


def to_fragment(block, distance):
    devices = lax.axis_size("orb")
    return lax.ppermute(block, "orb", [(i, (i + distance) % devices) for i in range(devices)])


def with_twin(block):
    return lax.ppermute(block, "orb", [(i, i ^ 1) for i in range(lax.axis_size("orb"))])


def with_member(block, bit):
    return lax.ppermute(block, "grp", [(i, i ^ bit) for i in range(lax.axis_size("grp"))])


def together(*arrays):
    return lax.optimization_barrier(arrays)


def shards(orbitals, kernel, anchors, pair_count, pair_first, pair_second, pair_reach):
    groups = lax.axis_size("grp")
    fragment = lax.axis_index("orb")
    member = lax.axis_index("grp")
    odd = fragment % 2 == 1
    orb_dev, edge, plane = orbitals.shape
    chunks = plane // LANES
    rows = edge * chunks
    slab = rows // groups
    frag_size = groups * orb_dev
    places = jnp.stack([fragment, member]).astype(jnp.int32)
    screen = screen_terms(kernel)

    ahead_two = [to_fragment(orbitals[o : o + 1], -2) for o in range(orb_dev)]
    ahead_one = [
        with_twin(jnp.where(odd, orbitals[o : o + 1], ahead_two[o])) for o in range(orb_dev)
    ]
    pieces = {0: orbitals}
    bit = groups // 2
    while bit:
        for k in list(pieces):
            pieces[k ^ bit] = with_member(pieces[k], bit)
        bit //= 2
    pieces = [pieces[k] for k in range(groups)]

    (act, sent), back = pair_terms(
        places, pair_count, pair_first, pair_second, pair_reach, anchors, screen,
        pieces, ahead_one + ahead_two,
    )

    def own_slab(array, k):
        array = array.reshape(array.shape[0], groups, slab, LANES)
        return lax.dynamic_slice_in_dim(array, member ^ k, 1, axis=1)[:, 0]

    def halved(array, received):
        array = array + received
        half = array.shape[0] // 2
        cut = frag_size // orb_dev
        parts = [array[half:, i : i + cut] for i in range(0, frag_size, cut)]
        return array[:half], parts

    home = [None] * orb_dev
    twin = with_twin(back[orb_dev])
    received = with_member(sent, 1)
    twin, received = together(twin, received)
    act, parts = halved(act, received)
    bit = 2
    arrived = []
    for o in range(orb_dev):
        two = to_fragment(back[2 * orb_dev + o] + jnp.where(odd, 0.0, twin), 2)
        following = with_twin(back[orb_dev + o + 1]) if o + 1 < orb_dev else twin
        if bit < groups:
            arrived.append(with_member(parts[o], bit))
            two, following, arrived[-1] = together(two, following, arrived[-1])
        else:
            two, following = together(two, following)
        home[o] = back[o] + two + jnp.where(odd, twin, 0.0)
        twin = following
    while bit < groups:
        received = jnp.concatenate(arrived, axis=1)
        bit *= 2
        if bit < groups:
            act, parts = halved(act, received)
            arrived = [with_member(part, bit) for part in parts]
        else:
            act = act + received
    act = act[0]

    flat = [piece.reshape(orb_dev, rows, LANES) for piece in pieces]
    phi = jnp.stack([own_slab(piece, 0) for piece in flat])

    backs = [[None] * orb_dev for _ in range(groups)]
    for o in range(orb_dev):
        held = {0: {k: own_slab(home[o], k) for k in range(groups)}}
        bit = groups // 2
        while bit:
            for origin in list(held):
                going = [k for k in held[origin] if k & bit]
                staying = {k: v for k, v in held[origin].items() if not k & bit}
                moved = with_member(jnp.concatenate([held[origin][k] for k in going]), bit)
                held[origin] = staying
                held[origin ^ bit] = {k ^ bit: moved[i : i + 1] for i, k in enumerate(going)}
            bit //= 2
        for origin in range(groups):
            backs[origin][o] = held[origin][0]
    backs = [jnp.concatenate(parts) for parts in backs]

    correlation = correlation_terms(places, edge, act, home, phi, flat)
    bit = 1
    while bit < groups:
        correlation = correlation + with_member(correlation, bit)
        bit *= 2
    correlation = correlation[:, :frag_size]
    lagrange = 0.5 * (correlation + correlation.T)
    gradient = gradient_terms(places, edge, lagrange, act, phi, backs)
    return (gradient, lagrange[None])


def solution(mesh):
    placed = (P(("orb", "grp"), None, None), P(), P(), P("orb"), P("orb"), P("orb"), P("orb"))
    return jax.shard_map(
        shards,
        mesh=mesh,
        in_specs=placed,
        out_specs=(P("orb", "grp", None), P("orb", None, None)),
        check_vma=False,
    )
```

```python
import functools
import math

import jax
import jax.numpy as jnp
import numpy as np
from jax import lax
from jax.experimental import pallas as pl
from jax.experimental.pallas import tpu as pltpu
from jax.sharding import PartitionSpec as P

REACH = 2
LANES = 128
ROWS = 8
HALF = LANES // 2


class Number:
    def __init__(self, real, imag=None):
        self.real, self.imag = real, imag

    def __add__(self, other):
        if self.imag is None or other.imag is None:
            imag = self.imag if other.imag is None else other.imag
        else:
            imag = self.imag + other.imag
        return Number(self.real + other.real, imag)

    def __sub__(self, other):
        if other.imag is None:
            imag = self.imag
        else:
            imag = -other.imag if self.imag is None else self.imag - other.imag
        return Number(self.real - other.real, imag)

    def conj(self):
        return self if self.imag is None else Number(self.real, -self.imag)

    def scaled(self, factor):
        return Number(self.real * factor, None if self.imag is None else self.imag * factor)

    def turned(self, sign):
        if self.imag is None:
            return Number(jnp.zeros_like(self.real), self.real if sign > 0 else -self.real)
        return Number(-self.imag, self.real) if sign > 0 else Number(self.imag, -self.real)

    def plus_turned(self, other, sign):
        if sign < 0:
            return self.minus_turned(other)
        real = self.real if other.imag is None else self.real - other.imag
        return Number(real, other.real if self.imag is None else self.imag + other.real)

    def minus_turned(self, other):
        real = self.real if other.imag is None else self.real + other.imag
        return Number(real, -other.real if self.imag is None else self.imag - other.real)

    def times(self, angle):
        real, imag = math.cos(angle), math.sin(angle)
        if abs(imag) < 1e-12:
            return self if real > 0 else self.scaled(-1.0)
        if abs(real) < 1e-12:
            return self.turned(imag)
        if self.imag is None:
            return Number(self.real * real, self.real * imag)
        return Number(self.real * real - self.imag * imag, self.real * imag + self.imag * real)


def coprime(n):
    for p in (2, 3, 5, 7):
        power = 1
        while n % (power * p) == 0:
            power *= p
        if 1 < power < n:
            return power, n // power
    return None


def radix(n):
    return next((p for p in (4, 2, 3, 5, 7) if n % p == 0 and n > p), None)


def meeting(i, j, first, second):
    return next(k for k in range(first * second) if k % first == i and k % second == j)


def dft(values, sign):
    n = len(values)
    if n == 1:
        return values
    if n == 2:
        return [values[0] + values[1], values[0] - values[1]]
    if n == 3:
        a, b, c = values
        total, side = b + c, (b - c).scaled(math.sqrt(0.75))
        middle = a - total.scaled(0.5)
        return [a + total, middle.plus_turned(side, sign), middle.plus_turned(side, -sign)]
    if n == 4:
        a, b, c, d = values
        s, t, u, v = a + c, a - c, b + d, b - d
        return [s + u, t.plus_turned(v, sign), s - u, t.plus_turned(v, -sign)]
    out = [None] * n
    if coprime(n):
        first, second = coprime(n)
        columns = [
            dft([values[(i * second + j * first) % n] for i in range(first)], sign)
            for j in range(second)
        ]
        for i in range(first):
            row = dft([column[i] for column in columns], sign)
            for j in range(second):
                out[meeting(i, j, first, second)] = row[j]
        return out
    p = radix(n)
    if p:
        rest = n // p
        columns = [dft(values[j::p], sign) for j in range(p)]
        for i in range(rest):
            row = dft(
                [columns[j][i].times(sign * 2.0 * math.pi * i * j / n) for j in range(p)], sign
            )
            for j in range(p):
                out[i + rest * j] = row[j]
        return out
    for k in range(n):
        total = values[0]
        for j in range(1, n):
            total = total + values[j].times(sign * 2.0 * math.pi * (j * k % n) / n)
        out[k] = total
    return out


def real_dft(values):
    n = len(values)
    if n <= 4:
        out = dft(values, -1)
    else:
        out = [None] * n
        if coprime(n):
            first, second = coprime(n)
            columns = [
                real_dft([values[(i * second + j * first) % n] for i in range(first)])
                for j in range(second)
            ]
            for i in range(first // 2 + 1):
                entries = [column[i] for column in columns]
                alone = 2 * i % first == 0
                row = real_dft(entries) if alone else dft(entries, -1)
                for j in range(second):
                    out[meeting(i, j, first, second)] = row[j]
        elif radix(n):
            p = radix(n)
            rest = n // p
            columns = [real_dft(values[j::p]) for j in range(p)]
            for i in range(rest // 2 + 1):
                row = dft(
                    [columns[j][i].times(-2.0 * math.pi * i * j / n) for j in range(p)], -1
                )
                for j in range(p):
                    out[i + rest * j] = row[j]
        else:
            out = dft(values, -1)
    for k in range(1, n):
        if out[k] is None or (k > n // 2 and out[n - k] is not None):
            out[k] = out[n - k].conj()
    out[0] = Number(out[0].real)
    if n % 2 == 0:
        out[n // 2] = Number(out[n // 2].real)
    return out


def real_back(values):
    n = len(values)
    if n == 1:
        return [values[0].real]
    if n == 2:
        return [values[0].real + values[1].real, values[0].real - values[1].real]
    if n == 3:
        a, b = values[0].real, values[1]
        side = b.imag * math.sqrt(3.0)
        middle = a - b.real
        return [a + 2.0 * b.real, middle - side, middle + side]
    if n == 4:
        s, t = values[0].real + values[2].real, values[0].real - values[2].real
        u, v = 2.0 * values[1].real, 2.0 * values[1].imag
        return [s + u, t - v, s - u, t + v]
    out = [None] * n
    if coprime(n):
        first, second = coprime(n)
        rows = []
        for i in range(first // 2 + 1):
            entries = [values[meeting(i, j, first, second)] for j in range(second)]
            if 2 * i % first == 0:
                rows.append([Number(value) for value in real_back(entries)])
            else:
                rows.append(dft(entries, 1))
        for b in range(second):
            half = [row[b] for row in rows]
            whole = half + [half[first - i].conj() for i in range(len(half), first)]
            for a, value in enumerate(real_back(whole)):
                out[(a * second + b * first) % n] = value
        return out
    p = radix(n)
    if p:
        rest = n // p
        parts = []
        for i in range(p // 2 + 1):
            entries = values[i::p]
            if i == 0:
                parts.append([Number(value) for value in real_back(entries)])
            else:
                inner = dft(entries, 1)
                parts.append([inner[m].times(2.0 * math.pi * i * m / n) for m in range(rest)])
                if 2 * i == p:
                    parts[-1] = [Number(value.real) for value in parts[-1]]
        for m in range(rest):
            half = [part[m] for part in parts]
            whole = half + [half[p - i].conj() for i in range(len(half), p)]
            for j, value in enumerate(real_back(whole)):
                out[m + rest * j] = value
        return out
    return [value.real for value in dft(values, 1)]


def lane_matrices(edge):
    index = np.arange(edge)
    angles = 2.0 * np.pi / edge * (np.outer(index, index) % edge)
    found = []
    for sign in (-1.0, 1.0):
        full = np.zeros((2, 2, edge, 2, 2, edge))
        for side in range(2):
            full[0, side, :, 0, side] = np.cos(angles)
            full[0, side, :, 1, side] = sign * np.sin(angles)
            full[1, side, :, 0, side] = -sign * np.sin(angles)
            full[1, side, :, 1, side] = np.cos(angles)
        full = np.pad(full, [(0, 0), (0, 0), (0, HALF - edge)] * 2).reshape(2 * LANES, 2 * LANES)
        high = full.astype(jnp.bfloat16)
        low = (full - high.astype(np.float64)).astype(jnp.bfloat16)
        found.append(np.stack([high, low]))
    return found


def split_dot(real, imag, matrix):
    value = jnp.concatenate([real, imag], axis=1)
    high = value.astype(jnp.bfloat16)
    low = (value - high.astype(jnp.float32)).astype(jnp.bfloat16)
    product = jnp.dot(high, matrix[0], preferred_element_type=jnp.float32)
    product += jnp.dot(low, matrix[0], preferred_element_type=jnp.float32)
    product += jnp.dot(high, matrix[1], preferred_element_type=jnp.float32)
    return product[:, :LANES], product[:, LANES:]


def padded_half(edge):
    return -(-(edge // 2 + 1) // ROWS) * ROWS


def screen_kernel(edge, kernel_ref, flip_ref, mirror_ref, out_ref, flipped):
    exact = dict(precision=lax.Precision.HIGHEST, preferred_element_type=jnp.float32)
    flipped[...] = jnp.dot(flip_ref[...], kernel_ref[...], **exact)
    height = padded_half(edge)
    lane = lax.broadcasted_iota(jnp.int32, (edge, LANES), 1)
    out_ref[...] = jnp.zeros_like(out_ref)

    def piece(ref, y):
        begin, offset = divmod(y * edge, LANES)
        value = ref[:, begin * LANES : (begin + 1) * LANES]
        value = pltpu.roll(value, LANES - offset, 1) if offset else value
        if offset + edge > LANES:
            more = ref[:, (begin + 1) * LANES : (begin + 2) * LANES]
            value = jnp.where(lane < LANES - offset, value, pltpu.roll(more, LANES - offset, 1))
        return value

    for y in range(edge // 2 + 1):
        value = piece(kernel_ref, y)
        value = jnp.where(lane < HALF, value, pltpu.roll(value, HALF, 1))
        value = value + jnp.dot(piece(flipped, (edge - y) % edge), mirror_ref[...], **exact)
        value = value * (0.5 / float(edge**3))
        for t in range(edge // ROWS):
            out_ref[pl.ds(t * ROWS * height + y, ROWS, stride=height), :] = value[t * ROWS : (t + 1) * ROWS]


def screen_terms(kernel):
    edge, plane = kernel.shape
    index = np.arange(edge)
    flip = np.zeros((edge, edge), np.float32)
    flip[index, -index % edge] = 1.0
    mirror = np.zeros((LANES, LANES), np.float32)
    mirror[-index % edge, index] = 1.0
    mirror[-index % edge, HALF + index] = 1.0
    vmem = pl.BlockSpec(memory_space=pltpu.VMEM)
    return pl.pallas_call(
        functools.partial(screen_kernel, edge),
        out_shape=jax.ShapeDtypeStruct((edge * padded_half(edge), LANES), jnp.float32),
        in_specs=[vmem] * 3,
        out_specs=vmem,
        scratch_shapes=[pltpu.VMEM((edge, plane), jnp.float32)],
        compiler_params=pltpu.CompilerParams(vmem_limit_bytes=16 << 20),
        name="screen_terms",
    )(kernel, jnp.asarray(flip), jnp.asarray(mirror))


def pair_kernel(
    shape,
    places_ref,
    count_ref,
    first_ref,
    second_ref,
    reach_ref,
    anchors_ref,
    *refs,
):
    edge, orb_dev, groups, fragments, slots = shape
    plane = edge * edge
    chunks = plane // LANES
    tiles = edge // ROWS
    half = edge // 2 + 1
    height = padded_half(edge)
    returns_count = (REACH + 1) * orb_dev
    tables, refs = refs[:4], refs[4:]
    phi_refs, refs = refs[:groups], refs[groups:]
    (twin_ref, relay_ref, one_ref, two_ref), refs = refs[:4], refs[4:]
    act_outs, back_outs, refs = refs[:2], refs[2:6], refs[6:]
    (act, back, near, far, wide, moved, dense, cube, lower, upper, listed, load_sem, out_sem) = refs[:13]
    spots_ref, screen_ref, ahead_ref, behind_ref = refs[13:17]
    table_sem = refs[17]

    fragment = places_ref[0]
    member = places_ref[1]
    table_copies = [
        pltpu.make_async_copy(table, hold, table_sem.at[i])
        for i, (table, hold) in enumerate(zip(tables, refs[13:17]))
    ]
    for copy in table_copies:
        copy.start()
    lane = lax.broadcasted_iota(jnp.int32, (edge, LANES), 1)
    row = lax.broadcasted_iota(jnp.int32, (edge, LANES), 0)
    period = edge * LANES // math.gcd(edge, LANES) // edge
    group_chunks = period * edge // LANES
    stretch = next(n for n in (6, 4, 3, 2, 1) if chunks % n == 0)
    middle = pl.ds(edge, edge)

    def list_slots(slot, found):
        mine = (slot < count_ref[0]) & (lax.div(second_ref[slot], orb_dev) == member)

        @pl.when(mine)
        def _():
            listed[found] = slot

        return found + mine.astype(jnp.int32)

    found = lax.fori_loop(0, slots, list_slots, 0)

    def slot_of(turn, side):
        at = 2 * turn + side
        live = at < found
        return listed[jnp.where(live, at, 2 * turn)], live

    def far_copy(side, source):
        return pltpu.make_async_copy(source, far.at[side], load_sem.at[1, side])

    def start_loads(turn):
        for side in range(2):
            slot, _ = slot_of(turn, side)
            first, second, reach = first_ref[slot], second_ref[slot], reach_ref[slot]
            relative = lax.div(first, orb_dev) ^ member
            for k in range(groups):
                @pl.when(relative == k)
                def _():
                    pltpu.make_async_copy(
                        phi_refs[k].at[lax.rem(first, orb_dev)], near.at[side], load_sem.at[0, side]
                    ).start()
            own = lax.rem(second, orb_dev)

            @pl.when(reach == 0)
            def _():
                far_copy(side, phi_refs[0].at[own]).start()

            @pl.when((reach == 1) & (own == 0) & (lax.rem(fragment, 2) == 0))
            def _():
                far_copy(side, twin_ref.at[0]).start()

            @pl.when((reach == 1) & (own == 0) & (lax.rem(fragment, 2) == 1))
            def _():
                far_copy(side, relay_ref.at[0]).start()

            @pl.when((reach == 1) & (own > 0))
            def _():
                far_copy(side, one_ref.at[jnp.maximum(own - 1, 0)]).start()

            @pl.when(reach == 2)
            def _():
                far_copy(side, two_ref.at[own]).start()

    def wait_loads():
        for side in range(2):
            pltpu.make_async_copy(phi_refs[0].at[0], near.at[side], load_sem.at[0, side]).wait()
            far_copy(side, phi_refs[0].at[0]).wait()

    @pl.when(found > 0)
    def _():
        start_loads(0)

    act[...] = jnp.zeros_like(act)
    back[...] = jnp.zeros_like(back)
    for copy in table_copies:
        copy.wait()

    def offset_of(slot):
        partner = lax.rem(fragment + reach_ref[slot], fragments)
        return [anchors_ref[partner, i] - anchors_ref[fragment, i] for i in range(3)]

    def columns(k):
        return pl.ds(pl.multiple_of(k * LANES, LANES), LANES)

    def shifted(source, delta, k, count):
        shift = lax.rem(delta[1] * edge + delta[2] + 4 * plane, plane)
        start = lax.rem(plane - shift, plane)
        whole, part = lax.div(start, LANES), lax.rem(start, LANES)
        turn = lax.rem(LANES - part, LANES)
        down = edge - jnp.clip(delta[0], -edge, edge)
        x = row - delta[0]
        rows_inside = (x >= 0) & (x < edge)
        pieces = [
            pltpu.roll(source[lax.rem(k + i + whole, chunks), pl.ds(down, edge), :], turn, 1)
            for i in range(count + 1)
        ]
        out = []
        for i in range(count):
            value = jnp.where(lane < LANES - part, pieces[i], pieces[i + 1])
            y = spots_ref[0, pl.ds(k + i, 1), :] - delta[1]
            z = spots_ref[1, pl.ds(k + i, 1), :] - delta[2]
            inside = (y >= 0) & (y < edge) & (z >= 0) & (z < edge)
            out.append(jnp.where(inside & rows_inside, value, 0.0))
        return out

    def solve_two(turn, _):
        @pl.when(turn > 0)
        def _():
            start_loads(turn)

        wait_loads()
        picked = [slot_of(turn, side) for side in range(2)]
        offsets = [offset_of(slot) for slot, _ in picked]
        weights = [live.astype(jnp.float32) for _, live in picked]

        def widen(g, _):
            for side in range(2):
                for i in range(stretch):
                    k = g * stretch + i
                    wide[side, k, middle, :] = far[side, :, columns(k)]
            return 0

        lax.fori_loop(0, chunks // stretch, widen, 0)

        def make_density(g, _):
            for side in range(2):
                values = shifted(wide.at[side], offsets[side], g * stretch, stretch)
                for i, value in enumerate(values):
                    k = g * stretch + i
                    moved[side, k] = value
                    dense[side, k, middle, :] = weights[side] * near[side, :, columns(k)] * value
            return 0

        lax.fori_loop(0, chunks // stretch, make_density, 0)

        def spread(g, _):
            parts = [
                [dense[side, g * group_chunks + q, middle, :] for q in range(group_chunks)]
                for side in range(2)
            ]
            for i in range(period):
                begin, offset = divmod(i * edge, LANES)
                sides = []
                for side in range(2):
                    shift = (side * HALF - offset) % LANES
                    value = parts[side][begin]
                    value = pltpu.roll(value, shift, 1) if shift else value
                    if offset + edge > LANES:
                        more = parts[side][begin + 1]
                        more = pltpu.roll(more, shift, 1) if shift else more
                        value = jnp.where(lane < side * HALF + LANES - offset, value, more)
                    sides.append(value)
                at = pl.multiple_of((g * period + i) * edge, ROWS)
                cube[pl.ds(at, edge), :] = jnp.where(lane < HALF, sides[0], sides[1])
            return 0

        lax.fori_loop(0, edge // period, spread, 0)

        def tile(t, i, size):
            return pl.ds(pl.multiple_of(i * size + t * ROWS, ROWS), ROWS)

        def across(t, i, size):
            return pl.ds(t * (ROWS * size) + i, ROWS, stride=size)

        def over_y(t, _):
            values = real_dft([Number(cube[tile(t, i, edge), :]) for i in range(edge)])
            for i in range(half):
                at = tile(t, i, edge)
                lower[0, at, :] = values[i].real
                lower[1, at, :] = (
                    jnp.zeros((ROWS, LANES), jnp.float32) if values[i].imag is None else values[i].imag
                )
            return 0

        lax.fori_loop(0, tiles, over_y, 0)

        def over_x(t, _):
            at = [across(t, i, edge) for i in range(edge)]
            values = dft([Number(lower[0, a, :], lower[1, a, :]) for a in at], -1)
            for i in range(edge):
                upper[0, tile(t, i, height), :] = values[i].real
                upper[1, tile(t, i, height), :] = values[i].imag
            return 0

        lax.fori_loop(0, height // ROWS, over_x, 0)

        block = next(n for n in (512, 256, 128, 64, 32, 16, 8) if edge * height % n == 0)

        def screen(c, _):
            at = pl.ds(pl.multiple_of(c * block, block), block)
            real, imag = split_dot(upper[0, at, :], upper[1, at, :], ahead_ref)
            factor = screen_ref[at, :]
            real, imag = split_dot(real * factor, imag * factor, behind_ref)
            upper[0, at, :] = real
            upper[1, at, :] = imag
            return 0

        lax.fori_loop(0, edge * height // block, screen, 0)

        def back_x(t, _):
            at = [tile(t, i, height) for i in range(edge)]
            values = dft([Number(upper[0, a, :], upper[1, a, :]) for a in at], 1)
            for i in range(edge):
                upper[0, at[i], :] = values[i].real
                upper[1, at[i], :] = values[i].imag
            return 0

        lax.fori_loop(0, height // ROWS, back_x, 0)

        def back_y(t, _):
            at = [across(t, i, height) for i in range(half)]
            values = [Number(upper[0, a, :], upper[1, a, :]) for a in at]
            values = values + [values[edge - i].conj() for i in range(half, edge)]
            for i, value in enumerate(real_back(values)):
                cube[tile(t, i, edge), :] = value
            return 0

        lax.fori_loop(0, tiles, back_y, 0)

        firsts = [first_ref[slot] for slot, _ in picked]

        def collect(g, _):
            planes = [
                cube[pl.ds(pl.multiple_of((g * period + i) * edge, ROWS), edge), :]
                for i in range(period)
            ]
            for q in range(group_chunks):
                k = g * group_chunks + q
                for side in range(2):
                    value = None
                    for i in range(period):
                        begin = i * edge - q * LANES
                        if begin + edge <= 0 or begin >= LANES:
                            continue
                        shift = (begin - side * HALF) % LANES
                        piece = pltpu.roll(planes[i], shift, 1) if shift else planes[i]
                        value = piece if value is None else jnp.where(lane < begin, value, piece)
                    value = value * weights[side]
                    forward = value * moved[side, k]
                    dense[side, k, middle, :] = value * near[side, :, columns(k)]
                    for t in range(tiles):
                        at = pl.ds(t * (ROWS * chunks) + k, ROWS, stride=chunks)
                        act[firsts[side], at, :] += forward[t * ROWS : (t + 1) * ROWS]
            return 0

        lax.fori_loop(0, edge // period, collect, 0)

        homes = []
        for side in range(2):
            slot = picked[side][0]
            homes.append(reach_ref[slot] * orb_dev + lax.rem(second_ref[slot], orb_dev))
        returns = [[-d for d in delta] for delta in offsets]

        def send_back(g, _):
            for side in range(2):
                values = shifted(dense.at[side], returns[side], g * stretch, stretch)
                for i, value in enumerate(values):
                    for t in range(tiles):
                        at = pl.ds(t * (ROWS * chunks) + g * stretch + i, ROWS, stride=chunks)
                        back[homes[side], at, :] += value[t * ROWS : (t + 1) * ROWS]
            return 0

        lax.fori_loop(0, chunks // stretch, send_back, 0)
        return 0

    lax.fori_loop(0, lax.div(found + 1, 2), solve_two, 0)

    slab = plane * edge // LANES // groups
    copies = []
    spans = ((orb_dev, 1), (orb_dev + 1, orb_dev - 1), (2 * orb_dev, orb_dev), (0, orb_dev))
    for i, (begin, count) in enumerate(spans):
        copies.append(
            pltpu.make_async_copy(back.at[pl.ds(begin, count)], back_outs[i], out_sem.at[groups + i])
        )
    for k in range(groups):
        source = (member ^ k) * slab
        place = reversed_bits(k, groups)
        copies.append(
            pltpu.make_async_copy(
                act.at[:, pl.ds(pl.multiple_of(source, ROWS), slab), :],
                act_outs[2 * place // groups].at[place % (groups // 2)],
                out_sem.at[k],
            )
        )
    for copy in copies:
        copy.start()
    for copy in copies:
        copy.wait()


def reversed_bits(k, count):
    bits = count.bit_length() - 1
    return sum(((k >> i) & 1) << (bits - 1 - i) for i in range(bits))


def pair_terms(places, pair_count, pair_first, pair_second, pair_reach, anchors, screen, pieces, far):
    orb_dev, edge, plane = pieces[0].shape
    groups = len(pieces)
    frag_size = groups * orb_dev
    fragments = anchors.shape[0]
    slots = pair_first.shape[0]
    chunks = plane // LANES
    rows = edge * chunks
    height = padded_half(edge)
    returns_count = (REACH + 1) * orb_dev
    spots = np.arange(plane, dtype=np.int32).reshape(chunks, LANES)
    spots = jnp.asarray(np.stack([spots // edge, spots % edge]))
    ahead, behind = lane_matrices(edge)
    shape = (edge, orb_dev, groups, fragments, slots)
    smem = pl.BlockSpec(memory_space=pltpu.SMEM)
    hbm = pl.BlockSpec(memory_space=pltpu.HBM)
    f32 = jnp.float32
    tables = [spots, screen, jnp.asarray(ahead), jnp.asarray(behind)]
    found = pl.pallas_call(
        functools.partial(pair_kernel, shape),
        out_shape=[jax.ShapeDtypeStruct((groups // 2, frag_size, rows // groups, LANES), f32)] * 2
        + [
            jax.ShapeDtypeStruct((count, rows, LANES), f32)
            for count in (1, orb_dev - 1, orb_dev, orb_dev)
        ],
        in_specs=[smem] * 6 + [hbm] * (4 + groups + len(far)),
        out_specs=[hbm] * 6,
        scratch_shapes=[
            pltpu.VMEM((frag_size, rows, LANES), f32),
            pltpu.VMEM((returns_count, rows, LANES), f32),
            pltpu.VMEM((2, edge, plane), f32),
            pltpu.VMEM((2, edge, plane), f32),
            pltpu.VMEM((2, chunks, 3 * edge, LANES), f32),
            pltpu.VMEM((2, chunks, edge, LANES), f32),
            pltpu.VMEM((2, chunks, 3 * edge, LANES), f32),
            pltpu.VMEM((plane, LANES), f32),
            pltpu.VMEM((2, height * edge, LANES), f32),
            pltpu.VMEM((2, height * edge, LANES), f32),
            pltpu.SMEM((slots,), jnp.int32),
            pltpu.SemaphoreType.DMA((2, 2)),
            pltpu.SemaphoreType.DMA((groups + 4,)),
            *[pltpu.VMEM(table.shape, table.dtype) for table in tables],
            pltpu.SemaphoreType.DMA((4,)),
        ],
        compiler_params=pltpu.CompilerParams(vmem_limit_bytes=40 << 20),
        name="pair_terms",
    )(
        places, pair_count, pair_first, pair_second, pair_reach, anchors,
        *tables, *pieces, *far,
    )
    return found[:2], found[2:]


def flatten_kernel(shape, places_ref, *refs):
    edge, orb_dev, groups = shape
    pieces, (flat_ref, slab_ref) = refs[:groups], refs[groups:]
    member = places_ref[1]
    chunks = edge * edge // LANES
    slab = slab_ref.shape[1]
    for k in range(groups):
        for o in range(orb_dev):
            def move(j, _):
                value = pieces[k][o, :, pl.ds(pl.multiple_of(j * LANES, LANES), LANES)]
                for t in range(edge // ROWS):
                    at = pl.ds(t * (ROWS * chunks) + j, ROWS, stride=chunks)
                    flat_ref[k * orb_dev + o, at, :] = value[t * ROWS : (t + 1) * ROWS]
                return 0

            lax.fori_loop(0, chunks, move, 0)
    slab_ref[...] = flat_ref[:, pl.ds(pl.multiple_of(member * slab, ROWS), slab), :]


def flatten_terms(places, pieces):
    orb_dev, edge, plane = pieces[0].shape
    groups = len(pieces)
    rows = edge * plane // LANES
    frag_size = groups * orb_dev
    smem = pl.BlockSpec(memory_space=pltpu.SMEM)
    vmem = pl.BlockSpec(memory_space=pltpu.VMEM)
    return pl.pallas_call(
        functools.partial(flatten_kernel, (edge, orb_dev, groups)),
        out_shape=(
            jax.ShapeDtypeStruct((frag_size, rows, LANES), jnp.float32),
            jax.ShapeDtypeStruct((frag_size, rows // groups, LANES), jnp.float32),
        ),
        in_specs=[smem] + [vmem] * groups,
        out_specs=(vmem, vmem),
        compiler_params=pltpu.CompilerParams(vmem_limit_bytes=24 << 20),
        name="flatten_terms",
    )(places, *pieces)


def home_kernel(shape, places_ref, flat_ref, phi_ref, kept_ref, *refs):
    edge, orb_dev, groups, parts = shape
    arrived, refs = refs[:parts], refs[parts:]
    (own_ref, twin_ref, relay_ref, one_ref, two_ref), refs = refs[:5], refs[5:]
    act_ref, outs, total = refs[0], refs[1 : 1 + groups], refs[1 + groups]
    fragment, member = places_ref[0], places_ref[1]
    odd = lax.rem(fragment, 2) == 1
    frag_size = orb_dev * groups
    slab = act_ref.shape[1]
    rows = flat_ref.shape[1]
    cut = frag_size // parts
    for i in range(parts):
        span = slice(i * cut, (i + 1) * cut)
        act_ref[span] = kept_ref[0, span] + arrived[i][0]

    @pl.when(odd)
    def _():
        total[0] = own_ref[0] + two_ref[0] + twin_ref[0]

    @pl.when(jnp.logical_not(odd))
    def _():
        total[0] = own_ref[0] + two_ref[0] + relay_ref[0]

    for o in range(1, orb_dev):
        total[o] = own_ref[o] + two_ref[o] + one_ref[o - 1]

    row = lax.broadcasted_iota(jnp.int32, (frag_size, LANES), 0)
    lane = lax.broadcasted_iota(jnp.int32, (frag_size, LANES), 1)

    def products(lefts, rights, length, step):
        def add(i, sums):
            at = pl.ds(pl.multiple_of(i * step, ROWS), step)
            right = [ref[index, at, :].reshape(step // ROWS, ROWS, LANES) for ref, index in rights]
            out = []
            for n, (ref, index) in enumerate(lefts):
                left = ref[index, at, :].reshape(step // ROWS, ROWS, LANES)
                for m in range(len(rights)):
                    out.append(sums[n * len(rights) + m] + jnp.sum(left * right[m], axis=0))
            return tuple(out)

        zero = jnp.zeros((ROWS, LANES), jnp.float32)
        return lax.fori_loop(0, length // step, add, (zero,) * (len(lefts) * len(rights)))

    result = jnp.zeros((frag_size, LANES), jnp.float32)
    scale = 1.0 / float(edge**3)
    step = next(n for n in (72, 24, 8) if slab % n == 0)
    for half in range(0, frag_size, 4):
        bs = range(half, min(half + 4, frag_size))
        sums = products(
            [(phi_ref, a) for a in range(frag_size)], [(act_ref, b) for b in bs], slab, step
        )
        for a in range(frag_size):
            place = (member ^ (a // orb_dev)) * orb_dev + a % orb_dev
            for i, b in enumerate(bs):
                value = jnp.sum(sums[a * len(bs) + i], keepdims=True)
                result = jnp.where((row == place) & (lane == b), value, result)
    sums = products(
        [(flat_ref, a) for a in range(frag_size)], [(total, b) for b in range(orb_dev)], rows, step
    )
    for a in range(frag_size):
        place = (member ^ (a // orb_dev)) * orb_dev + a % orb_dev
        for b in range(orb_dev):
            value = jnp.sum(sums[a * orb_dev + b], keepdims=True)
            at = (row == place) & (lane == member * orb_dev + b)
            result = jnp.where(at, result + value, result)

    for k in range(groups):
        begin = pl.multiple_of((member ^ k) * slab, ROWS)
        for o in range(orb_dev):
            outs[k][o * slab : (o + 1) * slab, :] = total[o, pl.ds(begin, slab), :]
        outs[k][orb_dev * slab :, :] = result * scale


def home_terms(places, edge, flat, phi, kept, arrived, own, twin, relay, one, two):
    frag_size, slab = phi.shape[:2]
    orb_dev, rows = own.shape[:2]
    groups = frag_size // orb_dev
    smem = pl.BlockSpec(memory_space=pltpu.SMEM)
    vmem = pl.BlockSpec(memory_space=pltpu.VMEM)
    f32 = jnp.float32
    found = pl.pallas_call(
        functools.partial(home_kernel, (edge, orb_dev, groups, len(arrived))),
        out_shape=[jax.ShapeDtypeStruct((frag_size, slab, LANES), f32)]
        + [jax.ShapeDtypeStruct((orb_dev * slab + frag_size, LANES), f32)] * groups,
        in_specs=[smem] + [vmem] * (8 + len(arrived)),
        out_specs=[vmem] * (1 + groups),
        scratch_shapes=[pltpu.VMEM((orb_dev, rows, LANES), f32)],
        compiler_params=pltpu.CompilerParams(vmem_limit_bytes=32 << 20),
        name="home_terms",
    )(places, flat, phi, kept, *arrived, own, twin, relay, one, two)
    return found[0], found[1:]


def gradient_kernel(shape, places_ref, act_ref, phi_ref, *refs):
    edge, orb_dev, groups = shape
    parcels, (out_ref, lagrange_ref, weights, hold) = refs[:groups], refs[groups:]
    member = places_ref[1]
    frag_size = orb_dev * groups
    chunks = edge * edge // LANES
    slab_rows = edge // groups
    slab = slab_rows * chunks
    sums = [parcel[orb_dev * slab :, :] for parcel in parcels]
    while len(sums) > 1:
        sums = [sums[i] + sums[i + 1] for i in range(0, len(sums), 2)]
    square = jnp.concatenate([sums[0], jnp.zeros((LANES - frag_size, LANES), jnp.float32)], axis=0)
    lagrange = 0.5 * (square + square.T)[:frag_size, :]
    lagrange_ref[...] = lagrange[:, :frag_size]
    weights[...] = lagrange

    for k in range(groups):
        for o in range(orb_dev):
            a = (member ^ k) * orb_dev + o
            value = act_ref[a] + parcels[k][o * slab : (o + 1) * slab, :]
            lane = lax.broadcasted_iota(jnp.int32, (1, LANES), 1)
            for q in range(groups):
                for p in range(orb_dev):
                    line = weights[pl.ds((member ^ q) * orb_dev + p, 1), :]
                    factor = jnp.sum(jnp.where(lane == a, line, 0.0), axis=1, keepdims=True)
                    value = value - factor * phi_ref[q * orb_dev + p]
            hold[pl.ds(pl.multiple_of(a * slab, ROWS), slab), :] = value
    for x in range(slab_rows):
        for j in range(chunks):
            value = hold[pl.ds(x * chunks + j, frag_size, stride=slab), :]
            out_ref[x, :, j * LANES : (j + 1) * LANES] = value


def gradient_terms(places, edge, act, phi, parcels):
    groups = len(parcels)
    frag_size, slab = act.shape[:2]
    smem = pl.BlockSpec(memory_space=pltpu.SMEM)
    vmem = pl.BlockSpec(memory_space=pltpu.VMEM)
    f32 = jnp.float32
    gradient, lagrange = pl.pallas_call(
        functools.partial(gradient_kernel, (edge, frag_size // groups, groups)),
        out_shape=(
            jax.ShapeDtypeStruct((edge // groups, frag_size, edge * edge), f32),
            jax.ShapeDtypeStruct((frag_size, frag_size), f32),
        ),
        in_specs=[smem] + [vmem] * (2 + groups),
        out_specs=(vmem, vmem),
        scratch_shapes=[
            pltpu.VMEM((frag_size, LANES), f32),
            pltpu.VMEM((frag_size * slab, LANES), f32),
        ],
        compiler_params=pltpu.CompilerParams(vmem_limit_bytes=24 << 20),
        name="gradient_terms",
    )(places, act, phi, *parcels)
    return gradient.transpose(1, 0, 2), lagrange


def to_fragment(block, distance, senders=None):
    devices = lax.axis_size("orb")
    senders = range(devices) if senders is None else range(senders, devices, 2)
    return lax.ppermute(block, "orb", [(i, (i + distance) % devices) for i in senders])


def with_twin(block):
    return lax.ppermute(block, "orb", [(i, i ^ 1) for i in range(lax.axis_size("orb"))])


def with_member(block, bit):
    return lax.ppermute(block, "grp", [(i, i ^ bit) for i in range(lax.axis_size("grp"))])


def shards(orbitals, kernel, anchors, pair_count, pair_first, pair_second, pair_reach):
    groups = lax.axis_size("grp")
    orb_dev, edge, plane = orbitals.shape
    frag_size = groups * orb_dev
    places = jnp.stack([lax.axis_index("orb"), lax.axis_index("grp")]).astype(jnp.int32)
    screen = screen_terms(kernel)

    two = to_fragment(orbitals, -2)
    twin = with_twin(orbitals[:1])
    one = to_fragment(orbitals[1:], -1)
    relay = to_fragment(twin, -2, 1)
    pieces = {0: orbitals}
    bit = groups // 2
    while bit:
        for k in list(pieces):
            pieces[k ^ bit] = with_member(pieces[k], bit)
        bit //= 2
    pieces = [pieces[k] for k in range(groups)]

    (kept, sent), (back_first, back_rest, back_two, own) = pair_terms(
        places, pair_count, pair_first, pair_second, pair_reach, anchors, screen,
        pieces, [twin, relay, one, two],
    )

    two = to_fragment(back_two, 2)
    twin = with_twin(back_first)
    one = to_fragment(back_rest, 1)
    relay = to_fragment(twin, 2, 0)

    bit = 1
    arrived = [with_member(sent, bit)]
    while 2 * bit < groups:
        kept = kept + jnp.concatenate(arrived, axis=1)
        half = kept.shape[0] // 2
        cut = frag_size // orb_dev
        bit *= 2
        arrived = [
            with_member(kept[half:, i : i + cut], bit) for i in range(0, frag_size, cut)
        ]
        kept = kept[:half]

    flat, phi = flatten_terms(places, pieces)
    act, parcels = home_terms(places, edge, flat, phi, kept, arrived, own, twin, relay, one, two)
    received = []
    for k in range(groups):
        parcel, bit = parcels[k], groups // 2
        while bit:
            if k & bit:
                parcel = with_member(parcel, bit)
            bit //= 2
        received.append(parcel)
    gradient, lagrange = gradient_terms(places, edge, act, phi, received)
    return (gradient, lagrange[None])


def solution(mesh):
    placed = (P(("orb", "grp"), None, None), P(), P(), P("orb"), P("orb"), P("orb"), P("orb"))
    return jax.shard_map(
        shards,
        mesh=mesh,
        in_specs=placed,
        out_specs=(P("orb", "grp", None), P("orb", None, None)),
        check_vma=False,
    )
```

```python
import functools
import math

import jax
import jax.numpy as jnp
import numpy as np
from jax import lax
from jax.experimental import pallas as pl
from jax.experimental.pallas import tpu as pltpu
from jax.sharding import PartitionSpec as P

REACH = 2
LANES = 128
ROWS = 8
HALF = LANES // 2


class Number:
    def __init__(self, real, imag=None):
        self.real, self.imag = real, imag

    def __add__(self, other):
        if self.imag is None or other.imag is None:
            imag = self.imag if other.imag is None else other.imag
        else:
            imag = self.imag + other.imag
        return Number(self.real + other.real, imag)

    def __sub__(self, other):
        if other.imag is None:
            imag = self.imag
        else:
            imag = -other.imag if self.imag is None else self.imag - other.imag
        return Number(self.real - other.real, imag)

    def conj(self):
        return self if self.imag is None else Number(self.real, -self.imag)

    def scaled(self, factor):
        return Number(self.real * factor, None if self.imag is None else self.imag * factor)

    def turned(self, sign):
        if self.imag is None:
            return Number(jnp.zeros_like(self.real), self.real if sign > 0 else -self.real)
        return Number(-self.imag, self.real) if sign > 0 else Number(self.imag, -self.real)

    def plus_turned(self, other, sign):
        if sign < 0:
            return self.minus_turned(other)
        real = self.real if other.imag is None else self.real - other.imag
        return Number(real, other.real if self.imag is None else self.imag + other.real)

    def minus_turned(self, other):
        real = self.real if other.imag is None else self.real + other.imag
        return Number(real, -other.real if self.imag is None else self.imag - other.real)

    def times(self, angle):
        real, imag = math.cos(angle), math.sin(angle)
        if abs(imag) < 1e-12:
            return self if real > 0 else self.scaled(-1.0)
        if abs(real) < 1e-12:
            return self.turned(imag)
        if self.imag is None:
            return Number(self.real * real, self.real * imag)
        return Number(self.real * real - self.imag * imag, self.real * imag + self.imag * real)


def coprime(n):
    for p in (2, 3, 5, 7):
        power = 1
        while n % (power * p) == 0:
            power *= p
        if 1 < power < n:
            return power, n // power
    return None


def radix(n):
    return next((p for p in (4, 2, 3, 5, 7) if n % p == 0 and n > p), None)


def meeting(i, j, first, second):
    return next(k for k in range(first * second) if k % first == i and k % second == j)


def dft(values, sign):
    n = len(values)
    if n == 1:
        return values
    if n == 2:
        return [values[0] + values[1], values[0] - values[1]]
    if n == 3:
        a, b, c = values
        total, side = b + c, (b - c).scaled(math.sqrt(0.75))
        middle = a - total.scaled(0.5)
        return [a + total, middle.plus_turned(side, sign), middle.plus_turned(side, -sign)]
    if n == 4:
        a, b, c, d = values
        s, t, u, v = a + c, a - c, b + d, b - d
        return [s + u, t.plus_turned(v, sign), s - u, t.plus_turned(v, -sign)]
    out = [None] * n
    if coprime(n):
        first, second = coprime(n)
        columns = [
            dft([values[(i * second + j * first) % n] for i in range(first)], sign)
            for j in range(second)
        ]
        for i in range(first):
            row = dft([column[i] for column in columns], sign)
            for j in range(second):
                out[meeting(i, j, first, second)] = row[j]
        return out
    p = radix(n)
    if p:
        rest = n // p
        columns = [dft(values[j::p], sign) for j in range(p)]
        for i in range(rest):
            row = dft(
                [columns[j][i].times(sign * 2.0 * math.pi * i * j / n) for j in range(p)], sign
            )
            for j in range(p):
                out[i + rest * j] = row[j]
        return out
    for k in range(n):
        total = values[0]
        for j in range(1, n):
            total = total + values[j].times(sign * 2.0 * math.pi * (j * k % n) / n)
        out[k] = total
    return out


def real_dft(values):
    n = len(values)
    if n <= 4:
        out = dft(values, -1)
    else:
        out = [None] * n
        if coprime(n):
            first, second = coprime(n)
            columns = [
                real_dft([values[(i * second + j * first) % n] for i in range(first)])
                for j in range(second)
            ]
            for i in range(first // 2 + 1):
                entries = [column[i] for column in columns]
                alone = 2 * i % first == 0
                row = real_dft(entries) if alone else dft(entries, -1)
                for j in range(second):
                    out[meeting(i, j, first, second)] = row[j]
        elif radix(n):
            p = radix(n)
            rest = n // p
            columns = [real_dft(values[j::p]) for j in range(p)]
            for i in range(rest // 2 + 1):
                row = dft(
                    [columns[j][i].times(-2.0 * math.pi * i * j / n) for j in range(p)], -1
                )
                for j in range(p):
                    out[i + rest * j] = row[j]
        else:
            out = dft(values, -1)
    for k in range(1, n):
        if out[k] is None or (k > n // 2 and out[n - k] is not None):
            out[k] = out[n - k].conj()
    out[0] = Number(out[0].real)
    if n % 2 == 0:
        out[n // 2] = Number(out[n // 2].real)
    return out


def real_back(values):
    n = len(values)
    if n == 1:
        return [values[0].real]
    if n == 2:
        return [values[0].real + values[1].real, values[0].real - values[1].real]
    if n == 3:
        a, b = values[0].real, values[1]
        side = b.imag * math.sqrt(3.0)
        middle = a - b.real
        return [a + 2.0 * b.real, middle - side, middle + side]
    if n == 4:
        s, t = values[0].real + values[2].real, values[0].real - values[2].real
        u, v = 2.0 * values[1].real, 2.0 * values[1].imag
        return [s + u, t - v, s - u, t + v]
    out = [None] * n
    if coprime(n):
        first, second = coprime(n)
        rows = []
        for i in range(first // 2 + 1):
            entries = [values[meeting(i, j, first, second)] for j in range(second)]
            if 2 * i % first == 0:
                rows.append([Number(value) for value in real_back(entries)])
            else:
                rows.append(dft(entries, 1))
        for b in range(second):
            half = [row[b] for row in rows]
            whole = half + [half[first - i].conj() for i in range(len(half), first)]
            for a, value in enumerate(real_back(whole)):
                out[(a * second + b * first) % n] = value
        return out
    p = radix(n)
    if p:
        rest = n // p
        parts = []
        for i in range(p // 2 + 1):
            entries = values[i::p]
            if i == 0:
                parts.append([Number(value) for value in real_back(entries)])
            else:
                inner = dft(entries, 1)
                parts.append([inner[m].times(2.0 * math.pi * i * m / n) for m in range(rest)])
                if 2 * i == p:
                    parts[-1] = [Number(value.real) for value in parts[-1]]
        for m in range(rest):
            half = [part[m] for part in parts]
            whole = half + [half[p - i].conj() for i in range(len(half), p)]
            for j, value in enumerate(real_back(whole)):
                out[m + rest * j] = value
        return out
    return [value.real for value in dft(values, 1)]


def lane_matrices(edge):
    index = np.arange(edge)
    angles = 2.0 * np.pi / edge * (np.outer(index, index) % edge)
    found = []
    for sign in (-1.0, 1.0):
        full = np.zeros((2, 2, edge, 2, 2, edge))
        for side in range(2):
            full[0, side, :, 0, side] = np.cos(angles)
            full[0, side, :, 1, side] = sign * np.sin(angles)
            full[1, side, :, 0, side] = -sign * np.sin(angles)
            full[1, side, :, 1, side] = np.cos(angles)
        full = np.pad(full, [(0, 0), (0, 0), (0, HALF - edge)] * 2).reshape(2 * LANES, 2 * LANES)
        high = full.astype(jnp.bfloat16)
        low = (full - high.astype(np.float64)).astype(jnp.bfloat16)
        found.append(np.concatenate([high, high, low]))
    return found


def split_dot(real, imag, matrix):
    value = jnp.concatenate([real, imag], axis=1)
    high = value.astype(jnp.bfloat16)
    low = (value - high.astype(jnp.float32)).astype(jnp.bfloat16)
    product = jnp.dot(
        jnp.concatenate([high, low, high], axis=1), matrix[...], preferred_element_type=jnp.float32
    )
    return product[:, :LANES], product[:, LANES:]


def padded_half(edge):
    return -(-(edge // 2 + 1) // ROWS) * ROWS


def screen_kernel(edge, numbers_ref, kernel_ref, flip_ref, mirror_ref, out_ref, kept_ref, flipped):
    for i in range(numbers_ref.shape[0]):
        kept_ref[i] = numbers_ref[i]
    exact = dict(precision=lax.Precision.HIGHEST, preferred_element_type=jnp.float32)
    flipped[...] = jnp.dot(flip_ref[...], kernel_ref[...], **exact)
    height = padded_half(edge)
    lane = lax.broadcasted_iota(jnp.int32, (edge, LANES), 1)
    out_ref[...] = jnp.zeros_like(out_ref)

    def piece(ref, y):
        begin, offset = divmod(y * edge, LANES)
        value = ref[:, begin * LANES : (begin + 1) * LANES]
        value = pltpu.roll(value, LANES - offset, 1) if offset else value
        if offset + edge > LANES:
            more = ref[:, (begin + 1) * LANES : (begin + 2) * LANES]
            value = jnp.where(lane < LANES - offset, value, pltpu.roll(more, LANES - offset, 1))
        return value

    for y in range(edge // 2 + 1):
        value = piece(kernel_ref, y)
        value = jnp.where(lane < HALF, value, pltpu.roll(value, HALF, 1))
        value = value + jnp.dot(piece(flipped, (edge - y) % edge), mirror_ref[...], **exact)
        value = value * (0.5 / float(edge**3))
        for t in range(edge // ROWS):
            out_ref[pl.ds(t * ROWS * height + y, ROWS, stride=height), :] = value[t * ROWS : (t + 1) * ROWS]


def screen_terms(numbers, kernel):
    edge, plane = kernel.shape
    index = np.arange(edge)
    flip = np.zeros((edge, edge), np.float32)
    flip[index, -index % edge] = 1.0
    mirror = np.zeros((LANES, LANES), np.float32)
    mirror[-index % edge, index] = 1.0
    mirror[-index % edge, HALF + index] = 1.0
    smem = pl.BlockSpec(memory_space=pltpu.SMEM)
    vmem = pl.BlockSpec(memory_space=pltpu.VMEM)
    return pl.pallas_call(
        functools.partial(screen_kernel, edge),
        out_shape=(
            jax.ShapeDtypeStruct((edge * padded_half(edge), LANES), jnp.float32),
            jax.ShapeDtypeStruct(numbers.shape, numbers.dtype),
        ),
        in_specs=[smem] + [vmem] * 3,
        out_specs=(vmem, smem),
        scratch_shapes=[pltpu.VMEM((edge, plane), jnp.float32)],
        compiler_params=pltpu.CompilerParams(vmem_limit_bytes=16 << 20),
        name="screen_terms",
    )(numbers, kernel, jnp.asarray(flip), jnp.asarray(mirror))


def pair_kernel(
    shape,
    numbers_ref,
    *refs,
):
    edge, orb_dev, groups, fragments, slots = shape
    plane = edge * edge
    chunks = plane // LANES
    tiles = edge // ROWS
    half = edge // 2 + 1
    height = padded_half(edge)
    returns_count = (REACH + 1) * orb_dev
    tables, refs = refs[:3], refs[3:]
    phi_refs, refs = refs[:groups], refs[groups:]
    (twin_ref, relay_ref, one_ref, two_ref), refs = refs[:4], refs[4:]
    act_outs, back_outs, refs = refs[:2], refs[2:6], refs[6:]
    (act, back, near, far, wide, moved, dense, cube, lower, upper, listed, load_sem, out_sem) = refs[:13]
    screen_ref, ahead_ref, behind_ref, table_sem = refs[13:]

    fragment, member, live_slots = numbers_ref[0], numbers_ref[1], numbers_ref[2]

    def first_of(slot):
        return numbers_ref[3 + slot]

    def second_of(slot):
        return numbers_ref[3 + slots + slot]

    def reach_of(slot):
        return numbers_ref[3 + 2 * slots + slot]

    def anchor(place, axis):
        return numbers_ref[3 + 3 * slots + 3 * place + axis]

    table_copies = [
        pltpu.make_async_copy(table, hold, table_sem.at[i])
        for i, (table, hold) in enumerate(zip(tables, refs[13:16]))
    ]
    for copy in table_copies:
        copy.start()
    lane = lax.broadcasted_iota(jnp.int32, (edge, LANES), 1)
    row = lax.broadcasted_iota(jnp.int32, (edge, LANES), 0)
    period = edge * LANES // math.gcd(edge, LANES) // edge
    group_chunks = period * edge // LANES
    stretch = next(n for n in (6, 4, 3, 2, 1) if chunks % n == 0)
    middle = pl.ds(edge, edge)

    def list_slots(slot, found):
        mine = (slot < live_slots) & (lax.div(second_of(slot), orb_dev) == member)

        @pl.when(mine)
        def _():
            listed[found] = slot

        return found + mine.astype(jnp.int32)

    found = lax.fori_loop(0, slots, list_slots, 0)

    def slot_of(turn, side):
        at = 2 * turn + side
        live = at < found
        return listed[jnp.where(live, at, 2 * turn)], live

    def far_copy(side, source):
        return pltpu.make_async_copy(source, far.at[side], load_sem.at[1, side])

    def start_loads(turn):
        for side in range(2):
            slot, _ = slot_of(turn, side)
            first, second, reach = first_of(slot), second_of(slot), reach_of(slot)
            relative = lax.div(first, orb_dev) ^ member
            for k in range(groups):
                @pl.when(relative == k)
                def _():
                    pltpu.make_async_copy(
                        phi_refs[k].at[lax.rem(first, orb_dev)], near.at[side], load_sem.at[0, side]
                    ).start()
            own = lax.rem(second, orb_dev)

            @pl.when(reach == 0)
            def _():
                far_copy(side, phi_refs[0].at[own]).start()

            @pl.when((reach == 1) & (own == 0) & (lax.rem(fragment, 2) == 0))
            def _():
                far_copy(side, twin_ref.at[0]).start()

            @pl.when((reach == 1) & (own == 0) & (lax.rem(fragment, 2) == 1))
            def _():
                far_copy(side, relay_ref.at[0]).start()

            @pl.when((reach == 1) & (own > 0))
            def _():
                far_copy(side, one_ref.at[jnp.maximum(own - 1, 0)]).start()

            @pl.when(reach == 2)
            def _():
                far_copy(side, two_ref.at[own]).start()

    def wait_loads():
        for side in range(2):
            pltpu.make_async_copy(phi_refs[0].at[0], near.at[side], load_sem.at[0, side]).wait()
            far_copy(side, phi_refs[0].at[0]).wait()

    @pl.when(found > 0)
    def _():
        start_loads(0)

    act[...] = jnp.zeros_like(act)
    back[...] = jnp.zeros_like(back)
    for copy in table_copies:
        copy.wait()

    def offset_of(slot):
        partner = lax.rem(fragment + reach_of(slot), fragments)
        return [anchor(partner, i) - anchor(fragment, i) for i in range(3)]

    def steps(count, body, most):
        width = max(n for n in range(1, most + 1) if count % n == 0)

        def step(i, _):
            for j in range(width):
                body(i * width + j)
            return 0

        if width == count:
            step(0, 0)
        else:
            lax.fori_loop(0, count // width, step, 0)

    def columns(k):
        return pl.ds(pl.multiple_of(k * LANES, LANES), LANES)

    def shifted(source, delta, k, count):
        shift = lax.rem(delta[1] * edge + delta[2] + 4 * plane, plane)
        start = lax.rem(plane - shift, plane)
        whole, part = lax.div(start, LANES), lax.rem(start, LANES)
        turn = lax.rem(LANES - part, LANES)
        down = edge - jnp.clip(delta[0], -edge, edge)
        x = row - delta[0]
        rows_inside = (x >= 0) & (x < edge)
        pieces = [
            pltpu.roll(source[lax.rem(k + i + whole, chunks), pl.ds(down, edge), :], turn, 1)
            for i in range(count + 1)
        ]
        out = []
        for i in range(count):
            value = jnp.where(lane < LANES - part, pieces[i], pieces[i + 1])
            spot = (k + i) * LANES + lax.broadcasted_iota(jnp.int32, (1, LANES), 1)
            y = ((spot.astype(jnp.float32) + 0.5) * (1.0 / edge)).astype(jnp.int32)
            z = spot - y * edge - delta[2]
            y = y - delta[1]
            inside = (y >= 0) & (y < edge) & (z >= 0) & (z < edge)
            out.append(jnp.where(inside & rows_inside, value, 0.0))
        return out

    def solve_two(turn, _):
        @pl.when(turn > 0)
        def _():
            start_loads(turn)

        wait_loads()
        picked = [slot_of(turn, side) for side in range(2)]
        offsets = [offset_of(slot) for slot, _ in picked]
        weights = [live.astype(jnp.float32) for _, live in picked]

        def widen(g):
            for side in range(2):
                for i in range(stretch):
                    k = g * stretch + i
                    wide[side, k, middle, :] = far[side, :, columns(k)]

        steps(chunks // stretch, widen, 3)

        def make_density(g):
            for side in range(2):
                values = shifted(wide.at[side], offsets[side], g * stretch, stretch)
                for i, value in enumerate(values):
                    k = g * stretch + i
                    moved[side, k] = value
                    dense[side, k, middle, :] = weights[side] * near[side, :, columns(k)] * value

        steps(chunks // stretch, make_density, 3)

        def spread(g):
            parts = [
                [dense[side, g * group_chunks + q, middle, :] for q in range(group_chunks)]
                for side in range(2)
            ]
            for i in range(period):
                begin, offset = divmod(i * edge, LANES)
                sides = []
                for side in range(2):
                    shift = (side * HALF - offset) % LANES
                    value = parts[side][begin]
                    value = pltpu.roll(value, shift, 1) if shift else value
                    if offset + edge > LANES:
                        more = parts[side][begin + 1]
                        more = pltpu.roll(more, shift, 1) if shift else more
                        value = jnp.where(lane < side * HALF + LANES - offset, value, more)
                    sides.append(value)
                at = pl.multiple_of((g * period + i) * edge, ROWS)
                cube[pl.ds(at, edge), :] = jnp.where(lane < HALF, sides[0], sides[1])

        steps(edge // period, spread, 2)

        def tile(t, i, size):
            return pl.ds(pl.multiple_of(i * size + t * ROWS, ROWS), ROWS)

        def across(t, i, size):
            return pl.ds(t * (ROWS * size) + i, ROWS, stride=size)

        def over_y(t):
            values = real_dft([Number(cube[tile(t, i, edge), :]) for i in range(edge)])
            for i in range(half):
                at = tile(t, i, edge)
                lower[0, at, :] = values[i].real
                lower[1, at, :] = (
                    jnp.zeros((ROWS, LANES), jnp.float32) if values[i].imag is None else values[i].imag
                )

        steps(tiles, over_y, 3)

        def over_x(t):
            at = [across(t, i, edge) for i in range(edge)]
            values = dft([Number(lower[0, a, :], lower[1, a, :]) for a in at], -1)
            for i in range(edge):
                upper[0, tile(t, i, height), :] = values[i].real
                upper[1, tile(t, i, height), :] = values[i].imag

        steps(height // ROWS, over_x, 2)

        block = next(n for n in (512, 256, 128, 64, 32, 16, 8) if edge * height % n == 0)

        def screen(c):
            at = pl.ds(pl.multiple_of(c * block, block), block)
            real, imag = split_dot(upper[0, at, :], upper[1, at, :], ahead_ref)
            factor = screen_ref[at, :]
            real, imag = split_dot(real * factor, imag * factor, behind_ref)
            upper[0, at, :] = real
            upper[1, at, :] = imag

        steps(edge * height // block, screen, 3)

        def back_x(t):
            at = [tile(t, i, height) for i in range(edge)]
            values = dft([Number(upper[0, a, :], upper[1, a, :]) for a in at], 1)
            for i in range(edge):
                upper[0, at[i], :] = values[i].real
                upper[1, at[i], :] = values[i].imag

        steps(height // ROWS, back_x, 2)

        def back_y(t):
            at = [across(t, i, height) for i in range(half)]
            values = [Number(upper[0, a, :], upper[1, a, :]) for a in at]
            values = values + [values[edge - i].conj() for i in range(half, edge)]
            for i, value in enumerate(real_back(values)):
                cube[tile(t, i, edge), :] = value

        steps(tiles, back_y, 3)

        firsts = [first_of(slot) for slot, _ in picked]

        def collect(g):
            planes = [
                cube[pl.ds(pl.multiple_of((g * period + i) * edge, ROWS), edge), :]
                for i in range(period)
            ]
            for q in range(group_chunks):
                k = g * group_chunks + q
                for side in range(2):
                    value = None
                    for i in range(period):
                        begin = i * edge - q * LANES
                        if begin + edge <= 0 or begin >= LANES:
                            continue
                        shift = (begin - side * HALF) % LANES
                        piece = pltpu.roll(planes[i], shift, 1) if shift else planes[i]
                        value = piece if value is None else jnp.where(lane < begin, value, piece)
                    value = value * weights[side]
                    forward = value * moved[side, k]
                    dense[side, k, middle, :] = value * near[side, :, columns(k)]
                    for t in range(tiles):
                        at = pl.ds(t * (ROWS * chunks) + k, ROWS, stride=chunks)
                        act[firsts[side], at, :] += forward[t * ROWS : (t + 1) * ROWS]

        steps(edge // period, collect, 2)

        homes = []
        for side in range(2):
            slot = picked[side][0]
            homes.append(reach_of(slot) * orb_dev + lax.rem(second_of(slot), orb_dev))
        returns = [[-d for d in delta] for delta in offsets]

        def send_back(g):
            for side in range(2):
                values = shifted(dense.at[side], returns[side], g * stretch, stretch)
                for i, value in enumerate(values):
                    for t in range(tiles):
                        at = pl.ds(t * (ROWS * chunks) + g * stretch + i, ROWS, stride=chunks)
                        back[homes[side], at, :] += value[t * ROWS : (t + 1) * ROWS]

        steps(chunks // stretch, send_back, 3)
        return 0

    lax.fori_loop(0, lax.div(found + 1, 2), solve_two, 0)

    slab = plane * edge // LANES // groups
    copies = []
    spans = ((orb_dev, 1), (orb_dev + 1, orb_dev - 1), (2 * orb_dev, orb_dev), (0, orb_dev))
    for i, (begin, count) in enumerate(spans):
        copies.append(
            pltpu.make_async_copy(back.at[pl.ds(begin, count)], back_outs[i], out_sem.at[groups + i])
        )
    for k in range(groups):
        source = (member ^ k) * slab
        place = reversed_bits(k, groups)
        copies.append(
            pltpu.make_async_copy(
                act.at[:, pl.ds(pl.multiple_of(source, ROWS), slab), :],
                act_outs[2 * place // groups].at[place % (groups // 2)],
                out_sem.at[k],
            )
        )
    for copy in copies:
        copy.start()
    for copy in copies:
        copy.wait()


def reversed_bits(k, count):
    bits = count.bit_length() - 1
    return sum(((k >> i) & 1) << (bits - 1 - i) for i in range(bits))


def pair_terms(numbers, fragments, slots, screen, pieces, far):
    orb_dev, edge, plane = pieces[0].shape
    groups = len(pieces)
    frag_size = groups * orb_dev
    chunks = plane // LANES
    rows = edge * chunks
    height = padded_half(edge)
    returns_count = (REACH + 1) * orb_dev
    ahead, behind = lane_matrices(edge)
    shape = (edge, orb_dev, groups, fragments, slots)
    smem = pl.BlockSpec(memory_space=pltpu.SMEM)
    hbm = pl.BlockSpec(memory_space=pltpu.HBM)
    f32 = jnp.float32
    tables = [screen, jnp.asarray(ahead), jnp.asarray(behind)]
    found = pl.pallas_call(
        functools.partial(pair_kernel, shape),
        out_shape=[jax.ShapeDtypeStruct((groups // 2, frag_size, rows // groups, LANES), f32)] * 2
        + [
            jax.ShapeDtypeStruct((count, rows, LANES), f32)
            for count in (1, orb_dev - 1, orb_dev, orb_dev)
        ],
        in_specs=[smem] + [hbm] * (3 + groups + len(far)),
        out_specs=[hbm] * 6,
        scratch_shapes=[
            pltpu.VMEM((frag_size, rows, LANES), f32),
            pltpu.VMEM((returns_count, rows, LANES), f32),
            pltpu.VMEM((2, edge, plane), f32),
            pltpu.VMEM((2, edge, plane), f32),
            pltpu.VMEM((2, chunks, 3 * edge, LANES), f32),
            pltpu.VMEM((2, chunks, edge, LANES), f32),
            pltpu.VMEM((2, chunks, 3 * edge, LANES), f32),
            pltpu.VMEM((plane, LANES), f32),
            pltpu.VMEM((2, height * edge, LANES), f32),
            pltpu.VMEM((2, height * edge, LANES), f32),
            pltpu.SMEM((slots,), jnp.int32),
            pltpu.SemaphoreType.DMA((2, 2)),
            pltpu.SemaphoreType.DMA((groups + 4,)),
            *[pltpu.VMEM(table.shape, table.dtype) for table in tables],
            pltpu.SemaphoreType.DMA((3,)),
        ],
        compiler_params=pltpu.CompilerParams(vmem_limit_bytes=40 << 20),
        name="pair_terms",
    )(numbers, *tables, *pieces, *far)
    return found[:2], found[2:]


def flatten_kernel(shape, places_ref, *refs):
    edge, orb_dev, groups = shape
    pieces, (flat_ref, slab_ref) = refs[:groups], refs[groups:]
    member = places_ref[1]
    chunks = edge * edge // LANES
    slab = slab_ref.shape[1]
    for k in range(groups):
        for o in range(orb_dev):
            def move(j, _):
                value = pieces[k][o, :, pl.ds(pl.multiple_of(j * LANES, LANES), LANES)]
                for t in range(edge // ROWS):
                    at = pl.ds(t * (ROWS * chunks) + j, ROWS, stride=chunks)
                    flat_ref[k * orb_dev + o, at, :] = value[t * ROWS : (t + 1) * ROWS]
                return 0

            lax.fori_loop(0, chunks, move, 0)
    slab_ref[...] = flat_ref[:, pl.ds(pl.multiple_of(member * slab, ROWS), slab), :]


def flatten_terms(places, pieces):
    orb_dev, edge, plane = pieces[0].shape
    groups = len(pieces)
    rows = edge * plane // LANES
    frag_size = groups * orb_dev
    smem = pl.BlockSpec(memory_space=pltpu.SMEM)
    vmem = pl.BlockSpec(memory_space=pltpu.VMEM)
    return pl.pallas_call(
        functools.partial(flatten_kernel, (edge, orb_dev, groups)),
        out_shape=(
            jax.ShapeDtypeStruct((frag_size, rows, LANES), jnp.float32),
            jax.ShapeDtypeStruct((frag_size, rows // groups, LANES), jnp.float32),
        ),
        in_specs=[smem] + [vmem] * groups,
        out_specs=(vmem, vmem),
        compiler_params=pltpu.CompilerParams(vmem_limit_bytes=24 << 20),
        name="flatten_terms",
    )(places, *pieces)


def home_kernel(shape, places_ref, flat_ref, phi_ref, kept_ref, *refs):
    edge, orb_dev, groups, parts = shape
    arrived, refs = refs[:parts], refs[parts:]
    (own_ref, twin_ref, relay_ref, one_ref, two_ref), refs = refs[:5], refs[5:]
    act_ref, outs, total = refs[0], refs[1 : 1 + groups], refs[1 + groups]
    fragment, member = places_ref[0], places_ref[1]
    odd = lax.rem(fragment, 2) == 1
    frag_size = orb_dev * groups
    slab = act_ref.shape[1]
    rows = flat_ref.shape[1]
    cut = frag_size // parts
    for i in range(parts):
        span = slice(i * cut, (i + 1) * cut)
        act_ref[span] = kept_ref[0, span] + arrived[i][0]

    @pl.when(odd)
    def _():
        total[0] = own_ref[0] + two_ref[0] + twin_ref[0]

    @pl.when(jnp.logical_not(odd))
    def _():
        total[0] = own_ref[0] + two_ref[0] + relay_ref[0]

    for o in range(1, orb_dev):
        total[o] = own_ref[o] + two_ref[o] + one_ref[o - 1]

    row = lax.broadcasted_iota(jnp.int32, (frag_size, LANES), 0)
    lane = lax.broadcasted_iota(jnp.int32, (frag_size, LANES), 1)

    def products(lefts, rights, length, step):
        def add(i, sums):
            at = pl.ds(pl.multiple_of(i * step, ROWS), step)
            right = [ref[index, at, :].reshape(step // ROWS, ROWS, LANES) for ref, index in rights]
            out = []
            for n, (ref, index) in enumerate(lefts):
                left = ref[index, at, :].reshape(step // ROWS, ROWS, LANES)
                for m in range(len(rights)):
                    out.append(sums[n * len(rights) + m] + jnp.sum(left * right[m], axis=0))
            return tuple(out)

        zero = jnp.zeros((ROWS, LANES), jnp.float32)
        return lax.fori_loop(0, length // step, add, (zero,) * (len(lefts) * len(rights)))

    result = jnp.zeros((frag_size, LANES), jnp.float32)
    scale = 1.0 / float(edge**3)
    step = next(n for n in (72, 24, 8) if slab % n == 0)
    for half in range(0, frag_size, 4):
        bs = range(half, min(half + 4, frag_size))
        sums = products(
            [(phi_ref, a) for a in range(frag_size)], [(act_ref, b) for b in bs], slab, step
        )
        for a in range(frag_size):
            place = (member ^ (a // orb_dev)) * orb_dev + a % orb_dev
            for i, b in enumerate(bs):
                value = jnp.sum(sums[a * len(bs) + i], keepdims=True)
                result = jnp.where((row == place) & (lane == b), value, result)
    sums = products(
        [(flat_ref, a) for a in range(frag_size)], [(total, b) for b in range(orb_dev)], rows, step
    )
    for a in range(frag_size):
        place = (member ^ (a // orb_dev)) * orb_dev + a % orb_dev
        for b in range(orb_dev):
            value = jnp.sum(sums[a * orb_dev + b], keepdims=True)
            at = (row == place) & (lane == member * orb_dev + b)
            result = jnp.where(at, result + value, result)

    for k in range(groups):
        begin = pl.multiple_of((member ^ k) * slab, ROWS)
        for o in range(orb_dev):
            outs[k][o * slab : (o + 1) * slab, :] = total[o, pl.ds(begin, slab), :]
        outs[k][orb_dev * slab :, :] = result * scale


def home_terms(places, edge, flat, phi, kept, arrived, own, twin, relay, one, two):
    frag_size, slab = phi.shape[:2]
    orb_dev, rows = own.shape[:2]
    groups = frag_size // orb_dev
    smem = pl.BlockSpec(memory_space=pltpu.SMEM)
    vmem = pl.BlockSpec(memory_space=pltpu.VMEM)
    f32 = jnp.float32
    found = pl.pallas_call(
        functools.partial(home_kernel, (edge, orb_dev, groups, len(arrived))),
        out_shape=[jax.ShapeDtypeStruct((frag_size, slab, LANES), f32)]
        + [jax.ShapeDtypeStruct((orb_dev * slab + frag_size, LANES), f32)] * groups,
        in_specs=[smem] + [vmem] * (8 + len(arrived)),
        out_specs=[vmem] * (1 + groups),
        scratch_shapes=[pltpu.VMEM((orb_dev, rows, LANES), f32)],
        compiler_params=pltpu.CompilerParams(vmem_limit_bytes=32 << 20),
        name="home_terms",
    )(places, flat, phi, kept, *arrived, own, twin, relay, one, two)
    return found[0], found[1:]


def gradient_kernel(shape, places_ref, act_ref, phi_ref, *refs):
    edge, orb_dev, groups = shape
    parcels, (out_ref, lagrange_ref, weights, hold) = refs[:groups], refs[groups:]
    member = places_ref[1]
    frag_size = orb_dev * groups
    chunks = edge * edge // LANES
    slab_rows = edge // groups
    slab = slab_rows * chunks
    sums = [parcel[orb_dev * slab :, :] for parcel in parcels]
    while len(sums) > 1:
        sums = [sums[i] + sums[i + 1] for i in range(0, len(sums), 2)]
    square = jnp.concatenate([sums[0], jnp.zeros((LANES - frag_size, LANES), jnp.float32)], axis=0)
    lagrange = 0.5 * (square + square.T)[:frag_size, :]
    lagrange_ref[...] = lagrange[:, :frag_size]
    weights[...] = lagrange

    for k in range(groups):
        for o in range(orb_dev):
            a = (member ^ k) * orb_dev + o
            value = act_ref[a] + parcels[k][o * slab : (o + 1) * slab, :]
            lane = lax.broadcasted_iota(jnp.int32, (1, LANES), 1)
            for q in range(groups):
                for p in range(orb_dev):
                    line = weights[pl.ds((member ^ q) * orb_dev + p, 1), :]
                    factor = jnp.sum(jnp.where(lane == a, line, 0.0), axis=1, keepdims=True)
                    value = value - factor * phi_ref[q * orb_dev + p]
            hold[pl.ds(pl.multiple_of(a * slab, ROWS), slab), :] = value
    for x in range(slab_rows):
        for j in range(chunks):
            value = hold[pl.ds(x * chunks + j, frag_size, stride=slab), :]
            out_ref[x, :, j * LANES : (j + 1) * LANES] = value


def gradient_terms(places, edge, act, phi, parcels):
    groups = len(parcels)
    frag_size, slab = act.shape[:2]
    smem = pl.BlockSpec(memory_space=pltpu.SMEM)
    vmem = pl.BlockSpec(memory_space=pltpu.VMEM)
    f32 = jnp.float32
    gradient, lagrange = pl.pallas_call(
        functools.partial(gradient_kernel, (edge, frag_size // groups, groups)),
        out_shape=(
            jax.ShapeDtypeStruct((edge // groups, frag_size, edge * edge), f32),
            jax.ShapeDtypeStruct((frag_size, frag_size), f32),
        ),
        in_specs=[smem] + [vmem] * (2 + groups),
        out_specs=(vmem, vmem),
        scratch_shapes=[
            pltpu.VMEM((frag_size, LANES), f32),
            pltpu.VMEM((frag_size * slab, LANES), f32),
        ],
        compiler_params=pltpu.CompilerParams(vmem_limit_bytes=24 << 20),
        name="gradient_terms",
    )(places, act, phi, *parcels)
    return gradient.transpose(1, 0, 2), lagrange


def together(*arrays):
    return lax.optimization_barrier(arrays)


def to_fragment(block, distance, senders=None):
    devices = lax.axis_size("orb")
    senders = range(devices) if senders is None else range(senders, devices, 2)
    return lax.ppermute(block, "orb", [(i, (i + distance) % devices) for i in senders])


def with_twin(block):
    return lax.ppermute(block, "orb", [(i, i ^ 1) for i in range(lax.axis_size("orb"))])


def with_member(block, bit):
    return lax.ppermute(block, "grp", [(i, i ^ bit) for i in range(lax.axis_size("grp"))])


def shards(orbitals, kernel, anchors, pair_count, pair_first, pair_second, pair_reach):
    groups = lax.axis_size("grp")
    orb_dev, edge, plane = orbitals.shape
    frag_size = groups * orb_dev
    places = jnp.stack([lax.axis_index("orb"), lax.axis_index("grp")]).astype(jnp.int32)
    numbers = [places, pair_count, pair_first, pair_second, pair_reach, anchors.reshape(-1)]
    screen, numbers = screen_terms(jnp.concatenate(numbers), kernel)

    two = to_fragment(orbitals, -2)
    twin = with_twin(orbitals[:1])
    one = to_fragment(orbitals[1:], -1)
    relay = to_fragment(twin, -2, 1)
    pieces = {0: orbitals}
    bit = groups // 2
    while bit:
        for k in list(pieces):
            pieces[k ^ bit] = with_member(pieces[k], bit)
        if bit == groups // 2:
            pieces[bit], one = together(pieces[bit], one)
        bit //= 2
    pieces = [pieces[k] for k in range(groups)]

    (kept, sent), (back_first, back_rest, back_two, own) = pair_terms(
        numbers, anchors.shape[0], pair_first.shape[0], screen, pieces, [twin, relay, one, two]
    )

    two = to_fragment(back_two, 2)
    one = to_fragment(back_rest, 1)
    bit = 1
    arrived = [with_member(sent, bit)]
    while 2 * bit < groups:
        kept = kept + jnp.concatenate(arrived, axis=1)
        if bit == 1:
            kept, back_first = together(kept, back_first)
        half = kept.shape[0] // 2
        cut = frag_size // orb_dev
        bit *= 2
        arrived = [
            with_member(kept[half:, i : i + cut], bit) for i in range(0, frag_size, cut)
        ]
        kept = kept[:half]
    twin = with_twin(back_first)
    relay = to_fragment(twin, 2, 0)

    flat, phi = flatten_terms(places, pieces)
    act, parcels = home_terms(places, edge, flat, phi, kept, arrived, own, twin, relay, one, two)
    received = []
    for k in range(groups):
        parcel, bit = parcels[k], groups // 2
        while bit:
            if k & bit:
                parcel = with_member(parcel, bit)
            bit //= 2
        received.append(parcel)
    gradient, lagrange = gradient_terms(places, edge, act, phi, received)
    return (gradient, lagrange[None])


def solution(mesh):
    placed = (P(("orb", "grp"), None, None), P(), P(), P("orb"), P("orb"), P("orb"), P("orb"))
    return jax.shard_map(
        shards,
        mesh=mesh,
        in_specs=placed,
        out_specs=(P("orb", "grp", None), P("orb", None, None)),
        check_vma=False,
    )
```

```python
import functools
import math

import jax
import jax.numpy as jnp
import numpy as np
from jax import lax
from jax.experimental import pallas as pl
from jax.experimental.pallas import tpu as pltpu
from jax.sharding import PartitionSpec as P

REACH = 2
LANES = 128
ROWS = 8
HALF = LANES // 2


class Number:
    def __init__(self, real, imag=None):
        self.real, self.imag = real, imag

    def __add__(self, other):
        if self.imag is None or other.imag is None:
            imag = self.imag if other.imag is None else other.imag
        else:
            imag = self.imag + other.imag
        return Number(self.real + other.real, imag)

    def __sub__(self, other):
        if other.imag is None:
            imag = self.imag
        else:
            imag = -other.imag if self.imag is None else self.imag - other.imag
        return Number(self.real - other.real, imag)

    def conj(self):
        return self if self.imag is None else Number(self.real, -self.imag)

    def scaled(self, factor):
        return Number(self.real * factor, None if self.imag is None else self.imag * factor)

    def turned(self, sign):
        if self.imag is None:
            return Number(jnp.zeros_like(self.real), self.real if sign > 0 else -self.real)
        return Number(-self.imag, self.real) if sign > 0 else Number(self.imag, -self.real)

    def plus_turned(self, other, sign):
        if sign < 0:
            return self.minus_turned(other)
        real = self.real if other.imag is None else self.real - other.imag
        return Number(real, other.real if self.imag is None else self.imag + other.real)

    def minus_turned(self, other):
        real = self.real if other.imag is None else self.real + other.imag
        return Number(real, -other.real if self.imag is None else self.imag - other.real)

    def times(self, angle):
        real, imag = math.cos(angle), math.sin(angle)
        if abs(imag) < 1e-12:
            return self if real > 0 else self.scaled(-1.0)
        if abs(real) < 1e-12:
            return self.turned(imag)
        if self.imag is None:
            return Number(self.real * real, self.real * imag)
        return Number(self.real * real - self.imag * imag, self.real * imag + self.imag * real)


def coprime(n):
    for p in (2, 3, 5, 7):
        power = 1
        while n % (power * p) == 0:
            power *= p
        if 1 < power < n:
            return power, n // power
    return None


def radix(n):
    return next((p for p in (4, 2, 3, 5, 7) if n % p == 0 and n > p), None)


def meeting(i, j, first, second):
    return next(k for k in range(first * second) if k % first == i and k % second == j)


def dft(values, sign):
    n = len(values)
    if n == 1:
        return values
    if n == 2:
        return [values[0] + values[1], values[0] - values[1]]
    if n == 3:
        a, b, c = values
        total, side = b + c, (b - c).scaled(math.sqrt(0.75))
        middle = a - total.scaled(0.5)
        return [a + total, middle.plus_turned(side, sign), middle.plus_turned(side, -sign)]
    if n == 4:
        a, b, c, d = values
        s, t, u, v = a + c, a - c, b + d, b - d
        return [s + u, t.plus_turned(v, sign), s - u, t.plus_turned(v, -sign)]
    out = [None] * n
    if coprime(n):
        first, second = coprime(n)
        columns = [
            dft([values[(i * second + j * first) % n] for i in range(first)], sign)
            for j in range(second)
        ]
        for i in range(first):
            row = dft([column[i] for column in columns], sign)
            for j in range(second):
                out[meeting(i, j, first, second)] = row[j]
        return out
    p = radix(n)
    if p:
        rest = n // p
        columns = [dft(values[j::p], sign) for j in range(p)]
        for i in range(rest):
            row = dft(
                [columns[j][i].times(sign * 2.0 * math.pi * i * j / n) for j in range(p)], sign
            )
            for j in range(p):
                out[i + rest * j] = row[j]
        return out
    for k in range(n):
        total = values[0]
        for j in range(1, n):
            total = total + values[j].times(sign * 2.0 * math.pi * (j * k % n) / n)
        out[k] = total
    return out


def real_dft(values):
    n = len(values)
    if n <= 4:
        out = dft(values, -1)
    else:
        out = [None] * n
        if coprime(n):
            first, second = coprime(n)
            columns = [
                real_dft([values[(i * second + j * first) % n] for i in range(first)])
                for j in range(second)
            ]
            for i in range(first // 2 + 1):
                entries = [column[i] for column in columns]
                alone = 2 * i % first == 0
                row = real_dft(entries) if alone else dft(entries, -1)
                for j in range(second):
                    out[meeting(i, j, first, second)] = row[j]
        elif radix(n):
            p = radix(n)
            rest = n // p
            columns = [real_dft(values[j::p]) for j in range(p)]
            for i in range(rest // 2 + 1):
                row = dft(
                    [columns[j][i].times(-2.0 * math.pi * i * j / n) for j in range(p)], -1
                )
                for j in range(p):
                    out[i + rest * j] = row[j]
        else:
            out = dft(values, -1)
    for k in range(1, n):
        if out[k] is None or (k > n // 2 and out[n - k] is not None):
            out[k] = out[n - k].conj()
    out[0] = Number(out[0].real)
    if n % 2 == 0:
        out[n // 2] = Number(out[n // 2].real)
    return out


def real_back(values):
    n = len(values)
    if n == 1:
        return [values[0].real]
    if n == 2:
        return [values[0].real + values[1].real, values[0].real - values[1].real]
    if n == 3:
        a, b = values[0].real, values[1]
        side = b.imag * math.sqrt(3.0)
        middle = a - b.real
        return [a + 2.0 * b.real, middle - side, middle + side]
    if n == 4:
        s, t = values[0].real + values[2].real, values[0].real - values[2].real
        u, v = 2.0 * values[1].real, 2.0 * values[1].imag
        return [s + u, t - v, s - u, t + v]
    out = [None] * n
    if coprime(n):
        first, second = coprime(n)
        rows = []
        for i in range(first // 2 + 1):
            entries = [values[meeting(i, j, first, second)] for j in range(second)]
            if 2 * i % first == 0:
                rows.append([Number(value) for value in real_back(entries)])
            else:
                rows.append(dft(entries, 1))
        for b in range(second):
            half = [row[b] for row in rows]
            whole = half + [half[first - i].conj() for i in range(len(half), first)]
            for a, value in enumerate(real_back(whole)):
                out[(a * second + b * first) % n] = value
        return out
    p = radix(n)
    if p:
        rest = n // p
        parts = []
        for i in range(p // 2 + 1):
            entries = values[i::p]
            if i == 0:
                parts.append([Number(value) for value in real_back(entries)])
            else:
                inner = dft(entries, 1)
                parts.append([inner[m].times(2.0 * math.pi * i * m / n) for m in range(rest)])
                if 2 * i == p:
                    parts[-1] = [Number(value.real) for value in parts[-1]]
        for m in range(rest):
            half = [part[m] for part in parts]
            whole = half + [half[p - i].conj() for i in range(len(half), p)]
            for j, value in enumerate(real_back(whole)):
                out[m + rest * j] = value
        return out
    return [value.real for value in dft(values, 1)]


def lane_matrices(edge):
    index = np.arange(edge)
    angles = 2.0 * np.pi / edge * (np.outer(index, index) % edge)
    found = []
    for sign in (-1.0, 1.0):
        full = np.zeros((2, 2, edge, 2, 2, edge))
        for side in range(2):
            full[0, side, :, 0, side] = np.cos(angles)
            full[0, side, :, 1, side] = sign * np.sin(angles)
            full[1, side, :, 0, side] = -sign * np.sin(angles)
            full[1, side, :, 1, side] = np.cos(angles)
        full = np.pad(full, [(0, 0), (0, 0), (0, HALF - edge)] * 2).reshape(2 * LANES, 2 * LANES)
        high = full.astype(jnp.bfloat16)
        low = (full - high.astype(np.float64)).astype(jnp.bfloat16)
        found.append(np.concatenate([high, high, low]))
    return found


def split_dot(real, imag, matrix):
    value = jnp.concatenate([real, imag], axis=1)
    high = value.astype(jnp.bfloat16)
    low = (value - high.astype(jnp.float32)).astype(jnp.bfloat16)
    product = jnp.dot(
        jnp.concatenate([high, low, high], axis=1), matrix[...], preferred_element_type=jnp.float32
    )
    return product[:, :LANES], product[:, LANES:]


def padded_half(edge):
    return -(-(edge // 2 + 1) // ROWS) * ROWS


def screen_kernel(
    edge,
    numbers_ref,
    kernel_ref,
    flip_ref,
    mirror_ref,
    ahead_ref,
    behind_ref,
    out_ref,
    kept_ref,
    ahead_out,
    behind_out,
    flipped,
):
    for i in range(numbers_ref.shape[0]):
        kept_ref[i] = numbers_ref[i]
    ahead_out[...] = ahead_ref[...]
    behind_out[...] = behind_ref[...]
    exact = dict(precision=lax.Precision.HIGHEST, preferred_element_type=jnp.float32)
    flipped[...] = jnp.dot(flip_ref[...], kernel_ref[...], **exact)
    height = padded_half(edge)
    lane = lax.broadcasted_iota(jnp.int32, (edge, LANES), 1)
    out_ref[...] = jnp.zeros_like(out_ref)

    def piece(ref, y):
        begin, offset = divmod(y * edge, LANES)
        value = ref[:, begin * LANES : (begin + 1) * LANES]
        value = pltpu.roll(value, LANES - offset, 1) if offset else value
        if offset + edge > LANES:
            more = ref[:, (begin + 1) * LANES : (begin + 2) * LANES]
            value = jnp.where(lane < LANES - offset, value, pltpu.roll(more, LANES - offset, 1))
        return value

    for y in range(edge // 2 + 1):
        value = piece(kernel_ref, y)
        value = jnp.where(lane < HALF, value, pltpu.roll(value, HALF, 1))
        value = value + jnp.dot(piece(flipped, (edge - y) % edge), mirror_ref[...], **exact)
        value = value * (0.5 / float(edge**3))
        for t in range(edge // ROWS):
            out_ref[pl.ds(t * ROWS * height + y, ROWS, stride=height), :] = value[t * ROWS : (t + 1) * ROWS]


def screen_terms(numbers, kernel):
    edge, plane = kernel.shape
    index = np.arange(edge)
    flip = np.zeros((edge, edge), np.float32)
    flip[index, -index % edge] = 1.0
    mirror = np.zeros((LANES, LANES), np.float32)
    mirror[-index % edge, index] = 1.0
    mirror[-index % edge, HALF + index] = 1.0
    tables = [jnp.asarray(table) for table in lane_matrices(edge)]
    smem = pl.BlockSpec(memory_space=pltpu.SMEM)
    vmem = pl.BlockSpec(memory_space=pltpu.VMEM)
    return pl.pallas_call(
        functools.partial(screen_kernel, edge),
        out_shape=[
            jax.ShapeDtypeStruct((edge * padded_half(edge), LANES), jnp.float32),
            jax.ShapeDtypeStruct(numbers.shape, numbers.dtype),
        ]
        + [jax.ShapeDtypeStruct(table.shape, table.dtype) for table in tables],
        in_specs=[smem] + [vmem] * 5,
        out_specs=[vmem, smem, vmem, vmem],
        scratch_shapes=[pltpu.VMEM((edge, plane), jnp.float32)],
        compiler_params=pltpu.CompilerParams(vmem_limit_bytes=8 << 20),
        name="screen_terms",
    )(numbers, kernel, jnp.asarray(flip), jnp.asarray(mirror), *tables)


def pair_kernel(
    shape,
    numbers_ref,
    *refs,
):
    edge, orb_dev, groups, fragments, slots = shape
    plane = edge * edge
    chunks = plane // LANES
    tiles = edge // ROWS
    half = edge // 2 + 1
    height = padded_half(edge)
    returns_count = (REACH + 1) * orb_dev
    tables, refs = refs[:3], refs[3:]
    phi_refs, refs = refs[:groups], refs[groups:]
    (twin_ref, relay_ref, one_ref, two_ref, rest_ref), refs = refs[:5], refs[5:]
    act_outs, back_outs, refs = refs[:2], refs[2:6], refs[6:]
    (act, back, near, far, wide, moved, dense, cube, lower, upper, listed, load_sem, out_sem) = refs[:13]
    screen_ref, ahead_ref, behind_ref, table_sem = refs[13:]

    fragment, member, live_slots = numbers_ref[0], numbers_ref[1], numbers_ref[2]

    def first_of(slot):
        return numbers_ref[3 + slot]

    def second_of(slot):
        return numbers_ref[3 + slots + slot]

    def reach_of(slot):
        return numbers_ref[3 + 2 * slots + slot]

    def anchor(place, axis):
        return numbers_ref[3 + 3 * slots + 3 * place + axis]

    table_copies = [
        pltpu.make_async_copy(table, hold, table_sem.at[i])
        for i, (table, hold) in enumerate(zip(tables, refs[13:16]))
    ]
    for copy in table_copies:
        copy.start()
    lane = lax.broadcasted_iota(jnp.int32, (edge, LANES), 1)
    row = lax.broadcasted_iota(jnp.int32, (edge, LANES), 0)
    period = edge * LANES // math.gcd(edge, LANES) // edge
    group_chunks = period * edge // LANES
    stretch = next(n for n in (6, 4, 3, 2, 1) if chunks % n == 0)
    middle = pl.ds(edge, edge)

    def list_slots(slot, found):
        mine = (slot < live_slots) & (lax.div(second_of(slot), orb_dev) == member)

        @pl.when(mine)
        def _():
            listed[found] = slot

        return found + mine.astype(jnp.int32)

    found = lax.fori_loop(0, slots, list_slots, 0)
    turns = lax.div(found + 1, 2)

    def slot_of(turn, side):
        at = 2 * turn + side
        live = at < found
        return listed[jnp.where(live, at, 2 * turn)], live

    def far_copy(side, source):
        return pltpu.make_async_copy(source, far.at[side], load_sem.at[1, side])

    def start_loads(turn):
        for side in range(2):
            slot, _ = slot_of(turn, side)
            first, second, reach = first_of(slot), second_of(slot), reach_of(slot)
            relative = lax.div(first, orb_dev) ^ member
            for k in range(groups):
                @pl.when(relative == k)
                def _():
                    pltpu.make_async_copy(
                        phi_refs[k].at[lax.rem(first, orb_dev)],
                        near.at[lax.rem(turn, 2), side],
                        load_sem.at[0, side],
                    ).start()
            own = lax.rem(second, orb_dev)

            @pl.when(reach == 0)
            def _():
                far_copy(side, phi_refs[0].at[own]).start()

            @pl.when((reach == 1) & (own == 0) & (lax.rem(fragment, 2) == 0))
            def _():
                far_copy(side, twin_ref.at[0]).start()

            @pl.when((reach == 1) & (own == 0) & (lax.rem(fragment, 2) == 1))
            def _():
                far_copy(side, relay_ref.at[0]).start()

            @pl.when((reach == 1) & (own > 0))
            def _():
                far_copy(side, one_ref.at[jnp.maximum(own - 1, 0)]).start()

            @pl.when((reach == 2) & (own == 0))
            def _():
                far_copy(side, two_ref.at[0]).start()

            @pl.when((reach == 2) & (own > 0))
            def _():
                far_copy(side, rest_ref.at[jnp.maximum(own - 1, 0)]).start()

    def wait_loads(turn):
        for side in range(2):
            pltpu.make_async_copy(
                phi_refs[0].at[0], near.at[lax.rem(turn, 2), side], load_sem.at[0, side]
            ).wait()
            far_copy(side, phi_refs[0].at[0]).wait()

    @pl.when(found > 0)
    def _():
        start_loads(0)

    act[...] = jnp.zeros_like(act)
    back[...] = jnp.zeros_like(back)
    for copy in table_copies:
        copy.wait()

    slab = plane * edge // LANES // groups
    act_copies = []
    for k in range(groups):
        source = (member ^ k) * slab
        place = reversed_bits(k, groups)
        act_copies.append(
            pltpu.make_async_copy(
                act.at[:, pl.ds(pl.multiple_of(source, ROWS), slab), :],
                act_outs[2 * place // groups].at[place % (groups // 2)],
                out_sem.at[k],
            )
        )

    def offset_of(slot):
        partner = lax.rem(fragment + reach_of(slot), fragments)
        return [anchor(partner, i) - anchor(fragment, i) for i in range(3)]

    def steps(count, body, most):
        width = max(n for n in range(1, most + 1) if count % n == 0)

        def step(i, _):
            for j in range(width):
                body(i * width + j)
            return 0

        if width == count:
            step(0, 0)
        else:
            lax.fori_loop(0, count // width, step, 0)

    def columns(k):
        return pl.ds(pl.multiple_of(k * LANES, LANES), LANES)

    def shifted(source, delta, k, count):
        shift = lax.rem(delta[1] * edge + delta[2] + 4 * plane, plane)
        start = lax.rem(plane - shift, plane)
        whole, part = lax.div(start, LANES), lax.rem(start, LANES)
        turn = lax.rem(LANES - part, LANES)
        down = edge - jnp.clip(delta[0], -edge, edge)
        x = row - delta[0]
        rows_inside = (x >= 0) & (x < edge)
        pieces = [
            pltpu.roll(source[lax.rem(k + i + whole, chunks), pl.ds(down, edge), :], turn, 1)
            for i in range(count + 1)
        ]
        out = []
        for i in range(count):
            value = jnp.where(lane < LANES - part, pieces[i], pieces[i + 1])
            spot = (k + i) * LANES + lax.broadcasted_iota(jnp.int32, (1, LANES), 1)
            y = ((spot.astype(jnp.float32) + 0.5) * (1.0 / edge)).astype(jnp.int32)
            z = spot - y * edge - delta[2]
            y = y - delta[1]
            inside = (y >= 0) & (y < edge) & (z >= 0) & (z < edge)
            out.append(jnp.where(inside & rows_inside, value, 0.0))
        return out

    def solve_two(turn, _):
        wait_loads(turn)
        near_now = near.at[lax.rem(turn, 2)]
        picked = [slot_of(turn, side) for side in range(2)]
        offsets = [offset_of(slot) for slot, _ in picked]
        weights = [live.astype(jnp.float32) for _, live in picked]

        def widen(g):
            for side in range(2):
                for i in range(stretch):
                    k = g * stretch + i
                    wide[side, k, middle, :] = far[side, :, columns(k)]

        steps(chunks // stretch, widen, 3)

        @pl.when(turn + 1 < turns)
        def _():
            start_loads(turn + 1)


        def make_density(g):
            for side in range(2):
                values = shifted(wide.at[side], offsets[side], g * stretch, stretch)
                for i, value in enumerate(values):
                    k = g * stretch + i
                    moved[side, k] = value
                    dense[side, k, middle, :] = weights[side] * near_now[side, :, columns(k)] * value

        steps(chunks // stretch, make_density, 3)

        def spread(g):
            parts = [
                [dense[side, g * group_chunks + q, middle, :] for q in range(group_chunks)]
                for side in range(2)
            ]
            for i in range(period):
                begin, offset = divmod(i * edge, LANES)
                sides = []
                for side in range(2):
                    shift = (side * HALF - offset) % LANES
                    value = parts[side][begin]
                    value = pltpu.roll(value, shift, 1) if shift else value
                    if offset + edge > LANES:
                        more = parts[side][begin + 1]
                        more = pltpu.roll(more, shift, 1) if shift else more
                        value = jnp.where(lane < side * HALF + LANES - offset, value, more)
                    sides.append(value)
                at = pl.multiple_of((g * period + i) * edge, ROWS)
                cube[pl.ds(at, edge), :] = jnp.where(lane < HALF, sides[0], sides[1])

        steps(edge // period, spread, 2)

        def tile(t, i, size):
            return pl.ds(pl.multiple_of(i * size + t * ROWS, ROWS), ROWS)

        def across(t, i, size):
            return pl.ds(t * (ROWS * size) + i, ROWS, stride=size)

        def over_y(t):
            values = real_dft([Number(cube[tile(t, i, edge), :]) for i in range(edge)])
            for i in range(half):
                at = tile(t, i, edge)
                lower[0, at, :] = values[i].real
                lower[1, at, :] = (
                    jnp.zeros((ROWS, LANES), jnp.float32) if values[i].imag is None else values[i].imag
                )

        steps(tiles, over_y, 3)

        def over_x(t):
            at = [across(t, i, edge) for i in range(edge)]
            values = dft([Number(lower[0, a, :], lower[1, a, :]) for a in at], -1)
            for i in range(edge):
                upper[0, tile(t, i, height), :] = values[i].real
                upper[1, tile(t, i, height), :] = values[i].imag

        steps(height // ROWS, over_x, 2)

        block = next(n for n in (512, 256, 128, 64, 32, 16, 8) if edge * height % n == 0)

        def screen(c):
            at = pl.ds(pl.multiple_of(c * block, block), block)
            real, imag = split_dot(upper[0, at, :], upper[1, at, :], ahead_ref)
            factor = screen_ref[at, :]
            real, imag = split_dot(real * factor, imag * factor, behind_ref)
            upper[0, at, :] = real
            upper[1, at, :] = imag

        steps(edge * height // block, screen, 3)

        def back_x(t):
            at = [tile(t, i, height) for i in range(edge)]
            values = dft([Number(upper[0, a, :], upper[1, a, :]) for a in at], 1)
            for i in range(edge):
                upper[0, at[i], :] = values[i].real
                upper[1, at[i], :] = values[i].imag

        steps(height // ROWS, back_x, 2)

        def back_y(t):
            at = [across(t, i, height) for i in range(half)]
            values = [Number(upper[0, a, :], upper[1, a, :]) for a in at]
            values = values + [values[edge - i].conj() for i in range(half, edge)]
            for i, value in enumerate(real_back(values)):
                cube[tile(t, i, edge), :] = value

        steps(tiles, back_y, 3)

        firsts = [first_of(slot) for slot, _ in picked]

        def collect(g):
            planes = [
                cube[pl.ds(pl.multiple_of((g * period + i) * edge, ROWS), edge), :]
                for i in range(period)
            ]
            for q in range(group_chunks):
                k = g * group_chunks + q
                for side in range(2):
                    value = None
                    for i in range(period):
                        begin = i * edge - q * LANES
                        if begin + edge <= 0 or begin >= LANES:
                            continue
                        shift = (begin - side * HALF) % LANES
                        piece = pltpu.roll(planes[i], shift, 1) if shift else planes[i]
                        value = piece if value is None else jnp.where(lane < begin, value, piece)
                    value = value * weights[side]
                    forward = value * moved[side, k]
                    dense[side, k, middle, :] = value * near_now[side, :, columns(k)]
                    for t in range(tiles):
                        at = pl.ds(t * (ROWS * chunks) + k, ROWS, stride=chunks)
                        act[firsts[side], at, :] += forward[t * ROWS : (t + 1) * ROWS]

        steps(edge // period, collect, 2)

        @pl.when(turn + 1 == turns)
        def _():
            for copy in act_copies:
                copy.start()

        homes = []
        for side in range(2):
            slot = picked[side][0]
            homes.append(reach_of(slot) * orb_dev + lax.rem(second_of(slot), orb_dev))
        returns = [[-d for d in delta] for delta in offsets]

        def send_back(g):
            for side in range(2):
                values = shifted(dense.at[side], returns[side], g * stretch, stretch)
                for i, value in enumerate(values):
                    for t in range(tiles):
                        at = pl.ds(t * (ROWS * chunks) + g * stretch + i, ROWS, stride=chunks)
                        back[homes[side], at, :] += value[t * ROWS : (t + 1) * ROWS]

        steps(chunks // stretch, send_back, 3)
        return 0

    @pl.when(found == 0)
    def _():
        for copy in act_copies:
            copy.start()

    lax.fori_loop(0, turns, solve_two, 0)
    spans = ((orb_dev, 1), (orb_dev + 1, orb_dev - 1), (2 * orb_dev, orb_dev), (0, orb_dev))
    back_copies = [
        pltpu.make_async_copy(back.at[pl.ds(begin, count)], back_outs[i], out_sem.at[groups + i])
        for i, (begin, count) in enumerate(spans)
    ]
    for copy in back_copies:
        copy.start()
    for copy in act_copies + back_copies:
        copy.wait()


def reversed_bits(k, count):
    bits = count.bit_length() - 1
    return sum(((k >> i) & 1) << (bits - 1 - i) for i in range(bits))


def pair_terms(numbers, fragments, slots, tables, pieces, far):
    orb_dev, edge, plane = pieces[0].shape
    groups = len(pieces)
    frag_size = groups * orb_dev
    chunks = plane // LANES
    rows = edge * chunks
    height = padded_half(edge)
    returns_count = (REACH + 1) * orb_dev
    shape = (edge, orb_dev, groups, fragments, slots)
    smem = pl.BlockSpec(memory_space=pltpu.SMEM)
    hbm = pl.BlockSpec(memory_space=pltpu.HBM)
    f32 = jnp.float32
    found = pl.pallas_call(
        functools.partial(pair_kernel, shape),
        out_shape=[jax.ShapeDtypeStruct((groups // 2, frag_size, rows // groups, LANES), f32)] * 2
        + [
            jax.ShapeDtypeStruct((count, rows, LANES), f32)
            for count in (1, orb_dev - 1, orb_dev, orb_dev)
        ],
        in_specs=[smem] + [hbm] * (3 + groups + len(far)),
        out_specs=[hbm] * 6,
        scratch_shapes=[
            pltpu.VMEM((frag_size, rows, LANES), f32),
            pltpu.VMEM((returns_count, rows, LANES), f32),
            pltpu.VMEM((2, 2, edge, plane), f32),
            pltpu.VMEM((2, edge, plane), f32),
            pltpu.VMEM((2, chunks, 3 * edge, LANES), f32),
            pltpu.VMEM((2, chunks, edge, LANES), f32),
            pltpu.VMEM((2, chunks, 3 * edge, LANES), f32),
            pltpu.VMEM((plane, LANES), f32),
            pltpu.VMEM((2, height * edge, LANES), f32),
            pltpu.VMEM((2, height * edge, LANES), f32),
            pltpu.SMEM((slots,), jnp.int32),
            pltpu.SemaphoreType.DMA((2, 2)),
            pltpu.SemaphoreType.DMA((groups + 4,)),
            *[pltpu.VMEM(table.shape, table.dtype) for table in tables],
            pltpu.SemaphoreType.DMA((3,)),
        ],
        compiler_params=pltpu.CompilerParams(vmem_limit_bytes=30 << 20),
        name="pair_terms",
    )(numbers, *tables, *pieces, *far)
    return found[:2], found[2:]


def flatten_kernel(shape, places_ref, *refs):
    edge, orb_dev, groups = shape
    pieces, (flat_ref, slab_ref) = refs[:groups], refs[groups:]
    member = places_ref[1]
    chunks = edge * edge // LANES
    slab = slab_ref.shape[1]
    for k in range(groups):
        for o in range(orb_dev):
            def move(j, _):
                value = pieces[k][o, :, pl.ds(pl.multiple_of(j * LANES, LANES), LANES)]
                for t in range(edge // ROWS):
                    at = pl.ds(t * (ROWS * chunks) + j, ROWS, stride=chunks)
                    flat_ref[k * orb_dev + o, at, :] = value[t * ROWS : (t + 1) * ROWS]
                return 0

            lax.fori_loop(0, chunks, move, 0)
    slab_ref[...] = flat_ref[:, pl.ds(pl.multiple_of(member * slab, ROWS), slab), :]


def flatten_terms(places, pieces):
    orb_dev, edge, plane = pieces[0].shape
    groups = len(pieces)
    rows = edge * plane // LANES
    frag_size = groups * orb_dev
    smem = pl.BlockSpec(memory_space=pltpu.SMEM)
    vmem = pl.BlockSpec(memory_space=pltpu.VMEM)
    return pl.pallas_call(
        functools.partial(flatten_kernel, (edge, orb_dev, groups)),
        out_shape=(
            jax.ShapeDtypeStruct((frag_size, rows, LANES), jnp.float32),
            jax.ShapeDtypeStruct((frag_size, rows // groups, LANES), jnp.float32),
        ),
        in_specs=[smem] + [vmem] * groups,
        out_specs=(vmem, vmem),
        compiler_params=pltpu.CompilerParams(vmem_limit_bytes=24 << 20),
        name="flatten_terms",
    )(places, *pieces)


def home_kernel(shape, places_ref, flat_ref, phi_ref, kept_ref, *refs):
    edge, orb_dev, groups, parts = shape
    arrived, refs = refs[:parts], refs[parts:]
    (own_ref, twin_ref, relay_ref, one_ref, two_ref), refs = refs[:5], refs[5:]
    act_ref, outs, total = refs[0], refs[1 : 1 + groups], refs[1 + groups]
    fragment, member = places_ref[0], places_ref[1]
    odd = lax.rem(fragment, 2) == 1
    frag_size = orb_dev * groups
    slab = act_ref.shape[1]
    rows = flat_ref.shape[1]
    cut = frag_size // parts
    for i in range(parts):
        span = slice(i * cut, (i + 1) * cut)
        act_ref[span] = kept_ref[0, span] + arrived[i][0]

    @pl.when(odd)
    def _():
        total[0] = own_ref[0] + two_ref[0] + twin_ref[0]

    @pl.when(jnp.logical_not(odd))
    def _():
        total[0] = own_ref[0] + two_ref[0] + relay_ref[0]

    for o in range(1, orb_dev):
        total[o] = own_ref[o] + two_ref[o] + one_ref[o - 1]

    row = lax.broadcasted_iota(jnp.int32, (frag_size, LANES), 0)
    lane = lax.broadcasted_iota(jnp.int32, (frag_size, LANES), 1)

    def products(lefts, rights, length, step):
        def add(i, sums):
            at = pl.ds(pl.multiple_of(i * step, ROWS), step)
            right = [ref[index, at, :].reshape(step // ROWS, ROWS, LANES) for ref, index in rights]
            out = []
            for n, (ref, index) in enumerate(lefts):
                left = ref[index, at, :].reshape(step // ROWS, ROWS, LANES)
                for m in range(len(rights)):
                    out.append(sums[n * len(rights) + m] + jnp.sum(left * right[m], axis=0))
            return tuple(out)

        zero = jnp.zeros((ROWS, LANES), jnp.float32)
        return lax.fori_loop(0, length // step, add, (zero,) * (len(lefts) * len(rights)))

    result = jnp.zeros((frag_size, LANES), jnp.float32)
    scale = 1.0 / float(edge**3)
    step = next(n for n in (72, 24, 8) if slab % n == 0)
    for half in range(0, frag_size, 4):
        bs = range(half, min(half + 4, frag_size))
        sums = products(
            [(phi_ref, a) for a in range(frag_size)], [(act_ref, b) for b in bs], slab, step
        )
        for a in range(frag_size):
            place = (member ^ (a // orb_dev)) * orb_dev + a % orb_dev
            for i, b in enumerate(bs):
                value = jnp.sum(sums[a * len(bs) + i], keepdims=True)
                result = jnp.where((row == place) & (lane == b), value, result)
    sums = products(
        [(flat_ref, a) for a in range(frag_size)], [(total, b) for b in range(orb_dev)], rows, step
    )
    for a in range(frag_size):
        place = (member ^ (a // orb_dev)) * orb_dev + a % orb_dev
        for b in range(orb_dev):
            value = jnp.sum(sums[a * orb_dev + b], keepdims=True)
            at = (row == place) & (lane == member * orb_dev + b)
            result = jnp.where(at, result + value, result)

    for k in range(groups):
        begin = pl.multiple_of((member ^ k) * slab, ROWS)
        for o in range(orb_dev):
            outs[k][o * slab : (o + 1) * slab, :] = total[o, pl.ds(begin, slab), :]
        outs[k][orb_dev * slab :, :] = result * scale


def home_terms(places, edge, flat, phi, kept, arrived, own, twin, relay, one, two):
    frag_size, slab = phi.shape[:2]
    orb_dev, rows = own.shape[:2]
    groups = frag_size // orb_dev
    smem = pl.BlockSpec(memory_space=pltpu.SMEM)
    vmem = pl.BlockSpec(memory_space=pltpu.VMEM)
    f32 = jnp.float32
    found = pl.pallas_call(
        functools.partial(home_kernel, (edge, orb_dev, groups, len(arrived))),
        out_shape=[jax.ShapeDtypeStruct((frag_size, slab, LANES), f32)]
        + [jax.ShapeDtypeStruct((orb_dev * slab + frag_size, LANES), f32)] * groups,
        in_specs=[smem] + [vmem] * (8 + len(arrived)),
        out_specs=[vmem] * (1 + groups),
        scratch_shapes=[pltpu.VMEM((orb_dev, rows, LANES), f32)],
        compiler_params=pltpu.CompilerParams(vmem_limit_bytes=32 << 20),
        name="home_terms",
    )(places, flat, phi, kept, *arrived, own, twin, relay, one, two)
    return found[0], found[1:]


def gradient_kernel(shape, places_ref, act_ref, phi_ref, *refs):
    edge, orb_dev, groups = shape
    parcels, (out_ref, lagrange_ref, weights, hold) = refs[:groups], refs[groups:]
    member = places_ref[1]
    frag_size = orb_dev * groups
    chunks = edge * edge // LANES
    slab_rows = edge // groups
    slab = slab_rows * chunks
    sums = [parcel[orb_dev * slab :, :] for parcel in parcels]
    while len(sums) > 1:
        sums = [sums[i] + sums[i + 1] for i in range(0, len(sums), 2)]
    square = jnp.concatenate([sums[0], jnp.zeros((LANES - frag_size, LANES), jnp.float32)], axis=0)
    lagrange = 0.5 * (square + square.T)[:frag_size, :]
    lagrange_ref[...] = lagrange[:, :frag_size]
    weights[...] = lagrange

    for k in range(groups):
        for o in range(orb_dev):
            a = (member ^ k) * orb_dev + o
            value = act_ref[a] + parcels[k][o * slab : (o + 1) * slab, :]
            lane = lax.broadcasted_iota(jnp.int32, (1, LANES), 1)
            for q in range(groups):
                for p in range(orb_dev):
                    line = weights[pl.ds((member ^ q) * orb_dev + p, 1), :]
                    factor = jnp.sum(jnp.where(lane == a, line, 0.0), axis=1, keepdims=True)
                    value = value - factor * phi_ref[q * orb_dev + p]
            hold[pl.ds(pl.multiple_of(a * slab, ROWS), slab), :] = value
    for x in range(slab_rows):
        for j in range(chunks):
            value = hold[pl.ds(x * chunks + j, frag_size, stride=slab), :]
            out_ref[x, :, j * LANES : (j + 1) * LANES] = value


def gradient_terms(places, edge, act, phi, parcels):
    groups = len(parcels)
    frag_size, slab = act.shape[:2]
    smem = pl.BlockSpec(memory_space=pltpu.SMEM)
    vmem = pl.BlockSpec(memory_space=pltpu.VMEM)
    f32 = jnp.float32
    gradient, lagrange = pl.pallas_call(
        functools.partial(gradient_kernel, (edge, frag_size // groups, groups)),
        out_shape=(
            jax.ShapeDtypeStruct((edge // groups, frag_size, edge * edge), f32),
            jax.ShapeDtypeStruct((frag_size, frag_size), f32),
        ),
        in_specs=[smem] + [vmem] * (2 + groups),
        out_specs=(vmem, vmem),
        scratch_shapes=[
            pltpu.VMEM((frag_size, LANES), f32),
            pltpu.VMEM((frag_size * slab, LANES), f32),
        ],
        compiler_params=pltpu.CompilerParams(vmem_limit_bytes=24 << 20),
        name="gradient_terms",
    )(places, act, phi, *parcels)
    return gradient.transpose(1, 0, 2), lagrange


def together(*arrays):
    return lax.optimization_barrier(arrays)


def to_fragment(block, distance, senders=None):
    devices = lax.axis_size("orb")
    senders = range(devices) if senders is None else range(senders, devices, 2)
    return lax.ppermute(block, "orb", [(i, (i + distance) % devices) for i in senders])


def with_twin(block):
    return lax.ppermute(block, "orb", [(i, i ^ 1) for i in range(lax.axis_size("orb"))])


def with_member(block, bit):
    return lax.ppermute(block, "grp", [(i, i ^ bit) for i in range(lax.axis_size("grp"))])


def shards(orbitals, kernel, anchors, pair_count, pair_first, pair_second, pair_reach):
    groups = lax.axis_size("grp")
    orb_dev, edge, plane = orbitals.shape
    frag_size = groups * orb_dev
    places = jnp.stack([lax.axis_index("orb"), lax.axis_index("grp")]).astype(jnp.int32)
    numbers = [places, pair_count, pair_first, pair_second, pair_reach, anchors.reshape(-1)]
    screen, numbers, *tables = screen_terms(jnp.concatenate(numbers), kernel)
    tables = [screen, *tables]

    head, tail = orbitals[:1], orbitals[1:]
    two = to_fragment(head, -2)
    twin, two = together(with_twin(head), two)
    rest = to_fragment(tail, -2)
    one = to_fragment(tail, -1)
    relay = to_fragment(twin, -2, 1)
    pieces = {0: orbitals}
    bit = groups // 2
    while bit:
        for k in list(pieces):
            pieces[k ^ bit] = with_member(pieces[k], bit)
        if bit == groups // 2:
            pieces[bit], one, relay, rest = together(pieces[bit], one, relay, rest)
        bit //= 2
    pieces = [pieces[k] for k in range(groups)]

    (kept, sent), (back_first, back_rest, back_two, own) = pair_terms(
        numbers, anchors.shape[0], pair_first.shape[0], tables, pieces, [twin, relay, one, two, rest]
    )

    two = to_fragment(back_two, 2)
    one = to_fragment(back_rest, 1)
    bit = 1
    arrived = [with_member(sent, bit)]
    while 2 * bit < groups:
        kept = kept + jnp.concatenate(arrived, axis=1)
        if bit == 1:
            kept, back_first = together(kept, back_first)
        half = kept.shape[0] // 2
        cut = frag_size // orb_dev
        bit *= 2
        arrived = [
            with_member(kept[half:, i : i + cut], bit) for i in range(0, frag_size, cut)
        ]
        kept = kept[:half]
    twin = with_twin(back_first)
    relay = to_fragment(twin, 2, 0)

    flat, phi = flatten_terms(places, pieces)
    act, parcels = home_terms(places, edge, flat, phi, kept, arrived, own, twin, relay, one, two)
    received = []
    for k in range(groups):
        parcel, bit = parcels[k], groups // 2
        while bit:
            if k & bit:
                parcel = with_member(parcel, bit)
            bit //= 2
        received.append(parcel)
    gradient, lagrange = gradient_terms(places, edge, act, phi, received)
    return (gradient, lagrange[None])


def solution(mesh):
    placed = (P(("orb", "grp"), None, None), P(), P(), P("orb"), P("orb"), P("orb"), P("orb"))
    return jax.shard_map(
        shards,
        mesh=mesh,
        in_specs=placed,
        out_specs=(P("orb", "grp", None), P("orb", None, None)),
        check_vma=False,
    )
```

```python
import functools
import math

import jax
import jax.numpy as jnp
import numpy as np
from jax import lax
from jax.experimental import pallas as pl
from jax.experimental.pallas import tpu as pltpu
from jax.sharding import PartitionSpec as P

REACH = 2
LANES = 128
ROWS = 8
HALF = LANES // 2


class Number:
    def __init__(self, real, imag=None):
        self.real, self.imag = real, imag

    def __add__(self, other):
        if self.imag is None or other.imag is None:
            imag = self.imag if other.imag is None else other.imag
        else:
            imag = self.imag + other.imag
        return Number(self.real + other.real, imag)

    def __sub__(self, other):
        if other.imag is None:
            imag = self.imag
        else:
            imag = -other.imag if self.imag is None else self.imag - other.imag
        return Number(self.real - other.real, imag)

    def conj(self):
        return self if self.imag is None else Number(self.real, -self.imag)

    def scaled(self, factor):
        return Number(self.real * factor, None if self.imag is None else self.imag * factor)

    def turned(self, sign):
        if self.imag is None:
            return Number(jnp.zeros_like(self.real), self.real if sign > 0 else -self.real)
        return Number(-self.imag, self.real) if sign > 0 else Number(self.imag, -self.real)

    def plus_turned(self, other, sign):
        if sign < 0:
            return self.minus_turned(other)
        real = self.real if other.imag is None else self.real - other.imag
        return Number(real, other.real if self.imag is None else self.imag + other.real)

    def minus_turned(self, other):
        real = self.real if other.imag is None else self.real + other.imag
        return Number(real, -other.real if self.imag is None else self.imag - other.real)

    def times(self, angle):
        real, imag = math.cos(angle), math.sin(angle)
        if abs(imag) < 1e-12:
            return self if real > 0 else self.scaled(-1.0)
        if abs(real) < 1e-12:
            return self.turned(imag)
        if self.imag is None:
            return Number(self.real * real, self.real * imag)
        return Number(self.real * real - self.imag * imag, self.real * imag + self.imag * real)


def coprime(n):
    for p in (2, 3, 5, 7):
        power = 1
        while n % (power * p) == 0:
            power *= p
        if 1 < power < n:
            return power, n // power
    return None


def radix(n):
    return next((p for p in (4, 2, 3, 5, 7) if n % p == 0 and n > p), None)


def meeting(i, j, first, second):
    return next(k for k in range(first * second) if k % first == i and k % second == j)


def dft(values, sign):
    n = len(values)
    if n == 1:
        return values
    if n == 2:
        return [values[0] + values[1], values[0] - values[1]]
    if n == 3:
        a, b, c = values
        total, side = b + c, (b - c).scaled(math.sqrt(0.75))
        middle = a - total.scaled(0.5)
        return [a + total, middle.plus_turned(side, sign), middle.plus_turned(side, -sign)]
    if n == 4:
        a, b, c, d = values
        s, t, u, v = a + c, a - c, b + d, b - d
        return [s + u, t.plus_turned(v, sign), s - u, t.plus_turned(v, -sign)]
    out = [None] * n
    if coprime(n):
        first, second = coprime(n)
        columns = [
            dft([values[(i * second + j * first) % n] for i in range(first)], sign)
            for j in range(second)
        ]
        for i in range(first):
            row = dft([column[i] for column in columns], sign)
            for j in range(second):
                out[meeting(i, j, first, second)] = row[j]
        return out
    p = radix(n)
    if p:
        rest = n // p
        columns = [dft(values[j::p], sign) for j in range(p)]
        for i in range(rest):
            row = dft(
                [columns[j][i].times(sign * 2.0 * math.pi * i * j / n) for j in range(p)], sign
            )
            for j in range(p):
                out[i + rest * j] = row[j]
        return out
    for k in range(n):
        total = values[0]
        for j in range(1, n):
            total = total + values[j].times(sign * 2.0 * math.pi * (j * k % n) / n)
        out[k] = total
    return out


def real_dft(values):
    n = len(values)
    if n <= 4:
        out = dft(values, -1)
    else:
        out = [None] * n
        if coprime(n):
            first, second = coprime(n)
            columns = [
                real_dft([values[(i * second + j * first) % n] for i in range(first)])
                for j in range(second)
            ]
            for i in range(first // 2 + 1):
                entries = [column[i] for column in columns]
                alone = 2 * i % first == 0
                row = real_dft(entries) if alone else dft(entries, -1)
                for j in range(second):
                    out[meeting(i, j, first, second)] = row[j]
        elif radix(n):
            p = radix(n)
            rest = n // p
            columns = [real_dft(values[j::p]) for j in range(p)]
            for i in range(rest // 2 + 1):
                row = dft(
                    [columns[j][i].times(-2.0 * math.pi * i * j / n) for j in range(p)], -1
                )
                for j in range(p):
                    out[i + rest * j] = row[j]
        else:
            out = dft(values, -1)
    for k in range(1, n):
        if out[k] is None or (k > n // 2 and out[n - k] is not None):
            out[k] = out[n - k].conj()
    out[0] = Number(out[0].real)
    if n % 2 == 0:
        out[n // 2] = Number(out[n // 2].real)
    return out


def real_back(values):
    n = len(values)
    if n == 1:
        return [values[0].real]
    if n == 2:
        return [values[0].real + values[1].real, values[0].real - values[1].real]
    if n == 3:
        a, b = values[0].real, values[1]
        side = b.imag * math.sqrt(3.0)
        middle = a - b.real
        return [a + 2.0 * b.real, middle - side, middle + side]
    if n == 4:
        s, t = values[0].real + values[2].real, values[0].real - values[2].real
        u, v = 2.0 * values[1].real, 2.0 * values[1].imag
        return [s + u, t - v, s - u, t + v]
    out = [None] * n
    if coprime(n):
        first, second = coprime(n)
        rows = []
        for i in range(first // 2 + 1):
            entries = [values[meeting(i, j, first, second)] for j in range(second)]
            if 2 * i % first == 0:
                rows.append([Number(value) for value in real_back(entries)])
            else:
                rows.append(dft(entries, 1))
        for b in range(second):
            half = [row[b] for row in rows]
            whole = half + [half[first - i].conj() for i in range(len(half), first)]
            for a, value in enumerate(real_back(whole)):
                out[(a * second + b * first) % n] = value
        return out
    p = radix(n)
    if p:
        rest = n // p
        parts = []
        for i in range(p // 2 + 1):
            entries = values[i::p]
            if i == 0:
                parts.append([Number(value) for value in real_back(entries)])
            else:
                inner = dft(entries, 1)
                parts.append([inner[m].times(2.0 * math.pi * i * m / n) for m in range(rest)])
                if 2 * i == p:
                    parts[-1] = [Number(value.real) for value in parts[-1]]
        for m in range(rest):
            half = [part[m] for part in parts]
            whole = half + [half[p - i].conj() for i in range(len(half), p)]
            for j, value in enumerate(real_back(whole)):
                out[m + rest * j] = value
        return out
    return [value.real for value in dft(values, 1)]


def wave_table(edge):
    index = np.arange(edge)
    angles = 2.0 * np.pi / edge * (np.outer(index, index) % edge)
    full = np.zeros((2, 2, HALF, 2, HALF))
    for side in range(2):
        full[0, side, :edge, side, :edge] = np.cos(angles)
        full[1, side, :edge, side, :edge] = np.sin(angles)
    full = full.reshape(2, LANES, LANES)
    high = full.astype(jnp.bfloat16)
    low = (full - high.astype(np.float64)).astype(jnp.bfloat16)
    return np.stack([high, low])


def split_dot(real, imag, matrix):
    value = jnp.concatenate([real, imag], axis=1)
    high = value.astype(jnp.bfloat16)
    low = (value - high.astype(jnp.float32)).astype(jnp.bfloat16)
    product = jnp.dot(
        jnp.concatenate([high, low, high], axis=1), matrix[...], preferred_element_type=jnp.float32
    )
    return product[:, :LANES], product[:, LANES:]


def padded_half(edge):
    return -(-(edge // 2 + 1) // ROWS) * ROWS


def screen_kernel(edge, numbers_ref, kernel_ref, waves_ref, out_ref, kept_ref, ahead_ref, behind_ref, flipped):
    for i in range(numbers_ref.shape[0]):
        kept_ref[i] = numbers_ref[i]
    for table, sign in ((ahead_ref, -1), (behind_ref, 1)):
        for part, source in enumerate((0, 0, 1)):
            for i in range(2):
                for j in range(2):
                    value = waves_ref[source, (i + j) % 2]
                    if i != j and (i > j) == (sign > 0):
                        value = -value
                    rows = slice((2 * part + i) * LANES, (2 * part + i + 1) * LANES)
                    table[rows, j * LANES : (j + 1) * LANES] = value
    exact = dict(precision=lax.Precision.HIGHEST, preferred_element_type=jnp.float32)

    def index(shape, axis):
        return lax.broadcasted_iota(jnp.int32, shape, axis)

    square, whole = (edge, edge), (LANES, LANES)
    flip = index(square, 0) + index(square, 1)
    flip = ((flip == 0) | (flip == edge)).astype(jnp.float32)
    source, target = index(whole, 0), index(whole, 1)
    target = jnp.where(target < HALF, target, target - HALF)
    mirror = ((source + target == 0) | (source + target == edge)) & (source < edge) & (target < edge)
    mirror = mirror.astype(jnp.float32)
    flipped[...] = jnp.dot(flip, kernel_ref[...], **exact)
    height = padded_half(edge)
    lane = index((edge, LANES), 1)
    out_ref[...] = jnp.zeros_like(out_ref)

    def piece(ref, y):
        begin, offset = divmod(y * edge, LANES)
        value = ref[:, begin * LANES : (begin + 1) * LANES]
        value = pltpu.roll(value, LANES - offset, 1) if offset else value
        if offset + edge > LANES:
            more = ref[:, (begin + 1) * LANES : (begin + 2) * LANES]
            value = jnp.where(lane < LANES - offset, value, pltpu.roll(more, LANES - offset, 1))
        return value

    for y in range(edge // 2 + 1):
        value = piece(kernel_ref, y)
        value = jnp.where(lane < HALF, value, pltpu.roll(value, HALF, 1))
        value = value + jnp.dot(piece(flipped, (edge - y) % edge), mirror, **exact)
        value = value * (0.5 / float(edge**3))
        for t in range(edge // ROWS):
            at = pl.ds(t * ROWS * height + y, ROWS, stride=height)
            out_ref[at, :] = value[t * ROWS : (t + 1) * ROWS]


def screen_terms(numbers, kernel):
    edge, plane = kernel.shape
    smem = pl.BlockSpec(memory_space=pltpu.SMEM)
    vmem = pl.BlockSpec(memory_space=pltpu.VMEM)
    table = jax.ShapeDtypeStruct((6 * LANES, 2 * LANES), jnp.bfloat16)
    return pl.pallas_call(
        functools.partial(screen_kernel, edge),
        out_shape=[
            jax.ShapeDtypeStruct((edge * padded_half(edge), LANES), jnp.float32),
            jax.ShapeDtypeStruct(numbers.shape, numbers.dtype),
            table,
            table,
        ],
        in_specs=[smem, vmem, vmem],
        out_specs=[vmem, smem, vmem, vmem],
        scratch_shapes=[pltpu.VMEM((edge, plane), jnp.float32)],
        compiler_params=pltpu.CompilerParams(vmem_limit_bytes=8 << 20),
        name="screen_terms",
    )(numbers, kernel, jnp.asarray(wave_table(edge)))


def pair_kernel(
    shape,
    numbers_ref,
    *refs,
):
    edge, orb_dev, groups, fragments, slots = shape
    plane = edge * edge
    chunks = plane // LANES
    tiles = edge // ROWS
    half = edge // 2 + 1
    height = padded_half(edge)
    returns_count = (REACH + 1) * orb_dev
    tables, refs = refs[:3], refs[3:]
    phi_refs, own_ref, refs = refs[:groups], refs[groups], refs[groups + 1 :]
    (twin_ref, relay_ref, one_ref, two_ref, rest_ref), refs = refs[:5], refs[5:]
    act_outs, back_outs, refs = refs[:2], refs[2:6], refs[6:]
    (act, back, near, wide, moved, dense, lower, upper, masks, listed, load_sem, out_sem) = refs[:12]
    screen_ref, ahead_ref, behind_ref, table_sem = refs[12:]

    fragment, member, live_slots = numbers_ref[0], numbers_ref[1], numbers_ref[2]

    def first_of(slot):
        return numbers_ref[3 + slot]

    def second_of(slot):
        return numbers_ref[3 + slots + slot]

    def reach_of(slot):
        return numbers_ref[3 + 2 * slots + slot]

    def anchor(place, axis):
        return numbers_ref[3 + 3 * slots + 3 * place + axis]

    table_copies = [
        pltpu.make_async_copy(table, hold, table_sem.at[i])
        for i, (table, hold) in enumerate(zip(tables, refs[12:15]))
    ]
    for copy in table_copies:
        copy.start()
    lane = lax.broadcasted_iota(jnp.int32, (1, LANES), 1)
    stretch = next(n for n in (6, 4, 3, 2, 1) if chunks % n == 0)
    middle = pl.ds(edge, edge)

    def list_slots(slot, found):
        mine = (slot < live_slots) & (lax.div(second_of(slot), orb_dev) == member)

        @pl.when(mine)
        def _():
            listed[found] = slot

        return found + mine.astype(jnp.int32)

    found = lax.fori_loop(0, slots, list_slots, 0)
    turns = lax.div(found + 1, 2)

    def slot_of(turn, side):
        at = 2 * turn + side
        live = at < found
        return listed[jnp.where(live, at, 2 * turn)], live

    def far_copy(side, source):
        return pltpu.make_async_copy(source, wide.at[side, :, middle], load_sem.at[1, side])

    def start_loads(turn):
        for side in range(2):
            slot, _ = slot_of(turn, side)
            first, second, reach = first_of(slot), second_of(slot), reach_of(slot)
            relative = lax.div(first, orb_dev) ^ member
            for k in range(groups):
                @pl.when(relative == k)
                def _():
                    pltpu.make_async_copy(
                        phi_refs[k].at[lax.rem(first, orb_dev)],
                        near.at[lax.rem(turn, 2), side],
                        load_sem.at[0, side],
                    ).start()
            own = lax.rem(second, orb_dev)

            @pl.when(reach == 0)
            def _():
                far_copy(side, own_ref.at[own]).start()

            @pl.when((reach == 1) & (own == 0) & (lax.rem(fragment, 2) == 0))
            def _():
                far_copy(side, twin_ref.at[0]).start()

            @pl.when((reach == 1) & (own == 0) & (lax.rem(fragment, 2) == 1))
            def _():
                far_copy(side, relay_ref.at[0]).start()

            @pl.when((reach == 1) & (own > 0))
            def _():
                far_copy(side, one_ref.at[jnp.maximum(own - 1, 0)]).start()

            @pl.when((reach == 2) & (own == 0))
            def _():
                far_copy(side, two_ref.at[0]).start()

            @pl.when((reach == 2) & (own > 0))
            def _():
                far_copy(side, rest_ref.at[jnp.maximum(own - 1, 0)]).start()

    def wait_loads(turn):
        for side in range(2):
            pltpu.make_async_copy(
                phi_refs[0].at[0], near.at[lax.rem(turn, 2), side], load_sem.at[0, side]
            ).wait()
            far_copy(side, own_ref.at[0]).wait()

    @pl.when(found > 0)
    def _():
        start_loads(0)

    act[...] = jnp.zeros_like(act)
    back[...] = jnp.zeros_like(back)
    for copy in table_copies:
        copy.wait()

    slab = plane * edge // LANES // groups
    act_copies = []
    for k in range(groups):
        source = (member ^ k) * slab
        place = reversed_bits(k, groups)
        act_copies.append(
            pltpu.make_async_copy(
                act.at[:, pl.ds(pl.multiple_of(source, ROWS), slab), :],
                act_outs[2 * place // groups].at[place % (groups // 2)],
                out_sem.at[k],
            )
        )

    def offset_of(slot):
        partner = lax.rem(fragment + reach_of(slot), fragments)
        return [anchor(partner, i) - anchor(fragment, i) for i in range(3)]

    def steps(count, body, most):
        width = max(n for n in range(1, most + 1) if count % n == 0)

        def step(i, _):
            for j in range(width):
                body(i * width + j)
            return 0

        if width == count:
            step(0, 0)
        else:
            lax.fori_loop(0, count // width, step, 0)

    def columns(k):
        return pl.ds(pl.multiple_of(k * LANES, LANES), LANES)

    def set_masks(place, delta, weight):
        shape = masks.shape[1:]
        spot = lax.broadcasted_iota(jnp.int32, shape, 0) * LANES
        spot = spot + lax.broadcasted_iota(jnp.int32, shape, 1)
        y = ((spot.astype(jnp.float32) + 0.5) * (1.0 / edge)).astype(jnp.int32)
        z = spot - y * edge - delta[2]
        y = y - delta[1]
        inside = (y >= 0) & (y < edge) & (z >= 0) & (z < edge)
        masks[place] = jnp.where(inside, weight, 0.0)

    def shifted(source, place, delta, begin, count, ks):
        shift = lax.rem(delta[1] * edge + delta[2] + 4 * plane, plane)
        start = lax.rem(plane - shift, plane)
        whole, part = lax.div(start, LANES), lax.rem(start, LANES)
        turn = lax.rem(LANES - part, LANES)
        down = edge - jnp.clip(delta[0], -edge, edge) + begin
        x = lax.broadcasted_iota(jnp.int32, (count, LANES), 0) + (begin - delta[0])
        rows_inside = (x >= 0) & (x < edge)
        first = lane < LANES - part

        def piece(k):
            return pltpu.roll(source[lax.rem(k + whole, chunks), pl.ds(down, count), :], turn, 1)

        out = []
        low = piece(ks[0])
        for k in ks:
            high = piece(k + 1)
            value = jnp.where(first, low, high) * masks[place, pl.ds(k, 1), :]
            out.append(jnp.where(rows_inside, value, 0.0))
            low = high
        return out

    def tile(t, i, size):
        return pl.ds(pl.multiple_of(i * size + t * ROWS, ROWS), ROWS)

    def across(t, i, size):
        return pl.ds(t * (ROWS * size) + i, ROWS, stride=size)

    def solve_two(turn, _):
        wait_loads(turn)
        near_now = near.at[lax.rem(turn, 2)]
        picked = [slot_of(turn, side) for side in range(2)]
        offsets = [offset_of(slot) for slot, _ in picked]
        returns = [[-d for d in delta] for delta in offsets]
        for side in range(2):
            set_masks(side, offsets[side], picked[side][1].astype(jnp.float32))
            set_masks(2 + side, returns[side], 1.0)

        def over_y(t):
            densities = []
            begin = pl.multiple_of(t * ROWS, ROWS)
            rows = pl.ds(begin, ROWS)
            for side in range(2):
                values = shifted(wide.at[side], side, offsets[side], begin, ROWS, range(chunks))
                for k in range(chunks):
                    moved[side, k, rows, :] = values[k]
                    values[k] = values[k] * near_now[side, rows, k * LANES : (k + 1) * LANES]
                densities.append(values)
            planes = []
            for y in range(edge):
                first, offset = divmod(y * edge, LANES)
                sides = []
                for side in range(2):
                    shift = (side * HALF - offset) % LANES
                    value = densities[side][first]
                    value = pltpu.roll(value, shift, 1) if shift else value
                    if offset + edge > LANES:
                        more = densities[side][first + 1]
                        more = pltpu.roll(more, shift, 1) if shift else more
                        value = jnp.where(lane < side * HALF + LANES - offset, value, more)
                    sides.append(value)
                planes.append(Number(jnp.where(lane < HALF, sides[0], sides[1])))
            values = real_dft(planes)
            for i in range(half):
                at = tile(t, i, edge)
                lower[0, at, :] = values[i].real
                imag = values[i].imag
                lower[1, at, :] = jnp.zeros((ROWS, LANES), jnp.float32) if imag is None else imag

        steps(tiles, over_y, 2)

        @pl.when(turn + 1 < turns)
        def _():
            start_loads(turn + 1)

        def over_x(t):
            at = [across(t, i, edge) for i in range(edge)]
            values = dft([Number(lower[0, a, :], lower[1, a, :]) for a in at], -1)
            real = jnp.concatenate([value.real for value in values], axis=0)
            imag = jnp.concatenate([value.imag for value in values], axis=0)
            at = [tile(t, i, height) for i in range(edge)]
            factor = jnp.concatenate([screen_ref[a, :] for a in at], axis=0)
            real, imag = split_dot(real, imag, ahead_ref)
            real, imag = split_dot(real * factor, imag * factor, behind_ref)
            rows = [slice(i * ROWS, (i + 1) * ROWS) for i in range(edge)]
            values = dft([Number(real[r], imag[r]) for r in rows], 1)
            for i in range(edge):
                upper[0, at[i], :] = values[i].real
                upper[1, at[i], :] = values[i].imag

        steps(height // ROWS, over_x, 2)
        firsts = [first_of(slot) for slot, _ in picked]

        def back_y(t):
            begin = pl.multiple_of(t * ROWS, ROWS)
            rows = pl.ds(begin, ROWS)
            at = [across(t, i, height) for i in range(half)]
            values = [Number(upper[0, a, :], upper[1, a, :]) for a in at]
            values = values + [values[edge - i].conj() for i in range(half, edge)]
            planes = real_back(values)
            for side in range(2):
                forward = []
                for k in range(chunks):
                    value = None
                    for y in range(k * LANES // edge, edge):
                        begins = y * edge - k * LANES
                        if begins >= LANES:
                            break
                        shift = (begins - side * HALF) % LANES
                        piece = pltpu.roll(planes[y], shift, 1) if shift else planes[y]
                        value = piece if value is None else jnp.where(lane < begins, value, piece)
                    forward.append(value * moved[side, k, rows, :])
                    other = value * near_now[side, rows, k * LANES : (k + 1) * LANES]
                    dense[side, k, pl.ds(edge + begin, ROWS), :] = other
                at = [pl.ds(t * (ROWS * chunks) + k, ROWS, stride=chunks) for k in range(chunks)]
                sums = [act[firsts[side], at[k], :] + forward[k] for k in range(chunks)]
                for k in range(chunks):
                    act[firsts[side], at[k], :] = sums[k]

        steps(tiles, back_y, 2)

        @pl.when(turn + 1 == turns)
        def _():
            for copy in act_copies:
                copy.start()

        homes = []
        for side in range(2):
            slot = picked[side][0]
            homes.append(reach_of(slot) * orb_dev + lax.rem(second_of(slot), orb_dev))

        def send_back(g):
            for side in range(2):
                ks = [g * stretch + i for i in range(stretch)]
                values = shifted(dense.at[side], 2 + side, returns[side], 0, edge, ks)
                at = [
                    (i, t, pl.ds(t * (ROWS * chunks) + ks[i], ROWS, stride=chunks))
                    for i in range(stretch)
                    for t in range(tiles)
                ]
                sums = [
                    back[homes[side], a, :] + values[i][t * ROWS : (t + 1) * ROWS] for i, t, a in at
                ]
                for (i, t, a), value in zip(at, sums):
                    back[homes[side], a, :] = value

        steps(chunks // stretch, send_back, 3)
        return 0

    @pl.when(found == 0)
    def _():
        for copy in act_copies:
            copy.start()

    lax.fori_loop(0, turns, solve_two, 0)
    spans = ((orb_dev, 1), (orb_dev + 1, orb_dev - 1), (2 * orb_dev, orb_dev), (0, orb_dev))
    back_copies = [
        pltpu.make_async_copy(back.at[pl.ds(begin, count)], back_outs[i], out_sem.at[groups + i])
        for i, (begin, count) in enumerate(spans)
    ]
    for copy in back_copies:
        copy.start()
    for copy in act_copies + back_copies:
        copy.wait()


def reversed_bits(k, count):
    bits = count.bit_length() - 1
    return sum(((k >> i) & 1) << (bits - 1 - i) for i in range(bits))


def pair_terms(numbers, fragments, slots, tables, pieces, own, far):
    orb_dev, edge, plane = pieces[0].shape
    groups = len(pieces)
    frag_size = groups * orb_dev
    chunks = plane // LANES
    rows = edge * chunks
    height = padded_half(edge)
    returns_count = (REACH + 1) * orb_dev
    shape = (edge, orb_dev, groups, fragments, slots)
    smem = pl.BlockSpec(memory_space=pltpu.SMEM)
    hbm = pl.BlockSpec(memory_space=pltpu.HBM)
    f32 = jnp.float32
    found = pl.pallas_call(
        functools.partial(pair_kernel, shape),
        out_shape=[jax.ShapeDtypeStruct((groups // 2, frag_size, rows // groups, LANES), f32)] * 2
        + [
            jax.ShapeDtypeStruct((count, rows, LANES), f32)
            for count in (1, orb_dev - 1, orb_dev, orb_dev)
        ],
        in_specs=[smem] + [hbm] * (4 + groups + len(far)),
        out_specs=[hbm] * 6,
        scratch_shapes=[
            pltpu.VMEM((frag_size, rows, LANES), f32),
            pltpu.VMEM((returns_count, rows, LANES), f32),
            pltpu.VMEM((2, 2, edge, plane), f32),
            pltpu.VMEM((2, chunks, 3 * edge, LANES), f32),
            pltpu.VMEM((2, chunks, edge, LANES), f32),
            pltpu.VMEM((2, chunks, 3 * edge, LANES), f32),
            pltpu.VMEM((2, height * edge, LANES), f32),
            pltpu.VMEM((2, height * edge, LANES), f32),
            pltpu.VMEM((4, -(-chunks // ROWS) * ROWS, LANES), f32),
            pltpu.SMEM((slots,), jnp.int32),
            pltpu.SemaphoreType.DMA((2, 2)),
            pltpu.SemaphoreType.DMA((groups + 4,)),
            *[pltpu.VMEM(table.shape, table.dtype) for table in tables],
            pltpu.SemaphoreType.DMA((3,)),
        ],
        compiler_params=pltpu.CompilerParams(vmem_limit_bytes=30 << 20),
        name="pair_terms",
    )(numbers, *tables, *pieces, own, *far)
    return found[:2], found[2:]


def flatten_kernel(shape, places_ref, *refs):
    edge, orb_dev, groups = shape
    pieces, (flat_ref, slab_ref) = refs[:groups], refs[groups:]
    member = places_ref[1]
    chunks = edge * edge // LANES
    slab = slab_ref.shape[1]
    for k in range(groups):
        for o in range(orb_dev):
            def move(j, _):
                value = pieces[k][o, :, pl.ds(pl.multiple_of(j * LANES, LANES), LANES)]
                for t in range(edge // ROWS):
                    at = pl.ds(t * (ROWS * chunks) + j, ROWS, stride=chunks)
                    flat_ref[k * orb_dev + o, at, :] = value[t * ROWS : (t + 1) * ROWS]
                return 0

            lax.fori_loop(0, chunks, move, 0)
    slab_ref[...] = flat_ref[:, pl.ds(pl.multiple_of(member * slab, ROWS), slab), :]


def flatten_terms(places, pieces):
    orb_dev, edge, plane = pieces[0].shape
    groups = len(pieces)
    rows = edge * plane // LANES
    frag_size = groups * orb_dev
    smem = pl.BlockSpec(memory_space=pltpu.SMEM)
    vmem = pl.BlockSpec(memory_space=pltpu.VMEM)
    return pl.pallas_call(
        functools.partial(flatten_kernel, (edge, orb_dev, groups)),
        out_shape=(
            jax.ShapeDtypeStruct((frag_size, rows, LANES), jnp.float32),
            jax.ShapeDtypeStruct((frag_size, rows // groups, LANES), jnp.float32),
        ),
        in_specs=[smem] + [vmem] * groups,
        out_specs=(vmem, vmem),
        compiler_params=pltpu.CompilerParams(vmem_limit_bytes=24 << 20),
        name="flatten_terms",
    )(places, *pieces)


def home_kernel(shape, places_ref, flat_ref, phi_ref, kept_ref, *refs):
    edge, orb_dev, groups, parts = shape
    arrived, refs = refs[:parts], refs[parts:]
    (own_ref, twin_ref, relay_ref, one_ref, two_ref), refs = refs[:5], refs[5:]
    act_ref, outs, total = refs[0], refs[1 : 1 + groups], refs[1 + groups]
    fragment, member = places_ref[0], places_ref[1]
    odd = lax.rem(fragment, 2) == 1
    frag_size = orb_dev * groups
    slab = act_ref.shape[1]
    rows = flat_ref.shape[1]
    cut = frag_size // parts
    for i in range(parts):
        span = slice(i * cut, (i + 1) * cut)
        act_ref[span] = kept_ref[0, span] + arrived[i][0]

    @pl.when(odd)
    def _():
        total[0] = own_ref[0] + two_ref[0] + twin_ref[0]

    @pl.when(jnp.logical_not(odd))
    def _():
        total[0] = own_ref[0] + two_ref[0] + relay_ref[0]

    for o in range(1, orb_dev):
        total[o] = own_ref[o] + two_ref[o] + one_ref[o - 1]

    row = lax.broadcasted_iota(jnp.int32, (frag_size, LANES), 0)
    lane = lax.broadcasted_iota(jnp.int32, (frag_size, LANES), 1)

    def products(lefts, rights, length, step):
        def add(i, sums):
            at = pl.ds(pl.multiple_of(i * step, ROWS), step)
            right = [ref[index, at, :].reshape(step // ROWS, ROWS, LANES) for ref, index in rights]
            out = []
            for n, (ref, index) in enumerate(lefts):
                left = ref[index, at, :].reshape(step // ROWS, ROWS, LANES)
                for m in range(len(rights)):
                    out.append(sums[n * len(rights) + m] + jnp.sum(left * right[m], axis=0))
            return tuple(out)

        zero = jnp.zeros((ROWS, LANES), jnp.float32)
        return lax.fori_loop(0, length // step, add, (zero,) * (len(lefts) * len(rights)))

    result = jnp.zeros((frag_size, LANES), jnp.float32)
    scale = 1.0 / float(edge**3)
    step = next(n for n in (72, 24, 8) if slab % n == 0)
    for half in range(0, frag_size, 4):
        bs = range(half, min(half + 4, frag_size))
        sums = products(
            [(phi_ref, a) for a in range(frag_size)], [(act_ref, b) for b in bs], slab, step
        )
        for a in range(frag_size):
            place = (member ^ (a // orb_dev)) * orb_dev + a % orb_dev
            for i, b in enumerate(bs):
                value = jnp.sum(sums[a * len(bs) + i], keepdims=True)
                result = jnp.where((row == place) & (lane == b), value, result)
    sums = products(
        [(flat_ref, a) for a in range(frag_size)], [(total, b) for b in range(orb_dev)], rows, step
    )
    for a in range(frag_size):
        place = (member ^ (a // orb_dev)) * orb_dev + a % orb_dev
        for b in range(orb_dev):
            value = jnp.sum(sums[a * orb_dev + b], keepdims=True)
            at = (row == place) & (lane == member * orb_dev + b)
            result = jnp.where(at, result + value, result)

    for k in range(groups):
        begin = pl.multiple_of((member ^ k) * slab, ROWS)
        for o in range(orb_dev):
            outs[k][o * slab : (o + 1) * slab, :] = total[o, pl.ds(begin, slab), :]
        outs[k][orb_dev * slab :, :] = result * scale


def home_terms(places, edge, flat, phi, kept, arrived, own, twin, relay, one, two):
    frag_size, slab = phi.shape[:2]
    orb_dev, rows = own.shape[:2]
    groups = frag_size // orb_dev
    smem = pl.BlockSpec(memory_space=pltpu.SMEM)
    vmem = pl.BlockSpec(memory_space=pltpu.VMEM)
    f32 = jnp.float32
    found = pl.pallas_call(
        functools.partial(home_kernel, (edge, orb_dev, groups, len(arrived))),
        out_shape=[jax.ShapeDtypeStruct((frag_size, slab, LANES), f32)]
        + [jax.ShapeDtypeStruct((orb_dev * slab + frag_size, LANES), f32)] * groups,
        in_specs=[smem] + [vmem] * (8 + len(arrived)),
        out_specs=[vmem] * (1 + groups),
        scratch_shapes=[pltpu.VMEM((orb_dev, rows, LANES), f32)],
        compiler_params=pltpu.CompilerParams(vmem_limit_bytes=32 << 20),
        name="home_terms",
    )(places, flat, phi, kept, *arrived, own, twin, relay, one, two)
    return found[0], found[1:]


def gradient_kernel(shape, places_ref, act_ref, phi_ref, *refs):
    edge, orb_dev, groups = shape
    parcels, (out_ref, lagrange_ref, weights, hold) = refs[:groups], refs[groups:]
    member = places_ref[1]
    frag_size = orb_dev * groups
    chunks = edge * edge // LANES
    slab_rows = edge // groups
    slab = slab_rows * chunks
    sums = [parcel[orb_dev * slab :, :] for parcel in parcels]
    while len(sums) > 1:
        sums = [sums[i] + sums[i + 1] for i in range(0, len(sums), 2)]
    square = jnp.concatenate([sums[0], jnp.zeros((LANES - frag_size, LANES), jnp.float32)], axis=0)
    lagrange = 0.5 * (square + square.T)[:frag_size, :]
    lagrange_ref[...] = lagrange[:, :frag_size]
    weights[...] = lagrange

    for k in range(groups):
        for o in range(orb_dev):
            a = (member ^ k) * orb_dev + o
            value = act_ref[a] + parcels[k][o * slab : (o + 1) * slab, :]
            lane = lax.broadcasted_iota(jnp.int32, (1, LANES), 1)
            for q in range(groups):
                for p in range(orb_dev):
                    line = weights[pl.ds((member ^ q) * orb_dev + p, 1), :]
                    factor = jnp.sum(jnp.where(lane == a, line, 0.0), axis=1, keepdims=True)
                    value = value - factor * phi_ref[q * orb_dev + p]
            hold[pl.ds(pl.multiple_of(a * slab, ROWS), slab), :] = value
    for x in range(slab_rows):
        for j in range(chunks):
            value = hold[pl.ds(x * chunks + j, frag_size, stride=slab), :]
            out_ref[x, :, j * LANES : (j + 1) * LANES] = value


def gradient_terms(places, edge, act, phi, parcels):
    groups = len(parcels)
    frag_size, slab = act.shape[:2]
    smem = pl.BlockSpec(memory_space=pltpu.SMEM)
    vmem = pl.BlockSpec(memory_space=pltpu.VMEM)
    f32 = jnp.float32
    gradient, lagrange = pl.pallas_call(
        functools.partial(gradient_kernel, (edge, frag_size // groups, groups)),
        out_shape=(
            jax.ShapeDtypeStruct((edge // groups, frag_size, edge * edge), f32),
            jax.ShapeDtypeStruct((frag_size, frag_size), f32),
        ),
        in_specs=[smem] + [vmem] * (2 + groups),
        out_specs=(vmem, vmem),
        scratch_shapes=[
            pltpu.VMEM((frag_size, LANES), f32),
            pltpu.VMEM((frag_size * slab, LANES), f32),
        ],
        compiler_params=pltpu.CompilerParams(vmem_limit_bytes=24 << 20),
        name="gradient_terms",
    )(places, act, phi, *parcels)
    return gradient.transpose(1, 0, 2), lagrange


def together(*arrays):
    return lax.optimization_barrier(arrays)


def to_fragment(block, distance, senders=None):
    devices = lax.axis_size("orb")
    senders = range(devices) if senders is None else range(senders, devices, 2)
    return lax.ppermute(block, "orb", [(i, (i + distance) % devices) for i in senders])


def with_twin(block):
    return lax.ppermute(block, "orb", [(i, i ^ 1) for i in range(lax.axis_size("orb"))])


def with_member(block, bit):
    return lax.ppermute(block, "grp", [(i, i ^ bit) for i in range(lax.axis_size("grp"))])


def shards(orbitals, kernel, anchors, pair_count, pair_first, pair_second, pair_reach):
    groups = lax.axis_size("grp")
    orb_dev, edge, plane = orbitals.shape
    frag_size = groups * orb_dev
    places = jnp.stack([lax.axis_index("orb"), lax.axis_index("grp")]).astype(jnp.int32)

    own = orbitals.reshape(orb_dev, edge, plane // LANES, LANES).transpose(0, 2, 1, 3)
    head, tail = own[:1], own[1:]
    two = to_fragment(head, -2)
    numbers = [places, pair_count, pair_first, pair_second, pair_reach, anchors.reshape(-1)]
    screen, numbers, *tables = screen_terms(jnp.concatenate(numbers), kernel)
    twin, two, screen, numbers, *tables = together(with_twin(head), two, screen, numbers, *tables)
    tables = [screen, *tables]
    rest = to_fragment(tail, -2)
    one = to_fragment(tail, -1)
    relay = to_fragment(twin, -2, 1)
    pieces = {0: orbitals}
    bit = groups // 2
    while bit:
        for k in list(pieces):
            pieces[k ^ bit] = with_member(pieces[k], bit)
        if bit == groups // 2:
            pieces[bit], one, relay, rest = together(pieces[bit], one, relay, rest)
        bit //= 2
    pieces = [pieces[k] for k in range(groups)]

    (kept, sent), (back_first, back_rest, back_two, own) = pair_terms(
        numbers, anchors.shape[0], pair_first.shape[0], tables, pieces, own,
        [twin, relay, one, two, rest],
    )

    two = to_fragment(back_two, 2)
    one = to_fragment(back_rest, 1)
    bit = 1
    arrived = [with_member(sent, bit)]
    while 2 * bit < groups:
        kept = kept + jnp.concatenate(arrived, axis=1)
        if bit == 1:
            kept, back_first = together(kept, back_first)
        half = kept.shape[0] // 2
        cut = frag_size // orb_dev
        bit *= 2
        arrived = [
            with_member(kept[half:, i : i + cut], bit) for i in range(0, frag_size, cut)
        ]
        kept = kept[:half]
    twin = with_twin(back_first)
    relay = to_fragment(twin, 2, 0)

    flat, phi = flatten_terms(places, pieces)
    act, parcels = home_terms(places, edge, flat, phi, kept, arrived, own, twin, relay, one, two)
    received = []
    for k in range(groups):
        parcel, bit = parcels[k], groups // 2
        while bit:
            if k & bit:
                parcel = with_member(parcel, bit)
            bit //= 2
        received.append(parcel)
    gradient, lagrange = gradient_terms(places, edge, act, phi, received)
    return (gradient, lagrange[None])


def solution(mesh):
    placed = (P(("orb", "grp"), None, None), P(), P(), P("orb"), P("orb"), P("orb"), P("orb"))
    return jax.shard_map(
        shards,
        mesh=mesh,
        in_specs=placed,
        out_specs=(P("orb", "grp", None), P("orb", None, None)),
        check_vma=False,
    )
```

```python
import functools
import math

import jax
import jax.numpy as jnp
import numpy as np
from jax import lax
from jax.experimental import pallas as pl
from jax.experimental.pallas import tpu as pltpu
from jax.sharding import PartitionSpec as P

REACH = 2
LANES = 128
ROWS = 8
HALF = LANES // 2


class Number:
    def __init__(self, real, imag=None):
        self.real, self.imag = real, imag

    def __add__(self, other):
        if self.imag is None or other.imag is None:
            imag = self.imag if other.imag is None else other.imag
        else:
            imag = self.imag + other.imag
        return Number(self.real + other.real, imag)

    def __sub__(self, other):
        if other.imag is None:
            imag = self.imag
        else:
            imag = -other.imag if self.imag is None else self.imag - other.imag
        return Number(self.real - other.real, imag)

    def conj(self):
        return self if self.imag is None else Number(self.real, -self.imag)

    def scaled(self, factor):
        return Number(self.real * factor, None if self.imag is None else self.imag * factor)

    def turned(self, sign):
        if self.imag is None:
            return Number(jnp.zeros_like(self.real), self.real if sign > 0 else -self.real)
        return Number(-self.imag, self.real) if sign > 0 else Number(self.imag, -self.real)

    def plus_turned(self, other, sign):
        if sign < 0:
            return self.minus_turned(other)
        real = self.real if other.imag is None else self.real - other.imag
        return Number(real, other.real if self.imag is None else self.imag + other.real)

    def minus_turned(self, other):
        real = self.real if other.imag is None else self.real + other.imag
        return Number(real, -other.real if self.imag is None else self.imag - other.real)

    def times(self, angle):
        real, imag = math.cos(angle), math.sin(angle)
        if abs(imag) < 1e-12:
            return self if real > 0 else self.scaled(-1.0)
        if abs(real) < 1e-12:
            return self.turned(imag)
        if self.imag is None:
            return Number(self.real * real, self.real * imag)
        return Number(self.real * real - self.imag * imag, self.real * imag + self.imag * real)


def coprime(n):
    for p in (2, 3, 5, 7):
        power = 1
        while n % (power * p) == 0:
            power *= p
        if 1 < power < n:
            return power, n // power
    return None


def radix(n):
    return next((p for p in (4, 2, 3, 5, 7) if n % p == 0 and n > p), None)


def meeting(i, j, first, second):
    return next(k for k in range(first * second) if k % first == i and k % second == j)


def dft(values, sign):
    n = len(values)
    if n == 1:
        return values
    if n == 2:
        return [values[0] + values[1], values[0] - values[1]]
    if n == 3:
        a, b, c = values
        total, side = b + c, (b - c).scaled(math.sqrt(0.75))
        middle = a - total.scaled(0.5)
        return [a + total, middle.plus_turned(side, sign), middle.plus_turned(side, -sign)]
    if n == 4:
        a, b, c, d = values
        s, t, u, v = a + c, a - c, b + d, b - d
        return [s + u, t.plus_turned(v, sign), s - u, t.plus_turned(v, -sign)]
    out = [None] * n
    if coprime(n):
        first, second = coprime(n)
        columns = [
            dft([values[(i * second + j * first) % n] for i in range(first)], sign)
            for j in range(second)
        ]
        for i in range(first):
            row = dft([column[i] for column in columns], sign)
            for j in range(second):
                out[meeting(i, j, first, second)] = row[j]
        return out
    p = radix(n)
    if p:
        rest = n // p
        columns = [dft(values[j::p], sign) for j in range(p)]
        for i in range(rest):
            row = dft(
                [columns[j][i].times(sign * 2.0 * math.pi * i * j / n) for j in range(p)], sign
            )
            for j in range(p):
                out[i + rest * j] = row[j]
        return out
    for k in range(n):
        total = values[0]
        for j in range(1, n):
            total = total + values[j].times(sign * 2.0 * math.pi * (j * k % n) / n)
        out[k] = total
    return out


def real_dft(values):
    n = len(values)
    if n <= 4:
        out = dft(values, -1)
    else:
        out = [None] * n
        if coprime(n):
            first, second = coprime(n)
            columns = [
                real_dft([values[(i * second + j * first) % n] for i in range(first)])
                for j in range(second)
            ]
            for i in range(first // 2 + 1):
                entries = [column[i] for column in columns]
                alone = 2 * i % first == 0
                row = real_dft(entries) if alone else dft(entries, -1)
                for j in range(second):
                    out[meeting(i, j, first, second)] = row[j]
        elif radix(n):
            p = radix(n)
            rest = n // p
            columns = [real_dft(values[j::p]) for j in range(p)]
            for i in range(rest // 2 + 1):
                row = dft(
                    [columns[j][i].times(-2.0 * math.pi * i * j / n) for j in range(p)], -1
                )
                for j in range(p):
                    out[i + rest * j] = row[j]
        else:
            out = dft(values, -1)
    for k in range(1, n):
        if out[k] is None or (k > n // 2 and out[n - k] is not None):
            out[k] = out[n - k].conj()
    out[0] = Number(out[0].real)
    if n % 2 == 0:
        out[n // 2] = Number(out[n // 2].real)
    return out


def real_back(values):
    n = len(values)
    if n == 1:
        return [values[0].real]
    if n == 2:
        return [values[0].real + values[1].real, values[0].real - values[1].real]
    if n == 3:
        a, b = values[0].real, values[1]
        side = b.imag * math.sqrt(3.0)
        middle = a - b.real
        return [a + 2.0 * b.real, middle - side, middle + side]
    if n == 4:
        s, t = values[0].real + values[2].real, values[0].real - values[2].real
        u, v = 2.0 * values[1].real, 2.0 * values[1].imag
        return [s + u, t - v, s - u, t + v]
    out = [None] * n
    if coprime(n):
        first, second = coprime(n)
        rows = []
        for i in range(first // 2 + 1):
            entries = [values[meeting(i, j, first, second)] for j in range(second)]
            if 2 * i % first == 0:
                rows.append([Number(value) for value in real_back(entries)])
            else:
                rows.append(dft(entries, 1))
        for b in range(second):
            half = [row[b] for row in rows]
            whole = half + [half[first - i].conj() for i in range(len(half), first)]
            for a, value in enumerate(real_back(whole)):
                out[(a * second + b * first) % n] = value
        return out
    p = radix(n)
    if p:
        rest = n // p
        parts = []
        for i in range(p // 2 + 1):
            entries = values[i::p]
            if i == 0:
                parts.append([Number(value) for value in real_back(entries)])
            else:
                inner = dft(entries, 1)
                parts.append([inner[m].times(2.0 * math.pi * i * m / n) for m in range(rest)])
                if 2 * i == p:
                    parts[-1] = [Number(value.real) for value in parts[-1]]
        for m in range(rest):
            half = [part[m] for part in parts]
            whole = half + [half[p - i].conj() for i in range(len(half), p)]
            for j, value in enumerate(real_back(whole)):
                out[m + rest * j] = value
        return out
    return [value.real for value in dft(values, 1)]


def wave_table(edge):
    index = np.arange(edge)
    angles = 2.0 * np.pi / edge * (np.outer(index, index) % edge)
    full = np.zeros((2, 2, HALF, 2, HALF))
    for side in range(2):
        full[0, side, :edge, side, :edge] = np.cos(angles)
        full[1, side, :edge, side, :edge] = np.sin(angles)
    full = full.reshape(2, LANES, LANES)
    high = full.astype(jnp.bfloat16)
    low = (full - high.astype(np.float64)).astype(jnp.bfloat16)
    return np.stack([high, low])


def split_dot(real, imag, matrix):
    value = jnp.concatenate([real, imag], axis=1)
    high = value.astype(jnp.bfloat16)
    low = (value - high.astype(jnp.float32)).astype(jnp.bfloat16)
    product = jnp.dot(
        jnp.concatenate([high, low, high], axis=1), matrix[...], preferred_element_type=jnp.float32
    )
    return product[:, :LANES], product[:, LANES:]


def padded_half(edge):
    return -(-(edge // 2 + 1) // ROWS) * ROWS


def screen_kernel(edge, numbers_ref, kernel_ref, waves_ref, out_ref, kept_ref, ahead_ref, behind_ref, flipped):
    for i in range(numbers_ref.shape[0]):
        kept_ref[i] = numbers_ref[i]
    for table, sign in ((ahead_ref, -1), (behind_ref, 1)):
        for part, source in enumerate((0, 0, 1)):
            for i in range(2):
                for j in range(2):
                    value = waves_ref[source, (i + j) % 2]
                    if i != j and (i > j) == (sign > 0):
                        value = -value
                    rows = slice((2 * part + i) * LANES, (2 * part + i + 1) * LANES)
                    table[rows, j * LANES : (j + 1) * LANES] = value
    exact = dict(precision=lax.Precision.HIGHEST, preferred_element_type=jnp.float32)

    def index(shape, axis):
        return lax.broadcasted_iota(jnp.int32, shape, axis)

    square, whole = (edge, edge), (LANES, LANES)
    flip = index(square, 0) + index(square, 1)
    flip = ((flip == 0) | (flip == edge)).astype(jnp.float32)
    source, target = index(whole, 0), index(whole, 1)
    target = jnp.where(target < HALF, target, target - HALF)
    mirror = ((source + target == 0) | (source + target == edge)) & (source < edge) & (target < edge)
    mirror = mirror.astype(jnp.float32)
    flipped[...] = jnp.dot(flip, kernel_ref[...], **exact)
    height = padded_half(edge)
    lane = index((edge, LANES), 1)
    out_ref[...] = jnp.zeros_like(out_ref)

    def piece(ref, y):
        begin, offset = divmod(y * edge, LANES)
        value = ref[:, begin * LANES : (begin + 1) * LANES]
        value = pltpu.roll(value, LANES - offset, 1) if offset else value
        if offset + edge > LANES:
            more = ref[:, (begin + 1) * LANES : (begin + 2) * LANES]
            value = jnp.where(lane < LANES - offset, value, pltpu.roll(more, LANES - offset, 1))
        return value

    for y in range(edge // 2 + 1):
        value = piece(kernel_ref, y)
        value = jnp.where(lane < HALF, value, pltpu.roll(value, HALF, 1))
        value = value + jnp.dot(piece(flipped, (edge - y) % edge), mirror, **exact)
        value = value * (0.5 / float(edge**3))
        for t in range(edge // ROWS):
            at = pl.ds(t * ROWS * height + y, ROWS, stride=height)
            out_ref[at, :] = value[t * ROWS : (t + 1) * ROWS]


def screen_terms(numbers, kernel):
    edge, plane = kernel.shape
    smem = pl.BlockSpec(memory_space=pltpu.SMEM)
    vmem = pl.BlockSpec(memory_space=pltpu.VMEM)
    table = jax.ShapeDtypeStruct((6 * LANES, 2 * LANES), jnp.bfloat16)
    return pl.pallas_call(
        functools.partial(screen_kernel, edge),
        out_shape=[
            jax.ShapeDtypeStruct((edge * padded_half(edge), LANES), jnp.float32),
            jax.ShapeDtypeStruct(numbers.shape, numbers.dtype),
            table,
            table,
        ],
        in_specs=[smem, vmem, vmem],
        out_specs=[vmem, smem, vmem, vmem],
        scratch_shapes=[pltpu.VMEM((edge, plane), jnp.float32)],
        compiler_params=pltpu.CompilerParams(vmem_limit_bytes=8 << 20),
        name="screen_terms",
    )(numbers, kernel, jnp.asarray(wave_table(edge)))


def pair_kernel(shape, second_part, numbers_ref, *refs):
    edge, orb_dev, groups, fragments, slots = shape
    plane = edge * edge
    chunks = plane // LANES
    tiles = edge // ROWS
    half = edge // 2 + 1
    height = padded_half(edge)
    returns_count = (REACH + 1) * orb_dev
    tables, refs = refs[:3], refs[3:]
    phi_refs, own_ref, refs = refs[:groups], refs[groups], refs[groups + 1 :]
    (twin_ref, two_ref), refs = refs[:2], refs[2:]
    if second_part:
        (relay_ref, one_ref, act_before, back_before), refs = refs[:4], refs[4:]
        act_outs, back_outs, refs = refs[:2], refs[2:6], refs[6:]
        (act, back, state_sem, out_sem), refs = refs[:4], refs[4:]
    else:
        (act, back), refs = refs[:2], refs[2:]
    (near, wide, moved, dense, lower, upper, masks, listed, load_sem) = refs[:9]
    screen_ref, ahead_ref, behind_ref, table_sem = refs[9:]

    fragment, member, live_slots = numbers_ref[0], numbers_ref[1], numbers_ref[2]

    def first_of(slot):
        return numbers_ref[3 + slot]

    def second_of(slot):
        return numbers_ref[3 + slots + slot]

    def reach_of(slot):
        return numbers_ref[3 + 2 * slots + slot]

    def anchor(place, axis):
        return numbers_ref[3 + 3 * slots + 3 * place + axis]

    table_copies = [
        pltpu.make_async_copy(table, hold, table_sem.at[i])
        for i, (table, hold) in enumerate(zip(tables, refs[9:12]))
    ]
    for copy in table_copies:
        copy.start()
    lane = lax.broadcasted_iota(jnp.int32, (1, LANES), 1)
    stretch = next(n for n in (6, 4, 3, 2, 1) if chunks % n == 0)
    middle = pl.ds(edge, edge)

    even = lax.rem(fragment, 2) == 0

    def list_slots(slot, counts):
        early, found = counts
        mine = (slot < live_slots) & (lax.div(second_of(slot), orb_dev) == member)
        reach = reach_of(slot)
        come = (reach == 0) | (reach == 2) | (even & (lax.rem(second_of(slot), orb_dev) == 0))
        taken = mine & come & (early < 2)
        chosen = mine & jnp.logical_not(taken) if second_part else taken

        @pl.when(chosen)
        def _():
            listed[found] = slot

        return early + taken.astype(jnp.int32), found + chosen.astype(jnp.int32)

    _, found = lax.fori_loop(0, slots, list_slots, (jnp.int32(0), jnp.int32(0)))
    turns = lax.div(found + 1, 2)

    def slot_of(turn, side):
        at = 2 * turn + side
        live = at < found
        return listed[jnp.where(live, at, 2 * turn)], live

    def far_copy(side, source):
        return pltpu.make_async_copy(source, wide.at[side, :, middle], load_sem.at[1, side])

    def start_loads(turn):
        for side in range(2):
            slot, _ = slot_of(turn, side)
            first, second, reach = first_of(slot), second_of(slot), reach_of(slot)
            relative = lax.div(first, orb_dev) ^ member
            for k in range(groups):
                @pl.when(relative == k)
                def _():
                    pltpu.make_async_copy(
                        phi_refs[k].at[lax.rem(first, orb_dev)],
                        near.at[lax.rem(turn, 2), side],
                        load_sem.at[0, side],
                    ).start()
            own = lax.rem(second, orb_dev)

            @pl.when(reach == 0)
            def _():
                far_copy(side, own_ref.at[own]).start()

            @pl.when((reach == 1) & (own == 0) & even)
            def _():
                far_copy(side, twin_ref.at[0]).start()

            @pl.when(reach == 2)
            def _():
                far_copy(side, two_ref.at[own]).start()

            if second_part:
                @pl.when((reach == 1) & (own == 0) & jnp.logical_not(even))
                def _():
                    far_copy(side, relay_ref.at[0]).start()

                @pl.when((reach == 1) & (own > 0))
                def _():
                    far_copy(side, one_ref.at[jnp.maximum(own - 1, 0)]).start()

    def wait_loads(turn):
        for side in range(2):
            pltpu.make_async_copy(
                phi_refs[0].at[0], near.at[lax.rem(turn, 2), side], load_sem.at[0, side]
            ).wait()
            far_copy(side, own_ref.at[0]).wait()

    @pl.when(found > 0)
    def _():
        start_loads(0)

    if second_part:
        state_copies = [
            pltpu.make_async_copy(before, now, state_sem.at[i])
            for i, (before, now) in enumerate(((act_before, act), (back_before, back)))
        ]
        for copy in state_copies:
            copy.start()
        slab = plane * edge // LANES // groups
        act_copies = []
        for k in range(groups):
            source = (member ^ k) * slab
            place = reversed_bits(k, groups)
            act_copies.append(
                pltpu.make_async_copy(
                    act.at[:, pl.ds(pl.multiple_of(source, ROWS), slab), :],
                    act_outs[2 * place // groups].at[place % (groups // 2)],
                    out_sem.at[k],
                )
            )
    else:
        act[...] = jnp.zeros_like(act)
        back[...] = jnp.zeros_like(back)
    for copy in table_copies:
        copy.wait()

    def offset_of(slot):
        partner = lax.rem(fragment + reach_of(slot), fragments)
        return [anchor(partner, i) - anchor(fragment, i) for i in range(3)]

    def steps(count, body, most):
        width = max(n for n in range(1, most + 1) if count % n == 0)

        def step(i, _):
            for j in range(width):
                body(i * width + j)
            return 0

        if width == count:
            step(0, 0)
        else:
            lax.fori_loop(0, count // width, step, 0)

    def columns(k):
        return pl.ds(pl.multiple_of(k * LANES, LANES), LANES)

    def set_masks(place, delta, weight):
        shape = masks.shape[1:]
        spot = lax.broadcasted_iota(jnp.int32, shape, 0) * LANES
        spot = spot + lax.broadcasted_iota(jnp.int32, shape, 1)
        y = ((spot.astype(jnp.float32) + 0.5) * (1.0 / edge)).astype(jnp.int32)
        z = spot - y * edge - delta[2]
        y = y - delta[1]
        inside = (y >= 0) & (y < edge) & (z >= 0) & (z < edge)
        masks[place] = jnp.where(inside, weight, 0.0)

    def shifted(source, place, delta, begin, count, ks):
        shift = lax.rem(delta[1] * edge + delta[2] + 4 * plane, plane)
        start = lax.rem(plane - shift, plane)
        whole, part = lax.div(start, LANES), lax.rem(start, LANES)
        turn = lax.rem(LANES - part, LANES)
        down = edge - jnp.clip(delta[0], -edge, edge) + begin
        x = lax.broadcasted_iota(jnp.int32, (count, LANES), 0) + (begin - delta[0])
        rows_inside = (x >= 0) & (x < edge)
        first = lane < LANES - part

        def piece(k):
            return pltpu.roll(source[lax.rem(k + whole, chunks), pl.ds(down, count), :], turn, 1)

        out = []
        low = piece(ks[0])
        for k in ks:
            high = piece(k + 1)
            value = jnp.where(first, low, high) * masks[place, pl.ds(k, 1), :]
            out.append(jnp.where(rows_inside, value, 0.0))
            low = high
        return out

    def tile(t, i, size):
        return pl.ds(pl.multiple_of(i * size + t * ROWS, ROWS), ROWS)

    def across(t, i, size):
        return pl.ds(t * (ROWS * size) + i, ROWS, stride=size)

    def solve_two(turn, _):
        wait_loads(turn)
        near_now = near.at[lax.rem(turn, 2)]
        picked = [slot_of(turn, side) for side in range(2)]
        offsets = [offset_of(slot) for slot, _ in picked]
        returns = [[-d for d in delta] for delta in offsets]
        for side in range(2):
            set_masks(side, offsets[side], picked[side][1].astype(jnp.float32))
            set_masks(2 + side, returns[side], 1.0)

        def over_y(t):
            densities = []
            begin = pl.multiple_of(t * ROWS, ROWS)
            rows = pl.ds(begin, ROWS)
            for side in range(2):
                values = shifted(wide.at[side], side, offsets[side], begin, ROWS, range(chunks))
                for k in range(chunks):
                    moved[side, k, rows, :] = values[k]
                    values[k] = values[k] * near_now[side, rows, k * LANES : (k + 1) * LANES]
                densities.append(values)
            planes = []
            for y in range(edge):
                first, offset = divmod(y * edge, LANES)
                sides = []
                for side in range(2):
                    shift = (side * HALF - offset) % LANES
                    value = densities[side][first]
                    value = pltpu.roll(value, shift, 1) if shift else value
                    if offset + edge > LANES:
                        more = densities[side][first + 1]
                        more = pltpu.roll(more, shift, 1) if shift else more
                        value = jnp.where(lane < side * HALF + LANES - offset, value, more)
                    sides.append(value)
                planes.append(Number(jnp.where(lane < HALF, sides[0], sides[1])))
            values = real_dft(planes)
            for i in range(half):
                at = tile(t, i, edge)
                lower[0, at, :] = values[i].real
                imag = values[i].imag
                lower[1, at, :] = jnp.zeros((ROWS, LANES), jnp.float32) if imag is None else imag

        steps(tiles, over_y, 2)

        @pl.when(turn + 1 < turns)
        def _():
            start_loads(turn + 1)

        def over_x(t):
            at = [across(t, i, edge) for i in range(edge)]
            values = dft([Number(lower[0, a, :], lower[1, a, :]) for a in at], -1)
            real = jnp.concatenate([value.real for value in values], axis=0)
            imag = jnp.concatenate([value.imag for value in values], axis=0)
            at = [tile(t, i, height) for i in range(edge)]
            factor = jnp.concatenate([screen_ref[a, :] for a in at], axis=0)
            real, imag = split_dot(real, imag, ahead_ref)
            real, imag = split_dot(real * factor, imag * factor, behind_ref)
            rows = [slice(i * ROWS, (i + 1) * ROWS) for i in range(edge)]
            values = dft([Number(real[r], imag[r]) for r in rows], 1)
            for i in range(edge):
                upper[0, at[i], :] = values[i].real
                upper[1, at[i], :] = values[i].imag

        steps(height // ROWS, over_x, 2)
        if second_part:
            @pl.when(turn == 0)
            def _():
                for copy in state_copies:
                    copy.wait()

        firsts = [first_of(slot) for slot, _ in picked]

        def back_y(t):
            begin = pl.multiple_of(t * ROWS, ROWS)
            rows = pl.ds(begin, ROWS)
            at = [across(t, i, height) for i in range(half)]
            values = [Number(upper[0, a, :], upper[1, a, :]) for a in at]
            values = values + [values[edge - i].conj() for i in range(half, edge)]
            planes = real_back(values)
            for side in range(2):
                forward = []
                for k in range(chunks):
                    value = None
                    for y in range(k * LANES // edge, edge):
                        begins = y * edge - k * LANES
                        if begins >= LANES:
                            break
                        shift = (begins - side * HALF) % LANES
                        piece = pltpu.roll(planes[y], shift, 1) if shift else planes[y]
                        value = piece if value is None else jnp.where(lane < begins, value, piece)
                    forward.append(value * moved[side, k, rows, :])
                    other = value * near_now[side, rows, k * LANES : (k + 1) * LANES]
                    dense[side, k, pl.ds(edge + begin, ROWS), :] = other
                at = [pl.ds(t * (ROWS * chunks) + k, ROWS, stride=chunks) for k in range(chunks)]
                sums = [act[firsts[side], at[k], :] + forward[k] for k in range(chunks)]
                for k in range(chunks):
                    act[firsts[side], at[k], :] = sums[k]

        steps(tiles, back_y, 2)

        if second_part:
            @pl.when(turn + 1 == turns)
            def _():
                for copy in act_copies:
                    copy.start()

        homes = []
        for side in range(2):
            slot = picked[side][0]
            homes.append(reach_of(slot) * orb_dev + lax.rem(second_of(slot), orb_dev))

        def send_back(g):
            for side in range(2):
                ks = [g * stretch + i for i in range(stretch)]
                values = shifted(dense.at[side], 2 + side, returns[side], 0, edge, ks)
                at = [
                    (i, t, pl.ds(t * (ROWS * chunks) + ks[i], ROWS, stride=chunks))
                    for i in range(stretch)
                    for t in range(tiles)
                ]
                sums = [
                    back[homes[side], a, :] + values[i][t * ROWS : (t + 1) * ROWS] for i, t, a in at
                ]
                for (i, t, a), value in zip(at, sums):
                    back[homes[side], a, :] = value

        steps(chunks // stretch, send_back, 3)
        return 0

    if not second_part:
        lax.fori_loop(0, turns, solve_two, 0)
        return

    @pl.when(found == 0)
    def _():
        for copy in state_copies:
            copy.wait()
        for copy in act_copies:
            copy.start()

    lax.fori_loop(0, turns, solve_two, 0)
    spans = ((orb_dev, 1), (orb_dev + 1, orb_dev - 1), (2 * orb_dev, orb_dev), (0, orb_dev))
    back_copies = [
        pltpu.make_async_copy(back.at[pl.ds(begin, count)], back_outs[i], out_sem.at[groups + i])
        for i, (begin, count) in enumerate(spans)
    ]
    for copy in back_copies:
        copy.start()
    for copy in act_copies + back_copies:
        copy.wait()


def reversed_bits(k, count):
    bits = count.bit_length() - 1
    return sum(((k >> i) & 1) << (bits - 1 - i) for i in range(bits))


def pair_terms(numbers, fragments, slots, tables, pieces, own, far, before=()):
    second_part = bool(before)
    orb_dev, edge, plane = pieces[0].shape
    groups = len(pieces)
    frag_size = groups * orb_dev
    chunks = plane // LANES
    rows = edge * chunks
    height = padded_half(edge)
    returns_count = (REACH + 1) * orb_dev
    shape = (edge, orb_dev, groups, fragments, slots)
    smem = pl.BlockSpec(memory_space=pltpu.SMEM)
    vmem = pl.BlockSpec(memory_space=pltpu.VMEM)
    hbm = pl.BlockSpec(memory_space=pltpu.HBM)
    f32 = jnp.float32
    sums = ((frag_size, rows, LANES), (returns_count, rows, LANES))
    out_shape = [jax.ShapeDtypeStruct(sum_shape, f32) for sum_shape in sums]
    out_specs, scratch = [vmem] * 2, []
    if second_part:
        out_shape = [jax.ShapeDtypeStruct((groups // 2, frag_size, rows // groups, LANES), f32)] * 2
        for count in (1, orb_dev - 1, orb_dev, orb_dev):
            out_shape.append(jax.ShapeDtypeStruct((count, rows, LANES), f32))
        out_specs = [hbm] * 6
        scratch = [pltpu.VMEM(sum_shape, f32) for sum_shape in sums]
        scratch += [pltpu.SemaphoreType.DMA((2,)), pltpu.SemaphoreType.DMA((groups + 4,))]
    return pl.pallas_call(
        functools.partial(pair_kernel, shape, second_part),
        out_shape=out_shape,
        in_specs=[smem] + [hbm] * (4 + groups + len(far) + len(before)),
        out_specs=out_specs,
        scratch_shapes=scratch
        + [
            pltpu.VMEM((2, 2, edge, plane), f32),
            pltpu.VMEM((2, chunks, 3 * edge, LANES), f32),
            pltpu.VMEM((2, chunks, edge, LANES), f32),
            pltpu.VMEM((2, chunks, 3 * edge, LANES), f32),
            pltpu.VMEM((2, height * edge, LANES), f32),
            pltpu.VMEM((2, height * edge, LANES), f32),
            pltpu.VMEM((4, -(-chunks // ROWS) * ROWS, LANES), f32),
            pltpu.SMEM((slots,), jnp.int32),
            pltpu.SemaphoreType.DMA((2, 2)),
            *[pltpu.VMEM(table.shape, table.dtype) for table in tables],
            pltpu.SemaphoreType.DMA((3,)),
        ],
        compiler_params=pltpu.CompilerParams(vmem_limit_bytes=30 << 20),
        name="late_pair_terms" if second_part else "early_pair_terms",
    )(numbers, *tables, *pieces, own, *far, *before)


def flatten_kernel(shape, places_ref, *refs):
    edge, orb_dev, groups = shape
    pieces, (flat_ref, slab_ref) = refs[:groups], refs[groups:]
    member = places_ref[1]
    chunks = edge * edge // LANES
    slab = slab_ref.shape[1]
    for k in range(groups):
        for o in range(orb_dev):
            def move(j, _):
                value = pieces[k][o, :, pl.ds(pl.multiple_of(j * LANES, LANES), LANES)]
                for t in range(edge // ROWS):
                    at = pl.ds(t * (ROWS * chunks) + j, ROWS, stride=chunks)
                    flat_ref[k * orb_dev + o, at, :] = value[t * ROWS : (t + 1) * ROWS]
                return 0

            lax.fori_loop(0, chunks, move, 0)
    slab_ref[...] = flat_ref[:, pl.ds(pl.multiple_of(member * slab, ROWS), slab), :]


def flatten_terms(places, pieces):
    orb_dev, edge, plane = pieces[0].shape
    groups = len(pieces)
    rows = edge * plane // LANES
    frag_size = groups * orb_dev
    smem = pl.BlockSpec(memory_space=pltpu.SMEM)
    vmem = pl.BlockSpec(memory_space=pltpu.VMEM)
    return pl.pallas_call(
        functools.partial(flatten_kernel, (edge, orb_dev, groups)),
        out_shape=(
            jax.ShapeDtypeStruct((frag_size, rows, LANES), jnp.float32),
            jax.ShapeDtypeStruct((frag_size, rows // groups, LANES), jnp.float32),
        ),
        in_specs=[smem] + [vmem] * groups,
        out_specs=(vmem, vmem),
        compiler_params=pltpu.CompilerParams(vmem_limit_bytes=24 << 20),
        name="flatten_terms",
    )(places, *pieces)


def home_kernel(shape, places_ref, flat_ref, phi_ref, kept_ref, *refs):
    edge, orb_dev, groups, parts = shape
    arrived, refs = refs[:parts], refs[parts:]
    (own_ref, twin_ref, relay_ref, one_ref, two_ref), refs = refs[:5], refs[5:]
    act_ref, outs, total = refs[0], refs[1 : 1 + groups], refs[1 + groups]
    fragment, member = places_ref[0], places_ref[1]
    odd = lax.rem(fragment, 2) == 1
    frag_size = orb_dev * groups
    slab = act_ref.shape[1]
    rows = flat_ref.shape[1]
    cut = frag_size // parts
    for i in range(parts):
        span = slice(i * cut, (i + 1) * cut)
        act_ref[span] = kept_ref[0, span] + arrived[i][0]

    @pl.when(odd)
    def _():
        total[0] = own_ref[0] + two_ref[0] + twin_ref[0]

    @pl.when(jnp.logical_not(odd))
    def _():
        total[0] = own_ref[0] + two_ref[0] + relay_ref[0]

    for o in range(1, orb_dev):
        total[o] = own_ref[o] + two_ref[o] + one_ref[o - 1]

    row = lax.broadcasted_iota(jnp.int32, (frag_size, LANES), 0)
    lane = lax.broadcasted_iota(jnp.int32, (frag_size, LANES), 1)

    def products(lefts, rights, length, step):
        def add(i, sums):
            at = pl.ds(pl.multiple_of(i * step, ROWS), step)
            right = [ref[index, at, :].reshape(step // ROWS, ROWS, LANES) for ref, index in rights]
            out = []
            for n, (ref, index) in enumerate(lefts):
                left = ref[index, at, :].reshape(step // ROWS, ROWS, LANES)
                for m in range(len(rights)):
                    out.append(sums[n * len(rights) + m] + jnp.sum(left * right[m], axis=0))
            return tuple(out)

        zero = jnp.zeros((ROWS, LANES), jnp.float32)
        return lax.fori_loop(0, length // step, add, (zero,) * (len(lefts) * len(rights)))

    result = jnp.zeros((frag_size, LANES), jnp.float32)
    scale = 1.0 / float(edge**3)
    step = next(n for n in (72, 24, 8) if slab % n == 0)
    for half in range(0, frag_size, 4):
        bs = range(half, min(half + 4, frag_size))
        sums = products(
            [(phi_ref, a) for a in range(frag_size)], [(act_ref, b) for b in bs], slab, step
        )
        for a in range(frag_size):
            place = (member ^ (a // orb_dev)) * orb_dev + a % orb_dev
            for i, b in enumerate(bs):
                value = jnp.sum(sums[a * len(bs) + i], keepdims=True)
                result = jnp.where((row == place) & (lane == b), value, result)
    sums = products(
        [(flat_ref, a) for a in range(frag_size)], [(total, b) for b in range(orb_dev)], rows, step
    )
    for a in range(frag_size):
        place = (member ^ (a // orb_dev)) * orb_dev + a % orb_dev
        for b in range(orb_dev):
            value = jnp.sum(sums[a * orb_dev + b], keepdims=True)
            at = (row == place) & (lane == member * orb_dev + b)
            result = jnp.where(at, result + value, result)

    for k in range(groups):
        begin = pl.multiple_of((member ^ k) * slab, ROWS)
        for o in range(orb_dev):
            outs[k][o * slab : (o + 1) * slab, :] = total[o, pl.ds(begin, slab), :]
        outs[k][orb_dev * slab :, :] = result * scale


def home_terms(places, edge, flat, phi, kept, arrived, own, twin, relay, one, two):
    frag_size, slab = phi.shape[:2]
    orb_dev, rows = own.shape[:2]
    groups = frag_size // orb_dev
    smem = pl.BlockSpec(memory_space=pltpu.SMEM)
    vmem = pl.BlockSpec(memory_space=pltpu.VMEM)
    f32 = jnp.float32
    found = pl.pallas_call(
        functools.partial(home_kernel, (edge, orb_dev, groups, len(arrived))),
        out_shape=[jax.ShapeDtypeStruct((frag_size, slab, LANES), f32)]
        + [jax.ShapeDtypeStruct((orb_dev * slab + frag_size, LANES), f32)] * groups,
        in_specs=[smem] + [vmem] * (8 + len(arrived)),
        out_specs=[vmem] * (1 + groups),
        scratch_shapes=[pltpu.VMEM((orb_dev, rows, LANES), f32)],
        compiler_params=pltpu.CompilerParams(vmem_limit_bytes=32 << 20),
        name="home_terms",
    )(places, flat, phi, kept, *arrived, own, twin, relay, one, two)
    return found[0], found[1:]


def gradient_kernel(shape, places_ref, act_ref, phi_ref, *refs):
    edge, orb_dev, groups = shape
    parcels, (out_ref, lagrange_ref, weights, hold) = refs[:groups], refs[groups:]
    member = places_ref[1]
    frag_size = orb_dev * groups
    chunks = edge * edge // LANES
    slab_rows = edge // groups
    slab = slab_rows * chunks
    sums = [parcel[orb_dev * slab :, :] for parcel in parcels]
    while len(sums) > 1:
        sums = [sums[i] + sums[i + 1] for i in range(0, len(sums), 2)]
    square = jnp.concatenate([sums[0], jnp.zeros((LANES - frag_size, LANES), jnp.float32)], axis=0)
    lagrange = 0.5 * (square + square.T)[:frag_size, :]
    lagrange_ref[...] = lagrange[:, :frag_size]
    weights[...] = lagrange

    for k in range(groups):
        for o in range(orb_dev):
            a = (member ^ k) * orb_dev + o
            value = act_ref[a] + parcels[k][o * slab : (o + 1) * slab, :]
            lane = lax.broadcasted_iota(jnp.int32, (1, LANES), 1)
            for q in range(groups):
                for p in range(orb_dev):
                    line = weights[pl.ds((member ^ q) * orb_dev + p, 1), :]
                    factor = jnp.sum(jnp.where(lane == a, line, 0.0), axis=1, keepdims=True)
                    value = value - factor * phi_ref[q * orb_dev + p]
            hold[pl.ds(pl.multiple_of(a * slab, ROWS), slab), :] = value
    for x in range(slab_rows):
        for j in range(chunks):
            value = hold[pl.ds(x * chunks + j, frag_size, stride=slab), :]
            out_ref[x, :, j * LANES : (j + 1) * LANES] = value


def gradient_terms(places, edge, act, phi, parcels):
    groups = len(parcels)
    frag_size, slab = act.shape[:2]
    smem = pl.BlockSpec(memory_space=pltpu.SMEM)
    vmem = pl.BlockSpec(memory_space=pltpu.VMEM)
    f32 = jnp.float32
    gradient, lagrange = pl.pallas_call(
        functools.partial(gradient_kernel, (edge, frag_size // groups, groups)),
        out_shape=(
            jax.ShapeDtypeStruct((edge // groups, frag_size, edge * edge), f32),
            jax.ShapeDtypeStruct((frag_size, frag_size), f32),
        ),
        in_specs=[smem] + [vmem] * (2 + groups),
        out_specs=(vmem, vmem),
        scratch_shapes=[
            pltpu.VMEM((frag_size, LANES), f32),
            pltpu.VMEM((frag_size * slab, LANES), f32),
        ],
        compiler_params=pltpu.CompilerParams(vmem_limit_bytes=24 << 20),
        name="gradient_terms",
    )(places, act, phi, *parcels)
    return gradient.transpose(1, 0, 2), lagrange


def together(*arrays):
    return lax.optimization_barrier(arrays)


def to_fragment(block, distance, senders=None):
    devices = lax.axis_size("orb")
    senders = range(devices) if senders is None else range(senders, devices, 2)
    return lax.ppermute(block, "orb", [(i, (i + distance) % devices) for i in senders])


def with_twin(block):
    return lax.ppermute(block, "orb", [(i, i ^ 1) for i in range(lax.axis_size("orb"))])


def with_member(block, bit):
    return lax.ppermute(block, "grp", [(i, i ^ bit) for i in range(lax.axis_size("grp"))])


def shards(orbitals, kernel, anchors, pair_count, pair_first, pair_second, pair_reach):
    groups = lax.axis_size("grp")
    orb_dev, edge, plane = orbitals.shape
    frag_size = groups * orb_dev
    places = jnp.stack([lax.axis_index("orb"), lax.axis_index("grp")]).astype(jnp.int32)

    own = orbitals.reshape(orb_dev, edge, plane // LANES, LANES).transpose(0, 2, 1, 3)
    numbers = [places, pair_count, pair_first, pair_second, pair_reach, anchors.reshape(-1)]
    screen, numbers, *tables = screen_terms(jnp.concatenate(numbers), kernel)
    two = to_fragment(own, -2)
    twin = with_twin(own[:1])
    pieces = {0: orbitals}
    bit = groups // 2
    while bit:
        for k in list(pieces):
            pieces[k ^ bit] = with_member(pieces[k], bit)
        if bit == groups // 2:
            two, twin, tail, pieces[bit], screen, numbers, *tables = together(
                two, twin, own[1:], pieces[bit], screen, numbers, *tables
            )
            one = to_fragment(tail, -1)
            relay = to_fragment(twin, -2, 1)
        bit //= 2
    pieces = [pieces[k] for k in range(groups)]
    tables = [screen, *tables]
    sizes = (anchors.shape[0], pair_first.shape[0])
    before = pair_terms(numbers, *sizes, tables, pieces, own, [twin, two])
    kept, sent, back_first, back_rest, back_two, own = pair_terms(
        numbers, *sizes, tables, pieces, own, [twin, two, relay, one], before
    )

    two = to_fragment(back_two, 2)
    one = to_fragment(back_rest, 1)
    bit = 1
    arrived = [with_member(sent, bit)]
    while 2 * bit < groups:
        kept = kept + jnp.concatenate(arrived, axis=1)
        if bit == 1:
            kept, back_first = together(kept, back_first)
        half = kept.shape[0] // 2
        cut = frag_size // orb_dev
        bit *= 2
        arrived = [
            with_member(kept[half:, i : i + cut], bit) for i in range(0, frag_size, cut)
        ]
        kept = kept[:half]
    twin = with_twin(back_first)
    relay = to_fragment(twin, 2, 0)

    flat, phi = flatten_terms(places, pieces)
    act, parcels = home_terms(places, edge, flat, phi, kept, arrived, own, twin, relay, one, two)
    received = []
    for k in range(groups):
        parcel, bit = parcels[k], groups // 2
        while bit:
            if k & bit:
                parcel = with_member(parcel, bit)
            bit //= 2
        received.append(parcel)
    gradient, lagrange = gradient_terms(places, edge, act, phi, received)
    return (gradient, lagrange[None])


def solution(mesh):
    placed = (P(("orb", "grp"), None, None), P(), P(), P("orb"), P("orb"), P("orb"), P("orb"))
    return jax.shard_map(
        shards,
        mesh=mesh,
        in_specs=placed,
        out_specs=(P("orb", "grp", None), P("orb", None, None)),
        check_vma=False,
    )
```

```python
import functools
import math

import jax
import jax.numpy as jnp
import numpy as np
from jax import lax
from jax.experimental import pallas as pl
from jax.experimental.pallas import tpu as pltpu
from jax.sharding import PartitionSpec as P

REACH = 2
LANES = 128
ROWS = 8
HALF = LANES // 2


class Number:
    def __init__(self, real, imag=None):
        self.real, self.imag = real, imag

    def __add__(self, other):
        if self.imag is None or other.imag is None:
            imag = self.imag if other.imag is None else other.imag
        else:
            imag = self.imag + other.imag
        return Number(self.real + other.real, imag)

    def __sub__(self, other):
        if other.imag is None:
            imag = self.imag
        else:
            imag = -other.imag if self.imag is None else self.imag - other.imag
        return Number(self.real - other.real, imag)

    def conj(self):
        return self if self.imag is None else Number(self.real, -self.imag)

    def scaled(self, factor):
        return Number(self.real * factor, None if self.imag is None else self.imag * factor)

    def turned(self, sign):
        if self.imag is None:
            return Number(jnp.zeros_like(self.real), self.real if sign > 0 else -self.real)
        return Number(-self.imag, self.real) if sign > 0 else Number(self.imag, -self.real)

    def plus_turned(self, other, sign):
        if sign < 0:
            return self.minus_turned(other)
        real = self.real if other.imag is None else self.real - other.imag
        return Number(real, other.real if self.imag is None else self.imag + other.real)

    def minus_turned(self, other):
        real = self.real if other.imag is None else self.real + other.imag
        return Number(real, -other.real if self.imag is None else self.imag - other.real)

    def times(self, angle):
        real, imag = math.cos(angle), math.sin(angle)
        if abs(imag) < 1e-12:
            return self if real > 0 else self.scaled(-1.0)
        if abs(real) < 1e-12:
            return self.turned(imag)
        if self.imag is None:
            return Number(self.real * real, self.real * imag)
        return Number(self.real * real - self.imag * imag, self.real * imag + self.imag * real)


def coprime(n):
    for p in (2, 3, 5, 7):
        power = 1
        while n % (power * p) == 0:
            power *= p
        if 1 < power < n:
            return power, n // power
    return None


def radix(n):
    return next((p for p in (4, 2, 3, 5, 7) if n % p == 0 and n > p), None)


def meeting(i, j, first, second):
    return next(k for k in range(first * second) if k % first == i and k % second == j)


def dft(values, sign):
    n = len(values)
    if n == 1:
        return values
    if n == 2:
        return [values[0] + values[1], values[0] - values[1]]
    if n == 3:
        a, b, c = values
        total, side = b + c, (b - c).scaled(math.sqrt(0.75))
        middle = a - total.scaled(0.5)
        return [a + total, middle.plus_turned(side, sign), middle.plus_turned(side, -sign)]
    if n == 4:
        a, b, c, d = values
        s, t, u, v = a + c, a - c, b + d, b - d
        return [s + u, t.plus_turned(v, sign), s - u, t.plus_turned(v, -sign)]
    out = [None] * n
    if coprime(n):
        first, second = coprime(n)
        columns = [
            dft([values[(i * second + j * first) % n] for i in range(first)], sign)
            for j in range(second)
        ]
        for i in range(first):
            row = dft([column[i] for column in columns], sign)
            for j in range(second):
                out[meeting(i, j, first, second)] = row[j]
        return out
    p = radix(n)
    if p:
        rest = n // p
        columns = [dft(values[j::p], sign) for j in range(p)]
        for i in range(rest):
            row = dft(
                [columns[j][i].times(sign * 2.0 * math.pi * i * j / n) for j in range(p)], sign
            )
            for j in range(p):
                out[i + rest * j] = row[j]
        return out
    for k in range(n):
        total = values[0]
        for j in range(1, n):
            total = total + values[j].times(sign * 2.0 * math.pi * (j * k % n) / n)
        out[k] = total
    return out


def real_dft(values):
    n = len(values)
    if n <= 4:
        out = dft(values, -1)
    else:
        out = [None] * n
        if coprime(n):
            first, second = coprime(n)
            columns = [
                real_dft([values[(i * second + j * first) % n] for i in range(first)])
                for j in range(second)
            ]
            for i in range(first // 2 + 1):
                entries = [column[i] for column in columns]
                alone = 2 * i % first == 0
                row = real_dft(entries) if alone else dft(entries, -1)
                for j in range(second):
                    out[meeting(i, j, first, second)] = row[j]
        elif radix(n):
            p = radix(n)
            rest = n // p
            columns = [real_dft(values[j::p]) for j in range(p)]
            for i in range(rest // 2 + 1):
                row = dft(
                    [columns[j][i].times(-2.0 * math.pi * i * j / n) for j in range(p)], -1
                )
                for j in range(p):
                    out[i + rest * j] = row[j]
        else:
            out = dft(values, -1)
    for k in range(1, n):
        if out[k] is None or (k > n // 2 and out[n - k] is not None):
            out[k] = out[n - k].conj()
    out[0] = Number(out[0].real)
    if n % 2 == 0:
        out[n // 2] = Number(out[n // 2].real)
    return out


def real_back(values):
    n = len(values)
    if n == 1:
        return [values[0].real]
    if n == 2:
        return [values[0].real + values[1].real, values[0].real - values[1].real]
    if n == 3:
        a, b = values[0].real, values[1]
        side = b.imag * math.sqrt(3.0)
        middle = a - b.real
        return [a + 2.0 * b.real, middle - side, middle + side]
    if n == 4:
        s, t = values[0].real + values[2].real, values[0].real - values[2].real
        u, v = 2.0 * values[1].real, 2.0 * values[1].imag
        return [s + u, t - v, s - u, t + v]
    out = [None] * n
    if coprime(n):
        first, second = coprime(n)
        rows = []
        for i in range(first // 2 + 1):
            entries = [values[meeting(i, j, first, second)] for j in range(second)]
            if 2 * i % first == 0:
                rows.append([Number(value) for value in real_back(entries)])
            else:
                rows.append(dft(entries, 1))
        for b in range(second):
            half = [row[b] for row in rows]
            whole = half + [half[first - i].conj() for i in range(len(half), first)]
            for a, value in enumerate(real_back(whole)):
                out[(a * second + b * first) % n] = value
        return out
    p = radix(n)
    if p:
        rest = n // p
        parts = []
        for i in range(p // 2 + 1):
            entries = values[i::p]
            if i == 0:
                parts.append([Number(value) for value in real_back(entries)])
            else:
                inner = dft(entries, 1)
                parts.append([inner[m].times(2.0 * math.pi * i * m / n) for m in range(rest)])
                if 2 * i == p:
                    parts[-1] = [Number(value.real) for value in parts[-1]]
        for m in range(rest):
            half = [part[m] for part in parts]
            whole = half + [half[p - i].conj() for i in range(len(half), p)]
            for j, value in enumerate(real_back(whole)):
                out[m + rest * j] = value
        return out
    return [value.real for value in dft(values, 1)]


def wave_table(edge):
    index = np.arange(edge)
    angles = 2.0 * np.pi / edge * (np.outer(index, index) % edge)
    full = np.zeros((2, 2, HALF, 2, HALF))
    for side in range(2):
        full[0, side, :edge, side, :edge] = np.cos(angles)
        full[1, side, :edge, side, :edge] = np.sin(angles)
    full = full.reshape(2, LANES, LANES)
    high = full.astype(jnp.bfloat16)
    low = (full - high.astype(np.float64)).astype(jnp.bfloat16)
    return np.stack([high, low])


def split_dot(real, imag, matrix):
    value = jnp.concatenate([real, imag], axis=1)
    high = value.astype(jnp.bfloat16)
    low = (value - high.astype(jnp.float32)).astype(jnp.bfloat16)
    product = jnp.dot(
        jnp.concatenate([high, low, high], axis=1), matrix[...], preferred_element_type=jnp.float32
    )
    return product[:, :LANES], product[:, LANES:]


def padded_half(edge):
    return -(-(edge // 2 + 1) // ROWS) * ROWS


def screen_kernel(edge, numbers_ref, kernel_ref, waves_ref, out_ref, kept_ref, ahead_ref, behind_ref, flipped):
    for i in range(numbers_ref.shape[0]):
        kept_ref[i] = numbers_ref[i]
    for table, sign in ((ahead_ref, -1), (behind_ref, 1)):
        for part, source in enumerate((0, 0, 1)):
            for i in range(2):
                for j in range(2):
                    value = waves_ref[source, (i + j) % 2]
                    if i != j and (i > j) == (sign > 0):
                        value = -value
                    rows = slice((2 * part + i) * LANES, (2 * part + i + 1) * LANES)
                    table[rows, j * LANES : (j + 1) * LANES] = value
    exact = dict(precision=lax.Precision.HIGHEST, preferred_element_type=jnp.float32)

    def index(shape, axis):
        return lax.broadcasted_iota(jnp.int32, shape, axis)

    square, whole = (edge, edge), (LANES, LANES)
    flip = index(square, 0) + index(square, 1)
    flip = ((flip == 0) | (flip == edge)).astype(jnp.float32)
    source, target = index(whole, 0), index(whole, 1)
    target = jnp.where(target < HALF, target, target - HALF)
    mirror = ((source + target == 0) | (source + target == edge)) & (source < edge) & (target < edge)
    mirror = mirror.astype(jnp.float32)
    flipped[...] = jnp.dot(flip, kernel_ref[...], **exact)
    height = padded_half(edge)
    lane = index((edge, LANES), 1)
    out_ref[...] = jnp.zeros_like(out_ref)

    def piece(ref, y):
        begin, offset = divmod(y * edge, LANES)
        value = ref[:, begin * LANES : (begin + 1) * LANES]
        value = pltpu.roll(value, LANES - offset, 1) if offset else value
        if offset + edge > LANES:
            more = ref[:, (begin + 1) * LANES : (begin + 2) * LANES]
            value = jnp.where(lane < LANES - offset, value, pltpu.roll(more, LANES - offset, 1))
        return value

    for y in range(edge // 2 + 1):
        value = piece(kernel_ref, y)
        value = jnp.where(lane < HALF, value, pltpu.roll(value, HALF, 1))
        value = value + jnp.dot(piece(flipped, (edge - y) % edge), mirror, **exact)
        value = value * (0.5 / float(edge**3))
        for t in range(edge // ROWS):
            at = pl.ds(t * ROWS * height + y, ROWS, stride=height)
            out_ref[at, :] = value[t * ROWS : (t + 1) * ROWS]


def screen_terms(numbers, kernel):
    edge, plane = kernel.shape
    smem = pl.BlockSpec(memory_space=pltpu.SMEM)
    vmem = pl.BlockSpec(memory_space=pltpu.VMEM)
    table = jax.ShapeDtypeStruct((6 * LANES, 2 * LANES), jnp.bfloat16)
    return pl.pallas_call(
        functools.partial(screen_kernel, edge),
        out_shape=[
            jax.ShapeDtypeStruct((edge * padded_half(edge), LANES), jnp.float32),
            jax.ShapeDtypeStruct(numbers.shape, numbers.dtype),
            table,
            table,
        ],
        in_specs=[smem, vmem, vmem],
        out_specs=[vmem, smem, vmem, vmem],
        scratch_shapes=[pltpu.VMEM((edge, plane), jnp.float32)],
        compiler_params=pltpu.CompilerParams(vmem_limit_bytes=8 << 20),
        name="screen_terms",
    )(numbers, kernel, jnp.asarray(wave_table(edge)))


def pair_kernel(shape, second_part, numbers_ref, *refs):
    edge, orb_dev, groups, fragments, slots = shape
    plane = edge * edge
    chunks = plane // LANES
    tiles = edge // ROWS
    half = edge // 2 + 1
    height = padded_half(edge)
    returns_count = (REACH + 1) * orb_dev
    tables, refs = refs[:3], refs[3:]
    phi_refs, own_ref, refs = refs[:groups], refs[groups], refs[groups + 1 :]
    (twin_ref, two_ref), refs = refs[:2], refs[2:]
    if second_part:
        (relay_ref, one_ref, act_before, back_before), refs = refs[:4], refs[4:]
        act_outs, back_outs, refs = refs[:2], refs[2:7], refs[7:]
        (act, back, state_sem, out_sem), refs = refs[:4], refs[4:]
    else:
        (act, back), refs = refs[:2], refs[2:]
    (near, wide, moved, dense, lower, upper, masks, listed, load_sem) = refs[:9]
    screen_ref, ahead_ref, behind_ref, table_sem = refs[9:]

    fragment, member, live_slots = numbers_ref[0], numbers_ref[1], numbers_ref[2]

    def first_of(slot):
        return numbers_ref[3 + slot]

    def second_of(slot):
        return numbers_ref[3 + slots + slot]

    def reach_of(slot):
        return numbers_ref[3 + 2 * slots + slot]

    def anchor(place, axis):
        return numbers_ref[3 + 3 * slots + 3 * place + axis]

    table_copies = [
        pltpu.make_async_copy(table, hold, table_sem.at[i])
        for i, (table, hold) in enumerate(zip(tables, refs[9:12]))
    ]
    for copy in table_copies:
        copy.start()
    lane = lax.broadcasted_iota(jnp.int32, (1, LANES), 1)
    stretch = next(n for n in (6, 4, 3, 2, 1) if chunks % n == 0)
    middle = pl.ds(edge, edge)

    even = lax.rem(fragment, 2) == 0

    def list_slots(slot, counts):
        early, found = counts
        mine = (slot < live_slots) & (lax.div(second_of(slot), orb_dev) == member)
        reach = reach_of(slot)
        come = (reach == 0) | (reach == 2) | (even & (lax.rem(second_of(slot), orb_dev) == 0))
        taken = mine & come & (early < 2)
        chosen = mine & jnp.logical_not(taken) if second_part else taken

        @pl.when(chosen)
        def _():
            listed[found] = slot

        return early + taken.astype(jnp.int32), found + chosen.astype(jnp.int32)

    _, found = lax.fori_loop(0, slots, list_slots, (jnp.int32(0), jnp.int32(0)))
    turns = lax.div(found + 1, 2)

    def slot_of(turn, side):
        at = 2 * turn + side
        live = at < found
        return listed[jnp.where(live, at, 2 * turn)], live

    def far_copy(side, source):
        return pltpu.make_async_copy(source, wide.at[side, :, middle], load_sem.at[1, side])

    def start_loads(turn):
        for side in range(2):
            slot, _ = slot_of(turn, side)
            first, second, reach = first_of(slot), second_of(slot), reach_of(slot)
            relative = lax.div(first, orb_dev) ^ member
            for k in range(groups):
                @pl.when(relative == k)
                def _():
                    pltpu.make_async_copy(
                        phi_refs[k].at[lax.rem(first, orb_dev)],
                        near.at[lax.rem(turn, 2), side],
                        load_sem.at[0, side],
                    ).start()
            own = lax.rem(second, orb_dev)

            @pl.when(reach == 0)
            def _():
                far_copy(side, own_ref.at[own]).start()

            @pl.when((reach == 1) & (own == 0) & even)
            def _():
                far_copy(side, twin_ref.at[0]).start()

            @pl.when(reach == 2)
            def _():
                far_copy(side, two_ref.at[own]).start()

            if second_part:
                @pl.when((reach == 1) & (own == 0) & jnp.logical_not(even))
                def _():
                    far_copy(side, relay_ref.at[0]).start()

                @pl.when((reach == 1) & (own > 0))
                def _():
                    far_copy(side, one_ref.at[jnp.maximum(own - 1, 0)]).start()

    def wait_loads(turn):
        for side in range(2):
            pltpu.make_async_copy(
                phi_refs[0].at[0], near.at[lax.rem(turn, 2), side], load_sem.at[0, side]
            ).wait()
            far_copy(side, own_ref.at[0]).wait()

    @pl.when(found > 0)
    def _():
        start_loads(0)

    if second_part:
        state_copies = [
            pltpu.make_async_copy(before, now, state_sem.at[i])
            for i, (before, now) in enumerate(((act_before, act), (back_before, back)))
        ]
        for copy in state_copies:
            copy.start()
        slab = plane * edge // LANES // groups
        act_copies = []
        for k in range(groups):
            source = (member ^ k) * slab
            place = reversed_bits(k, groups)
            act_copies.append(
                pltpu.make_async_copy(
                    act.at[:, pl.ds(pl.multiple_of(source, ROWS), slab), :],
                    act_outs[2 * place // groups].at[place % (groups // 2)],
                    out_sem.at[k],
                )
            )
    else:
        act[...] = jnp.zeros_like(act)
        back[...] = jnp.zeros_like(back)
    for copy in table_copies:
        copy.wait()

    def offset_of(slot):
        partner = lax.rem(fragment + reach_of(slot), fragments)
        return [anchor(partner, i) - anchor(fragment, i) for i in range(3)]

    def steps(count, body, most):
        width = max(n for n in range(1, most + 1) if count % n == 0)

        def step(i, _):
            for j in range(width):
                body(i * width + j)
            return 0

        if width == count:
            step(0, 0)
        else:
            lax.fori_loop(0, count // width, step, 0)

    def columns(k):
        return pl.ds(pl.multiple_of(k * LANES, LANES), LANES)

    def set_masks(place, delta, weight):
        shape = masks.shape[1:]
        spot = lax.broadcasted_iota(jnp.int32, shape, 0) * LANES
        spot = spot + lax.broadcasted_iota(jnp.int32, shape, 1)
        y = ((spot.astype(jnp.float32) + 0.5) * (1.0 / edge)).astype(jnp.int32)
        z = spot - y * edge - delta[2]
        y = y - delta[1]
        inside = (y >= 0) & (y < edge) & (z >= 0) & (z < edge)
        masks[place] = jnp.where(inside, weight, 0.0)

    def shifted(source, place, delta, begin, count, ks):
        shift = lax.rem(delta[1] * edge + delta[2] + 4 * plane, plane)
        start = lax.rem(plane - shift, plane)
        whole, part = lax.div(start, LANES), lax.rem(start, LANES)
        turn = lax.rem(LANES - part, LANES)
        down = edge - jnp.clip(delta[0], -edge, edge) + begin
        x = lax.broadcasted_iota(jnp.int32, (count, LANES), 0) + (begin - delta[0])
        rows_inside = (x >= 0) & (x < edge)
        first = lane < LANES - part

        def piece(k):
            return pltpu.roll(source[lax.rem(k + whole, chunks), pl.ds(down, count), :], turn, 1)

        out = []
        low = piece(ks[0])
        for k in ks:
            high = piece(k + 1)
            value = jnp.where(first, low, high) * masks[place, pl.ds(k, 1), :]
            out.append(jnp.where(rows_inside, value, 0.0))
            low = high
        return out

    def tile(t, i, size):
        return pl.ds(pl.multiple_of(i * size + t * ROWS, ROWS), ROWS)

    def across(t, i, size):
        return pl.ds(t * (ROWS * size) + i, ROWS, stride=size)

    def solve_two(turn, _):
        wait_loads(turn)
        near_now = near.at[lax.rem(turn, 2)]
        picked = [slot_of(turn, side) for side in range(2)]
        offsets = [offset_of(slot) for slot, _ in picked]
        returns = [[-d for d in delta] for delta in offsets]
        for side in range(2):
            set_masks(side, offsets[side], picked[side][1].astype(jnp.float32))
            set_masks(2 + side, returns[side], 1.0)

        def over_y(t):
            densities = []
            begin = pl.multiple_of(t * ROWS, ROWS)
            rows = pl.ds(begin, ROWS)
            for side in range(2):
                values = shifted(wide.at[side], side, offsets[side], begin, ROWS, range(chunks))
                for k in range(chunks):
                    moved[side, k, rows, :] = values[k]
                    values[k] = values[k] * near_now[side, rows, k * LANES : (k + 1) * LANES]
                densities.append(values)
            planes = []
            for y in range(edge):
                first, offset = divmod(y * edge, LANES)
                sides = []
                for side in range(2):
                    shift = (side * HALF - offset) % LANES
                    value = densities[side][first]
                    value = pltpu.roll(value, shift, 1) if shift else value
                    if offset + edge > LANES:
                        more = densities[side][first + 1]
                        more = pltpu.roll(more, shift, 1) if shift else more
                        value = jnp.where(lane < side * HALF + LANES - offset, value, more)
                    sides.append(value)
                planes.append(Number(jnp.where(lane < HALF, sides[0], sides[1])))
            values = real_dft(planes)
            for i in range(half):
                at = tile(t, i, edge)
                lower[0, at, :] = values[i].real
                imag = values[i].imag
                lower[1, at, :] = jnp.zeros((ROWS, LANES), jnp.float32) if imag is None else imag

        steps(tiles, over_y, 2)

        @pl.when(turn + 1 < turns)
        def _():
            start_loads(turn + 1)

        def over_x(t):
            at = [across(t, i, edge) for i in range(edge)]
            values = dft([Number(lower[0, a, :], lower[1, a, :]) for a in at], -1)
            real = jnp.concatenate([value.real for value in values], axis=0)
            imag = jnp.concatenate([value.imag for value in values], axis=0)
            at = [tile(t, i, height) for i in range(edge)]
            factor = jnp.concatenate([screen_ref[a, :] for a in at], axis=0)
            real, imag = split_dot(real, imag, ahead_ref)
            real, imag = split_dot(real * factor, imag * factor, behind_ref)
            rows = [slice(i * ROWS, (i + 1) * ROWS) for i in range(edge)]
            values = dft([Number(real[r], imag[r]) for r in rows], 1)
            for i in range(edge):
                upper[0, at[i], :] = values[i].real
                upper[1, at[i], :] = values[i].imag

        steps(height // ROWS, over_x, 2)
        if second_part:
            @pl.when(turn == 0)
            def _():
                for copy in state_copies:
                    copy.wait()

        firsts = [first_of(slot) for slot, _ in picked]

        def back_y(t):
            begin = pl.multiple_of(t * ROWS, ROWS)
            rows = pl.ds(begin, ROWS)
            at = [across(t, i, height) for i in range(half)]
            values = [Number(upper[0, a, :], upper[1, a, :]) for a in at]
            values = values + [values[edge - i].conj() for i in range(half, edge)]
            planes = real_back(values)
            for side in range(2):
                forward = []
                for k in range(chunks):
                    value = None
                    for y in range(k * LANES // edge, edge):
                        begins = y * edge - k * LANES
                        if begins >= LANES:
                            break
                        shift = (begins - side * HALF) % LANES
                        piece = pltpu.roll(planes[y], shift, 1) if shift else planes[y]
                        value = piece if value is None else jnp.where(lane < begins, value, piece)
                    forward.append(value * moved[side, k, rows, :])
                    other = value * near_now[side, rows, k * LANES : (k + 1) * LANES]
                    dense[side, k, pl.ds(edge + begin, ROWS), :] = other
                at = [pl.ds(t * (ROWS * chunks) + k, ROWS, stride=chunks) for k in range(chunks)]
                sums = [act[firsts[side], at[k], :] + forward[k] for k in range(chunks)]
                for k in range(chunks):
                    act[firsts[side], at[k], :] = sums[k]

        steps(tiles, back_y, 2)

        if second_part:
            @pl.when(turn + 1 == turns)
            def _():
                for copy in act_copies:
                    copy.start()

        homes = []
        for side in range(2):
            slot = picked[side][0]
            homes.append(reach_of(slot) * orb_dev + lax.rem(second_of(slot), orb_dev))

        def send_back(g):
            for side in range(2):
                ks = [g * stretch + i for i in range(stretch)]
                values = shifted(dense.at[side], 2 + side, returns[side], 0, edge, ks)
                at = [
                    (i, t, pl.ds(t * (ROWS * chunks) + ks[i], ROWS, stride=chunks))
                    for i in range(stretch)
                    for t in range(tiles)
                ]
                sums = [
                    back[homes[side], a, :] + values[i][t * ROWS : (t + 1) * ROWS] for i, t, a in at
                ]
                for (i, t, a), value in zip(at, sums):
                    back[homes[side], a, :] = value

        steps(chunks // stretch, send_back, 3)
        return 0

    if not second_part:
        lax.fori_loop(0, turns, solve_two, 0)
        return

    @pl.when(found == 0)
    def _():
        for copy in state_copies:
            copy.wait()
        for copy in act_copies:
            copy.start()

    lax.fori_loop(0, turns, solve_two, 0)
    spans = ((0, orb_dev),)
    for begin in (orb_dev, 2 * orb_dev):
        spans += ((begin, 1), (begin + 1, orb_dev - 1))
    back_copies = [
        pltpu.make_async_copy(back.at[pl.ds(begin, count)], back_outs[i], out_sem.at[groups + i])
        for i, (begin, count) in enumerate(spans)
    ]
    for copy in back_copies:
        copy.start()
    for copy in act_copies + back_copies:
        copy.wait()


def reversed_bits(k, count):
    bits = count.bit_length() - 1
    return sum(((k >> i) & 1) << (bits - 1 - i) for i in range(bits))


def pair_terms(numbers, fragments, slots, tables, pieces, own, far, before=()):
    second_part = bool(before)
    orb_dev, edge, plane = pieces[0].shape
    groups = len(pieces)
    frag_size = groups * orb_dev
    chunks = plane // LANES
    rows = edge * chunks
    height = padded_half(edge)
    returns_count = (REACH + 1) * orb_dev
    shape = (edge, orb_dev, groups, fragments, slots)
    smem = pl.BlockSpec(memory_space=pltpu.SMEM)
    vmem = pl.BlockSpec(memory_space=pltpu.VMEM)
    hbm = pl.BlockSpec(memory_space=pltpu.HBM)
    f32 = jnp.float32
    sums = ((frag_size, rows, LANES), (returns_count, rows, LANES))
    out_shape = [jax.ShapeDtypeStruct(sum_shape, f32) for sum_shape in sums]
    out_specs, scratch = [vmem] * 2, []
    if second_part:
        out_shape = [jax.ShapeDtypeStruct((groups // 2, frag_size, rows // groups, LANES), f32)] * 2
        for count in (orb_dev, 1, orb_dev - 1, 1, orb_dev - 1):
            out_shape.append(jax.ShapeDtypeStruct((count, rows, LANES), f32))
        out_specs = [hbm] * 7
        scratch = [pltpu.VMEM(sum_shape, f32) for sum_shape in sums]
        scratch += [pltpu.SemaphoreType.DMA((2,)), pltpu.SemaphoreType.DMA((groups + 5,))]
    return pl.pallas_call(
        functools.partial(pair_kernel, shape, second_part),
        out_shape=out_shape,
        in_specs=[smem] + [hbm] * (4 + groups + len(far) + len(before)),
        out_specs=out_specs,
        scratch_shapes=scratch
        + [
            pltpu.VMEM((2, 2, edge, plane), f32),
            pltpu.VMEM((2, chunks, 3 * edge, LANES), f32),
            pltpu.VMEM((2, chunks, edge, LANES), f32),
            pltpu.VMEM((2, chunks, 3 * edge, LANES), f32),
            pltpu.VMEM((2, height * edge, LANES), f32),
            pltpu.VMEM((2, height * edge, LANES), f32),
            pltpu.VMEM((4, -(-chunks // ROWS) * ROWS, LANES), f32),
            pltpu.SMEM((slots,), jnp.int32),
            pltpu.SemaphoreType.DMA((2, 2)),
            *[pltpu.VMEM(table.shape, table.dtype) for table in tables],
            pltpu.SemaphoreType.DMA((3,)),
        ],
        compiler_params=pltpu.CompilerParams(vmem_limit_bytes=30 << 20),
        name="late_pair_terms" if second_part else "early_pair_terms",
    )(numbers, *tables, *pieces, own, *far, *before)


def flatten_kernel(shape, places_ref, *refs):
    edge, orb_dev, groups = shape
    pieces, (flat_ref, slab_ref) = refs[:groups], refs[groups:]
    member = places_ref[1]
    chunks = edge * edge // LANES
    slab = slab_ref.shape[1]
    for k in range(groups):
        for o in range(orb_dev):
            def move(j, _):
                value = pieces[k][o, :, pl.ds(pl.multiple_of(j * LANES, LANES), LANES)]
                for t in range(edge // ROWS):
                    at = pl.ds(t * (ROWS * chunks) + j, ROWS, stride=chunks)
                    flat_ref[k * orb_dev + o, at, :] = value[t * ROWS : (t + 1) * ROWS]
                return 0

            lax.fori_loop(0, chunks, move, 0)
    slab_ref[...] = flat_ref[:, pl.ds(pl.multiple_of(member * slab, ROWS), slab), :]


def flatten_terms(places, pieces):
    orb_dev, edge, plane = pieces[0].shape
    groups = len(pieces)
    rows = edge * plane // LANES
    frag_size = groups * orb_dev
    smem = pl.BlockSpec(memory_space=pltpu.SMEM)
    vmem = pl.BlockSpec(memory_space=pltpu.VMEM)
    return pl.pallas_call(
        functools.partial(flatten_kernel, (edge, orb_dev, groups)),
        out_shape=(
            jax.ShapeDtypeStruct((frag_size, rows, LANES), jnp.float32),
            jax.ShapeDtypeStruct((frag_size, rows // groups, LANES), jnp.float32),
        ),
        in_specs=[smem] + [vmem] * groups,
        out_specs=(vmem, vmem),
        compiler_params=pltpu.CompilerParams(vmem_limit_bytes=24 << 20),
        name="flatten_terms",
    )(places, *pieces)


def products(lefts, rights, length, step):
    def add(i, sums):
        at = pl.ds(pl.multiple_of(i * step, ROWS), step)
        right = [ref[index, at, :].reshape(step // ROWS, ROWS, LANES) for ref, index in rights]
        out = []
        for n, (ref, index) in enumerate(lefts):
            left = ref[index, at, :].reshape(step // ROWS, ROWS, LANES)
            for m in range(len(rights)):
                out.append(sums[n * len(rights) + m] + jnp.sum(left * right[m], axis=0))
        return tuple(out)

    zero = jnp.zeros((ROWS, LANES), jnp.float32)
    return lax.fori_loop(0, length // step, add, (zero,) * (len(lefts) * len(rights)))


def placed(result, sums, rows, lanes):
    row = lax.broadcasted_iota(jnp.int32, result.shape, 0)
    lane = lax.broadcasted_iota(jnp.int32, result.shape, 1)
    for n, a in enumerate(rows):
        for m, b in enumerate(lanes):
            value = jnp.sum(sums[n * len(lanes) + m], keepdims=True)
            result = jnp.where((row == a) & (lane == b), result + value, result)
    return result


def step_of(length):
    return next(n for n in (72, 24, 8) if length % n == 0)


def action_kernel(shape, places_ref, phi_ref, kept_ref, *refs):
    orb_dev, groups, parts = shape
    arrived, (act_ref, share_ref) = refs[:parts], refs[parts:]
    member = places_ref[1]
    frag_size = orb_dev * groups
    slab = act_ref.shape[1]
    cut = frag_size // parts
    for i in range(parts):
        span = slice(i * cut, (i + 1) * cut)
        act_ref[span] = kept_ref[0, span] + arrived[i][0]
    rows = [(member ^ (a // orb_dev)) * orb_dev + a % orb_dev for a in range(frag_size)]
    result = jnp.zeros(share_ref.shape, jnp.float32)
    for half in range(0, frag_size, 4):
        bs = range(half, min(half + 4, frag_size))
        lefts, rights = [(phi_ref, a) for a in range(frag_size)], [(act_ref, b) for b in bs]
        result = placed(result, products(lefts, rights, slab, step_of(slab)), rows, bs)
    share_ref[...] = result


def action_terms(places, orb_dev, phi, kept, arrived):
    frag_size, slab = phi.shape[:2]
    smem = pl.BlockSpec(memory_space=pltpu.SMEM)
    vmem = pl.BlockSpec(memory_space=pltpu.VMEM)
    return pl.pallas_call(
        functools.partial(action_kernel, (orb_dev, frag_size // orb_dev, len(arrived))),
        out_shape=(
            jax.ShapeDtypeStruct((frag_size, slab, LANES), jnp.float32),
            jax.ShapeDtypeStruct((frag_size, LANES), jnp.float32),
        ),
        in_specs=[smem] + [vmem] * (2 + len(arrived)),
        out_specs=(vmem, vmem),
        compiler_params=pltpu.CompilerParams(vmem_limit_bytes=16 << 20),
        name="action_terms",
    )(places, phi, kept, *arrived)


def home_kernel(shape, places_ref, flat_ref, own_ref, *refs):
    edge, orb_dev, groups, first, count = shape
    if first == 0:
        (two_ref, twin_ref, relay_ref, share_ref), refs = refs[:4], refs[4:]
    else:
        (two_ref, one_ref), refs = refs[:2], refs[2:]
    outs, total = refs[:groups], refs[groups]
    fragment, member = places_ref[0], places_ref[1]
    frag_size = orb_dev * groups
    rows = flat_ref.shape[1]
    slab = rows // groups
    for i in range(count):
        value = own_ref[first + i] + two_ref[i]
        if first == 0:
            @pl.when(lax.rem(fragment, 2) == 1)
            def _():
                total[i] = value + twin_ref[i]

            @pl.when(lax.rem(fragment, 2) == 0)
            def _():
                total[i] = value + relay_ref[i]
        else:
            total[i] = value + one_ref[i]
    lefts, rights = [(flat_ref, a) for a in range(frag_size)], [(total, i) for i in range(count)]
    places = [(member ^ (a // orb_dev)) * orb_dev + a % orb_dev for a in range(frag_size)]
    result = share_ref[...] if first == 0 else jnp.zeros((frag_size, LANES), jnp.float32)
    sums = products(lefts, rights, rows, step_of(rows))
    result = placed(result, sums, places, [member * orb_dev + first + i for i in range(count)])
    result = result * (1.0 / float(edge**3))
    for k in range(groups):
        begin = pl.multiple_of((member ^ k) * slab, ROWS)
        for i in range(count):
            outs[k][i * slab : (i + 1) * slab, :] = total[i, pl.ds(begin, slab), :]
        outs[k][count * slab :, :] = result


def home_terms(places, edge, groups, flat, own, first, *came):
    frag_size, rows = flat.shape[:2]
    count = came[0].shape[0]
    smem = pl.BlockSpec(memory_space=pltpu.SMEM)
    vmem = pl.BlockSpec(memory_space=pltpu.VMEM)
    f32 = jnp.float32
    parcel = jax.ShapeDtypeStruct((count * rows // groups + frag_size, LANES), f32)
    return pl.pallas_call(
        functools.partial(home_kernel, (edge, frag_size // groups, groups, first, count)),
        out_shape=[parcel] * groups,
        in_specs=[smem] + [vmem] * (2 + len(came)),
        out_specs=[vmem] * groups,
        scratch_shapes=[pltpu.VMEM((count, rows, LANES), f32)],
        compiler_params=pltpu.CompilerParams(vmem_limit_bytes=16 << 20),
        name="home_terms",
    )(places, flat, own, *came)


def exchanged(value, axis, width):
    size = value.shape[axis]
    index = lax.broadcasted_iota(jnp.int32, value.shape, axis)
    below, above = pltpu.roll(value, width, axis), pltpu.roll(value, size - width, axis)
    return jnp.where((index & width) != 0, below, above)


def gradient_kernel(shape, places_ref, act_ref, phi_ref, *refs):
    edge, orb_dev, groups = shape
    heads, tails, refs = refs[:groups], refs[groups : 2 * groups], refs[2 * groups :]
    out_ref, lagrange_ref, hold = refs
    member = places_ref[1]
    frag_size = orb_dev * groups
    chunks = edge * edge // LANES
    slab_rows = edge // groups
    slab = slab_rows * chunks
    sums = [
        head[slab:, :] + tail[(orb_dev - 1) * slab :, :] for head, tail in zip(heads, tails)
    ]
    while len(sums) > 1:
        sums = [sums[i] + sums[i + 1] for i in range(0, len(sums), 2)]
    square = jnp.concatenate([sums[0], jnp.zeros((LANES - frag_size, LANES), jnp.float32)], axis=0)
    lagrange = 0.5 * (square + square.T)[:frag_size, :]
    lagrange_ref[...] = lagrange[:, :frag_size]
    bit = 1
    while bit < groups:
        turned = exchanged(exchanged(lagrange, 0, bit * orb_dev), 1, bit * orb_dev)
        lagrange = jnp.where((member & bit) != 0, turned, lagrange)
        bit *= 2

    for k in range(groups):
        for o in range(orb_dev):
            a = (member ^ k) * orb_dev + o
            came = heads[k][:slab, :] if o == 0 else tails[k][(o - 1) * slab : o * slab, :]
            value = act_ref[a] + came
            for b in range(frag_size):
                factor = lagrange[b : b + 1, k * orb_dev + o : k * orb_dev + o + 1]
                value = value - factor * phi_ref[b]
            hold[pl.ds(pl.multiple_of(a * slab, ROWS), slab), :] = value
    for x in range(slab_rows):
        for j in range(chunks):
            value = hold[pl.ds(x * chunks + j, frag_size, stride=slab), :]
            out_ref[x, :, j * LANES : (j + 1) * LANES] = value


def gradient_terms(places, edge, act, phi, heads, tails):
    groups = len(heads)
    frag_size, slab = act.shape[:2]
    smem = pl.BlockSpec(memory_space=pltpu.SMEM)
    vmem = pl.BlockSpec(memory_space=pltpu.VMEM)
    f32 = jnp.float32
    gradient, lagrange = pl.pallas_call(
        functools.partial(gradient_kernel, (edge, frag_size // groups, groups)),
        out_shape=(
            jax.ShapeDtypeStruct((edge // groups, frag_size, edge * edge), f32),
            jax.ShapeDtypeStruct((frag_size, frag_size), f32),
        ),
        in_specs=[smem] + [vmem] * (2 + 2 * groups),
        out_specs=(vmem, vmem),
        scratch_shapes=[pltpu.VMEM((frag_size * slab, LANES), f32)],
        compiler_params=pltpu.CompilerParams(vmem_limit_bytes=16 << 20),
        name="gradient_terms",
    )(places, act, phi, *heads, *tails)
    return gradient.transpose(1, 0, 2), lagrange


def together(*arrays):
    return lax.optimization_barrier(arrays)


def to_fragment(block, distance, senders=None):
    devices = lax.axis_size("orb")
    senders = range(devices) if senders is None else range(senders, devices, 2)
    return lax.ppermute(block, "orb", [(i, (i + distance) % devices) for i in senders])


def with_twin(block):
    return lax.ppermute(block, "orb", [(i, i ^ 1) for i in range(lax.axis_size("orb"))])


def with_member(block, bit):
    return lax.ppermute(block, "grp", [(i, i ^ bit) for i in range(lax.axis_size("grp"))])


def by_member(parcels, after=None):
    groups = len(parcels)
    received = list(parcels)
    bit = groups // 2
    while bit:
        for k in reversed(range(groups)):
            if k & bit:
                received[k] = with_member(received[k], bit)
        if after is not None and bit == groups // 2:
            after, *received[bit:] = together(after, *received[bit:])
        bit //= 2
    return received, after


def shards(orbitals, kernel, anchors, pair_count, pair_first, pair_second, pair_reach):
    groups = lax.axis_size("grp")
    orb_dev, edge, plane = orbitals.shape
    frag_size = groups * orb_dev
    places = jnp.stack([lax.axis_index("orb"), lax.axis_index("grp")]).astype(jnp.int32)

    own = orbitals.reshape(orb_dev, edge, plane // LANES, LANES).transpose(0, 2, 1, 3)
    numbers = [places, pair_count, pair_first, pair_second, pair_reach, anchors.reshape(-1)]
    screen, numbers, *tables = screen_terms(jnp.concatenate(numbers), kernel)
    two = to_fragment(own, -2)
    twin = with_twin(own[:1])
    pieces = {0: orbitals}
    bit = groups // 2
    while bit:
        for k in list(pieces):
            pieces[k ^ bit] = with_member(pieces[k], bit)
        if bit == groups // 2:
            two, twin, tail, pieces[bit], screen, numbers, *tables = together(
                two, twin, own[1:], pieces[bit], screen, numbers, *tables
            )
            one = to_fragment(tail, -1)
            relay = to_fragment(twin, -2, 1)
        bit //= 2
    pieces = [pieces[k] for k in range(groups)]
    tables = [screen, *tables]
    sizes = (anchors.shape[0], pair_first.shape[0])
    before = pair_terms(numbers, *sizes, tables, pieces, own, [twin, two])
    kept, sent, own, one_head, one_tail, two_head, two_tail = pair_terms(
        numbers, *sizes, tables, pieces, own, [twin, two, relay, one], before
    )

    two_tail = to_fragment(two_tail, 2)
    one_tail = to_fragment(one_tail, 1)
    bit = 1
    arrived = [with_member(sent, bit)]
    while 2 * bit < groups:
        kept = kept + jnp.concatenate(arrived, axis=1)
        if bit == 1:
            kept, one_head = together(kept, one_head)
        half = kept.shape[0] // 2
        cut = frag_size // orb_dev
        bit *= 2
        arrived = [
            with_member(kept[half:, i : i + cut], bit) for i in range(0, frag_size, cut)
        ]
        kept = kept[:half]
    twin = with_twin(one_head)
    two_tail, two_head, twin = together(two_tail, two_head, twin)
    relay = to_fragment(twin, 2, 0)
    two_head = to_fragment(two_head, 2)

    flat, phi = flatten_terms(places, pieces)
    tails = home_terms(places, edge, groups, flat, own, 1, two_tail, one_tail)
    tails, two_head = by_member(tails, two_head)
    act, share = action_terms(places, orb_dev, phi, kept, arrived)
    heads, _ = by_member(
        home_terms(places, edge, groups, flat, own, 0, two_head, twin, relay, share)
    )
    gradient, lagrange = gradient_terms(places, edge, act, phi, heads, tails)
    return (gradient, lagrange[None])


def solution(mesh):
    placed = (P(("orb", "grp"), None, None), P(), P(), P("orb"), P("orb"), P("orb"), P("orb"))
    return jax.shard_map(
        shards,
        mesh=mesh,
        in_specs=placed,
        out_specs=(P("orb", "grp", None), P("orb", None, None)),
        check_vma=False,
    )
```

```python
import functools
import math

import jax
import jax.numpy as jnp
import numpy as np
from jax import lax
from jax.experimental import pallas as pl
from jax.experimental.pallas import tpu as pltpu
from jax.sharding import PartitionSpec as P

REACH = 2
LANES = 128
ROWS = 8
HALF = LANES // 2


class Number:
    def __init__(self, real, imag=None):
        self.real, self.imag = real, imag

    def __add__(self, other):
        if self.imag is None or other.imag is None:
            imag = self.imag if other.imag is None else other.imag
        else:
            imag = self.imag + other.imag
        return Number(self.real + other.real, imag)

    def __sub__(self, other):
        if other.imag is None:
            imag = self.imag
        else:
            imag = -other.imag if self.imag is None else self.imag - other.imag
        return Number(self.real - other.real, imag)

    def conj(self):
        return self if self.imag is None else Number(self.real, -self.imag)

    def scaled(self, factor):
        return Number(self.real * factor, None if self.imag is None else self.imag * factor)

    def turned(self, sign):
        if self.imag is None:
            return Number(jnp.zeros_like(self.real), self.real if sign > 0 else -self.real)
        return Number(-self.imag, self.real) if sign > 0 else Number(self.imag, -self.real)

    def plus_turned(self, other, sign):
        if sign < 0:
            return self.minus_turned(other)
        real = self.real if other.imag is None else self.real - other.imag
        return Number(real, other.real if self.imag is None else self.imag + other.real)

    def minus_turned(self, other):
        real = self.real if other.imag is None else self.real + other.imag
        return Number(real, -other.real if self.imag is None else self.imag - other.real)

    def times(self, angle):
        real, imag = math.cos(angle), math.sin(angle)
        if abs(imag) < 1e-12:
            return self if real > 0 else self.scaled(-1.0)
        if abs(real) < 1e-12:
            return self.turned(imag)
        if self.imag is None:
            return Number(self.real * real, self.real * imag)
        return Number(self.real * real - self.imag * imag, self.real * imag + self.imag * real)


def coprime(n):
    for p in (2, 3, 5, 7):
        power = 1
        while n % (power * p) == 0:
            power *= p
        if 1 < power < n:
            return power, n // power
    return None


def radix(n):
    return next((p for p in (4, 2, 3, 5, 7) if n % p == 0 and n > p), None)


def meeting(i, j, first, second):
    return next(k for k in range(first * second) if k % first == i and k % second == j)


def dft(values, sign):
    n = len(values)
    if n == 1:
        return values
    if n == 2:
        return [values[0] + values[1], values[0] - values[1]]
    if n == 3:
        a, b, c = values
        total, side = b + c, (b - c).scaled(math.sqrt(0.75))
        middle = a - total.scaled(0.5)
        return [a + total, middle.plus_turned(side, sign), middle.plus_turned(side, -sign)]
    if n == 4:
        a, b, c, d = values
        s, t, u, v = a + c, a - c, b + d, b - d
        return [s + u, t.plus_turned(v, sign), s - u, t.plus_turned(v, -sign)]
    out = [None] * n
    if coprime(n):
        first, second = coprime(n)
        columns = [
            dft([values[(i * second + j * first) % n] for i in range(first)], sign)
            for j in range(second)
        ]
        for i in range(first):
            row = dft([column[i] for column in columns], sign)
            for j in range(second):
                out[meeting(i, j, first, second)] = row[j]
        return out
    p = radix(n)
    if p:
        rest = n // p
        columns = [dft(values[j::p], sign) for j in range(p)]
        for i in range(rest):
            row = dft(
                [columns[j][i].times(sign * 2.0 * math.pi * i * j / n) for j in range(p)], sign
            )
            for j in range(p):
                out[i + rest * j] = row[j]
        return out
    for k in range(n):
        total = values[0]
        for j in range(1, n):
            total = total + values[j].times(sign * 2.0 * math.pi * (j * k % n) / n)
        out[k] = total
    return out


def real_dft(values):
    n = len(values)
    if n <= 4:
        out = dft(values, -1)
    else:
        out = [None] * n
        if coprime(n):
            first, second = coprime(n)
            columns = [
                real_dft([values[(i * second + j * first) % n] for i in range(first)])
                for j in range(second)
            ]
            for i in range(first // 2 + 1):
                entries = [column[i] for column in columns]
                alone = 2 * i % first == 0
                row = real_dft(entries) if alone else dft(entries, -1)
                for j in range(second):
                    out[meeting(i, j, first, second)] = row[j]
        elif radix(n):
            p = radix(n)
            rest = n // p
            columns = [real_dft(values[j::p]) for j in range(p)]
            for i in range(rest // 2 + 1):
                row = dft(
                    [columns[j][i].times(-2.0 * math.pi * i * j / n) for j in range(p)], -1
                )
                for j in range(p):
                    out[i + rest * j] = row[j]
        else:
            out = dft(values, -1)
    for k in range(1, n):
        if out[k] is None or (k > n // 2 and out[n - k] is not None):
            out[k] = out[n - k].conj()
    out[0] = Number(out[0].real)
    if n % 2 == 0:
        out[n // 2] = Number(out[n // 2].real)
    return out


def real_back(values):
    n = len(values)
    if n == 1:
        return [values[0].real]
    if n == 2:
        return [values[0].real + values[1].real, values[0].real - values[1].real]
    if n == 3:
        a, b = values[0].real, values[1]
        side = b.imag * math.sqrt(3.0)
        middle = a - b.real
        return [a + 2.0 * b.real, middle - side, middle + side]
    if n == 4:
        s, t = values[0].real + values[2].real, values[0].real - values[2].real
        u, v = 2.0 * values[1].real, 2.0 * values[1].imag
        return [s + u, t - v, s - u, t + v]
    out = [None] * n
    if coprime(n):
        first, second = coprime(n)
        rows = []
        for i in range(first // 2 + 1):
            entries = [values[meeting(i, j, first, second)] for j in range(second)]
            if 2 * i % first == 0:
                rows.append([Number(value) for value in real_back(entries)])
            else:
                rows.append(dft(entries, 1))
        for b in range(second):
            half = [row[b] for row in rows]
            whole = half + [half[first - i].conj() for i in range(len(half), first)]
            for a, value in enumerate(real_back(whole)):
                out[(a * second + b * first) % n] = value
        return out
    p = radix(n)
    if p:
        rest = n // p
        parts = []
        for i in range(p // 2 + 1):
            entries = values[i::p]
            if i == 0:
                parts.append([Number(value) for value in real_back(entries)])
            else:
                inner = dft(entries, 1)
                parts.append([inner[m].times(2.0 * math.pi * i * m / n) for m in range(rest)])
                if 2 * i == p:
                    parts[-1] = [Number(value.real) for value in parts[-1]]
        for m in range(rest):
            half = [part[m] for part in parts]
            whole = half + [half[p - i].conj() for i in range(len(half), p)]
            for j, value in enumerate(real_back(whole)):
                out[m + rest * j] = value
        return out
    return [value.real for value in dft(values, 1)]


def wave_table(edge):
    index = np.arange(edge)
    angles = 2.0 * np.pi / edge * (np.outer(index, index) % edge)
    full = np.zeros((2, 2, HALF, 2, HALF))
    for side in range(2):
        full[0, side, :edge, side, :edge] = np.cos(angles)
        full[1, side, :edge, side, :edge] = np.sin(angles)
    full = full.reshape(2, LANES, LANES)
    high = full.astype(jnp.bfloat16)
    low = (full - high.astype(np.float64)).astype(jnp.bfloat16)
    return np.stack([high, low])


def split_dot(real, imag, matrix):
    value = jnp.concatenate([real, imag], axis=1)
    high = value.astype(jnp.bfloat16)
    low = (value - high.astype(jnp.float32)).astype(jnp.bfloat16)
    product = jnp.dot(
        jnp.concatenate([high, low, high], axis=1), matrix[...], preferred_element_type=jnp.float32
    )
    return product[:, :LANES], product[:, LANES:]


def padded_half(edge):
    return -(-(edge // 2 + 1) // ROWS) * ROWS


def screen_kernel(edge, numbers_ref, kernel_ref, waves_ref, out_ref, kept_ref, ahead_ref, behind_ref, flipped):
    for i in range(numbers_ref.shape[0]):
        kept_ref[i] = numbers_ref[i]
    for table, sign in ((ahead_ref, -1), (behind_ref, 1)):
        for part, source in enumerate((0, 0, 1)):
            for i in range(2):
                for j in range(2):
                    value = waves_ref[source, (i + j) % 2]
                    if i != j and (i > j) == (sign > 0):
                        value = -value
                    rows = slice((2 * part + i) * LANES, (2 * part + i + 1) * LANES)
                    table[rows, j * LANES : (j + 1) * LANES] = value
    exact = dict(precision=lax.Precision.HIGHEST, preferred_element_type=jnp.float32)

    def index(shape, axis):
        return lax.broadcasted_iota(jnp.int32, shape, axis)

    square, whole = (edge, edge), (LANES, LANES)
    flip = index(square, 0) + index(square, 1)
    flip = ((flip == 0) | (flip == edge)).astype(jnp.float32)
    source, target = index(whole, 0), index(whole, 1)
    target = jnp.where(target < HALF, target, target - HALF)
    mirror = ((source + target == 0) | (source + target == edge)) & (source < edge) & (target < edge)
    mirror = mirror.astype(jnp.float32)
    flipped[...] = jnp.dot(flip, kernel_ref[...], **exact)
    height = padded_half(edge)
    lane = index((edge, LANES), 1)
    out_ref[...] = jnp.zeros_like(out_ref)

    def piece(ref, y):
        begin, offset = divmod(y * edge, LANES)
        value = ref[:, begin * LANES : (begin + 1) * LANES]
        value = pltpu.roll(value, LANES - offset, 1) if offset else value
        if offset + edge > LANES:
            more = ref[:, (begin + 1) * LANES : (begin + 2) * LANES]
            value = jnp.where(lane < LANES - offset, value, pltpu.roll(more, LANES - offset, 1))
        return value

    for y in range(edge // 2 + 1):
        value = piece(kernel_ref, y)
        value = jnp.where(lane < HALF, value, pltpu.roll(value, HALF, 1))
        value = value + jnp.dot(piece(flipped, (edge - y) % edge), mirror, **exact)
        value = value * (0.5 / float(edge**3))
        for t in range(edge // ROWS):
            at = pl.ds(t * ROWS * height + y, ROWS, stride=height)
            out_ref[at, :] = value[t * ROWS : (t + 1) * ROWS]


def screen_terms(numbers, kernel):
    edge, plane = kernel.shape
    smem = pl.BlockSpec(memory_space=pltpu.SMEM)
    vmem = pl.BlockSpec(memory_space=pltpu.VMEM)
    table = jax.ShapeDtypeStruct((6 * LANES, 2 * LANES), jnp.bfloat16)
    return pl.pallas_call(
        functools.partial(screen_kernel, edge),
        out_shape=[
            jax.ShapeDtypeStruct((edge * padded_half(edge), LANES), jnp.float32),
            jax.ShapeDtypeStruct(numbers.shape, numbers.dtype),
            table,
            table,
        ],
        in_specs=[smem, vmem, vmem],
        out_specs=[vmem, smem, vmem, vmem],
        scratch_shapes=[pltpu.VMEM((edge, plane), jnp.float32)],
        compiler_params=pltpu.CompilerParams(vmem_limit_bytes=8 << 20),
        name="screen_terms",
    )(numbers, kernel, jnp.asarray(wave_table(edge)))


def pair_kernel(shape, second_part, numbers_ref, *refs):
    edge, orb_dev, groups, fragments, slots = shape
    plane = edge * edge
    chunks = plane // LANES
    tiles = edge // ROWS
    half = edge // 2 + 1
    height = padded_half(edge)
    returns_count = (REACH + 1) * orb_dev
    tables, refs = refs[:3], refs[3:]
    phi_refs, own_ref, refs = refs[:groups], refs[groups], refs[groups + 1 :]
    (twin_ref, two_ref), refs = refs[:2], refs[2:]
    if second_part:
        (relay_ref, one_ref, act_before, back_before), refs = refs[:4], refs[4:]
        act_outs, back_outs, refs = refs[:2], refs[2:7], refs[7:]
        (act, back, state_sem, out_sem), refs = refs[:4], refs[4:]
    else:
        (act, back), refs = refs[:2], refs[2:]
    (near, wide, moved, dense, lower, upper, masks, listed, load_sem) = refs[:9]
    screen_ref, ahead_ref, behind_ref, table_sem = refs[9:]

    fragment, member, live_slots = numbers_ref[0], numbers_ref[1], numbers_ref[2]

    def first_of(slot):
        return numbers_ref[3 + slot]

    def second_of(slot):
        return numbers_ref[3 + slots + slot]

    def reach_of(slot):
        return numbers_ref[3 + 2 * slots + slot]

    def anchor(place, axis):
        return numbers_ref[3 + 3 * slots + 3 * place + axis]

    table_copies = [
        pltpu.make_async_copy(table, hold, table_sem.at[i])
        for i, (table, hold) in enumerate(zip(tables, refs[9:12]))
    ]
    lane = lax.broadcasted_iota(jnp.int32, (1, LANES), 1)
    stretch = next(n for n in (6, 4, 3, 2, 1) if chunks % n == 0)
    middle = pl.ds(edge, edge)

    even = lax.rem(fragment, 2) == 0

    def list_slots(slot, counts):
        early, found = counts
        mine = (slot < live_slots) & (lax.div(second_of(slot), orb_dev) == member)
        reach = reach_of(slot)
        come = (reach == 0) | (reach == 2) | (even & (lax.rem(second_of(slot), orb_dev) == 0))
        taken = mine & come & (early < 2)
        chosen = mine & jnp.logical_not(taken) if second_part else taken

        @pl.when(chosen)
        def _():
            listed[found] = slot

        return early + taken.astype(jnp.int32), found + chosen.astype(jnp.int32)

    _, found = lax.fori_loop(0, slots, list_slots, (jnp.int32(0), jnp.int32(0)))
    turns = lax.div(found + 1, 2)

    def slot_of(turn, side):
        at = 2 * turn + side
        live = at < found
        return listed[jnp.where(live, at, 2 * turn)], live

    def far_copy(side, source):
        return pltpu.make_async_copy(source, wide.at[side, :, middle], load_sem.at[1, side])

    def start_loads(turn):
        for side in range(2):
            slot, _ = slot_of(turn, side)
            first, second, reach = first_of(slot), second_of(slot), reach_of(slot)
            relative = lax.div(first, orb_dev) ^ member
            for k in range(groups):
                @pl.when(relative == k)
                def _():
                    pltpu.make_async_copy(
                        phi_refs[k].at[lax.rem(first, orb_dev)],
                        near.at[lax.rem(turn, 2), side],
                        load_sem.at[0, side],
                    ).start()
            own = lax.rem(second, orb_dev)

            @pl.when(reach == 0)
            def _():
                far_copy(side, own_ref.at[own]).start()

            @pl.when((reach == 1) & (own == 0) & even)
            def _():
                far_copy(side, twin_ref.at[0]).start()

            @pl.when(reach == 2)
            def _():
                far_copy(side, two_ref.at[own]).start()

            if second_part:
                @pl.when((reach == 1) & (own == 0) & jnp.logical_not(even))
                def _():
                    far_copy(side, relay_ref.at[0]).start()

                @pl.when((reach == 1) & (own > 0))
                def _():
                    far_copy(side, one_ref.at[jnp.maximum(own - 1, 0)]).start()

    def wait_loads(turn):
        for side in range(2):
            pltpu.make_async_copy(
                phi_refs[0].at[0], near.at[lax.rem(turn, 2), side], load_sem.at[0, side]
            ).wait()
            far_copy(side, own_ref.at[0]).wait()

    @pl.when(found > 0)
    def _():
        start_loads(0)
        for copy in table_copies:
            copy.start()

    if second_part:
        state_copies = [
            pltpu.make_async_copy(before, now, state_sem.at[i])
            for i, (before, now) in enumerate(((act_before, act), (back_before, back)))
        ]
        slab = plane * edge // LANES // groups
        act_copies = []
        for k in range(groups):
            source = (member ^ k) * slab
            place = reversed_bits(k, groups)
            act_copies.append(
                pltpu.make_async_copy(
                    act.at[:, pl.ds(pl.multiple_of(source, ROWS), slab), :],
                    act_outs[2 * place // groups].at[place % (groups // 2)],
                    out_sem.at[k],
                )
            )
    else:
        act[...] = jnp.zeros_like(act)
        back[...] = jnp.zeros_like(back)

    def offset_of(slot):
        partner = lax.rem(fragment + reach_of(slot), fragments)
        return [anchor(partner, i) - anchor(fragment, i) for i in range(3)]

    def steps(count, body, most):
        width = max(n for n in range(1, most + 1) if count % n == 0)

        def step(i, _):
            for j in range(width):
                body(i * width + j)
            return 0

        if width == count:
            step(0, 0)
        else:
            lax.fori_loop(0, count // width, step, 0)

    def columns(k):
        return pl.ds(pl.multiple_of(k * LANES, LANES), LANES)

    def set_masks(place, delta, weight):
        shape = masks.shape[1:]
        spot = lax.broadcasted_iota(jnp.int32, shape, 0) * LANES
        spot = spot + lax.broadcasted_iota(jnp.int32, shape, 1)
        y = ((spot.astype(jnp.float32) + 0.5) * (1.0 / edge)).astype(jnp.int32)
        z = spot - y * edge - delta[2]
        y = y - delta[1]
        inside = (y >= 0) & (y < edge) & (z >= 0) & (z < edge)
        masks[place] = jnp.where(inside, weight, 0.0)

    def shifted(source, place, delta, begin, count, ks):
        shift = lax.rem(delta[1] * edge + delta[2] + 4 * plane, plane)
        start = lax.rem(plane - shift, plane)
        whole, part = lax.div(start, LANES), lax.rem(start, LANES)
        turn = lax.rem(LANES - part, LANES)
        down = edge - jnp.clip(delta[0], -edge, edge) + begin
        x = lax.broadcasted_iota(jnp.int32, (count, LANES), 0) + (begin - delta[0])
        rows_inside = (x >= 0) & (x < edge)
        first = lane < LANES - part

        def piece(k):
            return pltpu.roll(source[lax.rem(k + whole, chunks), pl.ds(down, count), :], turn, 1)

        out = []
        low = piece(ks[0])
        for k in ks:
            high = piece(k + 1)
            value = jnp.where(first, low, high) * masks[place, pl.ds(k, 1), :]
            out.append(jnp.where(rows_inside, value, 0.0))
            low = high
        return out

    def tile(t, i, size):
        return pl.ds(pl.multiple_of(i * size + t * ROWS, ROWS), ROWS)

    def across(t, i, size):
        return pl.ds(t * (ROWS * size) + i, ROWS, stride=size)

    def solve_two(turn, _):
        wait_loads(turn)
        if second_part:
            @pl.when(turn == 0)
            def _():
                for copy in state_copies:
                    copy.start()

        near_now = near.at[lax.rem(turn, 2)]
        picked = [slot_of(turn, side) for side in range(2)]
        offsets = [offset_of(slot) for slot, _ in picked]
        returns = [[-d for d in delta] for delta in offsets]
        for side in range(2):
            set_masks(side, offsets[side], picked[side][1].astype(jnp.float32))
            set_masks(2 + side, returns[side], 1.0)

        def over_y(t):
            densities = []
            begin = pl.multiple_of(t * ROWS, ROWS)
            rows = pl.ds(begin, ROWS)
            for side in range(2):
                values = shifted(wide.at[side], side, offsets[side], begin, ROWS, range(chunks))
                for k in range(chunks):
                    moved[side, k, rows, :] = values[k]
                    values[k] = values[k] * near_now[side, rows, k * LANES : (k + 1) * LANES]
                densities.append(values)
            planes = []
            for y in range(edge):
                first, offset = divmod(y * edge, LANES)
                sides = []
                for side in range(2):
                    shift = (side * HALF - offset) % LANES
                    value = densities[side][first]
                    value = pltpu.roll(value, shift, 1) if shift else value
                    if offset + edge > LANES:
                        more = densities[side][first + 1]
                        more = pltpu.roll(more, shift, 1) if shift else more
                        value = jnp.where(lane < side * HALF + LANES - offset, value, more)
                    sides.append(value)
                planes.append(Number(jnp.where(lane < HALF, sides[0], sides[1])))
            values = real_dft(planes)
            for i in range(half):
                at = tile(t, i, edge)
                lower[0, at, :] = values[i].real
                imag = values[i].imag
                lower[1, at, :] = jnp.zeros((ROWS, LANES), jnp.float32) if imag is None else imag

        steps(tiles, over_y, 3)

        @pl.when(turn == 0)
        def _():
            for copy in table_copies:
                copy.wait()

        @pl.when(turn + 1 < turns)
        def _():
            start_loads(turn + 1)

        def over_x(t):
            at = [across(t, i, edge) for i in range(edge)]
            values = dft([Number(lower[0, a, :], lower[1, a, :]) for a in at], -1)
            real = jnp.concatenate([value.real for value in values], axis=0)
            imag = jnp.concatenate([value.imag for value in values], axis=0)
            at = [tile(t, i, height) for i in range(edge)]
            factor = jnp.concatenate([screen_ref[a, :] for a in at], axis=0)
            real, imag = split_dot(real, imag, ahead_ref)
            real, imag = split_dot(real * factor, imag * factor, behind_ref)
            rows = [slice(i * ROWS, (i + 1) * ROWS) for i in range(edge)]
            values = dft([Number(real[r], imag[r]) for r in rows], 1)
            for i in range(edge):
                upper[0, at[i], :] = values[i].real
                upper[1, at[i], :] = values[i].imag

        steps(height // ROWS, over_x, 4)
        if second_part:
            @pl.when(turn == 0)
            def _():
                for copy in state_copies:
                    copy.wait()

        firsts = [first_of(slot) for slot, _ in picked]

        def back_y(t):
            begin = pl.multiple_of(t * ROWS, ROWS)
            rows = pl.ds(begin, ROWS)
            at = [across(t, i, height) for i in range(half)]
            values = [Number(upper[0, a, :], upper[1, a, :]) for a in at]
            values = values + [values[edge - i].conj() for i in range(half, edge)]
            planes = real_back(values)
            for side in range(2):
                forward = []
                for k in range(chunks):
                    value = None
                    for y in range(k * LANES // edge, edge):
                        begins = y * edge - k * LANES
                        if begins >= LANES:
                            break
                        shift = (begins - side * HALF) % LANES
                        piece = pltpu.roll(planes[y], shift, 1) if shift else planes[y]
                        value = piece if value is None else jnp.where(lane < begins, value, piece)
                    forward.append(value * moved[side, k, rows, :])
                    other = value * near_now[side, rows, k * LANES : (k + 1) * LANES]
                    dense[side, k, pl.ds(edge + begin, ROWS), :] = other
                at = [pl.ds(t * (ROWS * chunks) + k, ROWS, stride=chunks) for k in range(chunks)]
                sums = [act[firsts[side], at[k], :] + forward[k] for k in range(chunks)]
                for k in range(chunks):
                    act[firsts[side], at[k], :] = sums[k]

        steps(tiles, back_y, 3)

        if second_part:
            @pl.when(turn + 1 == turns)
            def _():
                for copy in act_copies:
                    copy.start()

        homes = []
        for side in range(2):
            slot = picked[side][0]
            homes.append(reach_of(slot) * orb_dev + lax.rem(second_of(slot), orb_dev))

        def send_back(g):
            for side in range(2):
                ks = [g * stretch + i for i in range(stretch)]
                values = shifted(dense.at[side], 2 + side, returns[side], 0, edge, ks)
                at = [
                    (i, t, pl.ds(t * (ROWS * chunks) + ks[i], ROWS, stride=chunks))
                    for i in range(stretch)
                    for t in range(tiles)
                ]
                sums = [
                    back[homes[side], a, :] + values[i][t * ROWS : (t + 1) * ROWS] for i, t, a in at
                ]
                for (i, t, a), value in zip(at, sums):
                    back[homes[side], a, :] = value

        steps(chunks // stretch, send_back, 3)
        return 0

    if not second_part:
        lax.fori_loop(0, turns, solve_two, 0)
        return

    @pl.when(found == 0)
    def _():
        for copy in state_copies:
            copy.start()
        for copy in state_copies:
            copy.wait()
        for copy in act_copies:
            copy.start()

    lax.fori_loop(0, turns, solve_two, 0)
    spans = ((0, orb_dev),)
    for begin in (orb_dev, 2 * orb_dev):
        spans += ((begin, 1), (begin + 1, orb_dev - 1))
    back_copies = [
        pltpu.make_async_copy(back.at[pl.ds(begin, count)], back_outs[i], out_sem.at[groups + i])
        for i, (begin, count) in enumerate(spans)
    ]
    for copy in back_copies:
        copy.start()
    for copy in act_copies + back_copies:
        copy.wait()


def reversed_bits(k, count):
    bits = count.bit_length() - 1
    return sum(((k >> i) & 1) << (bits - 1 - i) for i in range(bits))


def pair_terms(numbers, fragments, slots, tables, pieces, own, far, before=()):
    second_part = bool(before)
    orb_dev, edge, plane = pieces[0].shape
    groups = len(pieces)
    frag_size = groups * orb_dev
    chunks = plane // LANES
    rows = edge * chunks
    height = padded_half(edge)
    returns_count = (REACH + 1) * orb_dev
    shape = (edge, orb_dev, groups, fragments, slots)
    smem = pl.BlockSpec(memory_space=pltpu.SMEM)
    vmem = pl.BlockSpec(memory_space=pltpu.VMEM)
    hbm = pl.BlockSpec(memory_space=pltpu.HBM)
    f32 = jnp.float32
    sums = ((frag_size, rows, LANES), (returns_count, rows, LANES))
    out_shape = [jax.ShapeDtypeStruct(sum_shape, f32) for sum_shape in sums]
    out_specs, scratch = [vmem] * 2, []
    if second_part:
        out_shape = [jax.ShapeDtypeStruct((groups // 2, frag_size, rows // groups, LANES), f32)] * 2
        for count in (orb_dev, 1, orb_dev - 1, 1, orb_dev - 1):
            out_shape.append(jax.ShapeDtypeStruct((count, rows, LANES), f32))
        out_specs = [hbm] * 7
        scratch = [pltpu.VMEM(sum_shape, f32) for sum_shape in sums]
        scratch += [pltpu.SemaphoreType.DMA((2,)), pltpu.SemaphoreType.DMA((groups + 5,))]
    return pl.pallas_call(
        functools.partial(pair_kernel, shape, second_part),
        out_shape=out_shape,
        in_specs=[smem] + [hbm] * (4 + groups + len(far) + len(before)),
        out_specs=out_specs,
        scratch_shapes=scratch
        + [
            pltpu.VMEM((2, 2, edge, plane), f32),
            pltpu.VMEM((2, chunks, 3 * edge, LANES), f32),
            pltpu.VMEM((2, chunks, edge, LANES), f32),
            pltpu.VMEM((2, chunks, 3 * edge, LANES), f32),
            pltpu.VMEM((2, height * edge, LANES), f32),
            pltpu.VMEM((2, height * edge, LANES), f32),
            pltpu.VMEM((4, -(-chunks // ROWS) * ROWS, LANES), f32),
            pltpu.SMEM((slots,), jnp.int32),
            pltpu.SemaphoreType.DMA((2, 2)),
            *[pltpu.VMEM(table.shape, table.dtype) for table in tables],
            pltpu.SemaphoreType.DMA((3,)),
        ],
        compiler_params=pltpu.CompilerParams(vmem_limit_bytes=30 << 20),
        name="late_pair_terms" if second_part else "early_pair_terms",
    )(numbers, *tables, *pieces, own, *far, *before)


def flatten_kernel(shape, places_ref, *refs):
    edge, orb_dev, groups = shape
    pieces, (flat_ref, slab_ref) = refs[:groups], refs[groups:]
    member = places_ref[1]
    chunks = edge * edge // LANES
    slab = slab_ref.shape[1]
    for k in range(groups):
        for o in range(orb_dev):
            def move(j, _):
                value = pieces[k][o, :, pl.ds(pl.multiple_of(j * LANES, LANES), LANES)]
                for t in range(edge // ROWS):
                    at = pl.ds(t * (ROWS * chunks) + j, ROWS, stride=chunks)
                    flat_ref[k * orb_dev + o, at, :] = value[t * ROWS : (t + 1) * ROWS]
                return 0

            lax.fori_loop(0, chunks, move, 0)
    slab_ref[...] = flat_ref[:, pl.ds(pl.multiple_of(member * slab, ROWS), slab), :]


def flatten_terms(places, pieces):
    orb_dev, edge, plane = pieces[0].shape
    groups = len(pieces)
    rows = edge * plane // LANES
    frag_size = groups * orb_dev
    smem = pl.BlockSpec(memory_space=pltpu.SMEM)
    vmem = pl.BlockSpec(memory_space=pltpu.VMEM)
    return pl.pallas_call(
        functools.partial(flatten_kernel, (edge, orb_dev, groups)),
        out_shape=(
            jax.ShapeDtypeStruct((frag_size, rows, LANES), jnp.float32),
            jax.ShapeDtypeStruct((frag_size, rows // groups, LANES), jnp.float32),
        ),
        in_specs=[smem] + [vmem] * groups,
        out_specs=(vmem, vmem),
        compiler_params=pltpu.CompilerParams(vmem_limit_bytes=24 << 20),
        name="flatten_terms",
    )(places, *pieces)


def products(lefts, rights, length, step):
    def add(i, sums):
        at = pl.ds(pl.multiple_of(i * step, ROWS), step)
        right = [ref[index, at, :].reshape(step // ROWS, ROWS, LANES) for ref, index in rights]
        out = []
        for n, (ref, index) in enumerate(lefts):
            left = ref[index, at, :].reshape(step // ROWS, ROWS, LANES)
            for m in range(len(rights)):
                out.append(sums[n * len(rights) + m] + jnp.sum(left * right[m], axis=0))
        return tuple(out)

    zero = jnp.zeros((ROWS, LANES), jnp.float32)
    return lax.fori_loop(0, length // step, add, (zero,) * (len(lefts) * len(rights)))


def placed(result, sums, rows, lanes):
    row = lax.broadcasted_iota(jnp.int32, result.shape, 0)
    lane = lax.broadcasted_iota(jnp.int32, result.shape, 1)
    for n, a in enumerate(rows):
        for m, b in enumerate(lanes):
            value = jnp.sum(sums[n * len(lanes) + m], keepdims=True)
            result = jnp.where((row == a) & (lane == b), result + value, result)
    return result


def step_of(length):
    return next(n for n in (72, 24, 8) if length % n == 0)


def action_kernel(shape, places_ref, phi_ref, kept_ref, *refs):
    orb_dev, groups, parts = shape
    arrived, (act_ref, share_ref) = refs[:parts], refs[parts:]
    member = places_ref[1]
    frag_size = orb_dev * groups
    slab = act_ref.shape[1]
    cut = frag_size // parts
    for i in range(parts):
        span = slice(i * cut, (i + 1) * cut)
        act_ref[span] = kept_ref[0, span] + arrived[i][0]
    rows = [(member ^ (a // orb_dev)) * orb_dev + a % orb_dev for a in range(frag_size)]
    result = jnp.zeros(share_ref.shape, jnp.float32)
    for half in range(0, frag_size, 4):
        bs = range(half, min(half + 4, frag_size))
        lefts, rights = [(phi_ref, a) for a in range(frag_size)], [(act_ref, b) for b in bs]
        result = placed(result, products(lefts, rights, slab, step_of(slab)), rows, bs)
    share_ref[...] = result


def action_terms(places, orb_dev, phi, kept, arrived):
    frag_size, slab = phi.shape[:2]
    smem = pl.BlockSpec(memory_space=pltpu.SMEM)
    vmem = pl.BlockSpec(memory_space=pltpu.VMEM)
    return pl.pallas_call(
        functools.partial(action_kernel, (orb_dev, frag_size // orb_dev, len(arrived))),
        out_shape=(
            jax.ShapeDtypeStruct((frag_size, slab, LANES), jnp.float32),
            jax.ShapeDtypeStruct((frag_size, LANES), jnp.float32),
        ),
        in_specs=[smem] + [vmem] * (2 + len(arrived)),
        out_specs=(vmem, vmem),
        compiler_params=pltpu.CompilerParams(vmem_limit_bytes=16 << 20),
        name="action_terms",
    )(places, phi, kept, *arrived)


def home_kernel(shape, places_ref, flat_ref, own_ref, *refs):
    edge, orb_dev, groups, first, count = shape
    if first == 0:
        (two_ref, twin_ref, relay_ref, share_ref), refs = refs[:4], refs[4:]
    else:
        (two_ref, one_ref), refs = refs[:2], refs[2:]
    outs, total = refs[:groups], refs[groups]
    fragment, member = places_ref[0], places_ref[1]
    frag_size = orb_dev * groups
    rows = flat_ref.shape[1]
    slab = rows // groups
    for i in range(count):
        value = own_ref[first + i] + two_ref[i]
        if first == 0:
            @pl.when(lax.rem(fragment, 2) == 1)
            def _():
                total[i] = value + twin_ref[i]

            @pl.when(lax.rem(fragment, 2) == 0)
            def _():
                total[i] = value + relay_ref[i]
        else:
            total[i] = value + one_ref[i]
    lefts, rights = [(flat_ref, a) for a in range(frag_size)], [(total, i) for i in range(count)]
    places = [(member ^ (a // orb_dev)) * orb_dev + a % orb_dev for a in range(frag_size)]
    result = share_ref[...] if first == 0 else jnp.zeros((frag_size, LANES), jnp.float32)
    sums = products(lefts, rights, rows, step_of(rows))
    result = placed(result, sums, places, [member * orb_dev + first + i for i in range(count)])
    result = result * (1.0 / float(edge**3))
    for k in range(groups):
        begin = pl.multiple_of((member ^ k) * slab, ROWS)
        for i in range(count):
            outs[k][i * slab : (i + 1) * slab, :] = total[i, pl.ds(begin, slab), :]
        outs[k][count * slab :, :] = result


def home_terms(places, edge, groups, flat, own, first, *came):
    frag_size, rows = flat.shape[:2]
    count = came[0].shape[0]
    smem = pl.BlockSpec(memory_space=pltpu.SMEM)
    vmem = pl.BlockSpec(memory_space=pltpu.VMEM)
    f32 = jnp.float32
    parcel = jax.ShapeDtypeStruct((count * rows // groups + frag_size, LANES), f32)
    return pl.pallas_call(
        functools.partial(home_kernel, (edge, frag_size // groups, groups, first, count)),
        out_shape=[parcel] * groups,
        in_specs=[smem] + [vmem] * (2 + len(came)),
        out_specs=[vmem] * groups,
        scratch_shapes=[pltpu.VMEM((count, rows, LANES), f32)],
        compiler_params=pltpu.CompilerParams(vmem_limit_bytes=16 << 20),
        name="home_terms",
    )(places, flat, own, *came)


def exchanged(value, axis, width):
    size = value.shape[axis]
    index = lax.broadcasted_iota(jnp.int32, value.shape, axis)
    below, above = pltpu.roll(value, width, axis), pltpu.roll(value, size - width, axis)
    return jnp.where((index & width) != 0, below, above)


def gradient_kernel(shape, places_ref, act_ref, phi_ref, *refs):
    edge, orb_dev, groups = shape
    heads, tails, refs = refs[:groups], refs[groups : 2 * groups], refs[2 * groups :]
    out_ref, lagrange_ref, hold, ready, sems = refs
    member = places_ref[1]
    frag_size = orb_dev * groups
    chunks = edge * edge // LANES
    slab_rows = edge // groups
    slab = slab_rows * chunks
    sums = [
        head[slab:, :] + tail[(orb_dev - 1) * slab :, :] for head, tail in zip(heads, tails)
    ]
    while len(sums) > 1:
        sums = [sums[i] + sums[i + 1] for i in range(0, len(sums), 2)]
    square = jnp.concatenate([sums[0], jnp.zeros((LANES - frag_size, LANES), jnp.float32)], axis=0)
    lagrange = 0.5 * (square + square.T)[:frag_size, :]
    lagrange_ref[...] = lagrange[:, :frag_size]
    bit = 1
    while bit < groups:
        turned = exchanged(exchanged(lagrange, 0, bit * orb_dev), 1, bit * orb_dev)
        lagrange = jnp.where((member & bit) != 0, turned, lagrange)
        bit *= 2

    copies = []
    count = next(n for n in (4, 3, 2, 1) if slab_rows % n == 0 and n * chunks % ROWS == 0)
    for x in range(0, slab_rows, count):
        at = slice(x * chunks, (x + count) * chunks)
        for k in range(groups):
            for o in range(orb_dev):
                a = (member ^ k) * orb_dev + o
                came = heads[k] if o == 0 else tails[k].at[(o - 1) * slab : o * slab]
                value = act_ref[a, at] + came[at, :]
                for b in range(frag_size):
                    factor = lagrange[b : b + 1, k * orb_dev + o : k * orb_dev + o + 1]
                    value = value - factor * phi_ref[b, at]
                begin = pl.multiple_of(a * slab + x * chunks, ROWS)
                hold[pl.ds(begin, count * chunks), :] = value
        for i in range(x, x + count):
            for j in range(chunks):
                value = hold[pl.ds(i * chunks + j, frag_size, stride=slab), :]
                ready[i, :, j * LANES : (j + 1) * LANES] = value
        rows = pl.ds(x, count)
        copies.append(pltpu.make_async_copy(ready.at[rows], out_ref.at[rows], sems.at[x // count]))
        copies[-1].start()
    for copy in copies:
        copy.wait()


def gradient_terms(places, edge, act, phi, heads, tails):
    groups = len(heads)
    frag_size, slab = act.shape[:2]
    smem = pl.BlockSpec(memory_space=pltpu.SMEM)
    vmem = pl.BlockSpec(memory_space=pltpu.VMEM)
    f32 = jnp.float32
    gradient, lagrange = pl.pallas_call(
        functools.partial(gradient_kernel, (edge, frag_size // groups, groups)),
        out_shape=(
            jax.ShapeDtypeStruct((edge // groups, frag_size, edge * edge), f32),
            jax.ShapeDtypeStruct((frag_size, frag_size), f32),
        ),
        in_specs=[smem] + [vmem] * (2 + 2 * groups),
        out_specs=(pl.BlockSpec(memory_space=pltpu.HBM), vmem),
        scratch_shapes=[
            pltpu.VMEM((frag_size * slab, LANES), f32),
            pltpu.VMEM((edge // groups, frag_size, edge * edge), f32),
            pltpu.SemaphoreType.DMA((edge // groups,)),
        ],
        compiler_params=pltpu.CompilerParams(vmem_limit_bytes=16 << 20),
        name="gradient_terms",
    )(places, act, phi, *heads, *tails)
    return gradient.transpose(1, 0, 2), lagrange


def together(*arrays):
    return lax.optimization_barrier(arrays)


def to_fragment(block, distance, senders=None):
    devices = lax.axis_size("orb")
    senders = range(devices) if senders is None else range(senders, devices, 2)
    return lax.ppermute(block, "orb", [(i, (i + distance) % devices) for i in senders])


def with_twin(block):
    return lax.ppermute(block, "orb", [(i, i ^ 1) for i in range(lax.axis_size("orb"))])


def with_member(block, bit):
    return lax.ppermute(block, "grp", [(i, i ^ bit) for i in range(lax.axis_size("grp"))])


def by_member(parcels, after=None):
    groups = len(parcels)
    received = list(parcels)
    bit = groups // 2
    while bit:
        for k in reversed(range(groups)):
            if k & bit:
                received[k] = with_member(received[k], bit)
        if after is not None and bit == groups // 2:
            after, *received[bit:] = together(after, *received[bit:])
        bit //= 2
    return received, after


def shards(orbitals, kernel, anchors, pair_count, pair_first, pair_second, pair_reach):
    groups = lax.axis_size("grp")
    orb_dev, edge, plane = orbitals.shape
    places = jnp.stack([lax.axis_index("orb"), lax.axis_index("grp")]).astype(jnp.int32)

    own = orbitals.reshape(orb_dev, edge, plane // LANES, LANES).transpose(0, 2, 1, 3)
    numbers = [places, pair_count, pair_first, pair_second, pair_reach, anchors.reshape(-1)]
    screen, numbers, *tables = screen_terms(jnp.concatenate(numbers), kernel)
    two = to_fragment(own, -2)
    twin = with_twin(own[:1])
    pieces = {0: orbitals}
    bit = groups // 2
    while bit:
        for k in list(pieces):
            pieces[k ^ bit] = with_member(pieces[k], bit)
        if bit == groups // 2:
            two, twin, tail, pieces[bit], screen, numbers, *tables = together(
                two, twin, own[1:], pieces[bit], screen, numbers, *tables
            )
            one = to_fragment(tail, -1)
            relay = to_fragment(twin, -2, 1)
        bit //= 2
    pieces = [pieces[k] for k in range(groups)]
    tables = [screen, *tables]
    sizes = (anchors.shape[0], pair_first.shape[0])
    before = pair_terms(numbers, *sizes, tables, pieces, own, [twin, two])
    kept, sent, own, one_head, one_tail, two_head, two_tail = pair_terms(
        numbers, *sizes, tables, pieces, own, [twin, two, relay, one], before
    )

    two_tail = to_fragment(two_tail, 2)
    one_tail = to_fragment(one_tail, 1)
    bit = 1
    arrived = with_member(sent, bit)
    while 2 * bit < groups:
        kept = kept + arrived
        if bit == 1:
            kept, one_head = together(kept, one_head)
        half = kept.shape[0] // 2
        bit *= 2
        arrived, kept = with_member(kept[half:], bit), kept[:half]
    twin = with_twin(one_head)
    relay = to_fragment(twin, 2, 0)
    two_tail, two_head = together(two_tail, two_head)
    two_head = to_fragment(two_head, 2)

    flat, phi = flatten_terms(places, pieces)
    tails = home_terms(places, edge, groups, flat, own, 1, two_tail, one_tail)
    tails, two_head = by_member(tails, two_head)
    act, share = action_terms(places, orb_dev, phi, kept, [arrived])
    heads, _ = by_member(
        home_terms(places, edge, groups, flat, own, 0, two_head, twin, relay, share)
    )
    gradient, lagrange = gradient_terms(places, edge, act, phi, heads, tails)
    return (gradient, lagrange[None])


def solution(mesh):
    placed = (P(("orb", "grp"), None, None), P(), P(), P("orb"), P("orb"), P("orb"), P("orb"))
    return jax.shard_map(
        shards,
        mesh=mesh,
        in_specs=placed,
        out_specs=(P("orb", "grp", None), P("orb", None, None)),
        check_vma=False,
    )
```

```python
import functools
import math

import jax
import jax.numpy as jnp
import numpy as np
from jax import lax
from jax.experimental import pallas as pl
from jax.experimental.pallas import tpu as pltpu
from jax.sharding import PartitionSpec as P

REACH = 2
LANES = 128
ROWS = 8
HALF = LANES // 2


class Number:
    def __init__(self, real, imag=None):
        self.real, self.imag = real, imag

    def __add__(self, other):
        if self.imag is None or other.imag is None:
            imag = self.imag if other.imag is None else other.imag
        else:
            imag = self.imag + other.imag
        return Number(self.real + other.real, imag)

    def __sub__(self, other):
        if other.imag is None:
            imag = self.imag
        else:
            imag = -other.imag if self.imag is None else self.imag - other.imag
        return Number(self.real - other.real, imag)

    def conj(self):
        return self if self.imag is None else Number(self.real, -self.imag)

    def scaled(self, factor):
        return Number(self.real * factor, None if self.imag is None else self.imag * factor)

    def turned(self, sign):
        if self.imag is None:
            return Number(jnp.zeros_like(self.real), self.real if sign > 0 else -self.real)
        return Number(-self.imag, self.real) if sign > 0 else Number(self.imag, -self.real)

    def plus_turned(self, other, sign):
        if sign < 0:
            return self.minus_turned(other)
        real = self.real if other.imag is None else self.real - other.imag
        return Number(real, other.real if self.imag is None else self.imag + other.real)

    def minus_turned(self, other):
        real = self.real if other.imag is None else self.real + other.imag
        return Number(real, -other.real if self.imag is None else self.imag - other.real)

    def times(self, angle):
        real, imag = math.cos(angle), math.sin(angle)
        if abs(imag) < 1e-12:
            return self if real > 0 else self.scaled(-1.0)
        if abs(real) < 1e-12:
            return self.turned(imag)
        if self.imag is None:
            return Number(self.real * real, self.real * imag)
        return Number(self.real * real - self.imag * imag, self.real * imag + self.imag * real)


def coprime(n):
    for p in (2, 3, 5, 7):
        power = 1
        while n % (power * p) == 0:
            power *= p
        if 1 < power < n:
            return power, n // power
    return None


def radix(n):
    return next((p for p in (4, 2, 3, 5, 7) if n % p == 0 and n > p), None)


def meeting(i, j, first, second):
    return next(k for k in range(first * second) if k % first == i and k % second == j)


def dft(values, sign):
    n = len(values)
    if n == 1:
        return values
    if n == 2:
        return [values[0] + values[1], values[0] - values[1]]
    if n == 3:
        a, b, c = values
        total, side = b + c, (b - c).scaled(math.sqrt(0.75))
        middle = a - total.scaled(0.5)
        return [a + total, middle.plus_turned(side, sign), middle.plus_turned(side, -sign)]
    if n == 4:
        a, b, c, d = values
        s, t, u, v = a + c, a - c, b + d, b - d
        return [s + u, t.plus_turned(v, sign), s - u, t.plus_turned(v, -sign)]
    out = [None] * n
    if coprime(n):
        first, second = coprime(n)
        columns = [
            dft([values[(i * second + j * first) % n] for i in range(first)], sign)
            for j in range(second)
        ]
        for i in range(first):
            row = dft([column[i] for column in columns], sign)
            for j in range(second):
                out[meeting(i, j, first, second)] = row[j]
        return out
    p = radix(n)
    if p:
        rest = n // p
        columns = [dft(values[j::p], sign) for j in range(p)]
        for i in range(rest):
            row = dft(
                [columns[j][i].times(sign * 2.0 * math.pi * i * j / n) for j in range(p)], sign
            )
            for j in range(p):
                out[i + rest * j] = row[j]
        return out
    for k in range(n):
        total = values[0]
        for j in range(1, n):
            total = total + values[j].times(sign * 2.0 * math.pi * (j * k % n) / n)
        out[k] = total
    return out


def real_dft(values):
    n = len(values)
    if n <= 4:
        out = dft(values, -1)
    else:
        out = [None] * n
        if coprime(n):
            first, second = coprime(n)
            columns = [
                real_dft([values[(i * second + j * first) % n] for i in range(first)])
                for j in range(second)
            ]
            for i in range(first // 2 + 1):
                entries = [column[i] for column in columns]
                alone = 2 * i % first == 0
                row = real_dft(entries) if alone else dft(entries, -1)
                for j in range(second):
                    out[meeting(i, j, first, second)] = row[j]
        elif radix(n):
            p = radix(n)
            rest = n // p
            columns = [real_dft(values[j::p]) for j in range(p)]
            for i in range(rest // 2 + 1):
                row = dft(
                    [columns[j][i].times(-2.0 * math.pi * i * j / n) for j in range(p)], -1
                )
                for j in range(p):
                    out[i + rest * j] = row[j]
        else:
            out = dft(values, -1)
    for k in range(1, n):
        if out[k] is None or (k > n // 2 and out[n - k] is not None):
            out[k] = out[n - k].conj()
    out[0] = Number(out[0].real)
    if n % 2 == 0:
        out[n // 2] = Number(out[n // 2].real)
    return out


def real_back(values):
    n = len(values)
    if n == 1:
        return [values[0].real]
    if n == 2:
        return [values[0].real + values[1].real, values[0].real - values[1].real]
    if n == 3:
        a, b = values[0].real, values[1]
        side = b.imag * math.sqrt(3.0)
        middle = a - b.real
        return [a + 2.0 * b.real, middle - side, middle + side]
    if n == 4:
        s, t = values[0].real + values[2].real, values[0].real - values[2].real
        u, v = 2.0 * values[1].real, 2.0 * values[1].imag
        return [s + u, t - v, s - u, t + v]
    out = [None] * n
    if coprime(n):
        first, second = coprime(n)
        rows = []
        for i in range(first // 2 + 1):
            entries = [values[meeting(i, j, first, second)] for j in range(second)]
            if 2 * i % first == 0:
                rows.append([Number(value) for value in real_back(entries)])
            else:
                rows.append(dft(entries, 1))
        for b in range(second):
            half = [row[b] for row in rows]
            whole = half + [half[first - i].conj() for i in range(len(half), first)]
            for a, value in enumerate(real_back(whole)):
                out[(a * second + b * first) % n] = value
        return out
    p = radix(n)
    if p:
        rest = n // p
        parts = []
        for i in range(p // 2 + 1):
            entries = values[i::p]
            if i == 0:
                parts.append([Number(value) for value in real_back(entries)])
            else:
                inner = dft(entries, 1)
                parts.append([inner[m].times(2.0 * math.pi * i * m / n) for m in range(rest)])
                if 2 * i == p:
                    parts[-1] = [Number(value.real) for value in parts[-1]]
        for m in range(rest):
            half = [part[m] for part in parts]
            whole = half + [half[p - i].conj() for i in range(len(half), p)]
            for j, value in enumerate(real_back(whole)):
                out[m + rest * j] = value
        return out
    return [value.real for value in dft(values, 1)]


def wave_table(edge):
    index = np.arange(edge)
    angles = 2.0 * np.pi / edge * (np.outer(index, index) % edge)
    full = np.zeros((2, 2, HALF, 2, HALF))
    for side in range(2):
        full[0, side, :edge, side, :edge] = np.cos(angles)
        full[1, side, :edge, side, :edge] = np.sin(angles)
    full = full.reshape(2, LANES, LANES)
    high = full.astype(jnp.bfloat16)
    low = (full - high.astype(np.float64)).astype(jnp.bfloat16)
    return np.stack([high, low])


def split_dot(real, imag, matrix):
    value = jnp.concatenate([real, imag], axis=1)
    high = value.astype(jnp.bfloat16)
    low = (value - high.astype(jnp.float32)).astype(jnp.bfloat16)
    product = jnp.dot(
        jnp.concatenate([high, low, high], axis=1), matrix[...], preferred_element_type=jnp.float32
    )
    return product[:, :LANES], product[:, LANES:]


def padded_half(edge):
    return -(-(edge // 2 + 1) // ROWS) * ROWS


def screen_kernel(edge, numbers_ref, kernel_ref, waves_ref, out_ref, kept_ref, ahead_ref, behind_ref, flipped):
    for i in range(numbers_ref.shape[0]):
        kept_ref[i] = numbers_ref[i]
    for table, sign in ((ahead_ref, -1), (behind_ref, 1)):
        for part, source in enumerate((0, 0, 1)):
            for i in range(2):
                for j in range(2):
                    value = waves_ref[source, (i + j) % 2]
                    if i != j and (i > j) == (sign > 0):
                        value = -value
                    rows = slice((2 * part + i) * LANES, (2 * part + i + 1) * LANES)
                    table[rows, j * LANES : (j + 1) * LANES] = value
    exact = dict(precision=lax.Precision.HIGHEST, preferred_element_type=jnp.float32)

    def index(shape, axis):
        return lax.broadcasted_iota(jnp.int32, shape, axis)

    square, whole = (edge, edge), (LANES, LANES)
    flip = index(square, 0) + index(square, 1)
    flip = ((flip == 0) | (flip == edge)).astype(jnp.float32)
    source, target = index(whole, 0), index(whole, 1)
    target = jnp.where(target < HALF, target, target - HALF)
    mirror = ((source + target == 0) | (source + target == edge)) & (source < edge) & (target < edge)
    mirror = mirror.astype(jnp.float32)
    flipped[...] = jnp.dot(flip, kernel_ref[...], **exact)
    height = padded_half(edge)
    lane = index((edge, LANES), 1)
    out_ref[...] = jnp.zeros_like(out_ref)

    def piece(ref, y):
        begin, offset = divmod(y * edge, LANES)
        value = ref[:, begin * LANES : (begin + 1) * LANES]
        value = pltpu.roll(value, LANES - offset, 1) if offset else value
        if offset + edge > LANES:
            more = ref[:, (begin + 1) * LANES : (begin + 2) * LANES]
            value = jnp.where(lane < LANES - offset, value, pltpu.roll(more, LANES - offset, 1))
        return value

    for y in range(edge // 2 + 1):
        value = piece(kernel_ref, y)
        value = jnp.where(lane < HALF, value, pltpu.roll(value, HALF, 1))
        value = value + jnp.dot(piece(flipped, (edge - y) % edge), mirror, **exact)
        value = value * (0.5 / float(edge**3))
        for t in range(edge // ROWS):
            at = pl.ds(t * ROWS * height + y, ROWS, stride=height)
            out_ref[at, :] = value[t * ROWS : (t + 1) * ROWS]


def screen_terms(numbers, kernel):
    edge, plane = kernel.shape
    smem = pl.BlockSpec(memory_space=pltpu.SMEM)
    vmem = pl.BlockSpec(memory_space=pltpu.VMEM)
    table = jax.ShapeDtypeStruct((6 * LANES, 2 * LANES), jnp.bfloat16)
    return pl.pallas_call(
        functools.partial(screen_kernel, edge),
        out_shape=[
            jax.ShapeDtypeStruct((edge * padded_half(edge), LANES), jnp.float32),
            jax.ShapeDtypeStruct(numbers.shape, numbers.dtype),
            table,
            table,
        ],
        in_specs=[smem, vmem, vmem],
        out_specs=[vmem, smem, vmem, vmem],
        scratch_shapes=[pltpu.VMEM((edge, plane), jnp.float32)],
        compiler_params=pltpu.CompilerParams(vmem_limit_bytes=8 << 20),
        name="screen_terms",
    )(numbers, kernel, jnp.asarray(wave_table(edge)))


def pair_kernel(shape, second_part, numbers_ref, *refs):
    edge, orb_dev, groups, fragments, slots = shape
    plane = edge * edge
    chunks = plane // LANES
    tiles = edge // ROWS
    half = edge // 2 + 1
    height = padded_half(edge)
    returns_count = (REACH + 1) * orb_dev
    tables, refs = refs[:3], refs[3:]
    phi_refs, refs = refs[:groups], refs[groups:]
    (twin_ref, two_ref), refs = refs[:2], refs[2:]
    if second_part:
        (relay_ref, one_ref, act_before, back_before), refs = refs[:4], refs[4:]
        act_outs, back_outs, refs = refs[:2], refs[2:7], refs[7:]
        (act, back, state_sem, out_sem), refs = refs[:4], refs[4:]
    else:
        (act, back), refs = refs[:2], refs[2:]
    (near, far, wide, moved, dense, lower, upper, masks, listed, load_sem) = refs[:10]
    screen_ref, ahead_ref, behind_ref, table_sem = refs[10:]

    fragment, member, live_slots = numbers_ref[0], numbers_ref[1], numbers_ref[2]

    def first_of(slot):
        return numbers_ref[3 + slot]

    def second_of(slot):
        return numbers_ref[3 + slots + slot]

    def reach_of(slot):
        return numbers_ref[3 + 2 * slots + slot]

    def anchor(place, axis):
        return numbers_ref[3 + 3 * slots + 3 * place + axis]

    table_copies = [
        pltpu.make_async_copy(table, hold, table_sem.at[i])
        for i, (table, hold) in enumerate(zip(tables, refs[10:13]))
    ]
    lane = lax.broadcasted_iota(jnp.int32, (1, LANES), 1)
    stretch = next(n for n in (6, 4, 3, 2, 1) if chunks % n == 0)
    middle = pl.ds(edge, edge)

    even = lax.rem(fragment, 2) == 0

    def list_slots(slot, counts):
        early, found = counts
        mine = (slot < live_slots) & (lax.div(second_of(slot), orb_dev) == member)
        reach = reach_of(slot)
        come = (reach == 0) | (reach == 2) | (even & (lax.rem(second_of(slot), orb_dev) == 0))
        taken = mine & come & (early < 2)
        chosen = mine & jnp.logical_not(taken) if second_part else taken

        @pl.when(chosen)
        def _():
            listed[found] = slot

        return early + taken.astype(jnp.int32), found + chosen.astype(jnp.int32)

    _, found = lax.fori_loop(0, slots, list_slots, (jnp.int32(0), jnp.int32(0)))
    turns = lax.div(found + 1, 2)

    def slot_of(turn, side):
        at = 2 * turn + side
        live = at < found
        return listed[jnp.where(live, at, 2 * turn)], live

    def far_copy(side, source):
        return pltpu.make_async_copy(source, far.at[side], load_sem.at[1, side])

    def start_loads(turn):
        for side in range(2):
            slot, _ = slot_of(turn, side)
            first, second, reach = first_of(slot), second_of(slot), reach_of(slot)
            relative = lax.div(first, orb_dev) ^ member
            for k in range(groups):
                @pl.when(relative == k)
                def _():
                    pltpu.make_async_copy(
                        phi_refs[k].at[lax.rem(first, orb_dev)],
                        near.at[lax.rem(turn, 2), side],
                        load_sem.at[0, side],
                    ).start()
            own = lax.rem(second, orb_dev)

            @pl.when(reach == 0)
            def _():
                far_copy(side, phi_refs[0].at[own]).start()

            @pl.when((reach == 1) & (own == 0) & even)
            def _():
                far_copy(side, twin_ref.at[0]).start()

            @pl.when(reach == 2)
            def _():
                far_copy(side, two_ref.at[own]).start()

            if second_part:
                @pl.when((reach == 1) & (own == 0) & jnp.logical_not(even))
                def _():
                    far_copy(side, relay_ref.at[0]).start()

                @pl.when((reach == 1) & (own > 0))
                def _():
                    far_copy(side, one_ref.at[jnp.maximum(own - 1, 0)]).start()

    def wait_loads(turn):
        for side in range(2):
            pltpu.make_async_copy(
                phi_refs[0].at[0], near.at[lax.rem(turn, 2), side], load_sem.at[0, side]
            ).wait()
            far_copy(side, phi_refs[0].at[0]).wait()

    @pl.when(found > 0)
    def _():
        start_loads(0)
        for copy in table_copies:
            copy.start()

    if second_part:
        state_copies = [
            pltpu.make_async_copy(before, now, state_sem.at[i])
            for i, (before, now) in enumerate(((act_before, act), (back_before, back)))
        ]
        slab = plane * edge // LANES // groups
        act_copies = []
        for k in range(groups):
            source = (member ^ k) * slab
            place = reversed_bits(k, groups)
            act_copies.append(
                pltpu.make_async_copy(
                    act.at[:, pl.ds(pl.multiple_of(source, ROWS), slab), :],
                    act_outs[2 * place // groups].at[place % (groups // 2)],
                    out_sem.at[k],
                )
            )
    else:
        act[...] = jnp.zeros_like(act)
        back[...] = jnp.zeros_like(back)

    def offset_of(slot):
        partner = lax.rem(fragment + reach_of(slot), fragments)
        return [anchor(partner, i) - anchor(fragment, i) for i in range(3)]

    def steps(count, body, most):
        width = max(n for n in range(1, most + 1) if count % n == 0)

        def step(i, _):
            for j in range(width):
                body(i * width + j)
            return 0

        if width == count:
            step(0, 0)
        else:
            lax.fori_loop(0, count // width, step, 0)

    def columns(k):
        return pl.ds(pl.multiple_of(k * LANES, LANES), LANES)

    def set_masks(place, delta, weight):
        shape = masks.shape[1:]
        spot = lax.broadcasted_iota(jnp.int32, shape, 0) * LANES
        spot = spot + lax.broadcasted_iota(jnp.int32, shape, 1)
        y = ((spot.astype(jnp.float32) + 0.5) * (1.0 / edge)).astype(jnp.int32)
        z = spot - y * edge - delta[2]
        y = y - delta[1]
        inside = (y >= 0) & (y < edge) & (z >= 0) & (z < edge)
        masks[place] = jnp.where(inside, weight, 0.0)

    def shifted(source, place, delta, begin, count, ks):
        shift = lax.rem(delta[1] * edge + delta[2] + 4 * plane, plane)
        start = lax.rem(plane - shift, plane)
        whole, part = lax.div(start, LANES), lax.rem(start, LANES)
        turn = lax.rem(LANES - part, LANES)
        down = edge - jnp.clip(delta[0], -edge, edge) + begin
        x = lax.broadcasted_iota(jnp.int32, (count, LANES), 0) + (begin - delta[0])
        rows_inside = (x >= 0) & (x < edge)
        first = lane < LANES - part

        def piece(k):
            return pltpu.roll(source[lax.rem(k + whole, chunks), pl.ds(down, count), :], turn, 1)

        out = []
        low = piece(ks[0])
        for k in ks:
            high = piece(k + 1)
            value = jnp.where(first, low, high) * masks[place, pl.ds(k, 1), :]
            out.append(jnp.where(rows_inside, value, 0.0))
            low = high
        return out

    def tile(t, i, size):
        return pl.ds(pl.multiple_of(i * size + t * ROWS, ROWS), ROWS)

    def across(t, i, size):
        return pl.ds(t * (ROWS * size) + i, ROWS, stride=size)

    def solve_two(turn, _):
        wait_loads(turn)
        if second_part:
            @pl.when(turn == 0)
            def _():
                for copy in state_copies:
                    copy.start()

        near_now = near.at[lax.rem(turn, 2)]
        picked = [slot_of(turn, side) for side in range(2)]
        offsets = [offset_of(slot) for slot, _ in picked]
        returns = [[-d for d in delta] for delta in offsets]
        for side in range(2):
            set_masks(side, offsets[side], picked[side][1].astype(jnp.float32))
            set_masks(2 + side, returns[side], 1.0)

        def widen(k):
            for side in range(2):
                wide[side, k, middle, :] = far[side, :, pl.ds(pl.multiple_of(k * LANES, LANES), LANES)]

        steps(chunks, widen, chunks)

        def over_y(t):
            densities = []
            begin = pl.multiple_of(t * ROWS, ROWS)
            rows = pl.ds(begin, ROWS)
            for side in range(2):
                values = shifted(wide.at[side], side, offsets[side], begin, ROWS, range(chunks))
                for k in range(chunks):
                    moved[side, k, rows, :] = values[k]
                    values[k] = values[k] * near_now[side, rows, k * LANES : (k + 1) * LANES]
                densities.append(values)
            planes = []
            for y in range(edge):
                first, offset = divmod(y * edge, LANES)
                sides = []
                for side in range(2):
                    shift = (side * HALF - offset) % LANES
                    value = densities[side][first]
                    value = pltpu.roll(value, shift, 1) if shift else value
                    if offset + edge > LANES:
                        more = densities[side][first + 1]
                        more = pltpu.roll(more, shift, 1) if shift else more
                        value = jnp.where(lane < side * HALF + LANES - offset, value, more)
                    sides.append(value)
                planes.append(Number(jnp.where(lane < HALF, sides[0], sides[1])))
            values = real_dft(planes)
            for i in range(half):
                at = tile(t, i, edge)
                lower[0, at, :] = values[i].real
                imag = values[i].imag
                lower[1, at, :] = jnp.zeros((ROWS, LANES), jnp.float32) if imag is None else imag

        steps(tiles, over_y, 3)

        @pl.when(turn == 0)
        def _():
            for copy in table_copies:
                copy.wait()

        @pl.when(turn + 1 < turns)
        def _():
            start_loads(turn + 1)

        def over_x(t):
            at = [across(t, i, edge) for i in range(edge)]
            values = dft([Number(lower[0, a, :], lower[1, a, :]) for a in at], -1)
            real = jnp.concatenate([value.real for value in values], axis=0)
            imag = jnp.concatenate([value.imag for value in values], axis=0)
            at = [tile(t, i, height) for i in range(edge)]
            factor = jnp.concatenate([screen_ref[a, :] for a in at], axis=0)
            real, imag = split_dot(real, imag, ahead_ref)
            real, imag = split_dot(real * factor, imag * factor, behind_ref)
            rows = [slice(i * ROWS, (i + 1) * ROWS) for i in range(edge)]
            values = dft([Number(real[r], imag[r]) for r in rows], 1)
            for i in range(edge):
                upper[0, at[i], :] = values[i].real
                upper[1, at[i], :] = values[i].imag

        steps(height // ROWS, over_x, 4)
        if second_part:
            @pl.when(turn == 0)
            def _():
                for copy in state_copies:
                    copy.wait()

        firsts = [first_of(slot) for slot, _ in picked]

        def back_y(t):
            begin = pl.multiple_of(t * ROWS, ROWS)
            rows = pl.ds(begin, ROWS)
            at = [across(t, i, height) for i in range(half)]
            values = [Number(upper[0, a, :], upper[1, a, :]) for a in at]
            values = values + [values[edge - i].conj() for i in range(half, edge)]
            planes = real_back(values)
            for side in range(2):
                forward = []
                for k in range(chunks):
                    value = None
                    for y in range(k * LANES // edge, edge):
                        begins = y * edge - k * LANES
                        if begins >= LANES:
                            break
                        shift = (begins - side * HALF) % LANES
                        piece = pltpu.roll(planes[y], shift, 1) if shift else planes[y]
                        value = piece if value is None else jnp.where(lane < begins, value, piece)
                    forward.append(value * moved[side, k, rows, :])
                    other = value * near_now[side, rows, k * LANES : (k + 1) * LANES]
                    dense[side, k, pl.ds(edge + begin, ROWS), :] = other
                at = [pl.ds(t * (ROWS * chunks) + k, ROWS, stride=chunks) for k in range(chunks)]
                sums = [act[firsts[side], at[k], :] + forward[k] for k in range(chunks)]
                for k in range(chunks):
                    act[firsts[side], at[k], :] = sums[k]

        steps(tiles, back_y, 3)

        if second_part:
            @pl.when(turn + 1 == turns)
            def _():
                for copy in act_copies:
                    copy.start()

        homes = []
        for side in range(2):
            slot = picked[side][0]
            homes.append(reach_of(slot) * orb_dev + lax.rem(second_of(slot), orb_dev))

        def send_back(g):
            for side in range(2):
                ks = [g * stretch + i for i in range(stretch)]
                values = shifted(dense.at[side], 2 + side, returns[side], 0, edge, ks)
                at = [
                    (i, t, pl.ds(t * (ROWS * chunks) + ks[i], ROWS, stride=chunks))
                    for i in range(stretch)
                    for t in range(tiles)
                ]
                sums = [
                    back[homes[side], a, :] + values[i][t * ROWS : (t + 1) * ROWS] for i, t, a in at
                ]
                for (i, t, a), value in zip(at, sums):
                    back[homes[side], a, :] = value

        steps(chunks // stretch, send_back, 3)
        return 0

    if not second_part:
        lax.fori_loop(0, turns, solve_two, 0)
        return

    @pl.when(found == 0)
    def _():
        for copy in state_copies:
            copy.start()
        for copy in state_copies:
            copy.wait()
        for copy in act_copies:
            copy.start()

    lax.fori_loop(0, turns, solve_two, 0)
    spans = ((0, orb_dev),)
    for begin in (orb_dev, 2 * orb_dev):
        spans += ((begin, 1), (begin + 1, orb_dev - 1))
    back_copies = [
        pltpu.make_async_copy(back.at[pl.ds(begin, count)], back_outs[i], out_sem.at[groups + i])
        for i, (begin, count) in enumerate(spans)
    ]
    for copy in back_copies:
        copy.start()
    for copy in act_copies + back_copies:
        copy.wait()


def reversed_bits(k, count):
    bits = count.bit_length() - 1
    return sum(((k >> i) & 1) << (bits - 1 - i) for i in range(bits))


def pair_terms(numbers, fragments, slots, tables, pieces, far, before=()):
    second_part = bool(before)
    orb_dev, edge, plane = pieces[0].shape
    groups = len(pieces)
    frag_size = groups * orb_dev
    chunks = plane // LANES
    rows = edge * chunks
    height = padded_half(edge)
    returns_count = (REACH + 1) * orb_dev
    shape = (edge, orb_dev, groups, fragments, slots)
    smem = pl.BlockSpec(memory_space=pltpu.SMEM)
    vmem = pl.BlockSpec(memory_space=pltpu.VMEM)
    hbm = pl.BlockSpec(memory_space=pltpu.HBM)
    f32 = jnp.float32
    sums = ((frag_size, rows, LANES), (returns_count, rows, LANES))
    out_shape = [jax.ShapeDtypeStruct(sum_shape, f32) for sum_shape in sums]
    out_specs, scratch = [vmem] * 2, []
    if second_part:
        out_shape = [jax.ShapeDtypeStruct((groups // 2, frag_size, rows // groups, LANES), f32)] * 2
        for count in (orb_dev, 1, orb_dev - 1, 1, orb_dev - 1):
            out_shape.append(jax.ShapeDtypeStruct((count, rows, LANES), f32))
        out_specs = [hbm] * 7
        scratch = [pltpu.VMEM(sum_shape, f32) for sum_shape in sums]
        scratch += [pltpu.SemaphoreType.DMA((2,)), pltpu.SemaphoreType.DMA((groups + 5,))]
    return pl.pallas_call(
        functools.partial(pair_kernel, shape, second_part),
        out_shape=out_shape,
        in_specs=[smem] + [hbm] * (3 + groups + len(far) + len(before)),
        out_specs=out_specs,
        scratch_shapes=scratch
        + [
            pltpu.VMEM((2, 2, edge, plane), f32),
            pltpu.VMEM((2, edge, plane), f32),
            pltpu.VMEM((2, chunks, 3 * edge, LANES), f32),
            pltpu.VMEM((2, chunks, edge, LANES), f32),
            pltpu.VMEM((2, chunks, 3 * edge, LANES), f32),
            pltpu.VMEM((2, height * edge, LANES), f32),
            pltpu.VMEM((2, height * edge, LANES), f32),
            pltpu.VMEM((4, -(-chunks // ROWS) * ROWS, LANES), f32),
            pltpu.SMEM((slots,), jnp.int32),
            pltpu.SemaphoreType.DMA((2, 2)),
            *[pltpu.VMEM(table.shape, table.dtype) for table in tables],
            pltpu.SemaphoreType.DMA((3,)),
        ],
        compiler_params=pltpu.CompilerParams(vmem_limit_bytes=30 << 20),
        name="late_pair_terms" if second_part else "early_pair_terms",
    )(numbers, *tables, *pieces, *far, *before)


def flatten_kernel(shape, places_ref, *refs):
    edge, orb_dev, groups = shape
    pieces, (flat_ref, slab_ref) = refs[:groups], refs[groups:]
    member = places_ref[1]
    chunks = edge * edge // LANES
    slab = slab_ref.shape[1]
    for k in range(groups):
        for o in range(orb_dev):
            def move(j, _):
                value = pieces[k][o, :, pl.ds(pl.multiple_of(j * LANES, LANES), LANES)]
                for t in range(edge // ROWS):
                    at = pl.ds(t * (ROWS * chunks) + j, ROWS, stride=chunks)
                    flat_ref[k * orb_dev + o, at, :] = value[t * ROWS : (t + 1) * ROWS]
                return 0

            lax.fori_loop(0, chunks, move, 0)
    slab_ref[...] = flat_ref[:, pl.ds(pl.multiple_of(member * slab, ROWS), slab), :]


def flatten_terms(places, pieces):
    orb_dev, edge, plane = pieces[0].shape
    groups = len(pieces)
    rows = edge * plane // LANES
    frag_size = groups * orb_dev
    smem = pl.BlockSpec(memory_space=pltpu.SMEM)
    vmem = pl.BlockSpec(memory_space=pltpu.VMEM)
    return pl.pallas_call(
        functools.partial(flatten_kernel, (edge, orb_dev, groups)),
        out_shape=(
            jax.ShapeDtypeStruct((frag_size, rows, LANES), jnp.float32),
            jax.ShapeDtypeStruct((frag_size, rows // groups, LANES), jnp.float32),
        ),
        in_specs=[smem] + [vmem] * groups,
        out_specs=(vmem, vmem),
        compiler_params=pltpu.CompilerParams(vmem_limit_bytes=24 << 20),
        name="flatten_terms",
    )(places, *pieces)


def products(lefts, rights, length, step):
    def add(i, sums):
        at = pl.ds(pl.multiple_of(i * step, ROWS), step)
        right = [ref[index, at, :].reshape(step // ROWS, ROWS, LANES) for ref, index in rights]
        out = []
        for n, (ref, index) in enumerate(lefts):
            left = ref[index, at, :].reshape(step // ROWS, ROWS, LANES)
            for m in range(len(rights)):
                out.append(sums[n * len(rights) + m] + jnp.sum(left * right[m], axis=0))
        return tuple(out)

    zero = jnp.zeros((ROWS, LANES), jnp.float32)
    return lax.fori_loop(0, length // step, add, (zero,) * (len(lefts) * len(rights)))


def placed(result, sums, rows, lanes):
    row = lax.broadcasted_iota(jnp.int32, result.shape, 0)
    lane = lax.broadcasted_iota(jnp.int32, result.shape, 1)
    for n, a in enumerate(rows):
        for m, b in enumerate(lanes):
            value = jnp.sum(sums[n * len(lanes) + m], keepdims=True)
            result = jnp.where((row == a) & (lane == b), result + value, result)
    return result


def step_of(length):
    return next(n for n in (72, 24, 8) if length % n == 0)


def action_kernel(shape, places_ref, phi_ref, kept_ref, *refs):
    orb_dev, groups, parts = shape
    arrived, (act_ref, share_ref) = refs[:parts], refs[parts:]
    member = places_ref[1]
    frag_size = orb_dev * groups
    slab = act_ref.shape[1]
    cut = frag_size // parts
    for i in range(parts):
        span = slice(i * cut, (i + 1) * cut)
        act_ref[span] = kept_ref[0, span] + arrived[i][0]
    rows = [(member ^ (a // orb_dev)) * orb_dev + a % orb_dev for a in range(frag_size)]
    result = jnp.zeros(share_ref.shape, jnp.float32)
    for half in range(0, frag_size, 4):
        bs = range(half, min(half + 4, frag_size))
        lefts, rights = [(phi_ref, a) for a in range(frag_size)], [(act_ref, b) for b in bs]
        result = placed(result, products(lefts, rights, slab, step_of(slab)), rows, bs)
    share_ref[...] = result


def action_terms(places, orb_dev, phi, kept, arrived):
    frag_size, slab = phi.shape[:2]
    smem = pl.BlockSpec(memory_space=pltpu.SMEM)
    vmem = pl.BlockSpec(memory_space=pltpu.VMEM)
    return pl.pallas_call(
        functools.partial(action_kernel, (orb_dev, frag_size // orb_dev, len(arrived))),
        out_shape=(
            jax.ShapeDtypeStruct((frag_size, slab, LANES), jnp.float32),
            jax.ShapeDtypeStruct((frag_size, LANES), jnp.float32),
        ),
        in_specs=[smem] + [vmem] * (2 + len(arrived)),
        out_specs=(vmem, vmem),
        compiler_params=pltpu.CompilerParams(vmem_limit_bytes=16 << 20),
        name="action_terms",
    )(places, phi, kept, *arrived)


def home_kernel(shape, places_ref, flat_ref, own_ref, *refs):
    edge, orb_dev, groups, first, count = shape
    if first == 0:
        (two_ref, twin_ref, relay_ref, share_ref), refs = refs[:4], refs[4:]
    else:
        (two_ref, one_ref), refs = refs[:2], refs[2:]
    outs, total = refs[:groups], refs[groups]
    fragment, member = places_ref[0], places_ref[1]
    frag_size = orb_dev * groups
    rows = flat_ref.shape[1]
    slab = rows // groups
    for i in range(count):
        value = own_ref[first + i] + two_ref[i]
        if first == 0:
            @pl.when(lax.rem(fragment, 2) == 1)
            def _():
                total[i] = value + twin_ref[i]

            @pl.when(lax.rem(fragment, 2) == 0)
            def _():
                total[i] = value + relay_ref[i]
        else:
            total[i] = value + one_ref[i]
    lefts, rights = [(flat_ref, a) for a in range(frag_size)], [(total, i) for i in range(count)]
    places = [(member ^ (a // orb_dev)) * orb_dev + a % orb_dev for a in range(frag_size)]
    result = share_ref[...] if first == 0 else jnp.zeros((frag_size, LANES), jnp.float32)
    sums = products(lefts, rights, rows, step_of(rows))
    result = placed(result, sums, places, [member * orb_dev + first + i for i in range(count)])
    result = result * (1.0 / float(edge**3))
    for k in range(groups):
        begin = pl.multiple_of((member ^ k) * slab, ROWS)
        for i in range(count):
            outs[k][i * slab : (i + 1) * slab, :] = total[i, pl.ds(begin, slab), :]
        outs[k][count * slab :, :] = result


def home_terms(places, edge, groups, flat, own, first, *came):
    frag_size, rows = flat.shape[:2]
    count = came[0].shape[0]
    smem = pl.BlockSpec(memory_space=pltpu.SMEM)
    vmem = pl.BlockSpec(memory_space=pltpu.VMEM)
    f32 = jnp.float32
    parcel = jax.ShapeDtypeStruct((count * rows // groups + frag_size, LANES), f32)
    return pl.pallas_call(
        functools.partial(home_kernel, (edge, frag_size // groups, groups, first, count)),
        out_shape=[parcel] * groups,
        in_specs=[smem] + [vmem] * (2 + len(came)),
        out_specs=[vmem] * groups,
        scratch_shapes=[pltpu.VMEM((count, rows, LANES), f32)],
        compiler_params=pltpu.CompilerParams(vmem_limit_bytes=16 << 20),
        name="home_terms",
    )(places, flat, own, *came)


def exchanged(value, axis, width):
    size = value.shape[axis]
    index = lax.broadcasted_iota(jnp.int32, value.shape, axis)
    below, above = pltpu.roll(value, width, axis), pltpu.roll(value, size - width, axis)
    return jnp.where((index & width) != 0, below, above)


def gradient_kernel(shape, places_ref, act_ref, phi_ref, *refs):
    edge, orb_dev, groups = shape
    heads, tails, refs = refs[:groups], refs[groups : 2 * groups], refs[2 * groups :]
    out_ref, lagrange_ref, hold = refs
    member = places_ref[1]
    frag_size = orb_dev * groups
    chunks = edge * edge // LANES
    slab_rows = edge // groups
    slab = slab_rows * chunks
    sums = [
        head[slab:, :] + tail[(orb_dev - 1) * slab :, :] for head, tail in zip(heads, tails)
    ]
    while len(sums) > 1:
        sums = [sums[i] + sums[i + 1] for i in range(0, len(sums), 2)]
    square = jnp.concatenate([sums[0], jnp.zeros((LANES - frag_size, LANES), jnp.float32)], axis=0)
    lagrange = 0.5 * (square + square.T)[:frag_size, :]
    lagrange_ref[...] = lagrange[:, :frag_size]
    bit = 1
    while bit < groups:
        turned = exchanged(exchanged(lagrange, 0, bit * orb_dev), 1, bit * orb_dev)
        lagrange = jnp.where((member & bit) != 0, turned, lagrange)
        bit *= 2

    for k in range(groups):
        for o in range(orb_dev):
            a = (member ^ k) * orb_dev + o
            came = heads[k][:slab, :] if o == 0 else tails[k][(o - 1) * slab : o * slab, :]
            value = act_ref[a] + came
            for b in range(frag_size):
                factor = lagrange[b : b + 1, k * orb_dev + o : k * orb_dev + o + 1]
                value = value - factor * phi_ref[b]
            hold[pl.ds(pl.multiple_of(a * slab, ROWS), slab), :] = value
    for x in range(slab_rows):
        for j in range(chunks):
            value = hold[pl.ds(x * chunks + j, frag_size, stride=slab), :]
            out_ref[x, :, j * LANES : (j + 1) * LANES] = value


def gradient_terms(places, edge, act, phi, heads, tails):
    groups = len(heads)
    frag_size, slab = act.shape[:2]
    smem = pl.BlockSpec(memory_space=pltpu.SMEM)
    vmem = pl.BlockSpec(memory_space=pltpu.VMEM)
    f32 = jnp.float32
    gradient, lagrange = pl.pallas_call(
        functools.partial(gradient_kernel, (edge, frag_size // groups, groups)),
        out_shape=(
            jax.ShapeDtypeStruct((edge // groups, frag_size, edge * edge), f32),
            jax.ShapeDtypeStruct((frag_size, frag_size), f32),
        ),
        in_specs=[smem] + [vmem] * (2 + 2 * groups),
        out_specs=(vmem, vmem),
        scratch_shapes=[pltpu.VMEM((frag_size * slab, LANES), f32)],
        compiler_params=pltpu.CompilerParams(vmem_limit_bytes=16 << 20),
        name="gradient_terms",
    )(places, act, phi, *heads, *tails)
    return gradient.transpose(1, 0, 2), lagrange


def together(*arrays):
    return lax.optimization_barrier(arrays)


def to_fragment(block, distance, senders=None):
    devices = lax.axis_size("orb")
    senders = range(devices) if senders is None else range(senders, devices, 2)
    return lax.ppermute(block, "orb", [(i, (i + distance) % devices) for i in senders])


def with_twin(block):
    return lax.ppermute(block, "orb", [(i, i ^ 1) for i in range(lax.axis_size("orb"))])


def with_member(block, bit):
    return lax.ppermute(block, "grp", [(i, i ^ bit) for i in range(lax.axis_size("grp"))])


def by_member(parcels, after=None):
    groups = len(parcels)
    received = list(parcels)
    bit = groups // 2
    while bit:
        for k in reversed(range(groups)):
            if k & bit:
                received[k] = with_member(received[k], bit)
        if after is not None and bit == groups // 2:
            after, *received[bit:] = together(after, *received[bit:])
        bit //= 2
    return received, after


def shards(orbitals, kernel, anchors, pair_count, pair_first, pair_second, pair_reach):
    groups = lax.axis_size("grp")
    orb_dev, edge, plane = orbitals.shape
    places = jnp.stack([lax.axis_index("orb"), lax.axis_index("grp")]).astype(jnp.int32)

    numbers = [places, pair_count, pair_first, pair_second, pair_reach, anchors.reshape(-1)]
    screen, numbers, *tables = screen_terms(jnp.concatenate(numbers), kernel)
    two = to_fragment(orbitals, -2)
    twin = with_twin(orbitals[:1])
    pieces = {0: orbitals}
    bit = groups // 2
    while bit:
        for k in list(pieces):
            pieces[k ^ bit] = with_member(pieces[k], bit)
        if bit == groups // 2:
            two, twin, tail, pieces[bit], screen, numbers, *tables = together(
                two, twin, orbitals[1:], pieces[bit], screen, numbers, *tables
            )
            one = to_fragment(tail, -1)
            relay = to_fragment(twin, -2, 1)
        bit //= 2
    pieces = [pieces[k] for k in range(groups)]
    tables = [screen, *tables]
    sizes = (anchors.shape[0], pair_first.shape[0])
    before = pair_terms(numbers, *sizes, tables, pieces, [twin, two])
    kept, sent, own, one_head, one_tail, two_head, two_tail = pair_terms(
        numbers, *sizes, tables, pieces, [twin, two, relay, one], before
    )

    two_tail = to_fragment(two_tail, 2)
    twin = with_twin(one_head)
    bit = 1
    arrived = with_member(sent, bit)
    while 2 * bit < groups:
        kept = kept + arrived
        if bit == 1:
            _, twin, one_tail = together(kept, twin, one_tail)
        half = kept.shape[0] // 2
        bit *= 2
        arrived, kept = with_member(kept[half:], bit), kept[:half]
    one_tail = to_fragment(one_tail, 1)
    relay = to_fragment(twin, 2, 0)
    two_tail, two_head = together(two_tail, two_head)
    two_head = to_fragment(two_head, 2)

    flat, phi = flatten_terms(places, pieces)
    tails = home_terms(places, edge, groups, flat, own, 1, two_tail, one_tail)
    tails, two_head = by_member(tails, two_head)
    act, share = action_terms(places, orb_dev, phi, kept, [arrived])
    heads, _ = by_member(
        home_terms(places, edge, groups, flat, own, 0, two_head, twin, relay, share)
    )
    gradient, lagrange = gradient_terms(places, edge, act, phi, heads, tails)
    return (gradient, lagrange[None])


def solution(mesh):
    placed = (P(("orb", "grp"), None, None), P(), P(), P("orb"), P("orb"), P("orb"), P("orb"))
    return jax.shard_map(
        shards,
        mesh=mesh,
        in_specs=placed,
        out_specs=(P("orb", "grp", None), P("orb", None, None)),
        check_vma=False,
    )
```

```python
import functools
import math

import jax
import jax.numpy as jnp
import numpy as np
from jax import lax
from jax.experimental import pallas as pl
from jax.experimental.pallas import tpu as pltpu
from jax.sharding import PartitionSpec as P

REACH = 2
LANES = 128
ROWS = 8
HALF = LANES // 2


class Number:
    def __init__(self, real, imag=None):
        self.real, self.imag = real, imag

    def __add__(self, other):
        if self.imag is None or other.imag is None:
            imag = self.imag if other.imag is None else other.imag
        else:
            imag = self.imag + other.imag
        return Number(self.real + other.real, imag)

    def __sub__(self, other):
        if other.imag is None:
            imag = self.imag
        else:
            imag = -other.imag if self.imag is None else self.imag - other.imag
        return Number(self.real - other.real, imag)

    def conj(self):
        return self if self.imag is None else Number(self.real, -self.imag)

    def scaled(self, factor):
        return Number(self.real * factor, None if self.imag is None else self.imag * factor)

    def turned(self, sign):
        if self.imag is None:
            return Number(jnp.zeros_like(self.real), self.real if sign > 0 else -self.real)
        return Number(-self.imag, self.real) if sign > 0 else Number(self.imag, -self.real)

    def plus_turned(self, other, sign):
        if sign < 0:
            return self.minus_turned(other)
        real = self.real if other.imag is None else self.real - other.imag
        return Number(real, other.real if self.imag is None else self.imag + other.real)

    def minus_turned(self, other):
        real = self.real if other.imag is None else self.real + other.imag
        return Number(real, -other.real if self.imag is None else self.imag - other.real)

    def times(self, angle):
        real, imag = math.cos(angle), math.sin(angle)
        if abs(imag) < 1e-12:
            return self if real > 0 else self.scaled(-1.0)
        if abs(real) < 1e-12:
            return self.turned(imag)
        if self.imag is None:
            return Number(self.real * real, self.real * imag)
        return Number(self.real * real - self.imag * imag, self.real * imag + self.imag * real)


def coprime(n):
    for p in (2, 3, 5, 7):
        power = 1
        while n % (power * p) == 0:
            power *= p
        if 1 < power < n:
            return power, n // power
    return None


def radix(n):
    return next((p for p in (4, 2, 3, 5, 7) if n % p == 0 and n > p), None)


def meeting(i, j, first, second):
    return next(k for k in range(first * second) if k % first == i and k % second == j)


def dft(values, sign):
    n = len(values)
    if n == 1:
        return values
    if n == 2:
        return [values[0] + values[1], values[0] - values[1]]
    if n == 3:
        a, b, c = values
        total, side = b + c, (b - c).scaled(math.sqrt(0.75))
        middle = a - total.scaled(0.5)
        return [a + total, middle.plus_turned(side, sign), middle.plus_turned(side, -sign)]
    if n == 4:
        a, b, c, d = values
        s, t, u, v = a + c, a - c, b + d, b - d
        return [s + u, t.plus_turned(v, sign), s - u, t.plus_turned(v, -sign)]
    out = [None] * n
    if coprime(n):
        first, second = coprime(n)
        columns = [
            dft([values[(i * second + j * first) % n] for i in range(first)], sign)
            for j in range(second)
        ]
        for i in range(first):
            row = dft([column[i] for column in columns], sign)
            for j in range(second):
                out[meeting(i, j, first, second)] = row[j]
        return out
    p = radix(n)
    if p:
        rest = n // p
        columns = [dft(values[j::p], sign) for j in range(p)]
        for i in range(rest):
            row = dft(
                [columns[j][i].times(sign * 2.0 * math.pi * i * j / n) for j in range(p)], sign
            )
            for j in range(p):
                out[i + rest * j] = row[j]
        return out
    for k in range(n):
        total = values[0]
        for j in range(1, n):
            total = total + values[j].times(sign * 2.0 * math.pi * (j * k % n) / n)
        out[k] = total
    return out


def real_dft(values):
    n = len(values)
    if n <= 4:
        out = dft(values, -1)
    else:
        out = [None] * n
        if coprime(n):
            first, second = coprime(n)
            columns = [
                real_dft([values[(i * second + j * first) % n] for i in range(first)])
                for j in range(second)
            ]
            for i in range(first // 2 + 1):
                entries = [column[i] for column in columns]
                alone = 2 * i % first == 0
                row = real_dft(entries) if alone else dft(entries, -1)
                for j in range(second):
                    out[meeting(i, j, first, second)] = row[j]
        elif radix(n):
            p = radix(n)
            rest = n // p
            columns = [real_dft(values[j::p]) for j in range(p)]
            for i in range(rest // 2 + 1):
                row = dft(
                    [columns[j][i].times(-2.0 * math.pi * i * j / n) for j in range(p)], -1
                )
                for j in range(p):
                    out[i + rest * j] = row[j]
        else:
            out = dft(values, -1)
    for k in range(1, n):
        if out[k] is None or (k > n // 2 and out[n - k] is not None):
            out[k] = out[n - k].conj()
    out[0] = Number(out[0].real)
    if n % 2 == 0:
        out[n // 2] = Number(out[n // 2].real)
    return out


def real_back(values):
    n = len(values)
    if n == 1:
        return [values[0].real]
    if n == 2:
        return [values[0].real + values[1].real, values[0].real - values[1].real]
    if n == 3:
        a, b = values[0].real, values[1]
        side = b.imag * math.sqrt(3.0)
        middle = a - b.real
        return [a + 2.0 * b.real, middle - side, middle + side]
    if n == 4:
        s, t = values[0].real + values[2].real, values[0].real - values[2].real
        u, v = 2.0 * values[1].real, 2.0 * values[1].imag
        return [s + u, t - v, s - u, t + v]
    out = [None] * n
    if coprime(n):
        first, second = coprime(n)
        rows = []
        for i in range(first // 2 + 1):
            entries = [values[meeting(i, j, first, second)] for j in range(second)]
            if 2 * i % first == 0:
                rows.append([Number(value) for value in real_back(entries)])
            else:
                rows.append(dft(entries, 1))
        for b in range(second):
            half = [row[b] for row in rows]
            whole = half + [half[first - i].conj() for i in range(len(half), first)]
            for a, value in enumerate(real_back(whole)):
                out[(a * second + b * first) % n] = value
        return out
    p = radix(n)
    if p:
        rest = n // p
        parts = []
        for i in range(p // 2 + 1):
            entries = values[i::p]
            if i == 0:
                parts.append([Number(value) for value in real_back(entries)])
            else:
                inner = dft(entries, 1)
                parts.append([inner[m].times(2.0 * math.pi * i * m / n) for m in range(rest)])
                if 2 * i == p:
                    parts[-1] = [Number(value.real) for value in parts[-1]]
        for m in range(rest):
            half = [part[m] for part in parts]
            whole = half + [half[p - i].conj() for i in range(len(half), p)]
            for j, value in enumerate(real_back(whole)):
                out[m + rest * j] = value
        return out
    return [value.real for value in dft(values, 1)]


def wave_table(edge):
    index = np.arange(edge)
    angles = 2.0 * np.pi / edge * (np.outer(index, index) % edge)
    full = np.zeros((2, 2, HALF, 2, HALF))
    for side in range(2):
        full[0, side, :edge, side, :edge] = np.cos(angles)
        full[1, side, :edge, side, :edge] = np.sin(angles)
    full = full.reshape(2, LANES, LANES)
    high = full.astype(jnp.bfloat16)
    low = (full - high.astype(np.float64)).astype(jnp.bfloat16)
    return np.stack([high, low])


def split_dot(real, imag, matrix):
    value = jnp.concatenate([real, imag], axis=1)
    high = value.astype(jnp.bfloat16)
    low = (value - high.astype(jnp.float32)).astype(jnp.bfloat16)
    product = jnp.dot(
        jnp.concatenate([high, low, high], axis=1), matrix[...], preferred_element_type=jnp.float32
    )
    return product[:, :LANES], product[:, LANES:]


def padded_half(edge):
    return -(-(edge // 2 + 1) // ROWS) * ROWS


def screen_kernel(edge, numbers_ref, kernel_ref, waves_ref, out_ref, kept_ref, ahead_ref, behind_ref, flipped):
    for i in range(numbers_ref.shape[0]):
        kept_ref[i] = numbers_ref[i]
    for table, sign in ((ahead_ref, -1), (behind_ref, 1)):
        for part, source in enumerate((0, 0, 1)):
            for i in range(2):
                for j in range(2):
                    value = waves_ref[source, (i + j) % 2]
                    if i != j and (i > j) == (sign > 0):
                        value = -value
                    rows = slice((2 * part + i) * LANES, (2 * part + i + 1) * LANES)
                    table[rows, j * LANES : (j + 1) * LANES] = value
    exact = dict(precision=lax.Precision.HIGHEST, preferred_element_type=jnp.float32)

    def index(shape, axis):
        return lax.broadcasted_iota(jnp.int32, shape, axis)

    square, whole = (edge, edge), (LANES, LANES)
    flip = index(square, 0) + index(square, 1)
    flip = ((flip == 0) | (flip == edge)).astype(jnp.float32)
    source, target = index(whole, 0), index(whole, 1)
    target = jnp.where(target < HALF, target, target - HALF)
    mirror = ((source + target == 0) | (source + target == edge)) & (source < edge) & (target < edge)
    mirror = mirror.astype(jnp.float32)
    flipped[...] = jnp.dot(flip, kernel_ref[...], **exact)
    height = padded_half(edge)
    lane = index((edge, LANES), 1)
    out_ref[...] = jnp.zeros_like(out_ref)

    def piece(ref, y):
        begin, offset = divmod(y * edge, LANES)
        value = ref[:, begin * LANES : (begin + 1) * LANES]
        value = pltpu.roll(value, LANES - offset, 1) if offset else value
        if offset + edge > LANES:
            more = ref[:, (begin + 1) * LANES : (begin + 2) * LANES]
            value = jnp.where(lane < LANES - offset, value, pltpu.roll(more, LANES - offset, 1))
        return value

    for y in range(edge // 2 + 1):
        value = piece(kernel_ref, y)
        value = jnp.where(lane < HALF, value, pltpu.roll(value, HALF, 1))
        value = value + jnp.dot(piece(flipped, (edge - y) % edge), mirror, **exact)
        value = value * (0.5 / float(edge**3))
        for t in range(edge // ROWS):
            at = pl.ds(t * ROWS * height + y, ROWS, stride=height)
            out_ref[at, :] = value[t * ROWS : (t + 1) * ROWS]


def screen_terms(numbers, kernel):
    edge, plane = kernel.shape
    smem = pl.BlockSpec(memory_space=pltpu.SMEM)
    vmem = pl.BlockSpec(memory_space=pltpu.VMEM)
    table = jax.ShapeDtypeStruct((6 * LANES, 2 * LANES), jnp.bfloat16)
    return pl.pallas_call(
        functools.partial(screen_kernel, edge),
        out_shape=[
            jax.ShapeDtypeStruct((edge * padded_half(edge), LANES), jnp.float32),
            jax.ShapeDtypeStruct(numbers.shape, numbers.dtype),
            table,
            table,
        ],
        in_specs=[smem, vmem, vmem],
        out_specs=[vmem, smem, vmem, vmem],
        scratch_shapes=[pltpu.VMEM((edge, plane), jnp.float32)],
        compiler_params=pltpu.CompilerParams(vmem_limit_bytes=8 << 20),
        name="screen_terms",
    )(numbers, kernel, jnp.asarray(wave_table(edge)))


def pair_kernel(shape, second_part, numbers_ref, *refs):
    edge, orb_dev, groups, fragments, slots = shape
    plane = edge * edge
    chunks = plane // LANES
    tiles = edge // ROWS
    half = edge // 2 + 1
    height = padded_half(edge)
    tables, refs = refs[:3], refs[3:]
    phi_refs, refs = refs[:groups], refs[groups:]
    if second_part:
        (twin_ref, relay_ref, one_ref, act_before, back_before), refs = refs[:5], refs[5:]
        act_outs, back_outs, refs = refs[:2], refs[2:5], refs[5:]
        (act, back, state_sem, out_sem), refs = refs[:4], refs[4:]
    else:
        (twin_ref, two_ref, act), back_outs, refs = refs[:3], refs[3:6], refs[6:]
        (back, out_sem), refs = refs[:2], refs[2:]
    (near, far, wide, moved, dense, lower, upper, masks, listed, load_sem) = refs[:10]
    screen_ref, ahead_ref, behind_ref, table_sem = refs[10:]

    fragment, member, live_slots = numbers_ref[0], numbers_ref[1], numbers_ref[2]

    def first_of(slot):
        return numbers_ref[3 + slot]

    def second_of(slot):
        return numbers_ref[3 + slots + slot]

    def reach_of(slot):
        return numbers_ref[3 + 2 * slots + slot]

    def anchor(place, axis):
        return numbers_ref[3 + 3 * slots + 3 * place + axis]

    table_copies = [
        pltpu.make_async_copy(table, hold, table_sem.at[i])
        for i, (table, hold) in enumerate(zip(tables, refs[10:13]))
    ]
    lane = lax.broadcasted_iota(jnp.int32, (1, LANES), 1)
    stretch = next(n for n in (6, 4, 3, 2, 1) if chunks % n == 0)
    middle = pl.ds(edge, edge)

    even = lax.rem(fragment, 2) == 0

    def is_mine(slot):
        return (slot < live_slots) & (lax.div(second_of(slot), orb_dev) == member)

    def list_farthest(slot, found):
        chosen = is_mine(slot) & (reach_of(slot) == 2)

        @pl.when(chosen)
        def _():
            listed[found] = slot

        return found + chosen.astype(jnp.int32)

    farthest = lax.fori_loop(0, slots, list_farthest, jnp.int32(0))
    room = jnp.maximum(2, 2 * lax.div(farthest + 1, 2)) - farthest

    def list_others(slot, counts):
        early, found = counts
        mine = is_mine(slot) & (reach_of(slot) < 2)
        come = (reach_of(slot) == 0) | (even & (lax.rem(second_of(slot), orb_dev) == 0))
        taken = mine & come & (early < room)
        chosen = mine & jnp.logical_not(taken) if second_part else taken

        @pl.when(chosen)
        def _():
            listed[found] = slot

        return early + taken.astype(jnp.int32), found + chosen.astype(jnp.int32)

    begun = jnp.int32(0) if second_part else farthest
    _, found = lax.fori_loop(0, slots, list_others, (jnp.int32(0), begun))
    turns = lax.div(found + 1, 2)

    def slot_of(turn, side):
        at = 2 * turn + side
        live = at < found
        return listed[jnp.where(live, at, 2 * turn)], live

    def far_copy(side, source):
        return pltpu.make_async_copy(source, far.at[side], load_sem.at[1, side])

    def start_loads(turn):
        for side in range(2):
            slot, _ = slot_of(turn, side)
            first, second, reach = first_of(slot), second_of(slot), reach_of(slot)
            relative = lax.div(first, orb_dev) ^ member
            for k in range(groups):
                @pl.when(relative == k)
                def _():
                    pltpu.make_async_copy(
                        phi_refs[k].at[lax.rem(first, orb_dev)],
                        near.at[lax.rem(turn, 2), side],
                        load_sem.at[0, side],
                    ).start()
            own = lax.rem(second, orb_dev)

            @pl.when(reach == 0)
            def _():
                far_copy(side, phi_refs[0].at[own]).start()

            @pl.when((reach == 1) & (own == 0) & even)
            def _():
                far_copy(side, twin_ref.at[0]).start()

            if not second_part:
                @pl.when(reach == 2)
                def _():
                    far_copy(side, two_ref.at[own]).start()

            if second_part:
                @pl.when((reach == 1) & (own == 0) & jnp.logical_not(even))
                def _():
                    far_copy(side, relay_ref.at[0]).start()

                @pl.when((reach == 1) & (own > 0))
                def _():
                    far_copy(side, one_ref.at[jnp.maximum(own - 1, 0)]).start()

    def wait_loads(turn):
        for side in range(2):
            pltpu.make_async_copy(
                phi_refs[0].at[0], near.at[lax.rem(turn, 2), side], load_sem.at[0, side]
            ).wait()
            far_copy(side, phi_refs[0].at[0]).wait()

    @pl.when(found > 0)
    def _():
        start_loads(0)
        for copy in table_copies:
            copy.start()

    if second_part:
        state_copies = [
            pltpu.make_async_copy(before, now, state_sem.at[i])
            for i, (before, now) in enumerate(((act_before, act), (back_before, back)))
        ]
        slab = plane * edge // LANES // groups
        act_copies = []
        for k in range(groups):
            source = (member ^ k) * slab
            place = reversed_bits(k, groups)
            act_copies.append(
                pltpu.make_async_copy(
                    act.at[:, pl.ds(pl.multiple_of(source, ROWS), slab), :],
                    act_outs[2 * place // groups].at[place % (groups // 2)],
                    out_sem.at[3 + k],
                )
            )
    else:
        act[...] = jnp.zeros_like(act)
        back[...] = jnp.zeros_like(back)

    def offset_of(slot):
        partner = lax.rem(fragment + reach_of(slot), fragments)
        return [anchor(partner, i) - anchor(fragment, i) for i in range(3)]

    def steps(count, body, most):
        width = max(n for n in range(1, most + 1) if count % n == 0)

        def step(i, _):
            for j in range(width):
                body(i * width + j)
            return 0

        if width == count:
            step(0, 0)
        else:
            lax.fori_loop(0, count // width, step, 0)

    def columns(k):
        return pl.ds(pl.multiple_of(k * LANES, LANES), LANES)

    def set_masks(place, delta, weight):
        shape = masks.shape[1:]
        spot = lax.broadcasted_iota(jnp.int32, shape, 0) * LANES
        spot = spot + lax.broadcasted_iota(jnp.int32, shape, 1)
        y = ((spot.astype(jnp.float32) + 0.5) * (1.0 / edge)).astype(jnp.int32)
        z = spot - y * edge - delta[2]
        y = y - delta[1]
        inside = (y >= 0) & (y < edge) & (z >= 0) & (z < edge)
        masks[place] = jnp.where(inside, weight, 0.0)

    def shifted(source, place, delta, begin, count, ks):
        shift = lax.rem(delta[1] * edge + delta[2] + 4 * plane, plane)
        start = lax.rem(plane - shift, plane)
        whole, part = lax.div(start, LANES), lax.rem(start, LANES)
        turn = lax.rem(LANES - part, LANES)
        down = edge - jnp.clip(delta[0], -edge, edge) + begin
        x = lax.broadcasted_iota(jnp.int32, (count, LANES), 0) + (begin - delta[0])
        rows_inside = (x >= 0) & (x < edge)
        first = lane < LANES - part

        def piece(k):
            return pltpu.roll(source[lax.rem(k + whole, chunks), pl.ds(down, count), :], turn, 1)

        out = []
        low = piece(ks[0])
        for k in ks:
            high = piece(k + 1)
            value = jnp.where(first, low, high) * masks[place, pl.ds(k, 1), :]
            out.append(jnp.where(rows_inside, value, 0.0))
            low = high
        return out

    def tile(t, i, size):
        return pl.ds(pl.multiple_of(i * size + t * ROWS, ROWS), ROWS)

    def across(t, i, size):
        return pl.ds(t * (ROWS * size) + i, ROWS, stride=size)

    def solve_two(turn, _):
        wait_loads(turn)
        if second_part:
            @pl.when(turn == 0)
            def _():
                for copy in state_copies:
                    copy.start()

        near_now = near.at[lax.rem(turn, 2)]
        picked = [slot_of(turn, side) for side in range(2)]
        offsets = [offset_of(slot) for slot, _ in picked]
        returns = [[-d for d in delta] for delta in offsets]
        for side in range(2):
            set_masks(side, offsets[side], picked[side][1].astype(jnp.float32))
            set_masks(2 + side, returns[side], 1.0)

        def widen(k):
            for side in range(2):
                wide[side, k, middle, :] = far[side, :, pl.ds(pl.multiple_of(k * LANES, LANES), LANES)]

        steps(chunks, widen, chunks)

        def over_y(t):
            densities = []
            begin = pl.multiple_of(t * ROWS, ROWS)
            rows = pl.ds(begin, ROWS)
            for side in range(2):
                values = shifted(wide.at[side], side, offsets[side], begin, ROWS, range(chunks))
                for k in range(chunks):
                    moved[side, k, rows, :] = values[k]
                    values[k] = values[k] * near_now[side, rows, k * LANES : (k + 1) * LANES]
                densities.append(values)
            planes = []
            for y in range(edge):
                first, offset = divmod(y * edge, LANES)
                sides = []
                for side in range(2):
                    shift = (side * HALF - offset) % LANES
                    value = densities[side][first]
                    value = pltpu.roll(value, shift, 1) if shift else value
                    if offset + edge > LANES:
                        more = densities[side][first + 1]
                        more = pltpu.roll(more, shift, 1) if shift else more
                        value = jnp.where(lane < side * HALF + LANES - offset, value, more)
                    sides.append(value)
                planes.append(Number(jnp.where(lane < HALF, sides[0], sides[1])))
            values = real_dft(planes)
            for i in range(half):
                at = tile(t, i, edge)
                lower[0, at, :] = values[i].real
                imag = values[i].imag
                lower[1, at, :] = jnp.zeros((ROWS, LANES), jnp.float32) if imag is None else imag

        steps(tiles, over_y, 3)

        @pl.when(turn == 0)
        def _():
            for copy in table_copies:
                copy.wait()

        @pl.when(turn + 1 < turns)
        def _():
            start_loads(turn + 1)

        def over_x(t):
            at = [across(t, i, edge) for i in range(edge)]
            values = dft([Number(lower[0, a, :], lower[1, a, :]) for a in at], -1)
            real = jnp.concatenate([value.real for value in values], axis=0)
            imag = jnp.concatenate([value.imag for value in values], axis=0)
            at = [tile(t, i, height) for i in range(edge)]
            factor = jnp.concatenate([screen_ref[a, :] for a in at], axis=0)
            real, imag = split_dot(real, imag, ahead_ref)
            real, imag = split_dot(real * factor, imag * factor, behind_ref)
            rows = [slice(i * ROWS, (i + 1) * ROWS) for i in range(edge)]
            values = dft([Number(real[r], imag[r]) for r in rows], 1)
            for i in range(edge):
                upper[0, at[i], :] = values[i].real
                upper[1, at[i], :] = values[i].imag

        steps(height // ROWS, over_x, 4)
        if second_part:
            @pl.when(turn == 0)
            def _():
                for copy in state_copies:
                    copy.wait()

        firsts = [first_of(slot) for slot, _ in picked]

        def back_y(t):
            begin = pl.multiple_of(t * ROWS, ROWS)
            rows = pl.ds(begin, ROWS)
            at = [across(t, i, height) for i in range(half)]
            values = [Number(upper[0, a, :], upper[1, a, :]) for a in at]
            values = values + [values[edge - i].conj() for i in range(half, edge)]
            planes = real_back(values)
            for side in range(2):
                forward = []
                for k in range(chunks):
                    value = None
                    for y in range(k * LANES // edge, edge):
                        begins = y * edge - k * LANES
                        if begins >= LANES:
                            break
                        shift = (begins - side * HALF) % LANES
                        piece = pltpu.roll(planes[y], shift, 1) if shift else planes[y]
                        value = piece if value is None else jnp.where(lane < begins, value, piece)
                    forward.append(value * moved[side, k, rows, :])
                    other = value * near_now[side, rows, k * LANES : (k + 1) * LANES]
                    dense[side, k, pl.ds(edge + begin, ROWS), :] = other
                at = [pl.ds(t * (ROWS * chunks) + k, ROWS, stride=chunks) for k in range(chunks)]
                sums = [act[firsts[side], at[k], :] + forward[k] for k in range(chunks)]
                for k in range(chunks):
                    act[firsts[side], at[k], :] = sums[k]

        steps(tiles, back_y, 3)

        if second_part:
            @pl.when(turn + 1 == turns)
            def _():
                for copy in act_copies:
                    copy.start()

        homes = []
        for side in range(2):
            slot = picked[side][0]
            homes.append(reach_of(slot) * orb_dev + lax.rem(second_of(slot), orb_dev))

        def send_back(g):
            for side in range(2):
                ks = [g * stretch + i for i in range(stretch)]
                values = shifted(dense.at[side], 2 + side, returns[side], 0, edge, ks)
                at = [
                    (i, t, pl.ds(t * (ROWS * chunks) + ks[i], ROWS, stride=chunks))
                    for i in range(stretch)
                    for t in range(tiles)
                ]
                sums = [
                    back[homes[side], a, :] + values[i][t * ROWS : (t + 1) * ROWS] for i, t, a in at
                ]
                for (i, t, a), value in zip(at, sums):
                    back[homes[side], a, :] = value

        steps(chunks // stretch, send_back, 3)
        return 0

    if second_part:
        @pl.when(found == 0)
        def _():
            for copy in state_copies:
                copy.start()
            for copy in state_copies:
                copy.wait()
            for copy in act_copies:
                copy.start()

    lax.fori_loop(0, turns, solve_two, 0)
    if second_part:
        spans = ((orb_dev, 1), (orb_dev + 1, orb_dev - 1), (0, orb_dev))
    else:
        spans = ((2 * orb_dev + 1, orb_dev - 1), (2 * orb_dev, 1), (0, 2 * orb_dev))
    copies = [
        pltpu.make_async_copy(back.at[pl.ds(begin, count)], back_outs[i], out_sem.at[i])
        for i, (begin, count) in enumerate(spans)
    ]
    for copy in copies:
        copy.start()
    if second_part:
        copies += act_copies
    for copy in copies:
        copy.wait()


def reversed_bits(k, count):
    bits = count.bit_length() - 1
    return sum(((k >> i) & 1) << (bits - 1 - i) for i in range(bits))


def pair_terms(numbers, fragments, slots, tables, pieces, far, before=()):
    second_part = bool(before)
    orb_dev, edge, plane = pieces[0].shape
    groups = len(pieces)
    frag_size = groups * orb_dev
    chunks = plane // LANES
    rows = edge * chunks
    height = padded_half(edge)
    shape = (edge, orb_dev, groups, fragments, slots)
    smem = pl.BlockSpec(memory_space=pltpu.SMEM)
    vmem = pl.BlockSpec(memory_space=pltpu.VMEM)
    hbm = pl.BlockSpec(memory_space=pltpu.HBM)
    f32 = jnp.float32

    def fields(*counts):
        return [jax.ShapeDtypeStruct((count, rows, LANES), f32) for count in counts]

    if second_part:
        out_shape = [jax.ShapeDtypeStruct((groups // 2, frag_size, rows // groups, LANES), f32)] * 2
        out_shape += fields(1, orb_dev - 1, orb_dev)
        out_specs = [hbm] * 5
        scratch = [pltpu.VMEM(field.shape, f32) for field in fields(frag_size, REACH * orb_dev)]
        scratch += [pltpu.SemaphoreType.DMA((2,)), pltpu.SemaphoreType.DMA((3 + groups,))]
    else:
        out_shape = fields(frag_size, orb_dev - 1, 1, REACH * orb_dev)
        out_specs = [vmem, hbm, hbm, hbm]
        scratch = [pltpu.VMEM(((REACH + 1) * orb_dev, rows, LANES), f32)]
        scratch += [pltpu.SemaphoreType.DMA((3,))]
    return pl.pallas_call(
        functools.partial(pair_kernel, shape, second_part),
        out_shape=out_shape,
        in_specs=[smem] + [hbm] * (3 + groups + len(far) + len(before)),
        out_specs=out_specs,
        scratch_shapes=scratch
        + [
            pltpu.VMEM((2, 2, edge, plane), f32),
            pltpu.VMEM((2, edge, plane), f32),
            pltpu.VMEM((2, chunks, 3 * edge, LANES), f32),
            pltpu.VMEM((2, chunks, edge, LANES), f32),
            pltpu.VMEM((2, chunks, 3 * edge, LANES), f32),
            pltpu.VMEM((2, height * edge, LANES), f32),
            pltpu.VMEM((2, height * edge, LANES), f32),
            pltpu.VMEM((4, -(-chunks // ROWS) * ROWS, LANES), f32),
            pltpu.SMEM((slots,), jnp.int32),
            pltpu.SemaphoreType.DMA((2, 2)),
            *[pltpu.VMEM(table.shape, table.dtype) for table in tables],
            pltpu.SemaphoreType.DMA((3,)),
        ],
        compiler_params=pltpu.CompilerParams(vmem_limit_bytes=30 << 20),
        name="late_pair_terms" if second_part else "early_pair_terms",
    )(numbers, *tables, *pieces, *far, *before)


def flatten_kernel(shape, places_ref, *refs):
    edge, orb_dev, groups = shape
    pieces, (flat_ref, slab_ref) = refs[:groups], refs[groups:]
    member = places_ref[1]
    chunks = edge * edge // LANES
    slab = slab_ref.shape[1]
    for k in range(groups):
        for o in range(orb_dev):
            def move(j, _):
                value = pieces[k][o, :, pl.ds(pl.multiple_of(j * LANES, LANES), LANES)]
                for t in range(edge // ROWS):
                    at = pl.ds(t * (ROWS * chunks) + j, ROWS, stride=chunks)
                    flat_ref[k * orb_dev + o, at, :] = value[t * ROWS : (t + 1) * ROWS]
                return 0

            lax.fori_loop(0, chunks, move, 0)
    slab_ref[...] = flat_ref[:, pl.ds(pl.multiple_of(member * slab, ROWS), slab), :]


def flatten_terms(places, pieces):
    orb_dev, edge, plane = pieces[0].shape
    groups = len(pieces)
    rows = edge * plane // LANES
    frag_size = groups * orb_dev
    smem = pl.BlockSpec(memory_space=pltpu.SMEM)
    vmem = pl.BlockSpec(memory_space=pltpu.VMEM)
    return pl.pallas_call(
        functools.partial(flatten_kernel, (edge, orb_dev, groups)),
        out_shape=(
            jax.ShapeDtypeStruct((frag_size, rows, LANES), jnp.float32),
            jax.ShapeDtypeStruct((frag_size, rows // groups, LANES), jnp.float32),
        ),
        in_specs=[smem] + [vmem] * groups,
        out_specs=(vmem, vmem),
        compiler_params=pltpu.CompilerParams(vmem_limit_bytes=24 << 20),
        name="flatten_terms",
    )(places, *pieces)


def products(lefts, rights, length, step):
    def add(i, sums):
        at = pl.ds(pl.multiple_of(i * step, ROWS), step)
        right = [ref[index, at, :].reshape(step // ROWS, ROWS, LANES) for ref, index in rights]
        out = []
        for n, (ref, index) in enumerate(lefts):
            left = ref[index, at, :].reshape(step // ROWS, ROWS, LANES)
            for m in range(len(rights)):
                out.append(sums[n * len(rights) + m] + jnp.sum(left * right[m], axis=0))
        return tuple(out)

    zero = jnp.zeros((ROWS, LANES), jnp.float32)
    return lax.fori_loop(0, length // step, add, (zero,) * (len(lefts) * len(rights)))


def placed(result, sums, rows, lanes):
    row = lax.broadcasted_iota(jnp.int32, result.shape, 0)
    lane = lax.broadcasted_iota(jnp.int32, result.shape, 1)
    for n, a in enumerate(rows):
        for m, b in enumerate(lanes):
            value = jnp.sum(sums[n * len(lanes) + m], keepdims=True)
            result = jnp.where((row == a) & (lane == b), result + value, result)
    return result


def step_of(length):
    return next(n for n in (72, 24, 8) if length % n == 0)


def action_kernel(shape, places_ref, phi_ref, kept_ref, *refs):
    orb_dev, groups, parts = shape
    arrived, (act_ref, share_ref) = refs[:parts], refs[parts:]
    member = places_ref[1]
    frag_size = orb_dev * groups
    slab = act_ref.shape[1]
    cut = frag_size // parts
    for i in range(parts):
        span = slice(i * cut, (i + 1) * cut)
        act_ref[span] = kept_ref[0, span] + arrived[i][0]
    rows = [(member ^ (a // orb_dev)) * orb_dev + a % orb_dev for a in range(frag_size)]
    result = jnp.zeros(share_ref.shape, jnp.float32)
    for half in range(0, frag_size, 4):
        bs = range(half, min(half + 4, frag_size))
        lefts, rights = [(phi_ref, a) for a in range(frag_size)], [(act_ref, b) for b in bs]
        result = placed(result, products(lefts, rights, slab, step_of(slab)), rows, bs)
    share_ref[...] = result


def action_terms(places, orb_dev, phi, kept, arrived):
    frag_size, slab = phi.shape[:2]
    smem = pl.BlockSpec(memory_space=pltpu.SMEM)
    vmem = pl.BlockSpec(memory_space=pltpu.VMEM)
    return pl.pallas_call(
        functools.partial(action_kernel, (orb_dev, frag_size // orb_dev, len(arrived))),
        out_shape=(
            jax.ShapeDtypeStruct((frag_size, slab, LANES), jnp.float32),
            jax.ShapeDtypeStruct((frag_size, LANES), jnp.float32),
        ),
        in_specs=[smem] + [vmem] * (2 + len(arrived)),
        out_specs=(vmem, vmem),
        compiler_params=pltpu.CompilerParams(vmem_limit_bytes=16 << 20),
        name="action_terms",
    )(places, phi, kept, *arrived)


def home_kernel(shape, places_ref, flat_ref, own_ref, *refs):
    edge, orb_dev, groups, first, count = shape
    if first == 0:
        (two_ref, twin_ref, relay_ref, share_ref), refs = refs[:4], refs[4:]
    else:
        (two_ref, one_ref), refs = refs[:2], refs[2:]
    outs, total = refs[:groups], refs[groups]
    fragment, member = places_ref[0], places_ref[1]
    frag_size = orb_dev * groups
    rows = flat_ref.shape[1]
    slab = rows // groups
    for i in range(count):
        value = own_ref[first + i] + two_ref[i]
        if first == 0:
            @pl.when(lax.rem(fragment, 2) == 1)
            def _():
                total[i] = value + twin_ref[i]

            @pl.when(lax.rem(fragment, 2) == 0)
            def _():
                total[i] = value + relay_ref[i]
        else:
            total[i] = value + one_ref[i]
    lefts, rights = [(flat_ref, a) for a in range(frag_size)], [(total, i) for i in range(count)]
    places = [(member ^ (a // orb_dev)) * orb_dev + a % orb_dev for a in range(frag_size)]
    result = share_ref[...] if first == 0 else jnp.zeros((frag_size, LANES), jnp.float32)
    sums = products(lefts, rights, rows, step_of(rows))
    result = placed(result, sums, places, [member * orb_dev + first + i for i in range(count)])
    result = result * (1.0 / float(edge**3))
    for k in range(groups):
        begin = pl.multiple_of((member ^ k) * slab, ROWS)
        for i in range(count):
            outs[k][i * slab : (i + 1) * slab, :] = total[i, pl.ds(begin, slab), :]
        outs[k][count * slab :, :] = result


def home_terms(places, edge, groups, flat, own, first, *came):
    frag_size, rows = flat.shape[:2]
    count = came[0].shape[0]
    smem = pl.BlockSpec(memory_space=pltpu.SMEM)
    vmem = pl.BlockSpec(memory_space=pltpu.VMEM)
    f32 = jnp.float32
    parcel = jax.ShapeDtypeStruct((count * rows // groups + frag_size, LANES), f32)
    return pl.pallas_call(
        functools.partial(home_kernel, (edge, frag_size // groups, groups, first, count)),
        out_shape=[parcel] * groups,
        in_specs=[smem] + [vmem] * (2 + len(came)),
        out_specs=[vmem] * groups,
        scratch_shapes=[pltpu.VMEM((count, rows, LANES), f32)],
        compiler_params=pltpu.CompilerParams(vmem_limit_bytes=16 << 20),
        name="home_terms",
    )(places, flat, own, *came)


def exchanged(value, axis, width):
    size = value.shape[axis]
    index = lax.broadcasted_iota(jnp.int32, value.shape, axis)
    below, above = pltpu.roll(value, width, axis), pltpu.roll(value, size - width, axis)
    return jnp.where((index & width) != 0, below, above)


def gradient_kernel(shape, places_ref, act_ref, phi_ref, *refs):
    edge, orb_dev, groups = shape
    heads, tails, refs = refs[:groups], refs[groups : 2 * groups], refs[2 * groups :]
    out_ref, lagrange_ref, hold = refs
    member = places_ref[1]
    frag_size = orb_dev * groups
    chunks = edge * edge // LANES
    slab_rows = edge // groups
    slab = slab_rows * chunks
    sums = [
        head[slab:, :] + tail[(orb_dev - 1) * slab :, :] for head, tail in zip(heads, tails)
    ]
    while len(sums) > 1:
        sums = [sums[i] + sums[i + 1] for i in range(0, len(sums), 2)]
    square = jnp.concatenate([sums[0], jnp.zeros((LANES - frag_size, LANES), jnp.float32)], axis=0)
    lagrange = 0.5 * (square + square.T)[:frag_size, :]
    lagrange_ref[...] = lagrange[:, :frag_size]
    bit = 1
    while bit < groups:
        turned = exchanged(exchanged(lagrange, 0, bit * orb_dev), 1, bit * orb_dev)
        lagrange = jnp.where((member & bit) != 0, turned, lagrange)
        bit *= 2

    for k in range(groups):
        for o in range(orb_dev):
            a = (member ^ k) * orb_dev + o
            came = heads[k][:slab, :] if o == 0 else tails[k][(o - 1) * slab : o * slab, :]
            value = act_ref[a] + came
            for b in range(frag_size):
                factor = lagrange[b : b + 1, k * orb_dev + o : k * orb_dev + o + 1]
                value = value - factor * phi_ref[b]
            hold[pl.ds(pl.multiple_of(a * slab, ROWS), slab), :] = value
    for x in range(slab_rows):
        for j in range(chunks):
            value = hold[pl.ds(x * chunks + j, frag_size, stride=slab), :]
            out_ref[x, :, j * LANES : (j + 1) * LANES] = value


def gradient_terms(places, edge, act, phi, heads, tails):
    groups = len(heads)
    frag_size, slab = act.shape[:2]
    smem = pl.BlockSpec(memory_space=pltpu.SMEM)
    vmem = pl.BlockSpec(memory_space=pltpu.VMEM)
    f32 = jnp.float32
    gradient, lagrange = pl.pallas_call(
        functools.partial(gradient_kernel, (edge, frag_size // groups, groups)),
        out_shape=(
            jax.ShapeDtypeStruct((edge // groups, frag_size, edge * edge), f32),
            jax.ShapeDtypeStruct((frag_size, frag_size), f32),
        ),
        in_specs=[smem] + [vmem] * (2 + 2 * groups),
        out_specs=(vmem, vmem),
        scratch_shapes=[pltpu.VMEM((frag_size * slab, LANES), f32)],
        compiler_params=pltpu.CompilerParams(vmem_limit_bytes=16 << 20),
        name="gradient_terms",
    )(places, act, phi, *heads, *tails)
    return gradient.transpose(1, 0, 2), lagrange


def together(*arrays):
    return lax.optimization_barrier(arrays)


def to_fragment(block, distance, senders=None):
    devices = lax.axis_size("orb")
    senders = range(devices) if senders is None else range(senders, devices, 2)
    return lax.ppermute(block, "orb", [(i, (i + distance) % devices) for i in senders])


def with_twin(block):
    return lax.ppermute(block, "orb", [(i, i ^ 1) for i in range(lax.axis_size("orb"))])


def with_member(block, bit):
    return lax.ppermute(block, "grp", [(i, i ^ bit) for i in range(lax.axis_size("grp"))])


def by_member(parcels):
    groups = len(parcels)
    received = list(parcels)
    bit = groups // 2
    while bit:
        for k in reversed(range(groups)):
            if k & bit:
                received[k] = with_member(received[k], bit)
        bit //= 2
    return received


def shards(orbitals, kernel, anchors, pair_count, pair_first, pair_second, pair_reach):
    groups = lax.axis_size("grp")
    orb_dev, edge, plane = orbitals.shape
    places = jnp.stack([lax.axis_index("orb"), lax.axis_index("grp")]).astype(jnp.int32)

    numbers = [places, pair_count, pair_first, pair_second, pair_reach, anchors.reshape(-1)]
    screen, numbers, *tables = screen_terms(jnp.concatenate(numbers), kernel)
    two = to_fragment(orbitals, -2)
    twin = with_twin(orbitals[:1])
    pieces = {0: orbitals}
    bit = groups // 2
    while bit:
        for k in list(pieces):
            pieces[k ^ bit] = with_member(pieces[k], bit)
        if bit == groups // 2:
            two, twin, tail, pieces[bit], screen, numbers, *tables = together(
                two, twin, orbitals[1:], pieces[bit], screen, numbers, *tables
            )
            one = to_fragment(tail, -1)
            relay = to_fragment(twin, -2, 1)
        bit //= 2
    pieces = [pieces[k] for k in range(groups)]
    tables = [screen, *tables]
    sizes = (anchors.shape[0], pair_first.shape[0])
    act, two_tail, two_head, back = pair_terms(numbers, *sizes, tables, pieces, [twin, two])
    two_tail = to_fragment(two_tail, 2)
    kept, sent, one_head, one_tail, own = pair_terms(
        numbers, *sizes, tables, pieces, [twin, relay, one], [act, back]
    )

    sent, two_tail, two_head = together(sent, two_tail, two_head)
    two_head = to_fragment(two_head, 2)
    twin = with_twin(one_head)
    bit = 1
    arrived = with_member(sent, bit)
    while 2 * bit < groups:
        kept = kept + arrived
        if bit == 1:
            _, twin, one_tail, two_head = together(kept, twin, one_tail, two_head)
        half = kept.shape[0] // 2
        bit *= 2
        arrived, kept = with_member(kept[half:], bit), kept[:half]
    one_tail = to_fragment(one_tail, 1)
    relay = to_fragment(twin, 2, 0)

    flat, phi = flatten_terms(places, pieces)
    tails = home_terms(places, edge, groups, flat, own, 1, two_tail, one_tail)
    tails = by_member(tails)
    act, share = action_terms(places, orb_dev, phi, kept, [arrived])
    heads = by_member(
        home_terms(places, edge, groups, flat, own, 0, two_head, twin, relay, share)
    )
    gradient, lagrange = gradient_terms(places, edge, act, phi, heads, tails)
    return (gradient, lagrange[None])


def solution(mesh):
    placed = (P(("orb", "grp"), None, None), P(), P(), P("orb"), P("orb"), P("orb"), P("orb"))
    return jax.shard_map(
        shards,
        mesh=mesh,
        in_specs=placed,
        out_specs=(P("orb", "grp", None), P("orb", None, None)),
        check_vma=False,
    )
```

```python
import functools
import math

import jax
import jax.numpy as jnp
import numpy as np
from jax import lax
from jax.experimental import pallas as pl
from jax.experimental.pallas import tpu as pltpu
from jax.sharding import PartitionSpec as P

REACH = 2
LANES = 128
ROWS = 8
HALF = LANES // 2


class Number:
    def __init__(self, real, imag=None):
        self.real, self.imag = real, imag

    def __add__(self, other):
        if self.imag is None or other.imag is None:
            imag = self.imag if other.imag is None else other.imag
        else:
            imag = self.imag + other.imag
        return Number(self.real + other.real, imag)

    def __sub__(self, other):
        if other.imag is None:
            imag = self.imag
        else:
            imag = -other.imag if self.imag is None else self.imag - other.imag
        return Number(self.real - other.real, imag)

    def conj(self):
        return self if self.imag is None else Number(self.real, -self.imag)

    def scaled(self, factor):
        return Number(self.real * factor, None if self.imag is None else self.imag * factor)

    def turned(self, sign):
        if self.imag is None:
            return Number(jnp.zeros_like(self.real), self.real if sign > 0 else -self.real)
        return Number(-self.imag, self.real) if sign > 0 else Number(self.imag, -self.real)

    def plus_turned(self, other, sign):
        if sign < 0:
            return self.minus_turned(other)
        real = self.real if other.imag is None else self.real - other.imag
        return Number(real, other.real if self.imag is None else self.imag + other.real)

    def minus_turned(self, other):
        real = self.real if other.imag is None else self.real + other.imag
        return Number(real, -other.real if self.imag is None else self.imag - other.real)

    def times(self, angle):
        real, imag = math.cos(angle), math.sin(angle)
        if abs(imag) < 1e-12:
            return self if real > 0 else self.scaled(-1.0)
        if abs(real) < 1e-12:
            return self.turned(imag)
        if self.imag is None:
            return Number(self.real * real, self.real * imag)
        return Number(self.real * real - self.imag * imag, self.real * imag + self.imag * real)


def coprime(n):
    for p in (2, 3, 5, 7):
        power = 1
        while n % (power * p) == 0:
            power *= p
        if 1 < power < n:
            return power, n // power
    return None


def radix(n):
    return next((p for p in (4, 2, 3, 5, 7) if n % p == 0 and n > p), None)


def meeting(i, j, first, second):
    return next(k for k in range(first * second) if k % first == i and k % second == j)


def dft(values, sign):
    n = len(values)
    if n == 1:
        return values
    if n == 2:
        return [values[0] + values[1], values[0] - values[1]]
    if n == 3:
        a, b, c = values
        total, side = b + c, (b - c).scaled(math.sqrt(0.75))
        middle = a - total.scaled(0.5)
        return [a + total, middle.plus_turned(side, sign), middle.plus_turned(side, -sign)]
    if n == 4:
        a, b, c, d = values
        s, t, u, v = a + c, a - c, b + d, b - d
        return [s + u, t.plus_turned(v, sign), s - u, t.plus_turned(v, -sign)]
    out = [None] * n
    if coprime(n):
        first, second = coprime(n)
        columns = [
            dft([values[(i * second + j * first) % n] for i in range(first)], sign)
            for j in range(second)
        ]
        for i in range(first):
            row = dft([column[i] for column in columns], sign)
            for j in range(second):
                out[meeting(i, j, first, second)] = row[j]
        return out
    p = radix(n)
    if p:
        rest = n // p
        columns = [dft(values[j::p], sign) for j in range(p)]
        for i in range(rest):
            row = dft(
                [columns[j][i].times(sign * 2.0 * math.pi * i * j / n) for j in range(p)], sign
            )
            for j in range(p):
                out[i + rest * j] = row[j]
        return out
    for k in range(n):
        total = values[0]
        for j in range(1, n):
            total = total + values[j].times(sign * 2.0 * math.pi * (j * k % n) / n)
        out[k] = total
    return out


def real_dft(values):
    n = len(values)
    if n <= 4:
        out = dft(values, -1)
    else:
        out = [None] * n
        if coprime(n):
            first, second = coprime(n)
            columns = [
                real_dft([values[(i * second + j * first) % n] for i in range(first)])
                for j in range(second)
            ]
            for i in range(first // 2 + 1):
                entries = [column[i] for column in columns]
                alone = 2 * i % first == 0
                row = real_dft(entries) if alone else dft(entries, -1)
                for j in range(second):
                    out[meeting(i, j, first, second)] = row[j]
        elif radix(n):
            p = radix(n)
            rest = n // p
            columns = [real_dft(values[j::p]) for j in range(p)]
            for i in range(rest // 2 + 1):
                row = dft(
                    [columns[j][i].times(-2.0 * math.pi * i * j / n) for j in range(p)], -1
                )
                for j in range(p):
                    out[i + rest * j] = row[j]
        else:
            out = dft(values, -1)
    for k in range(1, n):
        if out[k] is None or (k > n // 2 and out[n - k] is not None):
            out[k] = out[n - k].conj()
    out[0] = Number(out[0].real)
    if n % 2 == 0:
        out[n // 2] = Number(out[n // 2].real)
    return out


def real_back(values):
    n = len(values)
    if n == 1:
        return [values[0].real]
    if n == 2:
        return [values[0].real + values[1].real, values[0].real - values[1].real]
    if n == 3:
        a, b = values[0].real, values[1]
        side = b.imag * math.sqrt(3.0)
        middle = a - b.real
        return [a + 2.0 * b.real, middle - side, middle + side]
    if n == 4:
        s, t = values[0].real + values[2].real, values[0].real - values[2].real
        u, v = 2.0 * values[1].real, 2.0 * values[1].imag
        return [s + u, t - v, s - u, t + v]
    out = [None] * n
    if coprime(n):
        first, second = coprime(n)
        rows = []
        for i in range(first // 2 + 1):
            entries = [values[meeting(i, j, first, second)] for j in range(second)]
            if 2 * i % first == 0:
                rows.append([Number(value) for value in real_back(entries)])
            else:
                rows.append(dft(entries, 1))
        for b in range(second):
            half = [row[b] for row in rows]
            whole = half + [half[first - i].conj() for i in range(len(half), first)]
            for a, value in enumerate(real_back(whole)):
                out[(a * second + b * first) % n] = value
        return out
    p = radix(n)
    if p:
        rest = n // p
        parts = []
        for i in range(p // 2 + 1):
            entries = values[i::p]
            if i == 0:
                parts.append([Number(value) for value in real_back(entries)])
            else:
                inner = dft(entries, 1)
                parts.append([inner[m].times(2.0 * math.pi * i * m / n) for m in range(rest)])
                if 2 * i == p:
                    parts[-1] = [Number(value.real) for value in parts[-1]]
        for m in range(rest):
            half = [part[m] for part in parts]
            whole = half + [half[p - i].conj() for i in range(len(half), p)]
            for j, value in enumerate(real_back(whole)):
                out[m + rest * j] = value
        return out
    return [value.real for value in dft(values, 1)]


def wave_table(edge):
    index = np.arange(edge)
    angles = 2.0 * np.pi / edge * (np.outer(index, index) % edge)
    full = np.zeros((2, 2, HALF, 2, HALF))
    for side in range(2):
        full[0, side, :edge, side, :edge] = np.cos(angles)
        full[1, side, :edge, side, :edge] = np.sin(angles)
    full = full.reshape(2, LANES, LANES)
    high = full.astype(jnp.bfloat16)
    low = (full - high.astype(np.float64)).astype(jnp.bfloat16)
    return np.stack([high, low])


def split_dot(real, imag, matrix):
    value = jnp.concatenate([real, imag], axis=1)
    high = value.astype(jnp.bfloat16)
    low = (value - high.astype(jnp.float32)).astype(jnp.bfloat16)
    product = jnp.dot(
        jnp.concatenate([high, low, high], axis=1), matrix[...], preferred_element_type=jnp.float32
    )
    return product[:, :LANES], product[:, LANES:]


def padded_half(edge):
    return -(-(edge // 2 + 1) // ROWS) * ROWS


def screen_kernel(edge, numbers_ref, kernel_ref, waves_ref, out_ref, kept_ref, ahead_ref, behind_ref, flipped):
    for i in range(numbers_ref.shape[0]):
        kept_ref[i] = numbers_ref[i]
    for table, sign in ((ahead_ref, -1), (behind_ref, 1)):
        for part, source in enumerate((0, 0, 1)):
            for i in range(2):
                for j in range(2):
                    value = waves_ref[source, (i + j) % 2]
                    if i != j and (i > j) == (sign > 0):
                        value = -value
                    rows = slice((2 * part + i) * LANES, (2 * part + i + 1) * LANES)
                    table[rows, j * LANES : (j + 1) * LANES] = value
    exact = dict(precision=lax.Precision.HIGHEST, preferred_element_type=jnp.float32)

    def index(shape, axis):
        return lax.broadcasted_iota(jnp.int32, shape, axis)

    square, whole = (edge, edge), (LANES, LANES)
    flip = index(square, 0) + index(square, 1)
    flip = ((flip == 0) | (flip == edge)).astype(jnp.float32)
    source, target = index(whole, 0), index(whole, 1)
    target = jnp.where(target < HALF, target, target - HALF)
    mirror = ((source + target == 0) | (source + target == edge)) & (source < edge) & (target < edge)
    mirror = mirror.astype(jnp.float32)
    flipped[...] = jnp.dot(flip, kernel_ref[...], **exact)
    height = padded_half(edge)
    lane = index((edge, LANES), 1)
    out_ref[...] = jnp.zeros_like(out_ref)

    def piece(ref, y):
        begin, offset = divmod(y * edge, LANES)
        value = ref[:, begin * LANES : (begin + 1) * LANES]
        value = pltpu.roll(value, LANES - offset, 1) if offset else value
        if offset + edge > LANES:
            more = ref[:, (begin + 1) * LANES : (begin + 2) * LANES]
            value = jnp.where(lane < LANES - offset, value, pltpu.roll(more, LANES - offset, 1))
        return value

    for y in range(edge // 2 + 1):
        value = piece(kernel_ref, y)
        value = jnp.where(lane < HALF, value, pltpu.roll(value, HALF, 1))
        value = value + jnp.dot(piece(flipped, (edge - y) % edge), mirror, **exact)
        value = value * (0.5 / float(edge**3))
        for t in range(edge // ROWS):
            at = pl.ds(t * ROWS * height + y, ROWS, stride=height)
            out_ref[at, :] = value[t * ROWS : (t + 1) * ROWS]


def screen_terms(numbers, kernel):
    edge, plane = kernel.shape
    smem = pl.BlockSpec(memory_space=pltpu.SMEM)
    vmem = pl.BlockSpec(memory_space=pltpu.VMEM)
    table = jax.ShapeDtypeStruct((6 * LANES, 2 * LANES), jnp.bfloat16)
    return pl.pallas_call(
        functools.partial(screen_kernel, edge),
        out_shape=[
            jax.ShapeDtypeStruct((edge * padded_half(edge), LANES), jnp.float32),
            jax.ShapeDtypeStruct(numbers.shape, numbers.dtype),
            table,
            table,
        ],
        in_specs=[smem, vmem, vmem],
        out_specs=[vmem, smem, vmem, vmem],
        scratch_shapes=[pltpu.VMEM((edge, plane), jnp.float32)],
        compiler_params=pltpu.CompilerParams(vmem_limit_bytes=8 << 20),
        name="screen_terms",
    )(numbers, kernel, jnp.asarray(wave_table(edge)))


def pair_kernel(shape, second_part, numbers_ref, *refs):
    edge, orb_dev, groups, fragments, slots = shape
    plane = edge * edge
    chunks = plane // LANES
    tiles = edge // ROWS
    half = edge // 2 + 1
    height = padded_half(edge)
    tables, refs = refs[:3], refs[3:]
    phi_refs, refs = refs[:groups], refs[groups:]
    if second_part:
        (twin_ref, relay_ref, one_ref, act_before, back_before), refs = refs[:5], refs[5:]
        act_outs, back_outs, refs = refs[:2], refs[2:5], refs[5:]
        (act, back, state_sem, out_sem), refs = refs[:4], refs[4:]
    else:
        (twin_ref, two_ref, act), back_outs, refs = refs[:3], refs[3:6], refs[6:]
        (back, out_sem), refs = refs[:2], refs[2:]
    (near, far, wide, moved, dense, lower, upper, masks, listed, load_sem) = refs[:10]
    screen_ref, ahead_ref, behind_ref, table_sem = refs[10:]

    fragment, member, live_slots = numbers_ref[0], numbers_ref[1], numbers_ref[2]

    def first_of(slot):
        return numbers_ref[3 + slot]

    def second_of(slot):
        return numbers_ref[3 + slots + slot]

    def reach_of(slot):
        return numbers_ref[3 + 2 * slots + slot]

    def anchor(place, axis):
        return numbers_ref[3 + 3 * slots + 3 * place + axis]

    table_copies = [
        pltpu.make_async_copy(table, hold, table_sem.at[i])
        for i, (table, hold) in enumerate(zip(tables, refs[10:13]))
    ]
    lane = lax.broadcasted_iota(jnp.int32, (1, LANES), 1)
    stretch = next(n for n in (6, 4, 3, 2, 1) if chunks % n == 0)
    middle = pl.ds(edge, edge)

    even = lax.rem(fragment, 2) == 0

    def is_mine(slot):
        return (slot < live_slots) & (lax.div(second_of(slot), orb_dev) == member)

    def list_farthest(slot, found):
        chosen = is_mine(slot) & (reach_of(slot) == 2)

        @pl.when(chosen)
        def _():
            listed[found] = slot

        return found + chosen.astype(jnp.int32)

    farthest = lax.fori_loop(0, slots, list_farthest, jnp.int32(0))
    room = jnp.maximum(2, 2 * lax.div(farthest + 1, 2)) - farthest

    def list_others(slot, counts):
        early, found = counts
        mine = is_mine(slot) & (reach_of(slot) < 2)
        come = (reach_of(slot) == 0) | (even & (lax.rem(second_of(slot), orb_dev) == 0))
        taken = mine & come & (early < room)
        chosen = mine & jnp.logical_not(taken) if second_part else taken

        @pl.when(chosen)
        def _():
            listed[found] = slot

        return early + taken.astype(jnp.int32), found + chosen.astype(jnp.int32)

    begun = jnp.int32(0) if second_part else farthest
    _, found = lax.fori_loop(0, slots, list_others, (jnp.int32(0), begun))
    turns = lax.div(found + 1, 2)

    def slot_of(turn, side):
        at = 2 * turn + side
        live = at < found
        return listed[jnp.where(live, at, 2 * turn)], live

    def far_copy(side, source):
        return pltpu.make_async_copy(source, far.at[side], load_sem.at[1, side])

    def start_loads(turn):
        for side in range(2):
            slot, _ = slot_of(turn, side)
            first, second, reach = first_of(slot), second_of(slot), reach_of(slot)
            relative = lax.div(first, orb_dev) ^ member
            for k in range(groups):
                @pl.when(relative == k)
                def _():
                    pltpu.make_async_copy(
                        phi_refs[k].at[lax.rem(first, orb_dev)],
                        near.at[lax.rem(turn, 2), side],
                        load_sem.at[0, side],
                    ).start()
            own = lax.rem(second, orb_dev)

            @pl.when(reach == 0)
            def _():
                far_copy(side, phi_refs[0].at[own]).start()

            @pl.when((reach == 1) & (own == 0) & even)
            def _():
                far_copy(side, twin_ref.at[0]).start()

            if not second_part:
                @pl.when(reach == 2)
                def _():
                    far_copy(side, two_ref.at[own]).start()

            if second_part:
                @pl.when((reach == 1) & (own == 0) & jnp.logical_not(even))
                def _():
                    far_copy(side, relay_ref.at[0]).start()

                @pl.when((reach == 1) & (own > 0))
                def _():
                    far_copy(side, one_ref.at[jnp.maximum(own - 1, 0)]).start()

    def wait_loads(turn):
        for side in range(2):
            pltpu.make_async_copy(
                phi_refs[0].at[0], near.at[lax.rem(turn, 2), side], load_sem.at[0, side]
            ).wait()
            far_copy(side, phi_refs[0].at[0]).wait()

    @pl.when(found > 0)
    def _():
        start_loads(0)
        for copy in table_copies:
            copy.start()

    if second_part:
        state_copies = [
            pltpu.make_async_copy(before, now, state_sem.at[i])
            for i, (before, now) in enumerate(((act_before, act), (back_before, back)))
        ]
        slab = plane * edge // LANES // groups
        act_copies = []
        for k in range(groups):
            source = (member ^ k) * slab
            place = reversed_bits(k, groups)
            act_copies.append(
                pltpu.make_async_copy(
                    act.at[:, pl.ds(pl.multiple_of(source, ROWS), slab), :],
                    act_outs[2 * place // groups].at[place % (groups // 2)],
                    out_sem.at[3 + k],
                )
            )
    else:
        act[...] = jnp.zeros_like(act)
        back[...] = jnp.zeros_like(back)

    def offset_of(slot):
        partner = lax.rem(fragment + reach_of(slot), fragments)
        return [anchor(partner, i) - anchor(fragment, i) for i in range(3)]

    def steps(count, body, most):
        width = max(n for n in range(1, most + 1) if count % n == 0)

        def step(i, _):
            for j in range(width):
                body(i * width + j)
            return 0

        if width == count:
            step(0, 0)
        else:
            lax.fori_loop(0, count // width, step, 0)

    def columns(k):
        return pl.ds(pl.multiple_of(k * LANES, LANES), LANES)

    def set_masks(place, delta, weight):
        shape = masks.shape[1:]
        spot = lax.broadcasted_iota(jnp.int32, shape, 0) * LANES
        spot = spot + lax.broadcasted_iota(jnp.int32, shape, 1)
        y = ((spot.astype(jnp.float32) + 0.5) * (1.0 / edge)).astype(jnp.int32)
        z = spot - y * edge - delta[2]
        y = y - delta[1]
        inside = (y >= 0) & (y < edge) & (z >= 0) & (z < edge)
        masks[place] = jnp.where(inside, weight, 0.0)

    def shifted(source, place, delta, begin, count, ks):
        shift = lax.rem(delta[1] * edge + delta[2] + 4 * plane, plane)
        start = lax.rem(plane - shift, plane)
        whole, part = lax.div(start, LANES), lax.rem(start, LANES)
        turn = lax.rem(LANES - part, LANES)
        down = edge - jnp.clip(delta[0], -edge, edge) + begin
        x = lax.broadcasted_iota(jnp.int32, (count, LANES), 0) + (begin - delta[0])
        rows_inside = (x >= 0) & (x < edge)
        first = lane < LANES - part

        def piece(k):
            return pltpu.roll(source[lax.rem(k + whole, chunks), pl.ds(down, count), :], turn, 1)

        out = []
        low = piece(ks[0])
        for k in ks:
            high = piece(k + 1)
            value = jnp.where(first, low, high) * masks[place, pl.ds(k, 1), :]
            out.append(jnp.where(rows_inside, value, 0.0))
            low = high
        return out

    def tile(t, i, size):
        return pl.ds(pl.multiple_of(i * size + t * ROWS, ROWS), ROWS)

    def across(t, i, size):
        return pl.ds(t * (ROWS * size) + i, ROWS, stride=size)

    def solve_two(turn, _):
        wait_loads(turn)
        if second_part:
            @pl.when(turn == 0)
            def _():
                for copy in state_copies:
                    copy.start()

        near_now = near.at[lax.rem(turn, 2)]
        picked = [slot_of(turn, side) for side in range(2)]
        offsets = [offset_of(slot) for slot, _ in picked]
        returns = [[-d for d in delta] for delta in offsets]
        for side in range(2):
            set_masks(side, offsets[side], picked[side][1].astype(jnp.float32))
            set_masks(2 + side, returns[side], 1.0)

        def widen(k):
            for side in range(2):
                wide[side, k, middle, :] = far[side, :, pl.ds(pl.multiple_of(k * LANES, LANES), LANES)]

        steps(chunks, widen, chunks)

        def over_y(t):
            densities = []
            begin = pl.multiple_of(t * ROWS, ROWS)
            rows = pl.ds(begin, ROWS)
            for side in range(2):
                values = shifted(wide.at[side], side, offsets[side], begin, ROWS, range(chunks))
                for k in range(chunks):
                    moved[side, k, rows, :] = values[k]
                    values[k] = values[k] * near_now[side, rows, k * LANES : (k + 1) * LANES]
                densities.append(values)
            planes = []
            for y in range(edge):
                first, offset = divmod(y * edge, LANES)
                sides = []
                for side in range(2):
                    shift = (side * HALF - offset) % LANES
                    value = densities[side][first]
                    value = pltpu.roll(value, shift, 1) if shift else value
                    if offset + edge > LANES:
                        more = densities[side][first + 1]
                        more = pltpu.roll(more, shift, 1) if shift else more
                        value = jnp.where(lane < side * HALF + LANES - offset, value, more)
                    sides.append(value)
                planes.append(Number(jnp.where(lane < HALF, sides[0], sides[1])))
            values = real_dft(planes)
            for i in range(half):
                at = tile(t, i, edge)
                lower[0, at, :] = values[i].real
                imag = values[i].imag
                lower[1, at, :] = jnp.zeros((ROWS, LANES), jnp.float32) if imag is None else imag

        steps(tiles, over_y, 3)

        @pl.when(turn == 0)
        def _():
            for copy in table_copies:
                copy.wait()

        @pl.when(turn + 1 < turns)
        def _():
            start_loads(turn + 1)

        def over_x(t):
            at = [across(t, i, edge) for i in range(edge)]
            values = dft([Number(lower[0, a, :], lower[1, a, :]) for a in at], -1)
            real = jnp.concatenate([value.real for value in values], axis=0)
            imag = jnp.concatenate([value.imag for value in values], axis=0)
            at = [tile(t, i, height) for i in range(edge)]
            factor = jnp.concatenate([screen_ref[a, :] for a in at], axis=0)
            real, imag = split_dot(real, imag, ahead_ref)
            real, imag = split_dot(real * factor, imag * factor, behind_ref)
            rows = [slice(i * ROWS, (i + 1) * ROWS) for i in range(edge)]
            values = dft([Number(real[r], imag[r]) for r in rows], 1)
            for i in range(edge):
                upper[0, at[i], :] = values[i].real
                upper[1, at[i], :] = values[i].imag

        steps(height // ROWS, over_x, 4)
        if second_part:
            @pl.when(turn == 0)
            def _():
                for copy in state_copies:
                    copy.wait()

        firsts = [first_of(slot) for slot, _ in picked]

        def back_y(t):
            begin = pl.multiple_of(t * ROWS, ROWS)
            rows = pl.ds(begin, ROWS)
            at = [across(t, i, height) for i in range(half)]
            values = [Number(upper[0, a, :], upper[1, a, :]) for a in at]
            values = values + [values[edge - i].conj() for i in range(half, edge)]
            planes = real_back(values)
            for side in range(2):
                forward = []
                for k in range(chunks):
                    value = None
                    for y in range(k * LANES // edge, edge):
                        begins = y * edge - k * LANES
                        if begins >= LANES:
                            break
                        shift = (begins - side * HALF) % LANES
                        piece = pltpu.roll(planes[y], shift, 1) if shift else planes[y]
                        value = piece if value is None else jnp.where(lane < begins, value, piece)
                    forward.append(value * moved[side, k, rows, :])
                    other = value * near_now[side, rows, k * LANES : (k + 1) * LANES]
                    dense[side, k, pl.ds(edge + begin, ROWS), :] = other
                at = [pl.ds(t * (ROWS * chunks) + k, ROWS, stride=chunks) for k in range(chunks)]
                sums = [act[firsts[side], at[k], :] + forward[k] for k in range(chunks)]
                for k in range(chunks):
                    act[firsts[side], at[k], :] = sums[k]

        steps(tiles, back_y, 3)

        if second_part:
            @pl.when(turn + 1 == turns)
            def _():
                for copy in act_copies:
                    copy.start()

        homes = []
        for side in range(2):
            slot = picked[side][0]
            homes.append(reach_of(slot) * orb_dev + lax.rem(second_of(slot), orb_dev))

        def send_back(g):
            for side in range(2):
                ks = [g * stretch + i for i in range(stretch)]
                values = shifted(dense.at[side], 2 + side, returns[side], 0, edge, ks)
                at = [
                    (i, t, pl.ds(t * (ROWS * chunks) + ks[i], ROWS, stride=chunks))
                    for i in range(stretch)
                    for t in range(tiles)
                ]
                sums = [
                    back[homes[side], a, :] + values[i][t * ROWS : (t + 1) * ROWS] for i, t, a in at
                ]
                for (i, t, a), value in zip(at, sums):
                    back[homes[side], a, :] = value

        steps(chunks // stretch, send_back, 3)
        return 0

    if second_part:
        @pl.when(found == 0)
        def _():
            for copy in state_copies:
                copy.start()
            for copy in state_copies:
                copy.wait()
            for copy in act_copies:
                copy.start()

    lax.fori_loop(0, turns, solve_two, 0)
    if second_part:
        spans = ((orb_dev, 1), (orb_dev + 1, orb_dev - 1), (0, orb_dev))
    else:
        spans = ((2 * orb_dev + 1, orb_dev - 1), (2 * orb_dev, 1), (0, 2 * orb_dev))
    copies = [
        pltpu.make_async_copy(back.at[pl.ds(begin, count)], back_outs[i], out_sem.at[i])
        for i, (begin, count) in enumerate(spans)
    ]
    for copy in copies:
        copy.start()
    if second_part:
        copies += act_copies
    for copy in copies:
        copy.wait()


def reversed_bits(k, count):
    bits = count.bit_length() - 1
    return sum(((k >> i) & 1) << (bits - 1 - i) for i in range(bits))


def pair_terms(numbers, fragments, slots, tables, pieces, far, before=()):
    second_part = bool(before)
    orb_dev, edge, plane = pieces[0].shape
    groups = len(pieces)
    frag_size = groups * orb_dev
    chunks = plane // LANES
    rows = edge * chunks
    height = padded_half(edge)
    shape = (edge, orb_dev, groups, fragments, slots)
    smem = pl.BlockSpec(memory_space=pltpu.SMEM)
    vmem = pl.BlockSpec(memory_space=pltpu.VMEM)
    hbm = pl.BlockSpec(memory_space=pltpu.HBM)
    f32 = jnp.float32

    def fields(*counts):
        return [jax.ShapeDtypeStruct((count, rows, LANES), f32) for count in counts]

    if second_part:
        out_shape = [jax.ShapeDtypeStruct((groups // 2, frag_size, rows // groups, LANES), f32)] * 2
        out_shape += fields(1, orb_dev - 1, orb_dev)
        out_specs = [hbm] * 5
        scratch = [pltpu.VMEM(field.shape, f32) for field in fields(frag_size, REACH * orb_dev)]
        scratch += [pltpu.SemaphoreType.DMA((2,)), pltpu.SemaphoreType.DMA((3 + groups,))]
    else:
        out_shape = fields(frag_size, orb_dev - 1, 1, REACH * orb_dev)
        out_specs = [vmem, hbm, hbm, hbm]
        scratch = [pltpu.VMEM(((REACH + 1) * orb_dev, rows, LANES), f32)]
        scratch += [pltpu.SemaphoreType.DMA((3,))]
    return pl.pallas_call(
        functools.partial(pair_kernel, shape, second_part),
        out_shape=out_shape,
        in_specs=[smem] + [hbm] * (3 + groups + len(far) + len(before)),
        out_specs=out_specs,
        scratch_shapes=scratch
        + [
            pltpu.VMEM((2, 2, edge, plane), f32),
            pltpu.VMEM((2, edge, plane), f32),
            pltpu.VMEM((2, chunks, 3 * edge, LANES), f32),
            pltpu.VMEM((2, chunks, edge, LANES), f32),
            pltpu.VMEM((2, chunks, 3 * edge, LANES), f32),
            pltpu.VMEM((2, height * edge, LANES), f32),
            pltpu.VMEM((2, height * edge, LANES), f32),
            pltpu.VMEM((4, -(-chunks // ROWS) * ROWS, LANES), f32),
            pltpu.SMEM((slots,), jnp.int32),
            pltpu.SemaphoreType.DMA((2, 2)),
            *[pltpu.VMEM(table.shape, table.dtype) for table in tables],
            pltpu.SemaphoreType.DMA((3,)),
        ],
        compiler_params=pltpu.CompilerParams(vmem_limit_bytes=30 << 20),
        name="late_pair_terms" if second_part else "early_pair_terms",
    )(numbers, *tables, *pieces, *far, *before)


def flatten_kernel(shape, places_ref, *refs):
    edge, orb_dev, groups = shape
    pieces, (flat_ref, slab_ref) = refs[:groups], refs[groups:]
    member = places_ref[1]
    chunks = edge * edge // LANES
    slab = slab_ref.shape[1]
    for k in range(groups):
        for o in range(orb_dev):
            def move(j, _):
                value = pieces[k][o, :, pl.ds(pl.multiple_of(j * LANES, LANES), LANES)]
                for t in range(edge // ROWS):
                    at = pl.ds(t * (ROWS * chunks) + j, ROWS, stride=chunks)
                    flat_ref[k * orb_dev + o, at, :] = value[t * ROWS : (t + 1) * ROWS]
                return 0

            lax.fori_loop(0, chunks, move, 0)
    slab_ref[...] = flat_ref[:, pl.ds(pl.multiple_of(member * slab, ROWS), slab), :]


def flatten_terms(places, pieces):
    orb_dev, edge, plane = pieces[0].shape
    groups = len(pieces)
    rows = edge * plane // LANES
    frag_size = groups * orb_dev
    smem = pl.BlockSpec(memory_space=pltpu.SMEM)
    vmem = pl.BlockSpec(memory_space=pltpu.VMEM)
    return pl.pallas_call(
        functools.partial(flatten_kernel, (edge, orb_dev, groups)),
        out_shape=(
            jax.ShapeDtypeStruct((frag_size, rows, LANES), jnp.float32),
            jax.ShapeDtypeStruct((frag_size, rows // groups, LANES), jnp.float32),
        ),
        in_specs=[smem] + [vmem] * groups,
        out_specs=(vmem, vmem),
        compiler_params=pltpu.CompilerParams(vmem_limit_bytes=24 << 20),
        name="flatten_terms",
    )(places, *pieces)


def products(lefts, rights, length, step):
    def add(i, sums):
        at = pl.ds(pl.multiple_of(i * step, ROWS), step)
        right = [ref[index, at, :].reshape(step // ROWS, ROWS, LANES) for ref, index in rights]
        out = []
        for n, (ref, index) in enumerate(lefts):
            left = ref[index, at, :].reshape(step // ROWS, ROWS, LANES)
            for m in range(len(rights)):
                out.append(sums[n * len(rights) + m] + jnp.sum(left * right[m], axis=0))
        return tuple(out)

    zero = jnp.zeros((ROWS, LANES), jnp.float32)
    return lax.fori_loop(0, length // step, add, (zero,) * (len(lefts) * len(rights)))


def placed(result, sums, rows, lanes):
    row = lax.broadcasted_iota(jnp.int32, result.shape, 0)
    lane = lax.broadcasted_iota(jnp.int32, result.shape, 1)
    for n, a in enumerate(rows):
        for m, b in enumerate(lanes):
            value = jnp.sum(sums[n * len(lanes) + m], keepdims=True)
            result = jnp.where((row == a) & (lane == b), result + value, result)
    return result


def step_of(length):
    return next(n for n in (72, 24, 8) if length % n == 0)


def action_kernel(shape, places_ref, phi_ref, kept_ref, *refs):
    orb_dev, groups, parts = shape
    arrived, (act_ref, share_ref) = refs[:parts], refs[parts:]
    member = places_ref[1]
    frag_size = orb_dev * groups
    slab = act_ref.shape[1]
    cut = frag_size // parts
    for i in range(parts):
        span = slice(i * cut, (i + 1) * cut)
        act_ref[span] = kept_ref[0, span] + arrived[i][0]
    rows = [(member ^ (a // orb_dev)) * orb_dev + a % orb_dev for a in range(frag_size)]
    result = jnp.zeros(share_ref.shape, jnp.float32)
    for half in range(0, frag_size, 4):
        bs = range(half, min(half + 4, frag_size))
        lefts, rights = [(phi_ref, a) for a in range(frag_size)], [(act_ref, b) for b in bs]
        result = placed(result, products(lefts, rights, slab, step_of(slab)), rows, bs)
    share_ref[...] = result


def action_terms(places, orb_dev, phi, kept, arrived):
    frag_size, slab = phi.shape[:2]
    smem = pl.BlockSpec(memory_space=pltpu.SMEM)
    vmem = pl.BlockSpec(memory_space=pltpu.VMEM)
    return pl.pallas_call(
        functools.partial(action_kernel, (orb_dev, frag_size // orb_dev, len(arrived))),
        out_shape=(
            jax.ShapeDtypeStruct((frag_size, slab, LANES), jnp.float32),
            jax.ShapeDtypeStruct((frag_size, LANES), jnp.float32),
        ),
        in_specs=[smem] + [vmem] * (2 + len(arrived)),
        out_specs=(vmem, vmem),
        compiler_params=pltpu.CompilerParams(vmem_limit_bytes=16 << 20),
        name="action_terms",
    )(places, phi, kept, *arrived)


def home_kernel(shape, places_ref, flat_ref, own_ref, *refs):
    edge, orb_dev, groups, first, count = shape
    if first == 0:
        (two_ref, twin_ref, relay_ref, share_ref), refs = refs[:4], refs[4:]
    else:
        (two_ref, one_ref), refs = refs[:2], refs[2:]
    outs, total = refs[:groups], refs[groups]
    fragment, member = places_ref[0], places_ref[1]
    frag_size = orb_dev * groups
    rows = flat_ref.shape[1]
    slab = rows // groups
    for i in range(count):
        value = own_ref[first + i] + two_ref[i]
        if first == 0:
            @pl.when(lax.rem(fragment, 2) == 1)
            def _():
                total[i] = value + twin_ref[i]

            @pl.when(lax.rem(fragment, 2) == 0)
            def _():
                total[i] = value + relay_ref[i]
        else:
            total[i] = value + one_ref[i]
    lefts, rights = [(flat_ref, a) for a in range(frag_size)], [(total, i) for i in range(count)]
    places = [(member ^ (a // orb_dev)) * orb_dev + a % orb_dev for a in range(frag_size)]
    result = share_ref[...] if first == 0 else jnp.zeros((frag_size, LANES), jnp.float32)
    sums = products(lefts, rights, rows, step_of(rows))
    result = placed(result, sums, places, [member * orb_dev + first + i for i in range(count)])
    result = result * (1.0 / float(edge**3))
    for k in range(groups):
        begin = pl.multiple_of((member ^ k) * slab, ROWS)
        for i in range(count):
            outs[k][i * slab : (i + 1) * slab, :] = total[i, pl.ds(begin, slab), :]
        outs[k][count * slab :, :] = result


def home_terms(places, edge, groups, flat, own, first, *came):
    frag_size, rows = flat.shape[:2]
    count = came[0].shape[0]
    smem = pl.BlockSpec(memory_space=pltpu.SMEM)
    vmem = pl.BlockSpec(memory_space=pltpu.VMEM)
    f32 = jnp.float32
    parcel = jax.ShapeDtypeStruct((count * rows // groups + frag_size, LANES), f32)
    return pl.pallas_call(
        functools.partial(home_kernel, (edge, frag_size // groups, groups, first, count)),
        out_shape=[parcel] * groups,
        in_specs=[smem] + [vmem] * (2 + len(came)),
        out_specs=[vmem] * groups,
        scratch_shapes=[pltpu.VMEM((count, rows, LANES), f32)],
        compiler_params=pltpu.CompilerParams(vmem_limit_bytes=16 << 20),
        name="home_terms",
    )(places, flat, own, *came)


def exchanged(value, axis, width):
    size = value.shape[axis]
    index = lax.broadcasted_iota(jnp.int32, value.shape, axis)
    below, above = pltpu.roll(value, width, axis), pltpu.roll(value, size - width, axis)
    return jnp.where((index & width) != 0, below, above)


def gradient_kernel(shape, places_ref, act_ref, phi_ref, *refs):
    edge, orb_dev, groups = shape
    heads, tails, refs = refs[:groups], refs[groups : 2 * groups], refs[2 * groups :]
    out_ref, lagrange_ref, hold = refs
    member = places_ref[1]
    frag_size = orb_dev * groups
    chunks = edge * edge // LANES
    slab_rows = edge // groups
    slab = slab_rows * chunks
    sums = [
        head[slab:, :] + tail[(orb_dev - 1) * slab :, :] for head, tail in zip(heads, tails)
    ]
    while len(sums) > 1:
        sums = [sums[i] + sums[i + 1] for i in range(0, len(sums), 2)]
    square = jnp.concatenate([sums[0], jnp.zeros((LANES - frag_size, LANES), jnp.float32)], axis=0)
    lagrange = 0.5 * (square + square.T)[:frag_size, :]
    lagrange_ref[...] = lagrange[:, :frag_size]
    bit = 1
    while bit < groups:
        turned = exchanged(exchanged(lagrange, 0, bit * orb_dev), 1, bit * orb_dev)
        lagrange = jnp.where((member & bit) != 0, turned, lagrange)
        bit *= 2

    for k in range(groups):
        for o in range(orb_dev):
            a = (member ^ k) * orb_dev + o
            came = heads[k][:slab, :] if o == 0 else tails[k][(o - 1) * slab : o * slab, :]
            value = act_ref[a] + came
            for b in range(frag_size):
                factor = lagrange[b : b + 1, k * orb_dev + o : k * orb_dev + o + 1]
                value = value - factor * phi_ref[b]
            hold[pl.ds(pl.multiple_of(a * slab, ROWS), slab), :] = value
    for x in range(slab_rows):
        for j in range(chunks):
            value = hold[pl.ds(x * chunks + j, frag_size, stride=slab), :]
            out_ref[x, :, j * LANES : (j + 1) * LANES] = value


def gradient_terms(places, edge, act, phi, heads, tails):
    groups = len(heads)
    frag_size, slab = act.shape[:2]
    smem = pl.BlockSpec(memory_space=pltpu.SMEM)
    vmem = pl.BlockSpec(memory_space=pltpu.VMEM)
    f32 = jnp.float32
    gradient, lagrange = pl.pallas_call(
        functools.partial(gradient_kernel, (edge, frag_size // groups, groups)),
        out_shape=(
            jax.ShapeDtypeStruct((edge // groups, frag_size, edge * edge), f32),
            jax.ShapeDtypeStruct((frag_size, frag_size), f32),
        ),
        in_specs=[smem] + [vmem] * (2 + 2 * groups),
        out_specs=(vmem, vmem),
        scratch_shapes=[pltpu.VMEM((frag_size * slab, LANES), f32)],
        compiler_params=pltpu.CompilerParams(vmem_limit_bytes=16 << 20),
        name="gradient_terms",
    )(places, act, phi, *heads, *tails)
    return gradient.transpose(1, 0, 2), lagrange


def together(*arrays):
    return lax.optimization_barrier(arrays)


def to_fragment(block, distance, senders=None):
    devices = lax.axis_size("orb")
    senders = range(devices) if senders is None else range(senders, devices, 2)
    return lax.ppermute(block, "orb", [(i, (i + distance) % devices) for i in senders])


def with_twin(block):
    return lax.ppermute(block, "orb", [(i, i ^ 1) for i in range(lax.axis_size("orb"))])


def with_member(block, bit):
    return lax.ppermute(block, "grp", [(i, i ^ bit) for i in range(lax.axis_size("grp"))])


def by_member(parcels):
    groups = len(parcels)
    received = list(parcels)
    bit = groups // 2
    while bit:
        for k in reversed(range(groups)):
            if k & bit:
                received[k] = with_member(received[k], bit)
        bit //= 2
    return received


def shards(orbitals, kernel, anchors, pair_count, pair_first, pair_second, pair_reach):
    groups = lax.axis_size("grp")
    orb_dev, edge, plane = orbitals.shape
    places = jnp.stack([lax.axis_index("orb"), lax.axis_index("grp")]).astype(jnp.int32)

    numbers = [places, pair_count, pair_first, pair_second, pair_reach, anchors.reshape(-1)]
    screen, numbers, *tables = screen_terms(jnp.concatenate(numbers), kernel)
    two = to_fragment(orbitals, -2)
    twin = with_twin(orbitals[:1])
    pieces = {0: orbitals}
    bit = groups // 2
    while bit:
        for k in list(pieces):
            pieces[k ^ bit] = with_member(pieces[k], bit)
        if bit == groups // 2:
            two, twin, tail, pieces[bit], screen, numbers, *tables = together(
                two, twin, orbitals[1:], pieces[bit], screen, numbers, *tables
            )
            one = to_fragment(tail, -1)
            relay = to_fragment(twin, -2, 1)
        bit //= 2
    pieces = [pieces[k] for k in range(groups)]
    tables = [screen, *tables]
    sizes = (anchors.shape[0], pair_first.shape[0])
    act, two_tail, two_head, back = pair_terms(numbers, *sizes, tables, pieces, [twin, two])
    two_tail, relay, one = together(two_tail, relay, one)
    two_tail = to_fragment(two_tail, 2)
    kept, sent, one_head, one_tail, own = pair_terms(
        numbers, *sizes, tables, pieces, [twin, relay, one], [act, back]
    )

    sent, two_tail, two_head = together(sent, two_tail, two_head)
    two_head = to_fragment(two_head, 2)
    twin = with_twin(one_head)
    bit = 1
    arrived = with_member(sent, bit)
    while 2 * bit < groups:
        kept = kept + arrived
        if bit == 1:
            _, twin, one_tail, two_head = together(kept, twin, one_tail, two_head)
        half = kept.shape[0] // 2
        bit *= 2
        arrived, kept = with_member(kept[half:], bit), kept[:half]
    one_tail = to_fragment(one_tail, 1)
    relay = to_fragment(twin, 2, 0)

    flat, phi = flatten_terms(places, pieces)
    tails = home_terms(places, edge, groups, flat, own, 1, two_tail, one_tail)
    tails = by_member(tails)
    act, share = action_terms(places, orb_dev, phi, kept, [arrived])
    heads = by_member(
        home_terms(places, edge, groups, flat, own, 0, two_head, twin, relay, share)
    )
    gradient, lagrange = gradient_terms(places, edge, act, phi, heads, tails)
    return (gradient, lagrange[None])


def solution(mesh):
    placed = (P(("orb", "grp"), None, None), P(), P(), P("orb"), P("orb"), P("orb"), P("orb"))
    return jax.shard_map(
        shards,
        mesh=mesh,
        in_specs=placed,
        out_specs=(P("orb", "grp", None), P("orb", None, None)),
        check_vma=False,
    )
```

```python
import functools
import math

import jax
import jax.numpy as jnp
import numpy as np
from jax import lax
from jax.experimental import pallas as pl
from jax.experimental.pallas import tpu as pltpu
from jax.sharding import PartitionSpec as P

REACH = 2
LANES = 128
ROWS = 8
HALF = LANES // 2


class Number:
    def __init__(self, real, imag=None):
        self.real, self.imag = real, imag

    def __add__(self, other):
        if self.imag is None or other.imag is None:
            imag = self.imag if other.imag is None else other.imag
        else:
            imag = self.imag + other.imag
        return Number(self.real + other.real, imag)

    def __sub__(self, other):
        if other.imag is None:
            imag = self.imag
        else:
            imag = -other.imag if self.imag is None else self.imag - other.imag
        return Number(self.real - other.real, imag)

    def conj(self):
        return self if self.imag is None else Number(self.real, -self.imag)

    def scaled(self, factor):
        return Number(self.real * factor, None if self.imag is None else self.imag * factor)

    def turned(self, sign):
        if self.imag is None:
            return Number(jnp.zeros_like(self.real), self.real if sign > 0 else -self.real)
        return Number(-self.imag, self.real) if sign > 0 else Number(self.imag, -self.real)

    def plus_turned(self, other, sign):
        if sign < 0:
            return self.minus_turned(other)
        real = self.real if other.imag is None else self.real - other.imag
        return Number(real, other.real if self.imag is None else self.imag + other.real)

    def minus_turned(self, other):
        real = self.real if other.imag is None else self.real + other.imag
        return Number(real, -other.real if self.imag is None else self.imag - other.real)

    def times(self, angle):
        real, imag = math.cos(angle), math.sin(angle)
        if abs(imag) < 1e-12:
            return self if real > 0 else self.scaled(-1.0)
        if abs(real) < 1e-12:
            return self.turned(imag)
        if self.imag is None:
            return Number(self.real * real, self.real * imag)
        return Number(self.real * real - self.imag * imag, self.real * imag + self.imag * real)


def coprime(n):
    for p in (2, 3, 5, 7):
        power = 1
        while n % (power * p) == 0:
            power *= p
        if 1 < power < n:
            return power, n // power
    return None


def radix(n):
    return next((p for p in (4, 2, 3, 5, 7) if n % p == 0 and n > p), None)


def meeting(i, j, first, second):
    return next(k for k in range(first * second) if k % first == i and k % second == j)


def dft(values, sign):
    n = len(values)
    if n == 1:
        return values
    if n == 2:
        return [values[0] + values[1], values[0] - values[1]]
    if n == 3:
        a, b, c = values
        total, side = b + c, (b - c).scaled(math.sqrt(0.75))
        middle = a - total.scaled(0.5)
        return [a + total, middle.plus_turned(side, sign), middle.plus_turned(side, -sign)]
    if n == 4:
        a, b, c, d = values
        s, t, u, v = a + c, a - c, b + d, b - d
        return [s + u, t.plus_turned(v, sign), s - u, t.plus_turned(v, -sign)]
    out = [None] * n
    if coprime(n):
        first, second = coprime(n)
        columns = [
            dft([values[(i * second + j * first) % n] for i in range(first)], sign)
            for j in range(second)
        ]
        for i in range(first):
            row = dft([column[i] for column in columns], sign)
            for j in range(second):
                out[meeting(i, j, first, second)] = row[j]
        return out
    p = radix(n)
    if p:
        rest = n // p
        columns = [dft(values[j::p], sign) for j in range(p)]
        for i in range(rest):
            row = dft(
                [columns[j][i].times(sign * 2.0 * math.pi * i * j / n) for j in range(p)], sign
            )
            for j in range(p):
                out[i + rest * j] = row[j]
        return out
    for k in range(n):
        total = values[0]
        for j in range(1, n):
            total = total + values[j].times(sign * 2.0 * math.pi * (j * k % n) / n)
        out[k] = total
    return out


def real_dft(values):
    n = len(values)
    if n <= 4:
        out = dft(values, -1)
    else:
        out = [None] * n
        if coprime(n):
            first, second = coprime(n)
            columns = [
                real_dft([values[(i * second + j * first) % n] for i in range(first)])
                for j in range(second)
            ]
            for i in range(first // 2 + 1):
                entries = [column[i] for column in columns]
                alone = 2 * i % first == 0
                row = real_dft(entries) if alone else dft(entries, -1)
                for j in range(second):
                    out[meeting(i, j, first, second)] = row[j]
        elif radix(n):
            p = radix(n)
            rest = n // p
            columns = [real_dft(values[j::p]) for j in range(p)]
            for i in range(rest // 2 + 1):
                row = dft(
                    [columns[j][i].times(-2.0 * math.pi * i * j / n) for j in range(p)], -1
                )
                for j in range(p):
                    out[i + rest * j] = row[j]
        else:
            out = dft(values, -1)
    for k in range(1, n):
        if out[k] is None or (k > n // 2 and out[n - k] is not None):
            out[k] = out[n - k].conj()
    out[0] = Number(out[0].real)
    if n % 2 == 0:
        out[n // 2] = Number(out[n // 2].real)
    return out


def real_back(values):
    n = len(values)
    if n == 1:
        return [values[0].real]
    if n == 2:
        return [values[0].real + values[1].real, values[0].real - values[1].real]
    if n == 3:
        a, b = values[0].real, values[1]
        side = b.imag * math.sqrt(3.0)
        middle = a - b.real
        return [a + 2.0 * b.real, middle - side, middle + side]
    if n == 4:
        s, t = values[0].real + values[2].real, values[0].real - values[2].real
        u, v = 2.0 * values[1].real, 2.0 * values[1].imag
        return [s + u, t - v, s - u, t + v]
    out = [None] * n
    if coprime(n):
        first, second = coprime(n)
        rows = []
        for i in range(first // 2 + 1):
            entries = [values[meeting(i, j, first, second)] for j in range(second)]
            if 2 * i % first == 0:
                rows.append([Number(value) for value in real_back(entries)])
            else:
                rows.append(dft(entries, 1))
        for b in range(second):
            half = [row[b] for row in rows]
            whole = half + [half[first - i].conj() for i in range(len(half), first)]
            for a, value in enumerate(real_back(whole)):
                out[(a * second + b * first) % n] = value
        return out
    p = radix(n)
    if p:
        rest = n // p
        parts = []
        for i in range(p // 2 + 1):
            entries = values[i::p]
            if i == 0:
                parts.append([Number(value) for value in real_back(entries)])
            else:
                inner = dft(entries, 1)
                parts.append([inner[m].times(2.0 * math.pi * i * m / n) for m in range(rest)])
                if 2 * i == p:
                    parts[-1] = [Number(value.real) for value in parts[-1]]
        for m in range(rest):
            half = [part[m] for part in parts]
            whole = half + [half[p - i].conj() for i in range(len(half), p)]
            for j, value in enumerate(real_back(whole)):
                out[m + rest * j] = value
        return out
    return [value.real for value in dft(values, 1)]


def wave_table(edge):
    index = np.arange(edge)
    angles = 2.0 * np.pi / edge * (np.outer(index, index) % edge)
    full = np.zeros((2, 2, HALF, 2, HALF))
    for side in range(2):
        full[0, side, :edge, side, :edge] = np.cos(angles)
        full[1, side, :edge, side, :edge] = np.sin(angles)
    full = full.reshape(2, LANES, LANES)
    high = full.astype(jnp.bfloat16)
    low = (full - high.astype(np.float64)).astype(jnp.bfloat16)
    return np.stack([high, low])


def split_dot(real, imag, matrix):
    value = jnp.concatenate([real, imag], axis=1)
    high = value.astype(jnp.bfloat16)
    low = (value - high.astype(jnp.float32)).astype(jnp.bfloat16)
    product = jnp.dot(
        jnp.concatenate([high, low, high], axis=1), matrix[...], preferred_element_type=jnp.float32
    )
    return product[:, :LANES], product[:, LANES:]


def padded_half(edge):
    return -(-(edge // 2 + 1) // ROWS) * ROWS


def screen_kernel(edge, numbers_ref, kernel_ref, waves_ref, out_ref, kept_ref, ahead_ref, behind_ref, flipped):
    for i in range(numbers_ref.shape[0]):
        kept_ref[i] = numbers_ref[i]
    for table, sign in ((ahead_ref, -1), (behind_ref, 1)):
        for part, source in enumerate((0, 0, 1)):
            for i in range(2):
                for j in range(2):
                    value = waves_ref[source, (i + j) % 2]
                    if i != j and (i > j) == (sign > 0):
                        value = -value
                    rows = slice((2 * part + i) * LANES, (2 * part + i + 1) * LANES)
                    table[rows, j * LANES : (j + 1) * LANES] = value
    exact = dict(precision=lax.Precision.HIGHEST, preferred_element_type=jnp.float32)

    def index(shape, axis):
        return lax.broadcasted_iota(jnp.int32, shape, axis)

    square, whole = (edge, edge), (LANES, LANES)
    flip = index(square, 0) + index(square, 1)
    flip = ((flip == 0) | (flip == edge)).astype(jnp.float32)
    source, target = index(whole, 0), index(whole, 1)
    target = jnp.where(target < HALF, target, target - HALF)
    mirror = ((source + target == 0) | (source + target == edge)) & (source < edge) & (target < edge)
    mirror = mirror.astype(jnp.float32)
    flipped[...] = jnp.dot(flip, kernel_ref[...], **exact)
    height = padded_half(edge)
    lane = index((edge, LANES), 1)
    out_ref[...] = jnp.zeros_like(out_ref)

    def piece(ref, y):
        begin, offset = divmod(y * edge, LANES)
        value = ref[:, begin * LANES : (begin + 1) * LANES]
        value = pltpu.roll(value, LANES - offset, 1) if offset else value
        if offset + edge > LANES:
            more = ref[:, (begin + 1) * LANES : (begin + 2) * LANES]
            value = jnp.where(lane < LANES - offset, value, pltpu.roll(more, LANES - offset, 1))
        return value

    for y in range(edge // 2 + 1):
        value = piece(kernel_ref, y)
        value = jnp.where(lane < HALF, value, pltpu.roll(value, HALF, 1))
        value = value + jnp.dot(piece(flipped, (edge - y) % edge), mirror, **exact)
        value = value * (0.5 / float(edge**3))
        for t in range(edge // ROWS):
            at = pl.ds(t * ROWS * height + y, ROWS, stride=height)
            out_ref[at, :] = value[t * ROWS : (t + 1) * ROWS]


def screen_terms(numbers, kernel):
    edge, plane = kernel.shape
    smem = pl.BlockSpec(memory_space=pltpu.SMEM)
    vmem = pl.BlockSpec(memory_space=pltpu.VMEM)
    table = jax.ShapeDtypeStruct((6 * LANES, 2 * LANES), jnp.bfloat16)
    return pl.pallas_call(
        functools.partial(screen_kernel, edge),
        out_shape=[
            jax.ShapeDtypeStruct((edge * padded_half(edge), LANES), jnp.float32),
            jax.ShapeDtypeStruct(numbers.shape, numbers.dtype),
            table,
            table,
        ],
        in_specs=[smem, vmem, vmem],
        out_specs=[vmem, smem, vmem, vmem],
        scratch_shapes=[pltpu.VMEM((edge, plane), jnp.float32)],
        compiler_params=pltpu.CompilerParams(vmem_limit_bytes=8 << 20),
        name="screen_terms",
    )(numbers, kernel, jnp.asarray(wave_table(edge)))


def pair_kernel(shape, second_part, numbers_ref, *refs):
    edge, orb_dev, groups, fragments, slots = shape
    plane = edge * edge
    chunks = plane // LANES
    tiles = edge // ROWS
    half = edge // 2 + 1
    height = padded_half(edge)
    tables, refs = refs[:3], refs[3:]
    phi_refs, refs = refs[:groups], refs[groups:]
    if second_part:
        (twin_ref, relay_ref, one_ref, act_before, back_before), refs = refs[:5], refs[5:]
        act_outs, back_outs, refs = refs[:groups], refs[groups : groups + 3], refs[groups + 3 :]
        (act, back, state_sem, out_sem), refs = refs[:4], refs[4:]
    else:
        (twin_ref, two_ref, act), back_outs, refs = refs[:3], refs[3:6], refs[6:]
        (back, out_sem), refs = refs[:2], refs[2:]
    (near, far, wide, moved, dense, lower, upper, masks, listed, load_sem) = refs[:10]
    screen_ref, ahead_ref, behind_ref, table_sem = refs[10:]

    fragment, member, live_slots = numbers_ref[0], numbers_ref[1], numbers_ref[2]

    def first_of(slot):
        return numbers_ref[3 + slot]

    def second_of(slot):
        return numbers_ref[3 + slots + slot]

    def reach_of(slot):
        return numbers_ref[3 + 2 * slots + slot]

    def anchor(place, axis):
        return numbers_ref[3 + 3 * slots + 3 * place + axis]

    table_copies = [
        pltpu.make_async_copy(table, hold, table_sem.at[i])
        for i, (table, hold) in enumerate(zip(tables, refs[10:13]))
    ]
    lane = lax.broadcasted_iota(jnp.int32, (1, LANES), 1)
    stretch = next(n for n in (6, 4, 3, 2, 1) if chunks % n == 0)
    middle = pl.ds(edge, edge)

    even = lax.rem(fragment, 2) == 0

    def is_mine(slot):
        return (slot < live_slots) & (lax.div(second_of(slot), orb_dev) == member)

    def list_farthest(slot, found):
        chosen = is_mine(slot) & (reach_of(slot) == 2)

        @pl.when(chosen)
        def _():
            listed[found] = slot

        return found + chosen.astype(jnp.int32)

    farthest = lax.fori_loop(0, slots, list_farthest, jnp.int32(0))
    room = jnp.maximum(2, 2 * lax.div(farthest + 1, 2)) - farthest

    def list_others(slot, counts):
        early, found = counts
        mine = is_mine(slot) & (reach_of(slot) < 2)
        come = (reach_of(slot) == 0) | (even & (lax.rem(second_of(slot), orb_dev) == 0))
        taken = mine & come & (early < room)
        chosen = mine & jnp.logical_not(taken) if second_part else taken

        @pl.when(chosen)
        def _():
            listed[found] = slot

        return early + taken.astype(jnp.int32), found + chosen.astype(jnp.int32)

    begun = jnp.int32(0) if second_part else farthest
    _, found = lax.fori_loop(0, slots, list_others, (jnp.int32(0), begun))
    turns = lax.div(found + 1, 2)

    def slot_of(turn, side):
        at = 2 * turn + side
        live = at < found
        return listed[jnp.where(live, at, 2 * turn)], live

    def far_copy(side, source):
        return pltpu.make_async_copy(source, far.at[side], load_sem.at[1, side])

    def start_loads(turn):
        def load(side):
            slot, _ = slot_of(turn, side)
            first, second, reach = first_of(slot), second_of(slot), reach_of(slot)
            relative = lax.div(first, orb_dev) ^ member
            for k in range(groups):
                @pl.when(relative == k)
                def _():
                    pltpu.make_async_copy(
                        phi_refs[k].at[lax.rem(first, orb_dev)],
                        near.at[lax.rem(turn, 2), side],
                        load_sem.at[0, side],
                    ).start()
            own = lax.rem(second, orb_dev)

            @pl.when(reach == 0)
            def _():
                far_copy(side, phi_refs[0].at[own]).start()

            @pl.when((reach == 1) & (own == 0) & even)
            def _():
                far_copy(side, twin_ref.at[0]).start()

            if not second_part:
                @pl.when(reach == 2)
                def _():
                    far_copy(side, two_ref.at[own]).start()

            if second_part:
                @pl.when((reach == 1) & (own == 0) & jnp.logical_not(even))
                def _():
                    far_copy(side, relay_ref.at[0]).start()

                @pl.when((reach == 1) & (own > 0))
                def _():
                    far_copy(side, one_ref.at[jnp.maximum(own - 1, 0)]).start()

        load(0)
        pl.when(2 * turn + 1 < found)(functools.partial(load, 1))

    def wait_loads(turn):
        def wait(side):
            pltpu.make_async_copy(
                phi_refs[0].at[0], near.at[lax.rem(turn, 2), side], load_sem.at[0, side]
            ).wait()
            far_copy(side, phi_refs[0].at[0]).wait()

        wait(0)
        pl.when(2 * turn + 1 < found)(functools.partial(wait, 1))

    @pl.when(found > 0)
    def _():
        start_loads(0)
        for copy in table_copies:
            copy.start()

    if second_part:
        state_copies = [
            pltpu.make_async_copy(before, now, state_sem.at[i])
            for i, (before, now) in enumerate(((act_before, act), (back_before, back)))
        ]
        slab = plane * edge // LANES // groups
        act_copies = []
        for k in range(groups):
            source = (member ^ k) * slab
            act_copies.append(
                pltpu.make_async_copy(
                    act.at[:, pl.ds(pl.multiple_of(source, ROWS), slab), :],
                    act_outs[k],
                    out_sem.at[3 + k],
                )
            )
    else:
        act[...] = jnp.zeros_like(act)
        back[...] = jnp.zeros_like(back)

    def offset_of(slot):
        partner = lax.rem(fragment + reach_of(slot), fragments)
        return [anchor(partner, i) - anchor(fragment, i) for i in range(3)]

    def steps(count, body, most):
        width = max(n for n in range(1, most + 1) if count % n == 0)

        def step(i, _):
            for j in range(width):
                body(i * width + j)
            return 0

        if width == count:
            step(0, 0)
        else:
            lax.fori_loop(0, count // width, step, 0)

    def columns(k):
        return pl.ds(pl.multiple_of(k * LANES, LANES), LANES)

    def set_masks(place, delta):
        shape = masks.shape[1:]
        spot = lax.broadcasted_iota(jnp.int32, shape, 0) * LANES
        spot = spot + lax.broadcasted_iota(jnp.int32, shape, 1)
        y = ((spot.astype(jnp.float32) + 0.5) * (1.0 / edge)).astype(jnp.int32)
        z = spot - y * edge - delta[2]
        y = y - delta[1]
        inside = (y >= 0) & (y < edge) & (z >= 0) & (z < edge)
        masks[place] = jnp.where(inside, 1.0, 0.0)

    def shifted(source, place, delta, begin, count, ks):
        shift = lax.rem(delta[1] * edge + delta[2] + 4 * plane, plane)
        start = lax.rem(plane - shift, plane)
        whole, part = lax.div(start, LANES), lax.rem(start, LANES)
        turn = lax.rem(LANES - part, LANES)
        down = edge - jnp.clip(delta[0], -edge, edge) + begin
        x = lax.broadcasted_iota(jnp.int32, (count, LANES), 0) + (begin - delta[0])
        rows_inside = (x >= 0) & (x < edge)
        first = lane < LANES - part

        def piece(k):
            return pltpu.roll(source[lax.rem(k + whole, chunks), pl.ds(down, count), :], turn, 1)

        out = []
        low = piece(ks[0])
        for k in ks:
            high = piece(k + 1)
            value = jnp.where(first, low, high) * masks[place, pl.ds(k, 1), :]
            out.append(jnp.where(rows_inside, value, 0.0))
            low = high
        return out

    def tile(t, i, size):
        return pl.ds(pl.multiple_of(i * size + t * ROWS, ROWS), ROWS)

    def across(t, i, size):
        return pl.ds(t * (ROWS * size) + i, ROWS, stride=size)

    def solve_two(turn, _):
        wait_loads(turn)
        if second_part:
            @pl.when(turn == 0)
            def _():
                for copy in state_copies:
                    copy.start()

        near_now = near.at[lax.rem(turn, 2)]
        picked = [slot_of(turn, side) for side in range(2)]
        offsets = [offset_of(slot) for slot, _ in picked]
        returns = [[-d for d in delta] for delta in offsets]
        for side in range(2):
            set_masks(side, offsets[side])
            set_masks(2 + side, returns[side])

        def with_sides(work):
            both = 2 * turn + 1 < found
            pl.when(both)(functools.partial(work, 2))
            pl.when(jnp.logical_not(both))(functools.partial(work, 1))

        def widen(sides, k):
            for side in range(sides):
                wide[side, k, middle, :] = far[side, :, pl.ds(pl.multiple_of(k * LANES, LANES), LANES)]

        def over_y(sides_now, t):
            densities = []
            begin = pl.multiple_of(t * ROWS, ROWS)
            rows = pl.ds(begin, ROWS)
            for side in range(sides_now):
                values = shifted(wide.at[side], side, offsets[side], begin, ROWS, range(chunks))
                for k in range(chunks):
                    moved[side, k, rows, :] = values[k]
                    values[k] = values[k] * near_now[side, rows, k * LANES : (k + 1) * LANES]
                densities.append(values)
            planes = []
            for y in range(edge):
                first, offset = divmod(y * edge, LANES)
                sides = []
                for side in range(sides_now):
                    shift = (side * HALF - offset) % LANES
                    value = densities[side][first]
                    value = pltpu.roll(value, shift, 1) if shift else value
                    if offset + edge > LANES:
                        more = densities[side][first + 1]
                        more = pltpu.roll(more, shift, 1) if shift else more
                        value = jnp.where(lane < side * HALF + LANES - offset, value, more)
                    sides.append(value)
                planes.append(Number(jnp.where(lane < HALF, sides[0], sides[1] if sides[1:] else 0.0)))
            values = real_dft(planes)
            for i in range(half):
                at = tile(t, i, edge)
                lower[0, at, :] = values[i].real
                imag = values[i].imag
                lower[1, at, :] = jnp.zeros((ROWS, LANES), jnp.float32) if imag is None else imag

        def densities_over_y(sides):
            steps(chunks, functools.partial(widen, sides), chunks)
            steps(tiles, functools.partial(over_y, sides), 3)

        with_sides(densities_over_y)

        @pl.when(turn == 0)
        def _():
            for copy in table_copies:
                copy.wait()

        @pl.when(turn + 1 < turns)
        def _():
            start_loads(turn + 1)

        def over_x(t):
            at = [across(t, i, edge) for i in range(edge)]
            values = dft([Number(lower[0, a, :], lower[1, a, :]) for a in at], -1)
            real = jnp.concatenate([value.real for value in values], axis=0)
            imag = jnp.concatenate([value.imag for value in values], axis=0)
            at = [tile(t, i, height) for i in range(edge)]
            factor = jnp.concatenate([screen_ref[a, :] for a in at], axis=0)
            real, imag = split_dot(real, imag, ahead_ref)
            real, imag = split_dot(real * factor, imag * factor, behind_ref)
            rows = [slice(i * ROWS, (i + 1) * ROWS) for i in range(edge)]
            values = dft([Number(real[r], imag[r]) for r in rows], 1)
            for i in range(edge):
                upper[0, at[i], :] = values[i].real
                upper[1, at[i], :] = values[i].imag

        steps(height // ROWS, over_x, 4)
        if second_part:
            @pl.when(turn == 0)
            def _():
                for copy in state_copies:
                    copy.wait()

        firsts = [first_of(slot) for slot, _ in picked]

        def back_y(sides, t):
            begin = pl.multiple_of(t * ROWS, ROWS)
            rows = pl.ds(begin, ROWS)
            at = [across(t, i, height) for i in range(half)]
            values = [Number(upper[0, a, :], upper[1, a, :]) for a in at]
            values = values + [values[edge - i].conj() for i in range(half, edge)]
            planes = real_back(values)
            for side in range(sides):
                forward = []
                for k in range(chunks):
                    value = None
                    for y in range(k * LANES // edge, edge):
                        begins = y * edge - k * LANES
                        if begins >= LANES:
                            break
                        shift = (begins - side * HALF) % LANES
                        piece = pltpu.roll(planes[y], shift, 1) if shift else planes[y]
                        value = piece if value is None else jnp.where(lane < begins, value, piece)
                    forward.append(value * moved[side, k, rows, :])
                    other = value * near_now[side, rows, k * LANES : (k + 1) * LANES]
                    dense[side, k, pl.ds(edge + begin, ROWS), :] = other
                at = [pl.ds(t * (ROWS * chunks) + k, ROWS, stride=chunks) for k in range(chunks)]
                sums = [act[firsts[side], at[k], :] + forward[k] for k in range(chunks)]
                for k in range(chunks):
                    act[firsts[side], at[k], :] = sums[k]

        with_sides(lambda sides: steps(tiles, functools.partial(back_y, sides), 3))

        if second_part:
            @pl.when(turn + 1 == turns)
            def _():
                for copy in act_copies:
                    copy.start()

        homes = []
        for side in range(2):
            slot = picked[side][0]
            homes.append(reach_of(slot) * orb_dev + lax.rem(second_of(slot), orb_dev))

        def send_back(sides, g):
            for side in range(sides):
                ks = [g * stretch + i for i in range(stretch)]
                values = shifted(dense.at[side], 2 + side, returns[side], 0, edge, ks)
                at = [
                    (i, t, pl.ds(t * (ROWS * chunks) + ks[i], ROWS, stride=chunks))
                    for i in range(stretch)
                    for t in range(tiles)
                ]
                sums = [
                    back[homes[side], a, :] + values[i][t * ROWS : (t + 1) * ROWS] for i, t, a in at
                ]
                for (i, t, a), value in zip(at, sums):
                    back[homes[side], a, :] = value

        with_sides(lambda sides: steps(chunks // stretch, functools.partial(send_back, sides), 3))
        return 0

    if second_part:
        @pl.when(found == 0)
        def _():
            for copy in state_copies:
                copy.start()
            for copy in state_copies:
                copy.wait()
            for copy in act_copies:
                copy.start()

    lax.fori_loop(0, turns, solve_two, 0)
    if second_part:
        spans = ((orb_dev, 1), (orb_dev + 1, orb_dev - 1), (0, orb_dev))
    else:
        spans = ((2 * orb_dev + 1, orb_dev - 1), (2 * orb_dev, 1), (0, 2 * orb_dev))
    copies = [
        pltpu.make_async_copy(back.at[pl.ds(begin, count)], back_outs[i], out_sem.at[i])
        for i, (begin, count) in enumerate(spans)
    ]
    for copy in copies:
        copy.start()
    if second_part:
        copies += act_copies
    for copy in copies:
        copy.wait()


def pair_terms(numbers, fragments, slots, tables, pieces, far, before=()):
    second_part = bool(before)
    orb_dev, edge, plane = pieces[0].shape
    groups = len(pieces)
    frag_size = groups * orb_dev
    chunks = plane // LANES
    rows = edge * chunks
    height = padded_half(edge)
    shape = (edge, orb_dev, groups, fragments, slots)
    smem = pl.BlockSpec(memory_space=pltpu.SMEM)
    vmem = pl.BlockSpec(memory_space=pltpu.VMEM)
    hbm = pl.BlockSpec(memory_space=pltpu.HBM)
    f32 = jnp.float32

    def fields(*counts):
        return [jax.ShapeDtypeStruct((count, rows, LANES), f32) for count in counts]

    if second_part:
        out_shape = [jax.ShapeDtypeStruct((frag_size, rows // groups, LANES), f32)] * groups
        out_shape += fields(1, orb_dev - 1, orb_dev)
        out_specs = [hbm] * (groups + 3)
        scratch = [pltpu.VMEM(field.shape, f32) for field in fields(frag_size, REACH * orb_dev)]
        scratch += [pltpu.SemaphoreType.DMA((2,)), pltpu.SemaphoreType.DMA((3 + groups,))]
    else:
        out_shape = fields(frag_size, orb_dev - 1, 1, REACH * orb_dev)
        out_specs = [vmem, hbm, hbm, hbm]
        scratch = [pltpu.VMEM(((REACH + 1) * orb_dev, rows, LANES), f32)]
        scratch += [pltpu.SemaphoreType.DMA((3,))]
    return pl.pallas_call(
        functools.partial(pair_kernel, shape, second_part),
        out_shape=out_shape,
        in_specs=[smem] + [hbm] * (3 + groups + len(far) + len(before)),
        out_specs=out_specs,
        scratch_shapes=scratch
        + [
            pltpu.VMEM((2, 2, edge, plane), f32),
            pltpu.VMEM((2, edge, plane), f32),
            pltpu.VMEM((2, chunks, 3 * edge, LANES), f32),
            pltpu.VMEM((2, chunks, edge, LANES), f32),
            pltpu.VMEM((2, chunks, 3 * edge, LANES), f32),
            pltpu.VMEM((2, height * edge, LANES), f32),
            pltpu.VMEM((2, height * edge, LANES), f32),
            pltpu.VMEM((4, -(-chunks // ROWS) * ROWS, LANES), f32),
            pltpu.SMEM((slots,), jnp.int32),
            pltpu.SemaphoreType.DMA((2, 2)),
            *[pltpu.VMEM(table.shape, table.dtype) for table in tables],
            pltpu.SemaphoreType.DMA((3,)),
        ],
        compiler_params=pltpu.CompilerParams(vmem_limit_bytes=30 << 20),
        name="late_pair_terms" if second_part else "early_pair_terms",
    )(numbers, *tables, *pieces, *far, *before)


def flatten_kernel(shape, places_ref, *refs):
    edge, orb_dev, groups = shape
    pieces, (flat_ref, slab_ref) = refs[:groups], refs[groups:]
    member = places_ref[1]
    chunks = edge * edge // LANES
    slab = slab_ref.shape[1]
    for k in range(groups):
        for o in range(orb_dev):
            def move(j, _):
                value = pieces[k][o, :, pl.ds(pl.multiple_of(j * LANES, LANES), LANES)]
                for t in range(edge // ROWS):
                    at = pl.ds(t * (ROWS * chunks) + j, ROWS, stride=chunks)
                    flat_ref[k * orb_dev + o, at, :] = value[t * ROWS : (t + 1) * ROWS]
                return 0

            lax.fori_loop(0, chunks, move, 0)
    slab_ref[...] = flat_ref[:, pl.ds(pl.multiple_of(member * slab, ROWS), slab), :]


def flatten_terms(places, pieces):
    orb_dev, edge, plane = pieces[0].shape
    groups = len(pieces)
    rows = edge * plane // LANES
    frag_size = groups * orb_dev
    smem = pl.BlockSpec(memory_space=pltpu.SMEM)
    vmem = pl.BlockSpec(memory_space=pltpu.VMEM)
    return pl.pallas_call(
        functools.partial(flatten_kernel, (edge, orb_dev, groups)),
        out_shape=(
            jax.ShapeDtypeStruct((frag_size, rows, LANES), jnp.float32),
            jax.ShapeDtypeStruct((frag_size, rows // groups, LANES), jnp.float32),
        ),
        in_specs=[smem] + [vmem] * groups,
        out_specs=(vmem, vmem),
        compiler_params=pltpu.CompilerParams(vmem_limit_bytes=24 << 20),
        name="flatten_terms",
    )(places, *pieces)


def products(lefts, rights, length, step):
    def add(i, sums):
        at = pl.ds(pl.multiple_of(i * step, ROWS), step)
        right = [ref[index, at, :].reshape(step // ROWS, ROWS, LANES) for ref, index in rights]
        out = []
        for n, (ref, index) in enumerate(lefts):
            left = ref[index, at, :].reshape(step // ROWS, ROWS, LANES)
            for m in range(len(rights)):
                out.append(sums[n * len(rights) + m] + jnp.sum(left * right[m], axis=0))
        return tuple(out)

    zero = jnp.zeros((ROWS, LANES), jnp.float32)
    return lax.fori_loop(0, length // step, add, (zero,) * (len(lefts) * len(rights)))


def placed(result, sums, rows, lanes):
    row = lax.broadcasted_iota(jnp.int32, result.shape, 0)
    lane = lax.broadcasted_iota(jnp.int32, result.shape, 1)
    for n, a in enumerate(rows):
        for m, b in enumerate(lanes):
            value = jnp.sum(sums[n * len(lanes) + m], keepdims=True)
            result = jnp.where((row == a) & (lane == b), result + value, result)
    return result


def step_of(length):
    return next(n for n in (72, 24, 8) if length % n == 0)


def action_kernel(shape, places_ref, phi_ref, *refs):
    orb_dev, groups = shape
    parts, (act_ref, share_ref) = refs[:-2], refs[-2:]
    member = places_ref[1]
    frag_size = orb_dev * groups
    slab = act_ref.shape[1]
    value = parts[0][...]
    for part in parts[1:]:
        value = value + part[...]
    act_ref[...] = value
    rows = [(member ^ (a // orb_dev)) * orb_dev + a % orb_dev for a in range(frag_size)]
    result = jnp.zeros(share_ref.shape, jnp.float32)
    for half in range(0, frag_size, 4):
        bs = range(half, min(half + 4, frag_size))
        lefts, rights = [(phi_ref, a) for a in range(frag_size)], [(act_ref, b) for b in bs]
        result = placed(result, products(lefts, rights, slab, step_of(slab)), rows, bs)
    share_ref[...] = result


def action_terms(places, orb_dev, phi, parts):
    frag_size, slab = phi.shape[:2]
    smem = pl.BlockSpec(memory_space=pltpu.SMEM)
    vmem = pl.BlockSpec(memory_space=pltpu.VMEM)
    return pl.pallas_call(
        functools.partial(action_kernel, (orb_dev, frag_size // orb_dev)),
        out_shape=(
            jax.ShapeDtypeStruct((frag_size, slab, LANES), jnp.float32),
            jax.ShapeDtypeStruct((frag_size, LANES), jnp.float32),
        ),
        in_specs=[smem] + [vmem] * (1 + len(parts)),
        out_specs=(vmem, vmem),
        compiler_params=pltpu.CompilerParams(vmem_limit_bytes=16 << 20),
        name="action_terms",
    )(places, phi, *parts)


def home_kernel(shape, places_ref, flat_ref, own_ref, *refs):
    edge, orb_dev, groups, first, count = shape
    if first == 0:
        (two_ref, twin_ref, relay_ref, share_ref), refs = refs[:4], refs[4:]
    else:
        (two_ref, one_ref), refs = refs[:2], refs[2:]
    outs, total = refs[:groups], refs[groups]
    fragment, member = places_ref[0], places_ref[1]
    frag_size = orb_dev * groups
    rows = flat_ref.shape[1]
    slab = rows // groups
    for i in range(count):
        value = own_ref[first + i] + two_ref[i]
        if first == 0:
            @pl.when(lax.rem(fragment, 2) == 1)
            def _():
                total[i] = value + twin_ref[i]

            @pl.when(lax.rem(fragment, 2) == 0)
            def _():
                total[i] = value + relay_ref[i]
        else:
            total[i] = value + one_ref[i]
    lefts, rights = [(flat_ref, a) for a in range(frag_size)], [(total, i) for i in range(count)]
    places = [(member ^ (a // orb_dev)) * orb_dev + a % orb_dev for a in range(frag_size)]
    result = share_ref[...] if first == 0 else jnp.zeros((frag_size, LANES), jnp.float32)
    sums = products(lefts, rights, rows, step_of(rows))
    result = placed(result, sums, places, [member * orb_dev + first + i for i in range(count)])
    result = result * (1.0 / float(edge**3))
    for k in range(groups):
        begin = pl.multiple_of((member ^ k) * slab, ROWS)
        for i in range(count):
            outs[k][i * slab : (i + 1) * slab, :] = total[i, pl.ds(begin, slab), :]
        outs[k][count * slab :, :] = result


def home_terms(places, edge, groups, flat, own, first, *came):
    frag_size, rows = flat.shape[:2]
    count = came[0].shape[0]
    smem = pl.BlockSpec(memory_space=pltpu.SMEM)
    vmem = pl.BlockSpec(memory_space=pltpu.VMEM)
    f32 = jnp.float32
    parcel = jax.ShapeDtypeStruct((count * rows // groups + frag_size, LANES), f32)
    return pl.pallas_call(
        functools.partial(home_kernel, (edge, frag_size // groups, groups, first, count)),
        out_shape=[parcel] * groups,
        in_specs=[smem] + [vmem] * (2 + len(came)),
        out_specs=[vmem] * groups,
        scratch_shapes=[pltpu.VMEM((count, rows, LANES), f32)],
        compiler_params=pltpu.CompilerParams(vmem_limit_bytes=16 << 20),
        name="home_terms",
    )(places, flat, own, *came)


def exchanged(value, axis, width):
    size = value.shape[axis]
    index = lax.broadcasted_iota(jnp.int32, value.shape, axis)
    below, above = pltpu.roll(value, width, axis), pltpu.roll(value, size - width, axis)
    return jnp.where((index & width) != 0, below, above)


def gradient_kernel(shape, places_ref, act_ref, phi_ref, *refs):
    edge, orb_dev, groups = shape
    heads, tails, refs = refs[:groups], refs[groups : 2 * groups], refs[2 * groups :]
    out_ref, lagrange_ref, hold = refs
    member = places_ref[1]
    frag_size = orb_dev * groups
    chunks = edge * edge // LANES
    slab_rows = edge // groups
    slab = slab_rows * chunks
    sums = [
        head[slab:, :] + tail[(orb_dev - 1) * slab :, :] for head, tail in zip(heads, tails)
    ]
    while len(sums) > 1:
        sums = [sums[i] + sums[i + 1] for i in range(0, len(sums), 2)]
    square = jnp.concatenate([sums[0], jnp.zeros((LANES - frag_size, LANES), jnp.float32)], axis=0)
    lagrange = 0.5 * (square + square.T)[:frag_size, :]
    lagrange_ref[...] = lagrange[:, :frag_size]
    bit = 1
    while bit < groups:
        turned = exchanged(exchanged(lagrange, 0, bit * orb_dev), 1, bit * orb_dev)
        lagrange = jnp.where((member & bit) != 0, turned, lagrange)
        bit *= 2

    for k in range(groups):
        for o in range(orb_dev):
            a = (member ^ k) * orb_dev + o
            came = heads[k][:slab, :] if o == 0 else tails[k][(o - 1) * slab : o * slab, :]
            value = act_ref[a] + came
            for b in range(frag_size):
                factor = lagrange[b : b + 1, k * orb_dev + o : k * orb_dev + o + 1]
                value = value - factor * phi_ref[b]
            hold[pl.ds(pl.multiple_of(a * slab, ROWS), slab), :] = value
    for x in range(slab_rows):
        for j in range(chunks):
            value = hold[pl.ds(x * chunks + j, frag_size, stride=slab), :]
            out_ref[x, :, j * LANES : (j + 1) * LANES] = value


def gradient_terms(places, edge, act, phi, heads, tails):
    groups = len(heads)
    frag_size, slab = act.shape[:2]
    smem = pl.BlockSpec(memory_space=pltpu.SMEM)
    vmem = pl.BlockSpec(memory_space=pltpu.VMEM)
    f32 = jnp.float32
    gradient, lagrange = pl.pallas_call(
        functools.partial(gradient_kernel, (edge, frag_size // groups, groups)),
        out_shape=(
            jax.ShapeDtypeStruct((edge // groups, frag_size, edge * edge), f32),
            jax.ShapeDtypeStruct((frag_size, frag_size), f32),
        ),
        in_specs=[smem] + [vmem] * (2 + 2 * groups),
        out_specs=(vmem, vmem),
        scratch_shapes=[pltpu.VMEM((frag_size * slab, LANES), f32)],
        compiler_params=pltpu.CompilerParams(vmem_limit_bytes=16 << 20),
        name="gradient_terms",
    )(places, act, phi, *heads, *tails)
    return gradient.transpose(1, 0, 2), lagrange


def together(*arrays):
    return lax.optimization_barrier(arrays)


def to_fragment(block, distance, senders=None):
    devices = lax.axis_size("orb")
    senders = range(devices) if senders is None else range(senders, devices, 2)
    return lax.ppermute(block, "orb", [(i, (i + distance) % devices) for i in senders])


def with_twin(block):
    return lax.ppermute(block, "orb", [(i, i ^ 1) for i in range(lax.axis_size("orb"))])


def with_member(block, bit):
    return lax.ppermute(block, "grp", [(i, i ^ bit) for i in range(lax.axis_size("grp"))])


def by_member(parcels):
    groups = len(parcels)
    received = list(parcels)
    bit = groups // 2
    while bit:
        for k in reversed(range(groups)):
            if k & bit:
                received[k] = with_member(received[k], bit)
        bit //= 2
    return received


def shards(orbitals, kernel, anchors, pair_count, pair_first, pair_second, pair_reach):
    groups = lax.axis_size("grp")
    orb_dev, edge, plane = orbitals.shape
    places = jnp.stack([lax.axis_index("orb"), lax.axis_index("grp")]).astype(jnp.int32)

    numbers = [places, pair_count, pair_first, pair_second, pair_reach, anchors.reshape(-1)]
    screen, numbers, *tables = screen_terms(jnp.concatenate(numbers), kernel)
    two = to_fragment(orbitals, -2)
    twin = with_twin(orbitals[:1])
    pieces = {0: orbitals}
    bit = groups // 2
    while bit:
        for k in list(pieces):
            pieces[k ^ bit] = with_member(pieces[k], bit)
        if bit == groups // 2:
            two, twin, tail, pieces[bit], screen, numbers, *tables = together(
                two, twin, orbitals[1:], pieces[bit], screen, numbers, *tables
            )
            one = to_fragment(tail, -1)
            relay = to_fragment(twin, -2, 1)
        bit //= 2
    pieces = [pieces[k] for k in range(groups)]
    tables = [screen, *tables]
    sizes = (anchors.shape[0], pair_first.shape[0])
    act, two_tail, two_head, back = pair_terms(numbers, *sizes, tables, pieces, [twin, two])
    two_tail, relay, one = together(two_tail, relay, one)
    two_tail = to_fragment(two_tail, 2)
    *acts, one_head, one_tail, own = pair_terms(
        numbers, *sizes, tables, pieces, [twin, relay, one], [act, back]
    )

    acts[-1], two_tail, two_head = together(acts[-1], two_tail, two_head)
    two_head = to_fragment(two_head, 2)
    twin = with_twin(one_head)
    bit = 1
    parts = {k: [act] for k, act in enumerate(acts)}
    while bit < groups:
        for k in sorted(parts, reverse=True):
            if k & bit:
                going = sum(parts[k][1:], parts[k][0])
                if bit == 2:
                    _, twin, one_tail, two_head = together(going, twin, one_tail, two_head)
                del parts[k]
                parts[k ^ bit].append(with_member(going, bit))
        bit *= 2
    one_tail = to_fragment(one_tail, 1)
    relay = to_fragment(twin, 2, 0)

    flat, phi = flatten_terms(places, pieces)
    tails = home_terms(places, edge, groups, flat, own, 1, two_tail, one_tail)
    tails = by_member(tails)
    act, share = action_terms(places, orb_dev, phi, parts[0])
    heads = by_member(
        home_terms(places, edge, groups, flat, own, 0, two_head, twin, relay, share)
    )
    gradient, lagrange = gradient_terms(places, edge, act, phi, heads, tails)
    return (gradient, lagrange[None])


def solution(mesh):
    placed = (P(("orb", "grp"), None, None), P(), P(), P("orb"), P("orb"), P("orb"), P("orb"))
    return jax.shard_map(
        shards,
        mesh=mesh,
        in_specs=placed,
        out_specs=(P("orb", "grp", None), P("orb", None, None)),
        check_vma=False,
    )
```

```python
import functools
import math

import jax
import jax.numpy as jnp
import numpy as np
from jax import lax
from jax.experimental import pallas as pl
from jax.experimental.pallas import tpu as pltpu
from jax.sharding import PartitionSpec as P

REACH = 2
LANES = 128
ROWS = 8
HALF = LANES // 2


class Number:
    def __init__(self, real, imag=None):
        self.real, self.imag = real, imag

    def __add__(self, other):
        if self.imag is None or other.imag is None:
            imag = self.imag if other.imag is None else other.imag
        else:
            imag = self.imag + other.imag
        return Number(self.real + other.real, imag)

    def __sub__(self, other):
        if other.imag is None:
            imag = self.imag
        else:
            imag = -other.imag if self.imag is None else self.imag - other.imag
        return Number(self.real - other.real, imag)

    def conj(self):
        return self if self.imag is None else Number(self.real, -self.imag)

    def scaled(self, factor):
        return Number(self.real * factor, None if self.imag is None else self.imag * factor)

    def turned(self, sign):
        if self.imag is None:
            return Number(jnp.zeros_like(self.real), self.real if sign > 0 else -self.real)
        return Number(-self.imag, self.real) if sign > 0 else Number(self.imag, -self.real)

    def plus_turned(self, other, sign):
        if sign < 0:
            return self.minus_turned(other)
        real = self.real if other.imag is None else self.real - other.imag
        return Number(real, other.real if self.imag is None else self.imag + other.real)

    def minus_turned(self, other):
        real = self.real if other.imag is None else self.real + other.imag
        return Number(real, -other.real if self.imag is None else self.imag - other.real)

    def times(self, angle):
        real, imag = math.cos(angle), math.sin(angle)
        if abs(imag) < 1e-12:
            return self if real > 0 else self.scaled(-1.0)
        if abs(real) < 1e-12:
            return self.turned(imag)
        if self.imag is None:
            return Number(self.real * real, self.real * imag)
        return Number(self.real * real - self.imag * imag, self.real * imag + self.imag * real)


def coprime(n):
    for p in (2, 3, 5, 7):
        power = 1
        while n % (power * p) == 0:
            power *= p
        if 1 < power < n:
            return power, n // power
    return None


def radix(n):
    return next((p for p in (4, 2, 3, 5, 7) if n % p == 0 and n > p), None)


def meeting(i, j, first, second):
    return next(k for k in range(first * second) if k % first == i and k % second == j)


def dft(values, sign):
    n = len(values)
    if n == 1:
        return values
    if n == 2:
        return [values[0] + values[1], values[0] - values[1]]
    if n == 3:
        a, b, c = values
        total, side = b + c, (b - c).scaled(math.sqrt(0.75))
        middle = a - total.scaled(0.5)
        return [a + total, middle.plus_turned(side, sign), middle.plus_turned(side, -sign)]
    if n == 4:
        a, b, c, d = values
        s, t, u, v = a + c, a - c, b + d, b - d
        return [s + u, t.plus_turned(v, sign), s - u, t.plus_turned(v, -sign)]
    out = [None] * n
    if coprime(n):
        first, second = coprime(n)
        columns = [
            dft([values[(i * second + j * first) % n] for i in range(first)], sign)
            for j in range(second)
        ]
        for i in range(first):
            row = dft([column[i] for column in columns], sign)
            for j in range(second):
                out[meeting(i, j, first, second)] = row[j]
        return out
    p = radix(n)
    if p:
        rest = n // p
        columns = [dft(values[j::p], sign) for j in range(p)]
        for i in range(rest):
            row = dft(
                [columns[j][i].times(sign * 2.0 * math.pi * i * j / n) for j in range(p)], sign
            )
            for j in range(p):
                out[i + rest * j] = row[j]
        return out
    for k in range(n):
        total = values[0]
        for j in range(1, n):
            total = total + values[j].times(sign * 2.0 * math.pi * (j * k % n) / n)
        out[k] = total
    return out


def real_dft(values):
    n = len(values)
    if n <= 4:
        out = dft(values, -1)
    else:
        out = [None] * n
        if coprime(n):
            first, second = coprime(n)
            columns = [
                real_dft([values[(i * second + j * first) % n] for i in range(first)])
                for j in range(second)
            ]
            for i in range(first // 2 + 1):
                entries = [column[i] for column in columns]
                alone = 2 * i % first == 0
                row = real_dft(entries) if alone else dft(entries, -1)
                for j in range(second):
                    out[meeting(i, j, first, second)] = row[j]
        elif radix(n):
            p = radix(n)
            rest = n // p
            columns = [real_dft(values[j::p]) for j in range(p)]
            for i in range(rest // 2 + 1):
                row = dft(
                    [columns[j][i].times(-2.0 * math.pi * i * j / n) for j in range(p)], -1
                )
                for j in range(p):
                    out[i + rest * j] = row[j]
        else:
            out = dft(values, -1)
    for k in range(1, n):
        if out[k] is None or (k > n // 2 and out[n - k] is not None):
            out[k] = out[n - k].conj()
    out[0] = Number(out[0].real)
    if n % 2 == 0:
        out[n // 2] = Number(out[n // 2].real)
    return out


def real_back(values):
    n = len(values)
    if n == 1:
        return [values[0].real]
    if n == 2:
        return [values[0].real + values[1].real, values[0].real - values[1].real]
    if n == 3:
        a, b = values[0].real, values[1]
        side = b.imag * math.sqrt(3.0)
        middle = a - b.real
        return [a + 2.0 * b.real, middle - side, middle + side]
    if n == 4:
        s, t = values[0].real + values[2].real, values[0].real - values[2].real
        u, v = 2.0 * values[1].real, 2.0 * values[1].imag
        return [s + u, t - v, s - u, t + v]
    out = [None] * n
    if coprime(n):
        first, second = coprime(n)
        rows = []
        for i in range(first // 2 + 1):
            entries = [values[meeting(i, j, first, second)] for j in range(second)]
            if 2 * i % first == 0:
                rows.append([Number(value) for value in real_back(entries)])
            else:
                rows.append(dft(entries, 1))
        for b in range(second):
            half = [row[b] for row in rows]
            whole = half + [half[first - i].conj() for i in range(len(half), first)]
            for a, value in enumerate(real_back(whole)):
                out[(a * second + b * first) % n] = value
        return out
    p = radix(n)
    if p:
        rest = n // p
        parts = []
        for i in range(p // 2 + 1):
            entries = values[i::p]
            if i == 0:
                parts.append([Number(value) for value in real_back(entries)])
            else:
                inner = dft(entries, 1)
                parts.append([inner[m].times(2.0 * math.pi * i * m / n) for m in range(rest)])
                if 2 * i == p:
                    parts[-1] = [Number(value.real) for value in parts[-1]]
        for m in range(rest):
            half = [part[m] for part in parts]
            whole = half + [half[p - i].conj() for i in range(len(half), p)]
            for j, value in enumerate(real_back(whole)):
                out[m + rest * j] = value
        return out
    return [value.real for value in dft(values, 1)]


def wave_table(edge):
    index = np.arange(edge)
    angles = 2.0 * np.pi / edge * (np.outer(index, index) % edge)
    full = np.zeros((2, 2, HALF, 2, HALF))
    for side in range(2):
        full[0, side, :edge, side, :edge] = np.cos(angles)
        full[1, side, :edge, side, :edge] = np.sin(angles)
    full = full.reshape(2, LANES, LANES)
    high = full.astype(jnp.bfloat16)
    low = (full - high.astype(np.float64)).astype(jnp.bfloat16)
    return np.stack([high, low])


def split_dot(real, imag, matrix):
    value = jnp.concatenate([real, imag], axis=1)
    high = value.astype(jnp.bfloat16)
    low = (value - high.astype(jnp.float32)).astype(jnp.bfloat16)
    product = jnp.dot(
        jnp.concatenate([high, low, high], axis=1), matrix[...], preferred_element_type=jnp.float32
    )
    return product[:, :LANES], product[:, LANES:]


def padded_half(edge):
    return -(-(edge // 2 + 1) // ROWS) * ROWS


def screen_kernel(edge, numbers_ref, kernel_ref, waves_ref, out_ref, kept_ref, ahead_ref, behind_ref, flipped):
    for i in range(numbers_ref.shape[0]):
        kept_ref[i] = numbers_ref[i]
    for table, sign in ((ahead_ref, -1), (behind_ref, 1)):
        for part, source in enumerate((0, 0, 1)):
            for i in range(2):
                for j in range(2):
                    value = waves_ref[source, (i + j) % 2]
                    if i != j and (i > j) == (sign > 0):
                        value = -value
                    rows = slice((2 * part + i) * LANES, (2 * part + i + 1) * LANES)
                    table[rows, j * LANES : (j + 1) * LANES] = value
    exact = dict(precision=lax.Precision.HIGHEST, preferred_element_type=jnp.float32)

    def index(shape, axis):
        return lax.broadcasted_iota(jnp.int32, shape, axis)

    square, whole = (edge, edge), (LANES, LANES)
    flip = index(square, 0) + index(square, 1)
    flip = ((flip == 0) | (flip == edge)).astype(jnp.float32)
    source, target = index(whole, 0), index(whole, 1)
    target = jnp.where(target < HALF, target, target - HALF)
    mirror = ((source + target == 0) | (source + target == edge)) & (source < edge) & (target < edge)
    mirror = mirror.astype(jnp.float32)
    flipped[...] = jnp.dot(flip, kernel_ref[...], **exact)
    height = padded_half(edge)
    lane = index((edge, LANES), 1)
    out_ref[...] = jnp.zeros_like(out_ref)

    def piece(ref, y):
        begin, offset = divmod(y * edge, LANES)
        value = ref[:, begin * LANES : (begin + 1) * LANES]
        value = pltpu.roll(value, LANES - offset, 1) if offset else value
        if offset + edge > LANES:
            more = ref[:, (begin + 1) * LANES : (begin + 2) * LANES]
            value = jnp.where(lane < LANES - offset, value, pltpu.roll(more, LANES - offset, 1))
        return value

    for y in range(edge // 2 + 1):
        value = piece(kernel_ref, y)
        value = jnp.where(lane < HALF, value, pltpu.roll(value, HALF, 1))
        value = value + jnp.dot(piece(flipped, (edge - y) % edge), mirror, **exact)
        value = value * (0.5 / float(edge**3))
        for t in range(edge // ROWS):
            at = pl.ds(t * ROWS * height + y, ROWS, stride=height)
            out_ref[at, :] = value[t * ROWS : (t + 1) * ROWS]


def screen_terms(numbers, kernel):
    edge, plane = kernel.shape
    smem = pl.BlockSpec(memory_space=pltpu.SMEM)
    vmem = pl.BlockSpec(memory_space=pltpu.VMEM)
    table = jax.ShapeDtypeStruct((6 * LANES, 2 * LANES), jnp.bfloat16)
    return pl.pallas_call(
        functools.partial(screen_kernel, edge),
        out_shape=[
            jax.ShapeDtypeStruct((edge * padded_half(edge), LANES), jnp.float32),
            jax.ShapeDtypeStruct(numbers.shape, numbers.dtype),
            table,
            table,
        ],
        in_specs=[smem, vmem, vmem],
        out_specs=[vmem, smem, vmem, vmem],
        scratch_shapes=[pltpu.VMEM((edge, plane), jnp.float32)],
        compiler_params=pltpu.CompilerParams(vmem_limit_bytes=8 << 20),
        name="screen_terms",
    )(numbers, kernel, jnp.asarray(wave_table(edge)))


def pair_kernel(shape, second_part, numbers_ref, *refs):
    edge, orb_dev, groups, fragments, slots = shape
    plane = edge * edge
    chunks = plane // LANES
    tiles = edge // ROWS
    half = edge // 2 + 1
    height = padded_half(edge)
    tables, refs = refs[:3], refs[3:]
    phi_refs, refs = refs[:groups], refs[groups:]
    if second_part:
        (twin_ref, relay_ref, one_ref, act_before, back_before), refs = refs[:5], refs[5:]
        act_outs, back_outs, refs = refs[:groups], refs[groups : groups + 3], refs[groups + 3 :]
        (act, back, state_sem, out_sem), refs = refs[:4], refs[4:]
    else:
        (twin_ref, two_ref, act), back_outs, refs = refs[:3], refs[3:6], refs[6:]
        (back, out_sem), refs = refs[:2], refs[2:]
    (near, far, wide, moved, dense, lower, upper, masks, listed, load_sem) = refs[:10]
    screen_ref, ahead_ref, behind_ref, table_sem = refs[10:]

    fragment, member, live_slots = numbers_ref[0], numbers_ref[1], numbers_ref[2]

    def first_of(slot):
        return numbers_ref[3 + slot]

    def second_of(slot):
        return numbers_ref[3 + slots + slot]

    def reach_of(slot):
        return numbers_ref[3 + 2 * slots + slot]

    def anchor(place, axis):
        return numbers_ref[3 + 3 * slots + 3 * place + axis]

    table_copies = [
        pltpu.make_async_copy(table, hold, table_sem.at[i])
        for i, (table, hold) in enumerate(zip(tables, refs[10:13]))
    ]
    lane = lax.broadcasted_iota(jnp.int32, (1, LANES), 1)
    stretch = next(n for n in (6, 4, 3, 2, 1) if chunks % n == 0)
    middle = pl.ds(edge, edge)

    even = lax.rem(fragment, 2) == 0

    def is_mine(slot):
        return (slot < live_slots) & (lax.div(second_of(slot), orb_dev) == member)

    def list_farthest(slot, found):
        chosen = is_mine(slot) & (reach_of(slot) == 2)

        @pl.when(chosen)
        def _():
            listed[found] = slot

        return found + chosen.astype(jnp.int32)

    farthest = lax.fori_loop(0, slots, list_farthest, jnp.int32(0))
    room = jnp.maximum(2, 2 * lax.div(farthest + 1, 2)) - farthest

    def list_others(slot, counts):
        early, found = counts
        mine = is_mine(slot) & (reach_of(slot) < 2)
        come = (reach_of(slot) == 0) | (even & (lax.rem(second_of(slot), orb_dev) == 0))
        taken = mine & come & (early < room)
        chosen = mine & jnp.logical_not(taken) if second_part else taken

        @pl.when(chosen)
        def _():
            listed[found] = slot

        return early + taken.astype(jnp.int32), found + chosen.astype(jnp.int32)

    begun = jnp.int32(0) if second_part else farthest
    _, found = lax.fori_loop(0, slots, list_others, (jnp.int32(0), begun))
    turns = lax.div(found + 1, 2)

    def slot_of(turn, side):
        at = 2 * turn + side
        live = at < found
        return listed[jnp.where(live, at, 2 * turn)], live

    def far_copy(side, source):
        return pltpu.make_async_copy(source, far.at[side], load_sem.at[1, side])

    def start_loads(turn):
        def load(side):
            slot, _ = slot_of(turn, side)
            first, second, reach = first_of(slot), second_of(slot), reach_of(slot)
            relative = lax.div(first, orb_dev) ^ member
            for k in range(groups):
                @pl.when(relative == k)
                def _():
                    pltpu.make_async_copy(
                        phi_refs[k].at[lax.rem(first, orb_dev)],
                        near.at[lax.rem(turn, 2), side],
                        load_sem.at[0, side],
                    ).start()
            own = lax.rem(second, orb_dev)

            @pl.when(reach == 0)
            def _():
                far_copy(side, phi_refs[0].at[own]).start()

            @pl.when((reach == 1) & (own == 0) & even)
            def _():
                far_copy(side, twin_ref.at[0]).start()

            if not second_part:
                @pl.when(reach == 2)
                def _():
                    far_copy(side, two_ref.at[own]).start()

            if second_part:
                @pl.when((reach == 1) & (own == 0) & jnp.logical_not(even))
                def _():
                    far_copy(side, relay_ref.at[0]).start()

                @pl.when((reach == 1) & (own > 0))
                def _():
                    far_copy(side, one_ref.at[jnp.maximum(own - 1, 0)]).start()

        load(0)
        pl.when(2 * turn + 1 < found)(functools.partial(load, 1))

    def wait_loads(turn):
        def wait(side):
            pltpu.make_async_copy(
                phi_refs[0].at[0], near.at[lax.rem(turn, 2), side], load_sem.at[0, side]
            ).wait()
            far_copy(side, phi_refs[0].at[0]).wait()

        wait(0)
        pl.when(2 * turn + 1 < found)(functools.partial(wait, 1))

    @pl.when(found > 0)
    def _():
        start_loads(0)
        for copy in table_copies:
            copy.start()

    if second_part:
        state_copies = [
            pltpu.make_async_copy(before, now, state_sem.at[i])
            for i, (before, now) in enumerate(((act_before, act), (back_before, back)))
        ]
        slab = plane * edge // LANES // groups
        act_copies = []
        for k in range(groups):
            source = (member ^ k) * slab
            act_copies.append(
                pltpu.make_async_copy(
                    act.at[:, pl.ds(pl.multiple_of(source, ROWS), slab), :],
                    act_outs[k],
                    out_sem.at[3 + k],
                )
            )
    else:
        act[...] = jnp.zeros_like(act)
        back[...] = jnp.zeros_like(back)

    def offset_of(slot):
        partner = lax.rem(fragment + reach_of(slot), fragments)
        return [anchor(partner, i) - anchor(fragment, i) for i in range(3)]

    def steps(count, body, most):
        width = max(n for n in range(1, most + 1) if count % n == 0)

        def step(i, _):
            for j in range(width):
                body(i * width + j)
            return 0

        if width == count:
            step(0, 0)
        else:
            lax.fori_loop(0, count // width, step, 0)

    def columns(k):
        return pl.ds(pl.multiple_of(k * LANES, LANES), LANES)

    def set_masks(place, delta):
        shape = masks.shape[1:]
        spot = lax.broadcasted_iota(jnp.int32, shape, 0) * LANES
        spot = spot + lax.broadcasted_iota(jnp.int32, shape, 1)
        y = ((spot.astype(jnp.float32) + 0.5) * (1.0 / edge)).astype(jnp.int32)
        z = spot - y * edge - delta[2]
        y = y - delta[1]
        inside = (y >= 0) & (y < edge) & (z >= 0) & (z < edge)
        masks[place] = jnp.where(inside, 1.0, 0.0)

    def shifted(source, place, delta, begin, count, ks):
        shift = lax.rem(delta[1] * edge + delta[2] + 4 * plane, plane)
        start = lax.rem(plane - shift, plane)
        whole, part = lax.div(start, LANES), lax.rem(start, LANES)
        turn = lax.rem(LANES - part, LANES)
        down = edge - jnp.clip(delta[0], -edge, edge) + begin
        x = lax.broadcasted_iota(jnp.int32, (count, LANES), 0) + (begin - delta[0])
        rows_inside = (x >= 0) & (x < edge)
        first = lane < LANES - part

        def piece(k):
            return pltpu.roll(source[lax.rem(k + whole, chunks), pl.ds(down, count), :], turn, 1)

        out = []
        low = piece(ks[0])
        for k in ks:
            high = piece(k + 1)
            value = jnp.where(first, low, high) * masks[place, pl.ds(k, 1), :]
            out.append(jnp.where(rows_inside, value, 0.0))
            low = high
        return out

    def tile(t, i, size):
        return pl.ds(pl.multiple_of(i * size + t * ROWS, ROWS), ROWS)

    def across(t, i, size):
        return pl.ds(t * (ROWS * size) + i, ROWS, stride=size)

    def solve_two(turn, _):
        wait_loads(turn)
        if second_part:
            @pl.when(turn == 0)
            def _():
                for copy in state_copies:
                    copy.start()

        near_now = near.at[lax.rem(turn, 2)]
        picked = [slot_of(turn, side) for side in range(2)]
        offsets = [offset_of(slot) for slot, _ in picked]
        returns = [[-d for d in delta] for delta in offsets]
        for side in range(2):
            set_masks(side, offsets[side])
            set_masks(2 + side, returns[side])

        def with_sides(work):
            both = 2 * turn + 1 < found
            pl.when(both)(functools.partial(work, 2))
            pl.when(jnp.logical_not(both))(functools.partial(work, 1))

        def widen(sides, k):
            for side in range(sides):
                wide[side, k, middle, :] = far[side, :, pl.ds(pl.multiple_of(k * LANES, LANES), LANES)]

        def over_y(sides_now, t):
            densities = []
            begin = pl.multiple_of(t * ROWS, ROWS)
            rows = pl.ds(begin, ROWS)
            for side in range(sides_now):
                values = shifted(wide.at[side], side, offsets[side], begin, ROWS, range(chunks))
                for k in range(chunks):
                    moved[side, k, rows, :] = values[k]
                    values[k] = values[k] * near_now[side, rows, k * LANES : (k + 1) * LANES]
                densities.append(values)
            planes = []
            for y in range(edge):
                first, offset = divmod(y * edge, LANES)
                sides = []
                for side in range(sides_now):
                    shift = (side * HALF - offset) % LANES
                    value = densities[side][first]
                    value = pltpu.roll(value, shift, 1) if shift else value
                    if offset + edge > LANES:
                        more = densities[side][first + 1]
                        more = pltpu.roll(more, shift, 1) if shift else more
                        value = jnp.where(lane < side * HALF + LANES - offset, value, more)
                    sides.append(value)
                planes.append(Number(jnp.where(lane < HALF, sides[0], sides[1] if sides[1:] else 0.0)))
            values = real_dft(planes)
            for i in range(half):
                at = tile(t, i, edge)
                lower[0, at, :] = values[i].real
                imag = values[i].imag
                lower[1, at, :] = jnp.zeros((ROWS, LANES), jnp.float32) if imag is None else imag

        def densities_over_y(sides):
            steps(chunks, functools.partial(widen, sides), chunks)
            steps(tiles, functools.partial(over_y, sides), 3)

        with_sides(densities_over_y)

        @pl.when(turn == 0)
        def _():
            for copy in table_copies:
                copy.wait()

        @pl.when(turn + 1 < turns)
        def _():
            start_loads(turn + 1)

        def over_x(t):
            at = [across(t, i, edge) for i in range(edge)]
            values = dft([Number(lower[0, a, :], lower[1, a, :]) for a in at], -1)
            real = jnp.concatenate([value.real for value in values], axis=0)
            imag = jnp.concatenate([value.imag for value in values], axis=0)
            at = [tile(t, i, height) for i in range(edge)]
            factor = jnp.concatenate([screen_ref[a, :] for a in at], axis=0)
            real, imag = split_dot(real, imag, ahead_ref)
            real, imag = split_dot(real * factor, imag * factor, behind_ref)
            rows = [slice(i * ROWS, (i + 1) * ROWS) for i in range(edge)]
            values = dft([Number(real[r], imag[r]) for r in rows], 1)
            for i in range(edge):
                upper[0, at[i], :] = values[i].real
                upper[1, at[i], :] = values[i].imag

        steps(height // ROWS, over_x, 4)
        if second_part:
            @pl.when(turn == 0)
            def _():
                for copy in state_copies:
                    copy.wait()

        firsts = [first_of(slot) for slot, _ in picked]

        def back_y(sides, t):
            begin = pl.multiple_of(t * ROWS, ROWS)
            rows = pl.ds(begin, ROWS)
            at = [across(t, i, height) for i in range(half)]
            values = [Number(upper[0, a, :], upper[1, a, :]) for a in at]
            values = values + [values[edge - i].conj() for i in range(half, edge)]
            planes = real_back(values)
            for side in range(sides):
                forward = []
                for k in range(chunks):
                    value = None
                    for y in range(k * LANES // edge, edge):
                        begins = y * edge - k * LANES
                        if begins >= LANES:
                            break
                        shift = (begins - side * HALF) % LANES
                        piece = pltpu.roll(planes[y], shift, 1) if shift else planes[y]
                        value = piece if value is None else jnp.where(lane < begins, value, piece)
                    forward.append(value * moved[side, k, rows, :])
                    other = value * near_now[side, rows, k * LANES : (k + 1) * LANES]
                    dense[side, k, pl.ds(edge + begin, ROWS), :] = other
                at = [pl.ds(t * (ROWS * chunks) + k, ROWS, stride=chunks) for k in range(chunks)]
                sums = [act[firsts[side], at[k], :] + forward[k] for k in range(chunks)]
                for k in range(chunks):
                    act[firsts[side], at[k], :] = sums[k]

        with_sides(lambda sides: steps(tiles, functools.partial(back_y, sides), 3))

        if second_part:
            @pl.when(turn + 1 == turns)
            def _():
                for copy in act_copies:
                    copy.start()

        homes = []
        for side in range(2):
            slot = picked[side][0]
            homes.append(reach_of(slot) * orb_dev + lax.rem(second_of(slot), orb_dev))

        def send_back(sides, g):
            for side in range(sides):
                ks = [g * stretch + i for i in range(stretch)]
                values = shifted(dense.at[side], 2 + side, returns[side], 0, edge, ks)
                at = [
                    (i, t, pl.ds(t * (ROWS * chunks) + ks[i], ROWS, stride=chunks))
                    for i in range(stretch)
                    for t in range(tiles)
                ]
                sums = [
                    back[homes[side], a, :] + values[i][t * ROWS : (t + 1) * ROWS] for i, t, a in at
                ]
                for (i, t, a), value in zip(at, sums):
                    back[homes[side], a, :] = value

        with_sides(lambda sides: steps(chunks // stretch, functools.partial(send_back, sides), 3))
        return 0

    if second_part:
        @pl.when(found == 0)
        def _():
            for copy in state_copies:
                copy.start()
            for copy in state_copies:
                copy.wait()
            for copy in act_copies:
                copy.start()

    lax.fori_loop(0, turns, solve_two, 0)
    if second_part:
        spans = ((orb_dev, 1), (orb_dev + 1, orb_dev - 1), (0, orb_dev))
    else:
        spans = ((2 * orb_dev + 1, orb_dev - 1), (2 * orb_dev, 1), (0, 2 * orb_dev))
    copies = [
        pltpu.make_async_copy(back.at[pl.ds(begin, count)], back_outs[i], out_sem.at[i])
        for i, (begin, count) in enumerate(spans)
    ]
    for copy in copies:
        copy.start()
    if second_part:
        copies += act_copies
    for copy in copies:
        copy.wait()


def pair_terms(numbers, fragments, slots, tables, pieces, far, before=()):
    second_part = bool(before)
    orb_dev, edge, plane = pieces[0].shape
    groups = len(pieces)
    frag_size = groups * orb_dev
    chunks = plane // LANES
    rows = edge * chunks
    height = padded_half(edge)
    shape = (edge, orb_dev, groups, fragments, slots)
    smem = pl.BlockSpec(memory_space=pltpu.SMEM)
    vmem = pl.BlockSpec(memory_space=pltpu.VMEM)
    hbm = pl.BlockSpec(memory_space=pltpu.HBM)
    f32 = jnp.float32

    def fields(*counts):
        return [jax.ShapeDtypeStruct((count, rows, LANES), f32) for count in counts]

    if second_part:
        out_shape = [jax.ShapeDtypeStruct((frag_size, rows // groups, LANES), f32)] * groups
        out_shape += fields(1, orb_dev - 1, orb_dev)
        out_specs = [hbm] * (groups + 3)
        scratch = [pltpu.VMEM(field.shape, f32) for field in fields(frag_size, REACH * orb_dev)]
        scratch += [pltpu.SemaphoreType.DMA((2,)), pltpu.SemaphoreType.DMA((3 + groups,))]
    else:
        out_shape = fields(frag_size, orb_dev - 1, 1, REACH * orb_dev)
        out_specs = [vmem, hbm, hbm, hbm]
        scratch = [pltpu.VMEM(((REACH + 1) * orb_dev, rows, LANES), f32)]
        scratch += [pltpu.SemaphoreType.DMA((3,))]
    return pl.pallas_call(
        functools.partial(pair_kernel, shape, second_part),
        out_shape=out_shape,
        in_specs=[smem] + [hbm] * (3 + groups + len(far) + len(before)),
        out_specs=out_specs,
        scratch_shapes=scratch
        + [
            pltpu.VMEM((2, 2, edge, plane), f32),
            pltpu.VMEM((2, edge, plane), f32),
            pltpu.VMEM((2, chunks, 3 * edge, LANES), f32),
            pltpu.VMEM((2, chunks, edge, LANES), f32),
            pltpu.VMEM((2, chunks, 3 * edge, LANES), f32),
            pltpu.VMEM((2, height * edge, LANES), f32),
            pltpu.VMEM((2, height * edge, LANES), f32),
            pltpu.VMEM((4, -(-chunks // ROWS) * ROWS, LANES), f32),
            pltpu.SMEM((slots,), jnp.int32),
            pltpu.SemaphoreType.DMA((2, 2)),
            *[pltpu.VMEM(table.shape, table.dtype) for table in tables],
            pltpu.SemaphoreType.DMA((3,)),
        ],
        compiler_params=pltpu.CompilerParams(vmem_limit_bytes=30 << 20),
        name="late_pair_terms" if second_part else "early_pair_terms",
    )(numbers, *tables, *pieces, *far, *before)


def flatten_kernel(shape, places_ref, *refs):
    edge, orb_dev, groups = shape
    pieces, (flat_ref, slab_ref) = refs[:groups], refs[groups:]
    member = places_ref[1]
    chunks = edge * edge // LANES
    slab = slab_ref.shape[1]
    for k in range(groups):
        for o in range(orb_dev):
            def move(j, _):
                value = pieces[k][o, :, pl.ds(pl.multiple_of(j * LANES, LANES), LANES)]
                for t in range(edge // ROWS):
                    at = pl.ds(t * (ROWS * chunks) + j, ROWS, stride=chunks)
                    flat_ref[k * orb_dev + o, at, :] = value[t * ROWS : (t + 1) * ROWS]
                return 0

            lax.fori_loop(0, chunks, move, 0)
    slab_ref[...] = flat_ref[:, pl.ds(pl.multiple_of(member * slab, ROWS), slab), :]


def flatten_terms(places, pieces):
    orb_dev, edge, plane = pieces[0].shape
    groups = len(pieces)
    rows = edge * plane // LANES
    frag_size = groups * orb_dev
    smem = pl.BlockSpec(memory_space=pltpu.SMEM)
    vmem = pl.BlockSpec(memory_space=pltpu.VMEM)
    return pl.pallas_call(
        functools.partial(flatten_kernel, (edge, orb_dev, groups)),
        out_shape=(
            jax.ShapeDtypeStruct((frag_size, rows, LANES), jnp.float32),
            jax.ShapeDtypeStruct((frag_size, rows // groups, LANES), jnp.float32),
        ),
        in_specs=[smem] + [vmem] * groups,
        out_specs=(vmem, vmem),
        compiler_params=pltpu.CompilerParams(vmem_limit_bytes=24 << 20),
        name="flatten_terms",
    )(places, *pieces)


def products(lefts, rights, length, step):
    def add(i, sums):
        at = pl.ds(pl.multiple_of(i * step, ROWS), step)
        right = [ref[index, at, :].reshape(step // ROWS, ROWS, LANES) for ref, index in rights]
        out = []
        for n, (ref, index) in enumerate(lefts):
            left = ref[index, at, :].reshape(step // ROWS, ROWS, LANES)
            for m in range(len(rights)):
                out.append(sums[n * len(rights) + m] + jnp.sum(left * right[m], axis=0))
        return tuple(out)

    zero = jnp.zeros((ROWS, LANES), jnp.float32)
    return lax.fori_loop(0, length // step, add, (zero,) * (len(lefts) * len(rights)))


def placed(result, sums, rows, lanes):
    row = lax.broadcasted_iota(jnp.int32, result.shape, 0)
    lane = lax.broadcasted_iota(jnp.int32, result.shape, 1)
    for n, a in enumerate(rows):
        for m, b in enumerate(lanes):
            value = jnp.sum(sums[n * len(lanes) + m], keepdims=True)
            result = jnp.where((row == a) & (lane == b), result + value, result)
    return result


def step_of(length):
    return next(n for n in (72, 24, 8) if length % n == 0)


def action_kernel(shape, places_ref, phi_ref, *refs):
    orb_dev, groups = shape
    parts, (act_ref, share_ref) = refs[:-2], refs[-2:]
    member = places_ref[1]
    frag_size = orb_dev * groups
    slab = act_ref.shape[1]
    value = parts[0][...]
    for part in parts[1:]:
        value = value + part[...]
    act_ref[...] = value
    rows = [(member ^ (a // orb_dev)) * orb_dev + a % orb_dev for a in range(frag_size)]
    result = jnp.zeros(share_ref.shape, jnp.float32)
    for half in range(0, frag_size, 4):
        bs = range(half, min(half + 4, frag_size))
        lefts, rights = [(phi_ref, a) for a in range(frag_size)], [(act_ref, b) for b in bs]
        result = placed(result, products(lefts, rights, slab, step_of(slab)), rows, bs)
    share_ref[...] = result


def action_terms(places, orb_dev, phi, parts):
    frag_size, slab = phi.shape[:2]
    smem = pl.BlockSpec(memory_space=pltpu.SMEM)
    vmem = pl.BlockSpec(memory_space=pltpu.VMEM)
    return pl.pallas_call(
        functools.partial(action_kernel, (orb_dev, frag_size // orb_dev)),
        out_shape=(
            jax.ShapeDtypeStruct((frag_size, slab, LANES), jnp.float32),
            jax.ShapeDtypeStruct((frag_size, LANES), jnp.float32),
        ),
        in_specs=[smem] + [vmem] * (1 + len(parts)),
        out_specs=(vmem, vmem),
        compiler_params=pltpu.CompilerParams(vmem_limit_bytes=16 << 20),
        name="action_terms",
    )(places, phi, *parts)


def home_kernel(shape, places_ref, flat_ref, own_ref, *refs):
    edge, orb_dev, groups, first, count = shape
    if first == 0:
        (two_ref, twin_ref, relay_ref), refs = refs[:3], refs[3:]
    else:
        (two_ref, one_ref, share_ref), refs = refs[:3], refs[3:]
    outs, total = refs[:groups], refs[groups]
    fragment, member = places_ref[0], places_ref[1]
    frag_size = orb_dev * groups
    rows = flat_ref.shape[1]
    slab = rows // groups
    for i in range(count):
        value = own_ref[first + i] + two_ref[i]
        if first == 0:
            @pl.when(lax.rem(fragment, 2) == 1)
            def _():
                total[i] = value + twin_ref[i]

            @pl.when(lax.rem(fragment, 2) == 0)
            def _():
                total[i] = value + relay_ref[i]
        else:
            total[i] = value + one_ref[i]
    lefts, rights = [(flat_ref, a) for a in range(frag_size)], [(total, i) for i in range(count)]
    places = [(member ^ (a // orb_dev)) * orb_dev + a % orb_dev for a in range(frag_size)]
    result = jnp.zeros((frag_size, LANES), jnp.float32) if first == 0 else share_ref[...]
    sums = products(lefts, rights, rows, step_of(rows))
    result = placed(result, sums, places, [member * orb_dev + first + i for i in range(count)])
    result = result * (1.0 / float(edge**3))
    for k in range(groups):
        begin = pl.multiple_of((member ^ k) * slab, ROWS)
        for i in range(count):
            outs[k][i * slab : (i + 1) * slab, :] = total[i, pl.ds(begin, slab), :]
        outs[k][count * slab :, :] = result


def home_terms(places, edge, groups, flat, own, first, *came):
    frag_size, rows = flat.shape[:2]
    count = came[0].shape[0]
    smem = pl.BlockSpec(memory_space=pltpu.SMEM)
    vmem = pl.BlockSpec(memory_space=pltpu.VMEM)
    f32 = jnp.float32
    parcel = jax.ShapeDtypeStruct((count * rows // groups + frag_size, LANES), f32)
    return pl.pallas_call(
        functools.partial(home_kernel, (edge, frag_size // groups, groups, first, count)),
        out_shape=[parcel] * groups,
        in_specs=[smem] + [vmem] * (2 + len(came)),
        out_specs=[vmem] * groups,
        scratch_shapes=[pltpu.VMEM((count, rows, LANES), f32)],
        compiler_params=pltpu.CompilerParams(vmem_limit_bytes=16 << 20),
        name="home_terms",
    )(places, flat, own, *came)


def exchanged(value, axis, width):
    size = value.shape[axis]
    index = lax.broadcasted_iota(jnp.int32, value.shape, axis)
    below, above = pltpu.roll(value, width, axis), pltpu.roll(value, size - width, axis)
    return jnp.where((index & width) != 0, below, above)


def gradient_kernel(shape, places_ref, act_ref, phi_ref, *refs):
    edge, orb_dev, groups = shape
    heads, tails, refs = refs[:groups], refs[groups : 2 * groups], refs[2 * groups :]
    out_ref, lagrange_ref, hold = refs
    member = places_ref[1]
    frag_size = orb_dev * groups
    chunks = edge * edge // LANES
    slab_rows = edge // groups
    slab = slab_rows * chunks
    sums = [
        head[slab:, :] + tail[(orb_dev - 1) * slab :, :] for head, tail in zip(heads, tails)
    ]
    while len(sums) > 1:
        sums = [sums[i] + sums[i + 1] for i in range(0, len(sums), 2)]
    square = jnp.concatenate([sums[0], jnp.zeros((LANES - frag_size, LANES), jnp.float32)], axis=0)
    lagrange = 0.5 * (square + square.T)[:frag_size, :]
    lagrange_ref[...] = lagrange[:, :frag_size]
    bit = 1
    while bit < groups:
        turned = exchanged(exchanged(lagrange, 0, bit * orb_dev), 1, bit * orb_dev)
        lagrange = jnp.where((member & bit) != 0, turned, lagrange)
        bit *= 2

    for k in range(groups):
        for o in range(orb_dev):
            a = (member ^ k) * orb_dev + o
            came = heads[k][:slab, :] if o == 0 else tails[k][(o - 1) * slab : o * slab, :]
            value = act_ref[a] + came
            for b in range(frag_size):
                factor = lagrange[b : b + 1, k * orb_dev + o : k * orb_dev + o + 1]
                value = value - factor * phi_ref[b]
            hold[pl.ds(pl.multiple_of(a * slab, ROWS), slab), :] = value
    for x in range(slab_rows):
        for j in range(chunks):
            value = hold[pl.ds(x * chunks + j, frag_size, stride=slab), :]
            out_ref[x, :, j * LANES : (j + 1) * LANES] = value


def gradient_terms(places, edge, act, phi, heads, tails):
    groups = len(heads)
    frag_size, slab = act.shape[:2]
    smem = pl.BlockSpec(memory_space=pltpu.SMEM)
    vmem = pl.BlockSpec(memory_space=pltpu.VMEM)
    f32 = jnp.float32
    gradient, lagrange = pl.pallas_call(
        functools.partial(gradient_kernel, (edge, frag_size // groups, groups)),
        out_shape=(
            jax.ShapeDtypeStruct((edge // groups, frag_size, edge * edge), f32),
            jax.ShapeDtypeStruct((frag_size, frag_size), f32),
        ),
        in_specs=[smem] + [vmem] * (2 + 2 * groups),
        out_specs=(vmem, vmem),
        scratch_shapes=[pltpu.VMEM((frag_size * slab, LANES), f32)],
        compiler_params=pltpu.CompilerParams(vmem_limit_bytes=16 << 20),
        name="gradient_terms",
    )(places, act, phi, *heads, *tails)
    return gradient.transpose(1, 0, 2), lagrange


def together(*arrays):
    return lax.optimization_barrier(arrays)


def to_fragment(block, distance, senders=None):
    devices = lax.axis_size("orb")
    senders = range(devices) if senders is None else range(senders, devices, 2)
    return lax.ppermute(block, "orb", [(i, (i + distance) % devices) for i in senders])


def with_twin(block):
    return lax.ppermute(block, "orb", [(i, i ^ 1) for i in range(lax.axis_size("orb"))])


def with_member(block, bit):
    return lax.ppermute(block, "grp", [(i, i ^ bit) for i in range(lax.axis_size("grp"))])


def by_member(parcels):
    groups = len(parcels)
    received = list(parcels)
    bit = groups // 2
    while bit:
        for k in reversed(range(groups)):
            if k & bit:
                received[k] = with_member(received[k], bit)
        bit //= 2
    return received


def shards(orbitals, kernel, anchors, pair_count, pair_first, pair_second, pair_reach):
    groups = lax.axis_size("grp")
    orb_dev, edge, plane = orbitals.shape
    places = jnp.stack([lax.axis_index("orb"), lax.axis_index("grp")]).astype(jnp.int32)

    numbers = [places, pair_count, pair_first, pair_second, pair_reach, anchors.reshape(-1)]
    screen, numbers, *tables = screen_terms(jnp.concatenate(numbers), kernel)
    two = to_fragment(orbitals, -2)
    twin = with_twin(orbitals[:1])
    pieces = {0: orbitals}
    bit = groups // 2
    while bit:
        for k in list(pieces):
            pieces[k ^ bit] = with_member(pieces[k], bit)
        if bit == groups // 2:
            two, twin, tail, pieces[bit], screen, numbers, *tables = together(
                two, twin, orbitals[1:], pieces[bit], screen, numbers, *tables
            )
            one = to_fragment(tail, -1)
            relay = to_fragment(twin, -2, 1)
        bit //= 2
    pieces = [pieces[k] for k in range(groups)]
    tables = [screen, *tables]
    sizes = (anchors.shape[0], pair_first.shape[0])
    act, two_tail, two_head, back = pair_terms(numbers, *sizes, tables, pieces, [twin, two])
    two_tail, relay, one = together(two_tail, relay, one)
    two_tail = to_fragment(two_tail, 2)
    *acts, one_head, one_tail, own = pair_terms(
        numbers, *sizes, tables, pieces, [twin, relay, one], [act, back]
    )

    acts[-1], two_tail, two_head = together(acts[-1], two_tail, two_head)
    two_head = to_fragment(two_head, 2)
    twin = with_twin(one_head)
    bit = 1
    parts = {k: [act] for k, act in enumerate(acts)}
    while bit < groups:
        for k in sorted(parts, reverse=True):
            if k & bit:
                going = sum(parts[k][1:], parts[k][0])
                if bit == 2:
                    _, twin, one_tail, two_head = together(going, twin, one_tail, two_head)
                del parts[k]
                parts[k ^ bit].append(with_member(going, bit))
        bit *= 2
    one_tail = to_fragment(one_tail, 1)
    relay = to_fragment(twin, 2, 0)

    flat, phi = flatten_terms(places, pieces)
    act, share = action_terms(places, orb_dev, phi, parts[0])
    share, relay = together(share, relay)
    tails = home_terms(places, edge, groups, flat, own, 1, two_tail, one_tail, share)
    heads = home_terms(places, edge, groups, flat, own, 0, two_head, twin, relay)
    tails, heads = by_member(tails), by_member(heads)
    gradient, lagrange = gradient_terms(places, edge, act, phi, heads, tails)
    return (gradient, lagrange[None])


def solution(mesh):
    placed = (P(("orb", "grp"), None, None), P(), P(), P("orb"), P("orb"), P("orb"), P("orb"))
    return jax.shard_map(
        shards,
        mesh=mesh,
        in_specs=placed,
        out_specs=(P("orb", "grp", None), P("orb", None, None)),
        check_vma=False,
    )
```

```python
import functools
import math

import jax
import jax.numpy as jnp
import numpy as np
from jax import lax
from jax.experimental import pallas as pl
from jax.experimental.pallas import tpu as pltpu
from jax.sharding import PartitionSpec as P

REACH = 2
LANES = 128
ROWS = 8
HALF = LANES // 2


class Number:
    def __init__(self, real, imag=None):
        self.real, self.imag = real, imag

    def __add__(self, other):
        if self.imag is None or other.imag is None:
            imag = self.imag if other.imag is None else other.imag
        else:
            imag = self.imag + other.imag
        return Number(self.real + other.real, imag)

    def __sub__(self, other):
        if other.imag is None:
            imag = self.imag
        else:
            imag = -other.imag if self.imag is None else self.imag - other.imag
        return Number(self.real - other.real, imag)

    def conj(self):
        return self if self.imag is None else Number(self.real, -self.imag)

    def scaled(self, factor):
        return Number(self.real * factor, None if self.imag is None else self.imag * factor)

    def turned(self, sign):
        if self.imag is None:
            return Number(jnp.zeros_like(self.real), self.real if sign > 0 else -self.real)
        return Number(-self.imag, self.real) if sign > 0 else Number(self.imag, -self.real)

    def plus_turned(self, other, sign):
        if sign < 0:
            return self.minus_turned(other)
        real = self.real if other.imag is None else self.real - other.imag
        return Number(real, other.real if self.imag is None else self.imag + other.real)

    def minus_turned(self, other):
        real = self.real if other.imag is None else self.real + other.imag
        return Number(real, -other.real if self.imag is None else self.imag - other.real)

    def times(self, angle):
        real, imag = math.cos(angle), math.sin(angle)
        if abs(imag) < 1e-12:
            return self if real > 0 else self.scaled(-1.0)
        if abs(real) < 1e-12:
            return self.turned(imag)
        if self.imag is None:
            return Number(self.real * real, self.real * imag)
        return Number(self.real * real - self.imag * imag, self.real * imag + self.imag * real)


def coprime(n):
    for p in (2, 3, 5, 7):
        power = 1
        while n % (power * p) == 0:
            power *= p
        if 1 < power < n:
            return power, n // power
    return None


def radix(n):
    return next((p for p in (4, 2, 3, 5, 7) if n % p == 0 and n > p), None)


def meeting(i, j, first, second):
    return next(k for k in range(first * second) if k % first == i and k % second == j)


def dft(values, sign):
    n = len(values)
    if n == 1:
        return values
    if n == 2:
        return [values[0] + values[1], values[0] - values[1]]
    if n == 3:
        a, b, c = values
        total, side = b + c, (b - c).scaled(math.sqrt(0.75))
        middle = a - total.scaled(0.5)
        return [a + total, middle.plus_turned(side, sign), middle.plus_turned(side, -sign)]
    if n == 4:
        a, b, c, d = values
        s, t, u, v = a + c, a - c, b + d, b - d
        return [s + u, t.plus_turned(v, sign), s - u, t.plus_turned(v, -sign)]
    out = [None] * n
    if coprime(n):
        first, second = coprime(n)
        columns = [
            dft([values[(i * second + j * first) % n] for i in range(first)], sign)
            for j in range(second)
        ]
        for i in range(first):
            row = dft([column[i] for column in columns], sign)
            for j in range(second):
                out[meeting(i, j, first, second)] = row[j]
        return out
    p = radix(n)
    if p:
        rest = n // p
        columns = [dft(values[j::p], sign) for j in range(p)]
        for i in range(rest):
            row = dft(
                [columns[j][i].times(sign * 2.0 * math.pi * i * j / n) for j in range(p)], sign
            )
            for j in range(p):
                out[i + rest * j] = row[j]
        return out
    for k in range(n):
        total = values[0]
        for j in range(1, n):
            total = total + values[j].times(sign * 2.0 * math.pi * (j * k % n) / n)
        out[k] = total
    return out


def real_dft(values):
    n = len(values)
    if n <= 4:
        out = dft(values, -1)
    else:
        out = [None] * n
        if coprime(n):
            first, second = coprime(n)
            columns = [
                real_dft([values[(i * second + j * first) % n] for i in range(first)])
                for j in range(second)
            ]
            for i in range(first // 2 + 1):
                entries = [column[i] for column in columns]
                alone = 2 * i % first == 0
                row = real_dft(entries) if alone else dft(entries, -1)
                for j in range(second):
                    out[meeting(i, j, first, second)] = row[j]
        elif radix(n):
            p = radix(n)
            rest = n // p
            columns = [real_dft(values[j::p]) for j in range(p)]
            for i in range(rest // 2 + 1):
                row = dft(
                    [columns[j][i].times(-2.0 * math.pi * i * j / n) for j in range(p)], -1
                )
                for j in range(p):
                    out[i + rest * j] = row[j]
        else:
            out = dft(values, -1)
    for k in range(1, n):
        if out[k] is None or (k > n // 2 and out[n - k] is not None):
            out[k] = out[n - k].conj()
    out[0] = Number(out[0].real)
    if n % 2 == 0:
        out[n // 2] = Number(out[n // 2].real)
    return out


def real_back(values):
    n = len(values)
    if n == 1:
        return [values[0].real]
    if n == 2:
        return [values[0].real + values[1].real, values[0].real - values[1].real]
    if n == 3:
        a, b = values[0].real, values[1]
        side = b.imag * math.sqrt(3.0)
        middle = a - b.real
        return [a + 2.0 * b.real, middle - side, middle + side]
    if n == 4:
        s, t = values[0].real + values[2].real, values[0].real - values[2].real
        u, v = 2.0 * values[1].real, 2.0 * values[1].imag
        return [s + u, t - v, s - u, t + v]
    out = [None] * n
    if coprime(n):
        first, second = coprime(n)
        rows = []
        for i in range(first // 2 + 1):
            entries = [values[meeting(i, j, first, second)] for j in range(second)]
            if 2 * i % first == 0:
                rows.append([Number(value) for value in real_back(entries)])
            else:
                rows.append(dft(entries, 1))
        for b in range(second):
            half = [row[b] for row in rows]
            whole = half + [half[first - i].conj() for i in range(len(half), first)]
            for a, value in enumerate(real_back(whole)):
                out[(a * second + b * first) % n] = value
        return out
    p = radix(n)
    if p:
        rest = n // p
        parts = []
        for i in range(p // 2 + 1):
            entries = values[i::p]
            if i == 0:
                parts.append([Number(value) for value in real_back(entries)])
            else:
                inner = dft(entries, 1)
                parts.append([inner[m].times(2.0 * math.pi * i * m / n) for m in range(rest)])
                if 2 * i == p:
                    parts[-1] = [Number(value.real) for value in parts[-1]]
        for m in range(rest):
            half = [part[m] for part in parts]
            whole = half + [half[p - i].conj() for i in range(len(half), p)]
            for j, value in enumerate(real_back(whole)):
                out[m + rest * j] = value
        return out
    return [value.real for value in dft(values, 1)]


def wave_table(edge):
    index = np.arange(edge)
    angles = 2.0 * np.pi / edge * (np.outer(index, index) % edge)
    full = np.zeros((2, 2, HALF, 2, HALF))
    for side in range(2):
        full[0, side, :edge, side, :edge] = np.cos(angles)
        full[1, side, :edge, side, :edge] = np.sin(angles)
    full = full.reshape(2, LANES, LANES)
    high = full.astype(jnp.bfloat16)
    low = (full - high.astype(np.float64)).astype(jnp.bfloat16)
    return np.stack([high, low])


def split_dot(real, imag, matrix):
    value = jnp.concatenate([real, imag], axis=1)
    high = value.astype(jnp.bfloat16)
    low = (value - high.astype(jnp.float32)).astype(jnp.bfloat16)
    product = jnp.dot(
        jnp.concatenate([high, low, high], axis=1), matrix[...], preferred_element_type=jnp.float32
    )
    return product[:, :LANES], product[:, LANES:]


def padded_half(edge):
    return -(-(edge // 2 + 1) // ROWS) * ROWS


def screen_kernel(edge, numbers_ref, kernel_ref, waves_ref, out_ref, kept_ref, ahead_ref, behind_ref, flipped):
    for i in range(numbers_ref.shape[0]):
        kept_ref[i] = numbers_ref[i]
    for table, sign in ((ahead_ref, -1), (behind_ref, 1)):
        for part, source in enumerate((0, 0, 1)):
            for i in range(2):
                for j in range(2):
                    value = waves_ref[source, (i + j) % 2]
                    if i != j and (i > j) == (sign > 0):
                        value = -value
                    rows = slice((2 * part + i) * LANES, (2 * part + i + 1) * LANES)
                    table[rows, j * LANES : (j + 1) * LANES] = value
    exact = dict(precision=lax.Precision.HIGHEST, preferred_element_type=jnp.float32)

    def index(shape, axis):
        return lax.broadcasted_iota(jnp.int32, shape, axis)

    square, whole = (edge, edge), (LANES, LANES)
    flip = index(square, 0) + index(square, 1)
    flip = ((flip == 0) | (flip == edge)).astype(jnp.float32)
    source, target = index(whole, 0), index(whole, 1)
    target = jnp.where(target < HALF, target, target - HALF)
    mirror = ((source + target == 0) | (source + target == edge)) & (source < edge) & (target < edge)
    mirror = mirror.astype(jnp.float32)
    flipped[...] = jnp.dot(flip, kernel_ref[...], **exact)
    height = padded_half(edge)
    lane = index((edge, LANES), 1)
    out_ref[...] = jnp.zeros_like(out_ref)

    def piece(ref, y):
        begin, offset = divmod(y * edge, LANES)
        value = ref[:, begin * LANES : (begin + 1) * LANES]
        value = pltpu.roll(value, LANES - offset, 1) if offset else value
        if offset + edge > LANES:
            more = ref[:, (begin + 1) * LANES : (begin + 2) * LANES]
            value = jnp.where(lane < LANES - offset, value, pltpu.roll(more, LANES - offset, 1))
        return value

    for y in range(edge // 2 + 1):
        value = piece(kernel_ref, y)
        value = jnp.where(lane < HALF, value, pltpu.roll(value, HALF, 1))
        value = value + jnp.dot(piece(flipped, (edge - y) % edge), mirror, **exact)
        value = value * (0.5 / float(edge**3))
        for t in range(edge // ROWS):
            at = pl.ds(t * ROWS * height + y, ROWS, stride=height)
            out_ref[at, :] = value[t * ROWS : (t + 1) * ROWS]


def screen_terms(numbers, kernel):
    edge, plane = kernel.shape
    smem = pl.BlockSpec(memory_space=pltpu.SMEM)
    vmem = pl.BlockSpec(memory_space=pltpu.VMEM)
    table = jax.ShapeDtypeStruct((6 * LANES, 2 * LANES), jnp.bfloat16)
    return pl.pallas_call(
        functools.partial(screen_kernel, edge),
        out_shape=[
            jax.ShapeDtypeStruct((edge * padded_half(edge), LANES), jnp.float32),
            jax.ShapeDtypeStruct(numbers.shape, numbers.dtype),
            table,
            table,
        ],
        in_specs=[smem, vmem, vmem],
        out_specs=[vmem, smem, vmem, vmem],
        scratch_shapes=[pltpu.VMEM((edge, plane), jnp.float32)],
        compiler_params=pltpu.CompilerParams(vmem_limit_bytes=8 << 20),
        name="screen_terms",
    )(numbers, kernel, jnp.asarray(wave_table(edge)))


def pair_kernel(shape, second_part, numbers_ref, *refs):
    edge, orb_dev, groups, fragments, slots = shape
    plane = edge * edge
    chunks = plane // LANES
    tiles = edge // ROWS
    half = edge // 2 + 1
    height = padded_half(edge)
    returns_count = (REACH + 1) * orb_dev
    tables, refs = refs[:3], refs[3:]
    phi_refs, refs = refs[:groups], refs[groups:]
    (twin_ref, two_ref), refs = refs[:2], refs[2:]
    if second_part:
        (relay_ref, one_ref, act_before, back_before), refs = refs[:4], refs[4:]
        act_outs, back_outs, refs = refs[:2], refs[2:7], refs[7:]
        (act, back, state_sem, out_sem), refs = refs[:4], refs[4:]
    else:
        (act, back), refs = refs[:2], refs[2:]
    (near, far, wide, moved, dense, lower, upper, masks, listed, load_sem) = refs[:10]
    screen_ref, ahead_ref, behind_ref, table_sem = refs[10:]

    fragment, member, live_slots = numbers_ref[0], numbers_ref[1], numbers_ref[2]

    def first_of(slot):
        return numbers_ref[3 + slot]

    def second_of(slot):
        return numbers_ref[3 + slots + slot]

    def reach_of(slot):
        return numbers_ref[3 + 2 * slots + slot]

    def anchor(place, axis):
        return numbers_ref[3 + 3 * slots + 3 * place + axis]

    table_copies = [
        pltpu.make_async_copy(table, hold, table_sem.at[i])
        for i, (table, hold) in enumerate(zip(tables, refs[10:13]))
    ]
    lane = lax.broadcasted_iota(jnp.int32, (1, LANES), 1)
    stretch = next(n for n in (6, 4, 3, 2, 1) if chunks % n == 0)
    middle = pl.ds(edge, edge)

    even = lax.rem(fragment, 2) == 0

    def list_slots(slot, counts):
        early, found = counts
        mine = (slot < live_slots) & (lax.div(second_of(slot), orb_dev) == member)
        reach = reach_of(slot)
        come = (reach == 0) | (reach == 2) | (even & (lax.rem(second_of(slot), orb_dev) == 0))
        taken = mine & come & (early < 2)
        chosen = mine & jnp.logical_not(taken) if second_part else taken

        @pl.when(chosen)
        def _():
            listed[found] = slot

        return early + taken.astype(jnp.int32), found + chosen.astype(jnp.int32)

    _, found = lax.fori_loop(0, slots, list_slots, (jnp.int32(0), jnp.int32(0)))
    turns = lax.div(found + 1, 2)

    def slot_of(turn, side):
        at = 2 * turn + side
        live = at < found
        return listed[jnp.where(live, at, 2 * turn)], live

    def far_copy(side, source):
        return pltpu.make_async_copy(source, far.at[side], load_sem.at[1, side])

    def start_loads(turn):
        def load(side):
            slot, _ = slot_of(turn, side)
            first, second, reach = first_of(slot), second_of(slot), reach_of(slot)
            relative = lax.div(first, orb_dev) ^ member
            for k in range(groups):
                @pl.when(relative == k)
                def _():
                    pltpu.make_async_copy(
                        phi_refs[k].at[lax.rem(first, orb_dev)],
                        near.at[lax.rem(turn, 2), side],
                        load_sem.at[0, side],
                    ).start()
            own = lax.rem(second, orb_dev)

            @pl.when(reach == 0)
            def _():
                far_copy(side, phi_refs[0].at[own]).start()

            @pl.when((reach == 1) & (own == 0) & even)
            def _():
                far_copy(side, twin_ref.at[0]).start()

            @pl.when(reach == 2)
            def _():
                far_copy(side, two_ref.at[own]).start()

            if second_part:
                @pl.when((reach == 1) & (own == 0) & jnp.logical_not(even))
                def _():
                    far_copy(side, relay_ref.at[0]).start()

                @pl.when((reach == 1) & (own > 0))
                def _():
                    far_copy(side, one_ref.at[jnp.maximum(own - 1, 0)]).start()

        load(0)
        pl.when(2 * turn + 1 < found)(functools.partial(load, 1))

    def wait_loads(turn):
        def wait(side):
            pltpu.make_async_copy(
                phi_refs[0].at[0], near.at[lax.rem(turn, 2), side], load_sem.at[0, side]
            ).wait()
            far_copy(side, phi_refs[0].at[0]).wait()

        wait(0)
        pl.when(2 * turn + 1 < found)(functools.partial(wait, 1))

    @pl.when(found > 0)
    def _():
        start_loads(0)
        for copy in table_copies:
            copy.start()

    if second_part:
        state_copies = [
            pltpu.make_async_copy(before, now, state_sem.at[i])
            for i, (before, now) in enumerate(((act_before, act), (back_before, back)))
        ]
        slab = plane * edge // LANES // groups
        act_copies = []
        for k in range(groups):
            source = (member ^ k) * slab
            place = reversed_bits(k, groups)
            act_copies.append(
                pltpu.make_async_copy(
                    act.at[:, pl.ds(pl.multiple_of(source, ROWS), slab), :],
                    act_outs[2 * place // groups].at[place % (groups // 2)],
                    out_sem.at[k],
                )
            )
    else:
        act[...] = jnp.zeros_like(act)
        back[...] = jnp.zeros_like(back)

    def offset_of(slot):
        partner = lax.rem(fragment + reach_of(slot), fragments)
        return [anchor(partner, i) - anchor(fragment, i) for i in range(3)]

    def steps(count, body, most):
        width = max(n for n in range(1, most + 1) if count % n == 0)

        def step(i, _):
            for j in range(width):
                body(i * width + j)
            return 0

        if width == count:
            step(0, 0)
        else:
            lax.fori_loop(0, count // width, step, 0)

    def columns(k):
        return pl.ds(pl.multiple_of(k * LANES, LANES), LANES)

    def set_masks(place, delta):
        shape = masks.shape[1:]
        spot = lax.broadcasted_iota(jnp.int32, shape, 0) * LANES
        spot = spot + lax.broadcasted_iota(jnp.int32, shape, 1)
        y = ((spot.astype(jnp.float32) + 0.5) * (1.0 / edge)).astype(jnp.int32)
        z = spot - y * edge - delta[2]
        y = y - delta[1]
        inside = (y >= 0) & (y < edge) & (z >= 0) & (z < edge)
        masks[place] = jnp.where(inside, 1.0, 0.0)

    def shifted(source, place, delta, begin, count, ks):
        shift = lax.rem(delta[1] * edge + delta[2] + 4 * plane, plane)
        start = lax.rem(plane - shift, plane)
        whole, part = lax.div(start, LANES), lax.rem(start, LANES)
        turn = lax.rem(LANES - part, LANES)
        down = edge - jnp.clip(delta[0], -edge, edge) + begin
        x = lax.broadcasted_iota(jnp.int32, (count, LANES), 0) + (begin - delta[0])
        rows_inside = (x >= 0) & (x < edge)
        first = lane < LANES - part

        def piece(k):
            return pltpu.roll(source[lax.rem(k + whole, chunks), pl.ds(down, count), :], turn, 1)

        out = []
        low = piece(ks[0])
        for k in ks:
            high = piece(k + 1)
            value = jnp.where(first, low, high) * masks[place, pl.ds(k, 1), :]
            out.append(jnp.where(rows_inside, value, 0.0))
            low = high
        return out

    def tile(t, i, size):
        return pl.ds(pl.multiple_of(i * size + t * ROWS, ROWS), ROWS)

    def across(t, i, size):
        return pl.ds(t * (ROWS * size) + i, ROWS, stride=size)

    def solve_two(turn, _):
        wait_loads(turn)
        if second_part:
            @pl.when(turn == 0)
            def _():
                for copy in state_copies:
                    copy.start()

        near_now = near.at[lax.rem(turn, 2)]
        picked = [slot_of(turn, side) for side in range(2)]
        offsets = [offset_of(slot) for slot, _ in picked]
        returns = [[-d for d in delta] for delta in offsets]
        for side in range(2):
            set_masks(side, offsets[side])
            set_masks(2 + side, returns[side])

        def with_sides(work):
            both = 2 * turn + 1 < found
            pl.when(both)(functools.partial(work, 2))
            pl.when(jnp.logical_not(both))(functools.partial(work, 1))

        def widen(sides, k):
            for side in range(sides):
                wide[side, k, middle, :] = far[side, :, pl.ds(pl.multiple_of(k * LANES, LANES), LANES)]

        def over_y(sides_now, t):
            densities = []
            begin = pl.multiple_of(t * ROWS, ROWS)
            rows = pl.ds(begin, ROWS)
            for side in range(sides_now):
                values = shifted(wide.at[side], side, offsets[side], begin, ROWS, range(chunks))
                for k in range(chunks):
                    moved[side, k, rows, :] = values[k]
                    values[k] = values[k] * near_now[side, rows, k * LANES : (k + 1) * LANES]
                densities.append(values)
            planes = []
            for y in range(edge):
                first, offset = divmod(y * edge, LANES)
                sides = []
                for side in range(sides_now):
                    shift = (side * HALF - offset) % LANES
                    value = densities[side][first]
                    value = pltpu.roll(value, shift, 1) if shift else value
                    if offset + edge > LANES:
                        more = densities[side][first + 1]
                        more = pltpu.roll(more, shift, 1) if shift else more
                        value = jnp.where(lane < side * HALF + LANES - offset, value, more)
                    sides.append(value)
                planes.append(Number(jnp.where(lane < HALF, sides[0], sides[1] if sides[1:] else 0.0)))
            values = real_dft(planes)
            for i in range(half):
                at = tile(t, i, edge)
                lower[0, at, :] = values[i].real
                imag = values[i].imag
                lower[1, at, :] = jnp.zeros((ROWS, LANES), jnp.float32) if imag is None else imag

        def densities_over_y(sides):
            steps(chunks, functools.partial(widen, sides), chunks)
            steps(tiles, functools.partial(over_y, sides), 3)

        with_sides(densities_over_y)

        @pl.when(turn == 0)
        def _():
            for copy in table_copies:
                copy.wait()

        @pl.when(turn + 1 < turns)
        def _():
            start_loads(turn + 1)

        def over_x(t):
            at = [across(t, i, edge) for i in range(edge)]
            values = dft([Number(lower[0, a, :], lower[1, a, :]) for a in at], -1)
            real = jnp.concatenate([value.real for value in values], axis=0)
            imag = jnp.concatenate([value.imag for value in values], axis=0)
            at = [tile(t, i, height) for i in range(edge)]
            factor = jnp.concatenate([screen_ref[a, :] for a in at], axis=0)
            real, imag = split_dot(real, imag, ahead_ref)
            real, imag = split_dot(real * factor, imag * factor, behind_ref)
            rows = [slice(i * ROWS, (i + 1) * ROWS) for i in range(edge)]
            values = dft([Number(real[r], imag[r]) for r in rows], 1)
            for i in range(edge):
                upper[0, at[i], :] = values[i].real
                upper[1, at[i], :] = values[i].imag

        steps(height // ROWS, over_x, 4)
        if second_part:
            @pl.when(turn == 0)
            def _():
                for copy in state_copies:
                    copy.wait()

        firsts = [first_of(slot) for slot, _ in picked]

        def back_y(sides, t):
            begin = pl.multiple_of(t * ROWS, ROWS)
            rows = pl.ds(begin, ROWS)
            at = [across(t, i, height) for i in range(half)]
            values = [Number(upper[0, a, :], upper[1, a, :]) for a in at]
            values = values + [values[edge - i].conj() for i in range(half, edge)]
            planes = real_back(values)
            for side in range(sides):
                forward = []
                for k in range(chunks):
                    value = None
                    for y in range(k * LANES // edge, edge):
                        begins = y * edge - k * LANES
                        if begins >= LANES:
                            break
                        shift = (begins - side * HALF) % LANES
                        piece = pltpu.roll(planes[y], shift, 1) if shift else planes[y]
                        value = piece if value is None else jnp.where(lane < begins, value, piece)
                    forward.append(value * moved[side, k, rows, :])
                    other = value * near_now[side, rows, k * LANES : (k + 1) * LANES]
                    dense[side, k, pl.ds(edge + begin, ROWS), :] = other
                at = [pl.ds(t * (ROWS * chunks) + k, ROWS, stride=chunks) for k in range(chunks)]
                sums = [act[firsts[side], at[k], :] + forward[k] for k in range(chunks)]
                for k in range(chunks):
                    act[firsts[side], at[k], :] = sums[k]

        with_sides(lambda sides: steps(tiles, functools.partial(back_y, sides), 3))

        if second_part:
            @pl.when(turn + 1 == turns)
            def _():
                for copy in act_copies:
                    copy.start()

        homes = []
        for side in range(2):
            slot = picked[side][0]
            homes.append(reach_of(slot) * orb_dev + lax.rem(second_of(slot), orb_dev))

        def send_back(sides, g):
            for side in range(sides):
                ks = [g * stretch + i for i in range(stretch)]
                values = shifted(dense.at[side], 2 + side, returns[side], 0, edge, ks)
                at = [
                    (i, t, pl.ds(t * (ROWS * chunks) + ks[i], ROWS, stride=chunks))
                    for i in range(stretch)
                    for t in range(tiles)
                ]
                sums = [
                    back[homes[side], a, :] + values[i][t * ROWS : (t + 1) * ROWS] for i, t, a in at
                ]
                for (i, t, a), value in zip(at, sums):
                    back[homes[side], a, :] = value

        with_sides(lambda sides: steps(chunks // stretch, functools.partial(send_back, sides), 3))
        return 0

    if not second_part:
        lax.fori_loop(0, turns, solve_two, 0)
        return

    @pl.when(found == 0)
    def _():
        for copy in state_copies:
            copy.start()
        for copy in state_copies:
            copy.wait()
        for copy in act_copies:
            copy.start()

    lax.fori_loop(0, turns, solve_two, 0)
    spans = ((0, orb_dev),)
    for begin in (orb_dev, 2 * orb_dev):
        spans += ((begin, 1), (begin + 1, orb_dev - 1))
    back_copies = [
        pltpu.make_async_copy(back.at[pl.ds(begin, count)], back_outs[i], out_sem.at[groups + i])
        for i, (begin, count) in enumerate(spans)
    ]
    for copy in back_copies:
        copy.start()
    for copy in act_copies + back_copies:
        copy.wait()


def reversed_bits(k, count):
    bits = count.bit_length() - 1
    return sum(((k >> i) & 1) << (bits - 1 - i) for i in range(bits))


def pair_terms(numbers, fragments, slots, tables, pieces, far, before=()):
    second_part = bool(before)
    orb_dev, edge, plane = pieces[0].shape
    groups = len(pieces)
    frag_size = groups * orb_dev
    chunks = plane // LANES
    rows = edge * chunks
    height = padded_half(edge)
    returns_count = (REACH + 1) * orb_dev
    shape = (edge, orb_dev, groups, fragments, slots)
    smem = pl.BlockSpec(memory_space=pltpu.SMEM)
    vmem = pl.BlockSpec(memory_space=pltpu.VMEM)
    hbm = pl.BlockSpec(memory_space=pltpu.HBM)
    f32 = jnp.float32
    sums = ((frag_size, rows, LANES), (returns_count, rows, LANES))
    out_shape = [jax.ShapeDtypeStruct(sum_shape, f32) for sum_shape in sums]
    out_specs, scratch = [vmem] * 2, []
    if second_part:
        out_shape = [jax.ShapeDtypeStruct((groups // 2, frag_size, rows // groups, LANES), f32)] * 2
        for count in (orb_dev, 1, orb_dev - 1, 1, orb_dev - 1):
            out_shape.append(jax.ShapeDtypeStruct((count, rows, LANES), f32))
        out_specs = [hbm] * 7
        scratch = [pltpu.VMEM(sum_shape, f32) for sum_shape in sums]
        scratch += [pltpu.SemaphoreType.DMA((2,)), pltpu.SemaphoreType.DMA((groups + 5,))]
    return pl.pallas_call(
        functools.partial(pair_kernel, shape, second_part),
        out_shape=out_shape,
        in_specs=[smem] + [hbm] * (3 + groups + len(far) + len(before)),
        out_specs=out_specs,
        scratch_shapes=scratch
        + [
            pltpu.VMEM((2, 2, edge, plane), f32),
            pltpu.VMEM((2, edge, plane), f32),
            pltpu.VMEM((2, chunks, 3 * edge, LANES), f32),
            pltpu.VMEM((2, chunks, edge, LANES), f32),
            pltpu.VMEM((2, chunks, 3 * edge, LANES), f32),
            pltpu.VMEM((2, height * edge, LANES), f32),
            pltpu.VMEM((2, height * edge, LANES), f32),
            pltpu.VMEM((4, -(-chunks // ROWS) * ROWS, LANES), f32),
            pltpu.SMEM((slots,), jnp.int32),
            pltpu.SemaphoreType.DMA((2, 2)),
            *[pltpu.VMEM(table.shape, table.dtype) for table in tables],
            pltpu.SemaphoreType.DMA((3,)),
        ],
        compiler_params=pltpu.CompilerParams(vmem_limit_bytes=30 << 20),
        name="late_pair_terms" if second_part else "early_pair_terms",
    )(numbers, *tables, *pieces, *far, *before)


def flatten_kernel(shape, places_ref, *refs):
    edge, orb_dev, groups = shape
    pieces, (flat_ref, slab_ref) = refs[:groups], refs[groups:]
    member = places_ref[1]
    chunks = edge * edge // LANES
    slab = slab_ref.shape[1]
    for k in range(groups):
        for o in range(orb_dev):
            def move(j, _):
                value = pieces[k][o, :, pl.ds(pl.multiple_of(j * LANES, LANES), LANES)]
                for t in range(edge // ROWS):
                    at = pl.ds(t * (ROWS * chunks) + j, ROWS, stride=chunks)
                    flat_ref[k * orb_dev + o, at, :] = value[t * ROWS : (t + 1) * ROWS]
                return 0

            lax.fori_loop(0, chunks, move, 0)
    slab_ref[...] = flat_ref[:, pl.ds(pl.multiple_of(member * slab, ROWS), slab), :]


def flatten_terms(places, pieces):
    orb_dev, edge, plane = pieces[0].shape
    groups = len(pieces)
    rows = edge * plane // LANES
    frag_size = groups * orb_dev
    smem = pl.BlockSpec(memory_space=pltpu.SMEM)
    vmem = pl.BlockSpec(memory_space=pltpu.VMEM)
    return pl.pallas_call(
        functools.partial(flatten_kernel, (edge, orb_dev, groups)),
        out_shape=(
            jax.ShapeDtypeStruct((frag_size, rows, LANES), jnp.float32),
            jax.ShapeDtypeStruct((frag_size, rows // groups, LANES), jnp.float32),
        ),
        in_specs=[smem] + [vmem] * groups,
        out_specs=(vmem, vmem),
        compiler_params=pltpu.CompilerParams(vmem_limit_bytes=24 << 20),
        name="flatten_terms",
    )(places, *pieces)


def products(lefts, rights, length, step):
    def add(i, sums):
        at = pl.ds(pl.multiple_of(i * step, ROWS), step)
        right = [ref[index, at, :].reshape(step // ROWS, ROWS, LANES) for ref, index in rights]
        out = []
        for n, (ref, index) in enumerate(lefts):
            left = ref[index, at, :].reshape(step // ROWS, ROWS, LANES)
            for m in range(len(rights)):
                out.append(sums[n * len(rights) + m] + jnp.sum(left * right[m], axis=0))
        return tuple(out)

    zero = jnp.zeros((ROWS, LANES), jnp.float32)
    return lax.fori_loop(0, length // step, add, (zero,) * (len(lefts) * len(rights)))


def placed(result, sums, rows, lanes):
    row = lax.broadcasted_iota(jnp.int32, result.shape, 0)
    lane = lax.broadcasted_iota(jnp.int32, result.shape, 1)
    for n, a in enumerate(rows):
        for m, b in enumerate(lanes):
            value = jnp.sum(sums[n * len(lanes) + m], keepdims=True)
            result = jnp.where((row == a) & (lane == b), result + value, result)
    return result


def step_of(length):
    return next(n for n in (72, 24, 8) if length % n == 0)


def action_kernel(shape, places_ref, phi_ref, kept_ref, *refs):
    orb_dev, groups, parts = shape
    arrived, (act_ref, share_ref) = refs[:parts], refs[parts:]
    member = places_ref[1]
    frag_size = orb_dev * groups
    slab = act_ref.shape[1]
    cut = frag_size // parts
    for i in range(parts):
        span = slice(i * cut, (i + 1) * cut)
        act_ref[span] = kept_ref[0, span] + arrived[i][0]
    rows = [(member ^ (a // orb_dev)) * orb_dev + a % orb_dev for a in range(frag_size)]
    result = jnp.zeros(share_ref.shape, jnp.float32)
    for half in range(0, frag_size, 4):
        bs = range(half, min(half + 4, frag_size))
        lefts, rights = [(phi_ref, a) for a in range(frag_size)], [(act_ref, b) for b in bs]
        result = placed(result, products(lefts, rights, slab, step_of(slab)), rows, bs)
    share_ref[...] = result


def action_terms(places, orb_dev, phi, kept, arrived):
    frag_size, slab = phi.shape[:2]
    smem = pl.BlockSpec(memory_space=pltpu.SMEM)
    vmem = pl.BlockSpec(memory_space=pltpu.VMEM)
    return pl.pallas_call(
        functools.partial(action_kernel, (orb_dev, frag_size // orb_dev, len(arrived))),
        out_shape=(
            jax.ShapeDtypeStruct((frag_size, slab, LANES), jnp.float32),
            jax.ShapeDtypeStruct((frag_size, LANES), jnp.float32),
        ),
        in_specs=[smem] + [vmem] * (2 + len(arrived)),
        out_specs=(vmem, vmem),
        compiler_params=pltpu.CompilerParams(vmem_limit_bytes=16 << 20),
        name="action_terms",
    )(places, phi, kept, *arrived)


def home_kernel(shape, places_ref, flat_ref, own_ref, *refs):
    edge, orb_dev, groups, first, count = shape
    if first == 0:
        (two_ref, twin_ref, relay_ref, share_ref), refs = refs[:4], refs[4:]
    else:
        (two_ref, one_ref), refs = refs[:2], refs[2:]
    outs, total = refs[:groups], refs[groups]
    fragment, member = places_ref[0], places_ref[1]
    frag_size = orb_dev * groups
    rows = flat_ref.shape[1]
    slab = rows // groups
    for i in range(count):
        value = own_ref[first + i] + two_ref[i]
        if first == 0:
            @pl.when(lax.rem(fragment, 2) == 1)
            def _():
                total[i] = value + twin_ref[i]

            @pl.when(lax.rem(fragment, 2) == 0)
            def _():
                total[i] = value + relay_ref[i]
        else:
            total[i] = value + one_ref[i]
    lefts, rights = [(flat_ref, a) for a in range(frag_size)], [(total, i) for i in range(count)]
    places = [(member ^ (a // orb_dev)) * orb_dev + a % orb_dev for a in range(frag_size)]
    result = share_ref[...] if first == 0 else jnp.zeros((frag_size, LANES), jnp.float32)
    sums = products(lefts, rights, rows, step_of(rows))
    result = placed(result, sums, places, [member * orb_dev + first + i for i in range(count)])
    result = result * (1.0 / float(edge**3))
    for k in range(groups):
        begin = pl.multiple_of((member ^ k) * slab, ROWS)
        for i in range(count):
            outs[k][i * slab : (i + 1) * slab, :] = total[i, pl.ds(begin, slab), :]
        outs[k][count * slab :, :] = result


def home_terms(places, edge, groups, flat, own, first, *came):
    frag_size, rows = flat.shape[:2]
    count = came[0].shape[0]
    smem = pl.BlockSpec(memory_space=pltpu.SMEM)
    vmem = pl.BlockSpec(memory_space=pltpu.VMEM)
    f32 = jnp.float32
    parcel = jax.ShapeDtypeStruct((count * rows // groups + frag_size, LANES), f32)
    return pl.pallas_call(
        functools.partial(home_kernel, (edge, frag_size // groups, groups, first, count)),
        out_shape=[parcel] * groups,
        in_specs=[smem] + [vmem] * (2 + len(came)),
        out_specs=[vmem] * groups,
        scratch_shapes=[pltpu.VMEM((count, rows, LANES), f32)],
        compiler_params=pltpu.CompilerParams(vmem_limit_bytes=16 << 20),
        name="home_terms",
    )(places, flat, own, *came)


def exchanged(value, axis, width):
    size = value.shape[axis]
    index = lax.broadcasted_iota(jnp.int32, value.shape, axis)
    below, above = pltpu.roll(value, width, axis), pltpu.roll(value, size - width, axis)
    return jnp.where((index & width) != 0, below, above)


def gradient_kernel(shape, places_ref, act_ref, phi_ref, *refs):
    edge, orb_dev, groups = shape
    heads, tails, refs = refs[:groups], refs[groups : 2 * groups], refs[2 * groups :]
    out_ref, lagrange_ref, hold = refs
    member = places_ref[1]
    frag_size = orb_dev * groups
    chunks = edge * edge // LANES
    slab_rows = edge // groups
    slab = slab_rows * chunks
    sums = [
        head[slab:, :] + tail[(orb_dev - 1) * slab :, :] for head, tail in zip(heads, tails)
    ]
    while len(sums) > 1:
        sums = [sums[i] + sums[i + 1] for i in range(0, len(sums), 2)]
    square = jnp.concatenate([sums[0], jnp.zeros((LANES - frag_size, LANES), jnp.float32)], axis=0)
    lagrange = 0.5 * (square + square.T)[:frag_size, :]
    lagrange_ref[...] = lagrange[:, :frag_size]
    bit = 1
    while bit < groups:
        turned = exchanged(exchanged(lagrange, 0, bit * orb_dev), 1, bit * orb_dev)
        lagrange = jnp.where((member & bit) != 0, turned, lagrange)
        bit *= 2

    for k in range(groups):
        for o in range(orb_dev):
            a = (member ^ k) * orb_dev + o
            came = heads[k][:slab, :] if o == 0 else tails[k][(o - 1) * slab : o * slab, :]
            value = act_ref[a] + came
            for b in range(frag_size):
                factor = lagrange[b : b + 1, k * orb_dev + o : k * orb_dev + o + 1]
                value = value - factor * phi_ref[b]
            hold[pl.ds(pl.multiple_of(a * slab, ROWS), slab), :] = value
    for x in range(slab_rows):
        for j in range(chunks):
            value = hold[pl.ds(x * chunks + j, frag_size, stride=slab), :]
            out_ref[x, :, j * LANES : (j + 1) * LANES] = value


def gradient_terms(places, edge, act, phi, heads, tails):
    groups = len(heads)
    frag_size, slab = act.shape[:2]
    smem = pl.BlockSpec(memory_space=pltpu.SMEM)
    vmem = pl.BlockSpec(memory_space=pltpu.VMEM)
    f32 = jnp.float32
    gradient, lagrange = pl.pallas_call(
        functools.partial(gradient_kernel, (edge, frag_size // groups, groups)),
        out_shape=(
            jax.ShapeDtypeStruct((edge // groups, frag_size, edge * edge), f32),
            jax.ShapeDtypeStruct((frag_size, frag_size), f32),
        ),
        in_specs=[smem] + [vmem] * (2 + 2 * groups),
        out_specs=(vmem, vmem),
        scratch_shapes=[pltpu.VMEM((frag_size * slab, LANES), f32)],
        compiler_params=pltpu.CompilerParams(vmem_limit_bytes=16 << 20),
        name="gradient_terms",
    )(places, act, phi, *heads, *tails)
    return gradient.transpose(1, 0, 2), lagrange


def together(*arrays):
    return lax.optimization_barrier(arrays)


def to_fragment(block, distance, senders=None):
    devices = lax.axis_size("orb")
    senders = range(devices) if senders is None else range(senders, devices, 2)
    return lax.ppermute(block, "orb", [(i, (i + distance) % devices) for i in senders])


def with_twin(block):
    return lax.ppermute(block, "orb", [(i, i ^ 1) for i in range(lax.axis_size("orb"))])


def with_member(block, bit):
    return lax.ppermute(block, "grp", [(i, i ^ bit) for i in range(lax.axis_size("grp"))])


def by_member(parcels, after=None):
    groups = len(parcels)
    received = list(parcels)
    bit = groups // 2
    while bit:
        for k in reversed(range(groups)):
            if k & bit:
                received[k] = with_member(received[k], bit)
        if after is not None and bit == groups // 2:
            after, *received[bit:] = together(after, *received[bit:])
        bit //= 2
    return received, after


def shards(orbitals, kernel, anchors, pair_count, pair_first, pair_second, pair_reach):
    groups = lax.axis_size("grp")
    orb_dev, edge, plane = orbitals.shape
    places = jnp.stack([lax.axis_index("orb"), lax.axis_index("grp")]).astype(jnp.int32)

    numbers = [places, pair_count, pair_first, pair_second, pair_reach, anchors.reshape(-1)]
    screen, numbers, *tables = screen_terms(jnp.concatenate(numbers), kernel)
    two = to_fragment(orbitals, -2)
    twin = with_twin(orbitals[:1])
    pieces = {0: orbitals}
    bit = groups // 2
    while bit:
        for k in list(pieces):
            pieces[k ^ bit] = with_member(pieces[k], bit)
        if bit == groups // 2:
            two, twin, tail, pieces[bit], screen, numbers, *tables = together(
                two, twin, orbitals[1:], pieces[bit], screen, numbers, *tables
            )
            one = to_fragment(tail, -1)
            relay = to_fragment(twin, -2, 1)
        bit //= 2
    pieces = [pieces[k] for k in range(groups)]
    tables = [screen, *tables]
    sizes = (anchors.shape[0], pair_first.shape[0])
    before = pair_terms(numbers, *sizes, tables, pieces, [twin, two])
    kept, sent, own, one_head, one_tail, two_head, two_tail = pair_terms(
        numbers, *sizes, tables, pieces, [twin, two, relay, one], before
    )

    two_tail = to_fragment(two_tail, 2)
    twin = with_twin(one_head)
    bit = 1
    arrived = with_member(sent, bit)
    while 2 * bit < groups:
        kept = kept + arrived
        if bit == 1:
            _, twin, one_tail = together(kept, twin, one_tail)
        half = kept.shape[0] // 2
        bit *= 2
        arrived, kept = with_member(kept[half:], bit), kept[:half]
    one_tail = to_fragment(one_tail, 1)
    relay = to_fragment(twin, 2, 0)
    two_tail, two_head = together(two_tail, two_head)
    two_head = to_fragment(two_head, 2)

    flat, phi = flatten_terms(places, pieces)
    tails = home_terms(places, edge, groups, flat, own, 1, two_tail, one_tail)
    tails, two_head = by_member(tails, two_head)
    act, share = action_terms(places, orb_dev, phi, kept, [arrived])
    heads, _ = by_member(
        home_terms(places, edge, groups, flat, own, 0, two_head, twin, relay, share)
    )
    gradient, lagrange = gradient_terms(places, edge, act, phi, heads, tails)
    return (gradient, lagrange[None])


def solution(mesh):
    placed = (P(("orb", "grp"), None, None), P(), P(), P("orb"), P("orb"), P("orb"), P("orb"))
    return jax.shard_map(
        shards,
        mesh=mesh,
        in_specs=placed,
        out_specs=(P("orb", "grp", None), P("orb", None, None)),
        check_vma=False,
    )
```
